32 devices in a mesh: wide: 16 (over z, y, core), narrow: 2 (over x).
Axes of the slice: x: 2, y: 2, z: 4, core: 2. Of those that a mesh axis runs over, the one named last changes fastest.
Arguments:
- features: bfloat16 [16, 256, 2, 256], P(None, 'wide', None, 'narrow'), may hold values from -6 to 6
- cotangent: bfloat16 [16, 256, 2, 256], P(None, 'wide', None, 'narrow'), may hold values from -6 to 6
- coarse_weight: bfloat16 [32, 16, 3, 3, 3], replicated, may hold values from -0.3125 to 0.3125
- fine_weight: bfloat16 [16, 48, 3, 3, 3], replicated, may hold values from -0.15625 to 0.15625
Outputs:
- output: bfloat16 [16, 256, 2, 256], P(None, 'wide', None, 'narrow')
- grad_features: bfloat16 [16, 256, 2, 256], P(None, 'wide', None, 'narrow')
- grad_fine: float32 [16, 48, 3, 3, 3], replicated
- grad_coarse: float32 [32, 16, 3, 3, 3], replicated
The draws below stay inside these ranges and needn't reach their ends.
All inputs are finite; a program needn't handle non-finite values.
Results may differ from the reference program's by a relative error of at most 0.012.
Values may be sent and summed in bfloat16 or wider, within the bound.
No kernel may reach another device: no remote copies, remote signals or barrier semaphores. Data moves between devices by JAX's collectives and lax.ppermute only.
A program may use at most 64 MiB of HBM per device.

```python
import math
import jax
import jax.numpy as jnp
from jax import lax

C1 = 16
C2 = 32
PLANES = 2
NX = 256
NY = 256
CELLS = 131072


def shard_levels(stream_key, dims, cuts, least, largest):
    level = 1.0
    for position, blocks in cuts:
        heights = jax.random.uniform(jax.random.fold_in(jax.random.fold_in(stream_key, 6), position), (blocks,), jnp.float32, least / len(cuts), largest / len(cuts))
        level = level * jnp.repeat(jnp.exp(heights), dims[position] // blocks).reshape((-1,) + (1,) * (len(dims) - 1 - position))
    return level


def centred(stream_key, extent, scale, most, cuts=(), kind=jnp.bfloat16):
    entries = jax.random.normal(stream_key, extent, jnp.float32) * scale
    if len(cuts) > 0:
        entries = shard_levels(stream_key, extent, cuts, -0.22, 0.18) * entries
    return jnp.clip(entries, min=-most, max=most).astype(kind)


def setup_inputs(seed: int = 0) -> dict:
    key_of = jax.random.split(jax.random.key(seed), 5)
    features = centred(key_of[0], (C1, NY, PLANES, NX), 1.0, 6.0, ((1, 16), (3, 2)))
    cotangent = centred(key_of[1], (C1, NY, PLANES, NX), 1.0, 6.0, ((1, 16), (3, 2)))
    coarse_weight = centred(key_of[2], (C2, C1, 3, 3, 3), (27 * C1) ** -0.5, 0.3125)
    fine_weight = centred(key_of[3], (C1, C1 + C2, 3, 3, 3), (27 * (C1 + C2)) ** -0.5, 0.15625)
    return dict(features=features, cotangent=cotangent, coarse_weight=coarse_weight, fine_weight=fine_weight)


def pad_all(field):
    return jnp.pad(field, ((0, 0), (1, 1), (1, 1), (1, 1)))

def correlate(padded, kernel):
    result = lax.conv_general_dilated(padded[None].astype(jnp.float32), kernel.astype(jnp.float32), (1, 1, 1), 'VALID', dimension_numbers=('NCHWD', 'OIHWD', 'NCHWD'), precision=lax.Precision.HIGHEST)
    return result[0]

def flipped(kernel):
    return jnp.transpose(kernel[:, :, ::-1, ::-1, ::-1], (1, 0, 2, 3, 4))

def pool_sum(field):
    chans, rows, planes, cols = field.shape
    return field.reshape(chans, rows // 2, 2, planes // 2, 2, cols // 2, 2).sum(axis=(2, 4, 6))

def upsample(field):
    chans, rows, planes, cols = field.shape
    spread = jnp.broadcast_to(field[:, :, None, :, None, :, None], (chans, rows, 2, planes, 2, cols, 2))
    return spread.reshape(chans, 2 * rows, 2 * planes, 2 * cols)

def silu_slope(value):
    sig = jax.nn.sigmoid(value)
    return sig * (1.0 + value * (1.0 - sig))

def weight_grad(padded, grad):
    outs, rows, planes, cols = grad.shape
    grad_wide = grad.astype(jnp.float32)
    pieces = []
    for off_y in range(3):
        for off_z in range(3):
            for off_x in range(3):
                window = padded[:, off_y:off_y + rows, off_z:off_z + planes, off_x:off_x + cols].astype(jnp.float32)
                pieces.append(jnp.einsum('oyzx,cyzx->oc', grad_wide, window, precision=lax.Precision.HIGHEST))
    stacked = jnp.stack(pieces, -1)
    return stacked.reshape(outs, padded.shape[0], 3, 3, 3)

def reference(features, cotangent, coarse_weight, fine_weight):
    pooled = (pool_sum(features.astype(jnp.float32)) / 8.0).astype(jnp.bfloat16)
    pooled_pad = pad_all(pooled)
    coarse_pre = correlate(pooled_pad, coarse_weight)
    coarse_act = jax.nn.silu(coarse_pre).astype(jnp.bfloat16)
    upsampled = upsample(coarse_act)
    joined_pad = pad_all(jnp.concatenate([features, upsampled], 0))
    output = correlate(joined_pad, fine_weight).astype(jnp.bfloat16)
    grad_fine = weight_grad(joined_pad, cotangent) / math.sqrt(CELLS)
    grad_joined = correlate(pad_all(cotangent), flipped(fine_weight))
    grad_act = pool_sum(grad_joined[C1:]).astype(jnp.bfloat16)
    grad_pre = (grad_act.astype(jnp.float32) * silu_slope(coarse_pre)).astype(jnp.bfloat16)
    grad_coarse = weight_grad(pooled_pad, grad_pre) / math.sqrt(CELLS // 8)
    grad_pooled = correlate(pad_all(grad_pre), flipped(coarse_weight)).astype(jnp.bfloat16)
    grad_features = (grad_joined[:C1] + upsample(grad_pooled).astype(jnp.float32) / 8.0).astype(jnp.bfloat16)
    return (output, grad_features, grad_fine, grad_coarse)
```

```python
import functools
import math

import jax
import jax.numpy as jnp
from jax import lax
from jax.experimental import pallas as pl
from jax.experimental.pallas import tpu as pltpu
from jax.sharding import PartitionSpec as P

C1, C2 = 16, 32
ROWS, COLS = 16, 128
HALO = 4
EXT = ROWS + 2 * HALO
BF, F32 = jnp.bfloat16, jnp.float32
VMEM_LIMIT = 48 * 1024 * 1024


def lanes_of(shape):
    return lax.broadcasted_iota(jnp.int32, shape, len(shape) - 1)


def row(index, count=1):
    return slice(index * COLS, (index + count) * COLS)


def pack_kernel(sides, f_ref, g_ref, s_ref, up_ref, down_ref, strip_ref, wide_ref):
    lane = lanes_of((C1, COLS))
    place = lax.axis_index("narrow")
    for a, ref in enumerate((f_ref, g_ref)):
        wide_ref[...] = ref[...].astype(F32)
        for z in range(2):
            chans = slice(a * 32 + z * 16, a * 32 + z * 16 + 16)
            strips = [jnp.zeros((C1, COLS), F32) for _ in range(sides)]
            for y in range(ROWS):
                value = wide_ref[pl.ds(2 * y + z, C1, stride=2 * ROWS), :]
                s_ref[chans, row(y)] = value.astype(BF)
                start = HALO * (y + HALO)
                inside = (lane >= start) & (lane < start + HALO)
                for side in range(sides):
                    if sides == 2:
                        shift = start + HALO * side
                    else:
                        shift = start + HALO * (1 - place)
                    strips[side] = jnp.where(inside, pltpu.roll(value, shift, 1), strips[side])
            for side in range(sides):
                strip_ref[chans, row(side)] = strips[side].astype(BF)
                turned = pltpu.roll(strips[side], 64, 1)
                up_ref[chans, row(HALO + side)] = jnp.where(lane < 16, turned, 0.0).astype(BF)
                down_ref[chans, row(HALO + side)] = jnp.where(
                    (lane >= 80) & (lane < 96), turned, 0.0
                ).astype(BF)
    up_ref[:, row(0, HALO)] = s_ref[:, row(ROWS - HALO, HALO)]
    down_ref[:, row(0, HALO)] = s_ref[:, row(0, HALO)]


def pack(features, cotangent, sides):
    flat = lambda a: a.reshape(C1 * ROWS * 2, COLS)
    message = jax.ShapeDtypeStruct((64, (HALO + sides) * COLS), BF)
    return pl.pallas_call(
        functools.partial(pack_kernel, sides),
        out_shape=(
            jax.ShapeDtypeStruct((64, ROWS * COLS), BF),
            message,
            message,
            jax.ShapeDtypeStruct((64, sides * COLS), BF),
        ),
        scratch_shapes=[pltpu.VMEM((C1 * ROWS * 2, COLS), F32)],
        compiler_params=pltpu.CompilerParams(vmem_limit_bytes=VMEM_LIMIT),
        cost_estimate=pl.CostEstimate(flops=10**6, bytes_accessed=10**6, transcendentals=0),
        name="pack",
    )(flat(features), flat(cotangent))


def turn(main, side, by):
    lane = lanes_of(main.shape)
    a, b = pltpu.roll(main, (-by) % COLS, 1), pltpu.roll(side, (-by) % COLS, 1)
    crossed = lane >= COLS - by if by > 0 else lane < -by
    return jnp.where(crossed, b, a), jnp.where(crossed, a, b)


def pair_sum(value):
    lane = lanes_of(value.shape)
    other = jnp.where(lane % 2 == 0, pltpu.roll(value, COLS - 1, 1), pltpu.roll(value, 1, 1))
    return value + other


def dot(a, b):
    return jnp.dot(a, b, preferred_element_type=F32)


def dot_nt(a, b):
    return lax.dot_general(a, b, (((1,), (1,)), ((), ())), preferred_element_type=F32)


def block_kernel(
    counts,
    s_ref, up_ref, down_ref, left_ref, right_ref, wo_ref, wg_ref, wc_ref, wq_ref,
    out_ref, gf_ref, gw_ref,
    ext_ref, side_ref, jst_ref, gst_ref, gsb_ref, pst_ref, psb_ref, qst_ref,
    pre_ref, prb_ref, ro_ref, rg_ref, rgb_ref, rq_ref, gp_ref, flat_ref, fa_ref, fb_ref, fc_ref,
):
    w, n = lax.axis_index("wide"), lax.axis_index("narrow")
    lane32 = lanes_of((C2, COLS))
    lane64 = lanes_of((64, COLS))
    flag = lambda is_there: jnp.where(is_there, 1.0, 0.0)
    has_left, has_right = flag(n > 0), flag(n < counts[1] - 1)
    has_above, has_below = flag(w > 0), flag(w < counts[0] - 1)

    ext_ref[:, row(0, HALO)] = up_ref[:, row(0, HALO)]
    ext_ref[:, row(HALO, ROWS)] = s_ref[...]
    ext_ref[:, row(HALO + ROWS, HALO)] = down_ref[:, row(0, HALO)]

    left = left_ref[...].astype(F32) * has_left
    right = right_ref[...].astype(F32) * has_right
    for r in range(EXT):
        at_right = pltpu.roll(right, (-HALO * r) % COLS, 1)
        at_left = pltpu.roll(left, (COLS - HALO - HALO * r) % COLS, 1)
        side_ref[:, row(r)] = jnp.where(
            lane64 < HALO, at_right, jnp.where(lane64 >= COLS - HALO, at_left, 0.0)
        ).astype(BF)

    half = [None, None]
    for r in range(EXT):
        both = [ref[0:32, row(r)].astype(F32) for ref in (ext_ref, side_ref)]
        if r % 2 == 0:
            half = both
        else:
            mean = []
            for first, second in zip(half, both):
                total = first + second
                mean.append((pair_sum(total[0:16] + total[16:32]) * 0.125).astype(BF).astype(F32))
            for d in range(3):
                a, b = mean if d == 1 else turn(mean[0], mean[1], 2 * (d - 1))
                pst_ref[d * 16 : d * 16 + 16, row(r // 2)] = a.astype(BF)
                psb_ref[d * 16 : d * 16 + 16, row(r // 2)] = b.astype(BF)
        if HALO - 1 <= r <= HALO + ROWS:
            at = r - HALO + 1
            for d in range(3):
                a = both[0] if d == 1 else turn(both[0], both[1], d - 1)[0]
                jst_ref[d * 64 : d * 64 + 32, row(at)] = a.astype(BF)

    pre_ref[...] = dot(wc_ref[...], pst_ref[...])
    prb_ref[...] = dot(wc_ref[...], psb_ref[...])

    for at in range(22):
        a0 = ext_ref[32:64, row(at + 1)].astype(F32)
        b0 = side_ref[32:64, row(at + 1)].astype(F32)
        for d in range(3):
            a, b = (a0, b0) if d == 1 else turn(a0, b0, d - 1)
            gst_ref[d * 32 : d * 32 + 32, row(at)] = a.astype(BF)
            gsb_ref[d * 32 : d * 32 + 32, row(at)] = b.astype(BF)
    rg_ref[...] = dot(wg_ref[...], gst_ref[...])
    for d in range(3):
        rgb_ref[d * 32 : d * 32 + 32, :] = dot(
            wg_ref[d * 64 + 32 : d * 64 + 64, :], gsb_ref[...]
        )

    for at in range(10):
        keep = has_above if at == 0 else has_below if at == 9 else 1.0
        keep_side = keep * jnp.where(lane32 < 64, has_right, has_left)
        act, grad = [], []
        for ref, joined_ref, base, size, kept in (
            (pre_ref, rg_ref, 32, 64, keep),
            (prb_ref, rgb_ref, 0, 32, keep_side),
        ):
            value = (
                ref[0:32, row(at)] + ref[32:64, row(at + 1)] + ref[64:96, row(at + 2)]
            )
            sig = 1.0 / (1.0 + jnp.exp(-value))
            act.append((value * sig * kept).astype(BF).astype(F32))
            total = jnp.zeros((C2, COLS), F32)
            for r in (2 * at, 2 * at + 1):
                for d in range(3):
                    lo = d * size + base
                    total = total + joined_ref[lo : lo + 32, row(r + d)]
            grad_act = pair_sum(total).astype(BF).astype(F32)
            grad_pre = grad_act * (sig * (1.0 + value * (1.0 - sig)))
            grad.append((grad_pre * kept).astype(BF).astype(F32))
        for d in range(3):
            a = act[0] if d == 1 else turn(act[0], act[1], d - 1)[0]
            a = a.astype(BF)
            for r in (2 * at - 1, 2 * at):
                if 0 <= r < 18:
                    jst_ref[d * 64 + 32 : d * 64 + 64, row(r)] = a
            q = grad[0] if d == 1 else turn(grad[0], grad[1], 2 * (d - 1))[0]
            qst_ref[d * 32 : d * 32 + 32, row(at)] = q.astype(BF)

    ro_ref[...] = dot(wo_ref[...], jst_ref[...])
    for y in range(ROWS):
        value = ro_ref[0:32, row(y)] + ro_ref[32:64, row(y + 1)] + ro_ref[64:96, row(y + 2)]
        for z in range(2):
            flat_ref[pl.ds(2 * y + z, C1, stride=2 * ROWS), :] = value[z * 16 : z * 16 + 16]
    out_ref[...] = flat_ref[...].astype(BF)

    rq_ref[...] = dot(wq_ref[...], qst_ref[...])
    for at in range(ROWS // 2):
        pooled = rq_ref[0:16, row(at)] + rq_ref[16:32, row(at + 1)] + rq_ref[32:48, row(at + 2)]
        pooled = pooled.astype(BF).astype(F32) * 0.125
        for y in (2 * at, 2 * at + 1):
            for z in range(2):
                total = pooled
                for d in range(3):
                    lo = d * 64 + z * 16
                    total = total + rg_ref[lo : lo + 16, row(y + 2 + d)]
                flat_ref[pl.ds(2 * y + z, C1, stride=2 * ROWS), :] = total
    gf_ref[...] = flat_ref[...].astype(BF)

    own = row(1, ROWS)
    fa_ref[0:16, :] = jst_ref[64:80, own]
    fa_ref[16:48, :] = jst_ref[96:128, own]
    fa_ref[48:64, :] = jst_ref[64:80, own]
    fa_ref[64:96, :] = jst_ref[96:128, own]
    fa_ref[96:128, :] = jnp.zeros((32, ROWS * COLS), BF)
    fb_ref[0:48, :] = jst_ref[80:128, own]
    fb_ref[48:96, :] = jst_ref[80:128, own]
    fb_ref[96:128, :] = jnp.zeros((32, ROWS * COLS), BF)
    fc_ref[0:96, :] = jnp.zeros((96, 8 * COLS), BF)
    fc_ref[96:128, :] = qst_ref[32:64, row(1, 8)]
    fine, coarse = {}, {}
    for ky in range(3):
        shifted = gst_ref[:, row(4 - ky, ROWS)]
        ra, rb = dot_nt(shifted, fa_ref[...]), dot_nt(shifted, fb_ref[...])
        rc = dot_nt(pst_ref[:, row(1 + ky, 8)], fc_ref[...])
        for kx in range(3):
            lo = (2 - kx) * 32
            fine[ky, 0, kx] = ra[lo + 16 : lo + 32]
            fine[ky, 1, kx] = ra[lo : lo + 16] + rb[lo + 16 : lo + 32]
            fine[ky, 2, kx] = rb[lo : lo + 16]
            coarse[ky, kx] = rc[kx * 16 : kx * 16 + 16] * 0.5
    lane16 = lanes_of((16, COLS))
    order = [(ky, kz, kx) for ky in range(3) for kz in range(3) for kx in range(3)]
    for i in range(16):
        value = jnp.zeros((16, COLS), F32)
        if i < 14:
            value = jnp.where(lane16 < 48, fine[order[i]], value)
        if i < 13:
            value = jnp.where((lane16 >= 48) & (lane16 < 96), fine[order[14 + i]], value)
        if i < 9:
            value = jnp.where(lane16 >= 96, coarse[i // 3, i % 3], value)
        gw_ref[i * 16 : i * 16 + 16, :] = value


def block(counts, operands):
    cells = (C1 * ROWS * 2, COLS)
    v = lambda rows_, lanes_, kind: pltpu.VMEM((rows_, lanes_ * COLS), kind)
    return pl.pallas_call(
        functools.partial(block_kernel, counts),
        out_shape=(
            jax.ShapeDtypeStruct(cells, BF),
            jax.ShapeDtypeStruct(cells, BF),
            jax.ShapeDtypeStruct((256, COLS), F32),
        ),
        scratch_shapes=[
            v(64, EXT, BF), v(64, EXT, BF),
            v(192, 18, BF),
            v(96, 22, BF), v(96, 22, BF),
            v(48, 12, BF), v(48, 12, BF),
            v(96, 10, BF),
            v(96, 12, F32), v(96, 12, F32),
            v(96, 18, F32),
            v(192, 22, F32), v(96, 22, F32),
            v(48, 10, F32),
            v(32, 8, BF),
            pltpu.VMEM(cells, F32),
            v(128, ROWS, BF), v(128, ROWS, BF), v(128, 8, BF),
        ],
        compiler_params=pltpu.CompilerParams(vmem_limit_bytes=VMEM_LIMIT),
        cost_estimate=pl.CostEstimate(flops=10**9, bytes_accessed=4 * 10**6, transcendentals=10**5),
        name="block",
    )(*operands)


def spread_kernel(fine_scale, coarse_scale, sum_ref, fine_ref, coarse_ref):
    for i in range(27):
        if i < 14:
            value = sum_ref[i * 16 : i * 16 + 16, :]
        else:
            value = pltpu.roll(sum_ref[(i - 14) * 16 : (i - 14) * 16 + 16, :], 80, 1)
        fine_ref[i * 16 : i * 16 + 16, :] = value[:, 0:48] * fine_scale
        ky, kz, kx = i // 9, i // 3 % 3, i % 3
        if kz == 1:
            at = (ky * 3 + kx) * 16
            value = pltpu.roll(sum_ref[at : at + 16, :], 32, 1)[:, 0:32] * coarse_scale
        else:
            value = jnp.zeros((16, 32), F32)
        coarse_ref[i * 16 : i * 16 + 16, :] = value


def spread(total, fine_scale, coarse_scale):
    return pl.pallas_call(
        functools.partial(spread_kernel, fine_scale, coarse_scale),
        out_shape=(
            jax.ShapeDtypeStruct((432, 48), F32),
            jax.ShapeDtypeStruct((432, 32), F32),
        ),
        compiler_params=pltpu.CompilerParams(vmem_limit_bytes=VMEM_LIMIT),
        name="spread",
    )(total)


def weight_matrices(coarse_weight, fine_weight):
    fine = jnp.transpose(fine_weight, (2, 3, 4, 0, 1))
    planes = []
    for zo in range(2):
        first, second = fine[:, 1 - zo], fine[:, 2 - zo]
        both = (first[..., C1:].astype(F32) + second[..., C1:].astype(F32)).astype(BF)
        planes.append(jnp.concatenate([first[..., :C1], second[..., :C1], both], -1))
    stacked = jnp.stack(planes, 1)
    wo = jnp.transpose(stacked, (0, 1, 3, 2, 4)).reshape(96, 192)
    wg = jnp.transpose(stacked[::-1, :, ::-1], (0, 4, 2, 1, 3)).reshape(192, 96)
    middle = coarse_weight[:, :, :, 1, :]
    wc = jnp.transpose(middle, (2, 0, 3, 1)).reshape(96, 48)
    wq = jnp.transpose(middle[:, :, ::-1, ::-1], (2, 1, 3, 0)).reshape(48, 96)
    return wo, wg, wc, wq


def shards(features, cotangent, coarse_weight, fine_weight):
    wide, narrow = lax.axis_size("wide"), lax.axis_size("narrow")
    matrices = weight_matrices(coarse_weight, fine_weight)
    sides = 1 if narrow == 2 else 2
    own, up, down, strip = pack(features, cotangent, sides)
    above = lax.ppermute(up, "wide", [(i, i + 1) for i in range(wide - 1)])
    below = lax.ppermute(down, "wide", [(i + 1, i) for i in range(wide - 1)])
    strip = strip + above[:, HALO * COLS :] + below[:, HALO * COLS :]
    if sides == 1:
        left = right = lax.ppermute(strip, "narrow", [(0, 1), (1, 0)])
    else:
        right = lax.ppermute(strip[:, :COLS], "narrow", [(i + 1, i) for i in range(narrow - 1)])
        left = lax.ppermute(strip[:, COLS:], "narrow", [(i, i + 1) for i in range(narrow - 1)])
    output, grad_features, grads = block(
        (wide, narrow), (own, above, below, left, right) + matrices
    )
    devices = wide * narrow
    share = -(-256 // devices)
    grads = jnp.pad(grads, ((0, share * devices - 256), (0, 0))).reshape(devices, share, COLS)
    both = ("wide", "narrow")
    parts = lax.all_to_all(grads, both, 0, 0, tiled=True)
    total = jnp.broadcast_to(jnp.sum(parts, 0, keepdims=True), parts.shape)
    total = lax.all_to_all(total, both, 0, 0, tiled=True)
    total = total.reshape(share * devices, COLS)[:256]
    all_cells = features.shape[1] * features.shape[2] * features.shape[3] * devices
    grad_fine, grad_coarse = spread(
        total, 1.0 / math.sqrt(all_cells), 1.0 / math.sqrt(all_cells // 8)
    )
    grad_fine = jnp.transpose(grad_fine.reshape(3, 3, 3, C1, C1 + C2), (3, 4, 0, 1, 2))
    grad_coarse = jnp.transpose(grad_coarse.reshape(3, 3, 3, C1, C2), (4, 3, 0, 1, 2))
    return (
        output.reshape(features.shape),
        grad_features.reshape(features.shape),
        grad_fine,
        grad_coarse,
    )


def solution(mesh):
    placed = P(None, "wide", None, "narrow")
    return jax.shard_map(
        shards,
        mesh=mesh,
        in_specs=(placed, placed, P(), P()),
        out_specs=(placed, placed, P(), P()),
        check_vma=False,
    )
```

```python
import functools
import math

import jax
import jax.numpy as jnp
from jax import lax
from jax.experimental import pallas as pl
from jax.experimental.pallas import tpu as pltpu
from jax.sharding import PartitionSpec as P

C1, C2 = 16, 32
ROWS, COLS = 16, 128
HALO = 4
EXT = ROWS + 2 * HALO
BF, F32 = jnp.bfloat16, jnp.float32
WIDE = ("far", "near")
VMEM_LIMIT = 48 * 1024 * 1024


def lanes_of(shape):
    return lax.broadcasted_iota(jnp.int32, shape, len(shape) - 1)


def row(index, count=1):
    return slice(index * COLS, (index + count) * COLS)


def pack_kernel(sides, f_ref, g_ref, s_ref, up_ref, down_ref, strip_ref, wide_ref):
    lane = lanes_of((C1, COLS))
    place = lax.axis_index("narrow")
    for a, ref in enumerate((f_ref, g_ref)):
        wide_ref[...] = ref[...].astype(F32)
        for z in range(2):
            chans = slice(a * 32 + z * 16, a * 32 + z * 16 + 16)
            strips = [jnp.zeros((C1, COLS), F32) for _ in range(sides)]
            for y in range(ROWS):
                value = wide_ref[pl.ds(2 * y + z, C1, stride=2 * ROWS), :]
                s_ref[chans, row(y)] = value.astype(BF)
                start = HALO * (y + HALO)
                inside = (lane >= start) & (lane < start + HALO)
                for side in range(sides):
                    if sides == 2:
                        shift = start + HALO * side
                    else:
                        shift = start + HALO * (1 - place)
                    strips[side] = jnp.where(inside, pltpu.roll(value, shift, 1), strips[side])
            for side in range(sides):
                strip_ref[chans, row(side)] = strips[side].astype(BF)
                turned = pltpu.roll(strips[side], 64, 1)
                up_ref[chans, row(HALO + side)] = jnp.where(lane < 16, turned, 0.0).astype(BF)
                down_ref[chans, row(HALO + side)] = jnp.where(
                    (lane >= 80) & (lane < 96), turned, 0.0
                ).astype(BF)
    up_ref[:, row(0, HALO)] = s_ref[:, row(ROWS - HALO, HALO)]
    down_ref[:, row(0, HALO)] = s_ref[:, row(0, HALO)]


def pack(features, cotangent, sides):
    flat = lambda a: a.reshape(C1 * ROWS * 2, COLS)
    message = jax.ShapeDtypeStruct((64, (HALO + sides) * COLS), BF)
    return pl.pallas_call(
        functools.partial(pack_kernel, sides),
        out_shape=(
            jax.ShapeDtypeStruct((64, ROWS * COLS), BF),
            message,
            message,
            jax.ShapeDtypeStruct((64, sides * COLS), BF),
        ),
        scratch_shapes=[pltpu.VMEM((C1 * ROWS * 2, COLS), F32)],
        compiler_params=pltpu.CompilerParams(vmem_limit_bytes=VMEM_LIMIT),
        cost_estimate=pl.CostEstimate(flops=10**6, bytes_accessed=10**6, transcendentals=0),
        name="pack",
    )(flat(features), flat(cotangent))


def turn(main, side, by):
    lane = lanes_of(main.shape)
    a, b = pltpu.roll(main, (-by) % COLS, 1), pltpu.roll(side, (-by) % COLS, 1)
    crossed = lane >= COLS - by if by > 0 else lane < -by
    return jnp.where(crossed, b, a), jnp.where(crossed, a, b)


def pair_sum(value):
    lane = lanes_of(value.shape)
    other = jnp.where(lane % 2 == 0, pltpu.roll(value, COLS - 1, 1), pltpu.roll(value, 1, 1))
    return value + other


def dot(a, b):
    return jnp.dot(a, b, preferred_element_type=F32)


def dot_nt(a, b):
    return lax.dot_general(a, b, (((1,), (1,)), ((), ())), preferred_element_type=F32)


def block_kernel(
    counts,
    s_ref, up_ref, down_ref, left_ref, right_ref, wo_ref, wg_ref, wc_ref, wq_ref,
    out_ref, gf_ref, gw_ref,
    ext_ref, side_ref, jst_ref, gst_ref, gsb_ref, pst_ref, psb_ref, qst_ref,
    pre_ref, prb_ref, ro_ref, rg_ref, rgb_ref, rq_ref, gp_ref, flat_ref, fa_ref, fb_ref, fc_ref,
):
    w, n = lax.axis_index(WIDE), lax.axis_index("narrow")
    lane32 = lanes_of((C2, COLS))
    lane64 = lanes_of((64, COLS))
    flag = lambda is_there: jnp.where(is_there, 1.0, 0.0)
    has_left, has_right = flag(n > 0), flag(n < counts[1] - 1)
    has_above, has_below = flag(w > 0), flag(w < counts[0] - 1)

    ext_ref[:, row(0, HALO)] = up_ref[:, row(0, HALO)]
    ext_ref[:, row(HALO, ROWS)] = s_ref[...]
    ext_ref[:, row(HALO + ROWS, HALO)] = down_ref[:, row(0, HALO)]

    left = left_ref[...].astype(F32) * has_left
    right = right_ref[...].astype(F32) * has_right
    for r in range(EXT):
        at_right = pltpu.roll(right, (-HALO * r) % COLS, 1)
        at_left = pltpu.roll(left, (COLS - HALO - HALO * r) % COLS, 1)
        side_ref[:, row(r)] = jnp.where(
            lane64 < HALO, at_right, jnp.where(lane64 >= COLS - HALO, at_left, 0.0)
        ).astype(BF)

    half = [None, None]
    for r in range(EXT):
        both = [ref[0:32, row(r)].astype(F32) for ref in (ext_ref, side_ref)]
        if r % 2 == 0:
            half = both
        else:
            mean = []
            for first, second in zip(half, both):
                total = first + second
                mean.append((pair_sum(total[0:16] + total[16:32]) * 0.125).astype(BF).astype(F32))
            for d in range(3):
                a, b = mean if d == 1 else turn(mean[0], mean[1], 2 * (d - 1))
                pst_ref[d * 16 : d * 16 + 16, row(r // 2)] = a.astype(BF)
                psb_ref[d * 16 : d * 16 + 16, row(r // 2)] = b.astype(BF)
        if HALO - 1 <= r <= HALO + ROWS:
            at = r - HALO + 1
            for d in range(3):
                a = both[0] if d == 1 else turn(both[0], both[1], d - 1)[0]
                jst_ref[d * 64 : d * 64 + 32, row(at)] = a.astype(BF)

    pre_ref[...] = dot(wc_ref[...], pst_ref[...])
    prb_ref[...] = dot(wc_ref[...], psb_ref[...])

    for at in range(22):
        a0 = ext_ref[32:64, row(at + 1)].astype(F32)
        b0 = side_ref[32:64, row(at + 1)].astype(F32)
        for d in range(3):
            a, b = (a0, b0) if d == 1 else turn(a0, b0, d - 1)
            gst_ref[d * 32 : d * 32 + 32, row(at)] = a.astype(BF)
            gsb_ref[d * 32 : d * 32 + 32, row(at)] = b.astype(BF)
    rg_ref[...] = dot(wg_ref[...], gst_ref[...])
    for d in range(3):
        rgb_ref[d * 32 : d * 32 + 32, :] = dot(
            wg_ref[d * 64 + 32 : d * 64 + 64, :], gsb_ref[...]
        )

    for at in range(10):
        keep = has_above if at == 0 else has_below if at == 9 else 1.0
        keep_side = keep * jnp.where(lane32 < 64, has_right, has_left)
        act, grad = [], []
        for ref, joined_ref, base, size, kept in (
            (pre_ref, rg_ref, 32, 64, keep),
            (prb_ref, rgb_ref, 0, 32, keep_side),
        ):
            value = (
                ref[0:32, row(at)] + ref[32:64, row(at + 1)] + ref[64:96, row(at + 2)]
            )
            sig = 1.0 / (1.0 + jnp.exp(-value))
            act.append((value * sig * kept).astype(BF).astype(F32))
            total = jnp.zeros((C2, COLS), F32)
            for r in (2 * at, 2 * at + 1):
                for d in range(3):
                    lo = d * size + base
                    total = total + joined_ref[lo : lo + 32, row(r + d)]
            grad_act = pair_sum(total).astype(BF).astype(F32)
            grad_pre = grad_act * (sig * (1.0 + value * (1.0 - sig)))
            grad.append((grad_pre * kept).astype(BF).astype(F32))
        for d in range(3):
            a = act[0] if d == 1 else turn(act[0], act[1], d - 1)[0]
            a = a.astype(BF)
            for r in (2 * at - 1, 2 * at):
                if 0 <= r < 18:
                    jst_ref[d * 64 + 32 : d * 64 + 64, row(r)] = a
            q = grad[0] if d == 1 else turn(grad[0], grad[1], 2 * (d - 1))[0]
            qst_ref[d * 32 : d * 32 + 32, row(at)] = q.astype(BF)

    ro_ref[...] = dot(wo_ref[...], jst_ref[...])
    for y in range(ROWS):
        value = ro_ref[0:32, row(y)] + ro_ref[32:64, row(y + 1)] + ro_ref[64:96, row(y + 2)]
        for z in range(2):
            flat_ref[pl.ds(2 * y + z, C1, stride=2 * ROWS), :] = value[z * 16 : z * 16 + 16]
    out_ref[...] = flat_ref[...].astype(BF)

    rq_ref[...] = dot(wq_ref[...], qst_ref[...])
    for at in range(ROWS // 2):
        pooled = rq_ref[0:16, row(at)] + rq_ref[16:32, row(at + 1)] + rq_ref[32:48, row(at + 2)]
        pooled = pooled.astype(BF).astype(F32) * 0.125
        for y in (2 * at, 2 * at + 1):
            for z in range(2):
                total = pooled
                for d in range(3):
                    lo = d * 64 + z * 16
                    total = total + rg_ref[lo : lo + 16, row(y + 2 + d)]
                flat_ref[pl.ds(2 * y + z, C1, stride=2 * ROWS), :] = total
    gf_ref[...] = flat_ref[...].astype(BF)

    own = row(1, ROWS)
    fa_ref[0:16, :] = jst_ref[64:80, own]
    fa_ref[16:48, :] = jst_ref[96:128, own]
    fa_ref[48:64, :] = jst_ref[64:80, own]
    fa_ref[64:96, :] = jst_ref[96:128, own]
    fa_ref[96:128, :] = jnp.zeros((32, ROWS * COLS), BF)
    fb_ref[0:48, :] = jst_ref[80:128, own]
    fb_ref[48:96, :] = jst_ref[80:128, own]
    fb_ref[96:128, :] = jnp.zeros((32, ROWS * COLS), BF)
    fc_ref[0:96, :] = jnp.zeros((96, 8 * COLS), BF)
    fc_ref[96:128, :] = qst_ref[32:64, row(1, 8)]
    fine, coarse = {}, {}
    for ky in range(3):
        shifted = gst_ref[:, row(4 - ky, ROWS)]
        ra, rb = dot_nt(shifted, fa_ref[...]), dot_nt(shifted, fb_ref[...])
        rc = dot_nt(pst_ref[:, row(1 + ky, 8)], fc_ref[...])
        for kx in range(3):
            lo = (2 - kx) * 32
            fine[ky, 0, kx] = ra[lo + 16 : lo + 32]
            fine[ky, 1, kx] = ra[lo : lo + 16] + rb[lo + 16 : lo + 32]
            fine[ky, 2, kx] = rb[lo : lo + 16]
            coarse[ky, kx] = rc[kx * 16 : kx * 16 + 16] * 0.5
    lane16 = lanes_of((16, COLS))
    order = [(ky, kz, kx) for ky in range(3) for kz in range(3) for kx in range(3)]
    for i in range(16):
        value = jnp.zeros((16, COLS), F32)
        if i < 14:
            value = jnp.where(lane16 < 48, fine[order[i]], value)
        if i < 13:
            value = jnp.where((lane16 >= 48) & (lane16 < 96), fine[order[14 + i]], value)
        if i < 9:
            value = jnp.where(lane16 >= 96, coarse[i // 3, i % 3], value)
        gw_ref[i * 16 : i * 16 + 16, :] = value


def block(counts, operands):
    cells = (C1 * ROWS * 2, COLS)
    v = lambda rows_, lanes_, kind: pltpu.VMEM((rows_, lanes_ * COLS), kind)
    return pl.pallas_call(
        functools.partial(block_kernel, counts),
        out_shape=(
            jax.ShapeDtypeStruct(cells, BF),
            jax.ShapeDtypeStruct(cells, BF),
            jax.ShapeDtypeStruct((256, COLS), F32),
        ),
        scratch_shapes=[
            v(64, EXT, BF), v(64, EXT, BF),
            v(192, 18, BF),
            v(96, 22, BF), v(96, 22, BF),
            v(48, 12, BF), v(48, 12, BF),
            v(96, 10, BF),
            v(96, 12, F32), v(96, 12, F32),
            v(96, 18, F32),
            v(192, 22, F32), v(96, 22, F32),
            v(48, 10, F32),
            v(32, 8, BF),
            pltpu.VMEM(cells, F32),
            v(128, ROWS, BF), v(128, ROWS, BF), v(128, 8, BF),
        ],
        compiler_params=pltpu.CompilerParams(vmem_limit_bytes=VMEM_LIMIT),
        cost_estimate=pl.CostEstimate(flops=10**9, bytes_accessed=4 * 10**6, transcendentals=10**5),
        name="block",
    )(*operands)


def spread_kernel(fine_scale, coarse_scale, sum_ref, fine_ref, coarse_ref):
    for i in range(27):
        if i < 14:
            value = sum_ref[i * 16 : i * 16 + 16, :]
        else:
            value = pltpu.roll(sum_ref[(i - 14) * 16 : (i - 14) * 16 + 16, :], 80, 1)
        fine_ref[i * 16 : i * 16 + 16, :] = value[:, 0:48] * fine_scale
        ky, kz, kx = i // 9, i // 3 % 3, i % 3
        if kz == 1:
            at = (ky * 3 + kx) * 16
            value = pltpu.roll(sum_ref[at : at + 16, :], 32, 1)[:, 0:32] * coarse_scale
        else:
            value = jnp.zeros((16, 32), F32)
        coarse_ref[i * 16 : i * 16 + 16, :] = value


def spread(total, fine_scale, coarse_scale):
    return pl.pallas_call(
        functools.partial(spread_kernel, fine_scale, coarse_scale),
        out_shape=(
            jax.ShapeDtypeStruct((432, 48), F32),
            jax.ShapeDtypeStruct((432, 32), F32),
        ),
        compiler_params=pltpu.CompilerParams(vmem_limit_bytes=VMEM_LIMIT),
        name="spread",
    )(total)


def weight_matrices(coarse_weight, fine_weight):
    fine = jnp.transpose(fine_weight, (2, 3, 4, 0, 1))
    planes = []
    for zo in range(2):
        first, second = fine[:, 1 - zo], fine[:, 2 - zo]
        both = (first[..., C1:].astype(F32) + second[..., C1:].astype(F32)).astype(BF)
        planes.append(jnp.concatenate([first[..., :C1], second[..., :C1], both], -1))
    stacked = jnp.stack(planes, 1)
    wo = jnp.transpose(stacked, (0, 1, 3, 2, 4)).reshape(96, 192)
    wg = jnp.transpose(stacked[::-1, :, ::-1], (0, 4, 2, 1, 3)).reshape(192, 96)
    middle = coarse_weight[:, :, :, 1, :]
    wc = jnp.transpose(middle, (2, 0, 3, 1)).reshape(96, 48)
    wq = jnp.transpose(middle[:, :, ::-1, ::-1], (2, 1, 3, 0)).reshape(48, 96)
    return wo, wg, wc, wq


def summed(grads):
    group, others = "far", ("near", "narrow")
    count = lax.axis_size(group)
    length = grads.shape[0]
    share = -(-length // count)
    grads = jnp.pad(grads, ((0, share * count - length), (0, 0))).reshape(count, share, COLS)
    part = jnp.sum(lax.all_to_all(grads, group, 0, 0, tiled=True), 0)
    copies = jnp.broadcast_to(part, (lax.axis_size(others),) + part.shape)
    part = jnp.sum(lax.all_to_all(copies, others, 0, 0, tiled=True), 0)
    copies = jnp.broadcast_to(part, (count,) + part.shape)
    total = lax.all_to_all(copies, group, 0, 0, tiled=True)
    return total.reshape(share * count, COLS)[:length]


def shards(features, cotangent, coarse_weight, fine_weight):
    wide, narrow = lax.axis_size(WIDE), lax.axis_size("narrow")
    matrices = weight_matrices(coarse_weight, fine_weight)
    sides = 1 if narrow == 2 else 2
    own, up, down, strip = pack(features, cotangent, sides)
    above = lax.ppermute(up, WIDE, [(i, i + 1) for i in range(wide - 1)])
    below = lax.ppermute(down, WIDE, [(i + 1, i) for i in range(wide - 1)])
    strip = strip + above[:, HALO * COLS :] + below[:, HALO * COLS :]
    if sides == 1:
        left = right = lax.ppermute(strip, "narrow", [(0, 1), (1, 0)])
    else:
        right = lax.ppermute(strip[:, :COLS], "narrow", [(i + 1, i) for i in range(narrow - 1)])
        left = lax.ppermute(strip[:, COLS:], "narrow", [(i, i + 1) for i in range(narrow - 1)])
    output, grad_features, grads = block(
        (wide, narrow), (own, above, below, left, right) + matrices
    )
    total = summed(grads)
    devices = wide * narrow
    all_cells = features.shape[1] * features.shape[2] * features.shape[3] * devices
    grad_fine, grad_coarse = spread(
        total, 1.0 / math.sqrt(all_cells), 1.0 / math.sqrt(all_cells // 8)
    )
    grad_fine = jnp.transpose(grad_fine.reshape(3, 3, 3, C1, C1 + C2), (3, 4, 0, 1, 2))
    grad_coarse = jnp.transpose(grad_coarse.reshape(3, 3, 3, C1, C2), (4, 3, 0, 1, 2))
    return (
        output.reshape(features.shape),
        grad_features.reshape(features.shape),
        grad_fine,
        grad_coarse,
    )


def solution(mesh):
    wide, narrow = mesh.shape["wide"], mesh.shape["narrow"]
    finer = jax.sharding.Mesh(mesh.devices.reshape(wide // 2, 2, narrow), WIDE + ("narrow",))
    placed = P(None, WIDE, None, "narrow")
    return jax.shard_map(
        shards,
        mesh=finer,
        in_specs=(placed, placed, P(), P()),
        out_specs=(placed, placed, P(), P()),
        check_vma=False,
    )
```

```python
import functools
import math

import jax
import jax.numpy as jnp
from jax import lax
from jax.experimental import pallas as pl
from jax.experimental.pallas import tpu as pltpu
from jax.sharding import PartitionSpec as P

C1, C2 = 16, 32
ROWS, COLS = 16, 128
HALO = 4
EXT = ROWS + 2 * HALO
BF, F32 = jnp.bfloat16, jnp.float32
VMEM_LIMIT = 48 * 1024 * 1024


def lanes_of(shape):
    return lax.broadcasted_iota(jnp.int32, shape, len(shape) - 1)


def row(index, count=1):
    return slice(index * COLS, (index + count) * COLS)


def pack_kernel(sides, f_hbm, g_hbm, s_ref, even_ref, odd_ref, strip_ref, f_ref, g_ref, wide_ref, sems):
    copies = [
        pltpu.make_async_copy(hbm, ref, sems.at[a])
        for a, (hbm, ref) in enumerate(((f_hbm, f_ref), (g_hbm, g_ref)))
    ]
    for copy in copies:
        copy.start()
    lane = lanes_of((C1, COLS))
    place = lax.axis_index("narrow")
    odd = lax.axis_index("wide") % 2
    for a, ref in enumerate((f_ref, g_ref)):
        copies[a].wait()
        wide_ref[...] = ref[...].astype(F32)
        for z in range(2):
            chans = slice(a * 32 + z * 16, a * 32 + z * 16 + 16)
            strips = [jnp.zeros((C1, COLS), F32) for _ in range(sides)]
            for y in range(ROWS):
                value = wide_ref[pl.ds(2 * y + z, C1, stride=2 * ROWS), :]
                s_ref[chans, row(y)] = value.astype(BF)
                start = HALO * (y + HALO)
                inside = (lane >= start) & (lane < start + HALO)
                for side in range(sides):
                    if sides == 2:
                        shift = start + HALO * side
                    else:
                        shift = start + HALO * (1 - place)
                    strips[side] = jnp.where(inside, pltpu.roll(value, shift, 1), strips[side])
            for side in range(sides):
                strip_ref[chans, row(side)] = strips[side].astype(BF)
                turned = pltpu.roll(strips[side], 64, 1)
                for ref, first in ((even_ref, 80 * odd), (odd_ref, 80 - 80 * odd)):
                    kept = (lane >= first) & (lane < first + 4 * HALO)
                    ref[chans, row(HALO + side)] = jnp.where(kept, turned, 0.0).astype(BF)
    last = (ROWS - HALO) * COLS
    for ref, first in ((even_ref, last - last * odd), (odd_ref, last * odd)):
        ref[:, row(0, HALO)] = s_ref[:, pl.ds(pl.multiple_of(first, COLS), HALO * COLS)]


def pack(features, cotangent, sides):
    flat = lambda a: a.reshape(C1 * ROWS * 2, COLS)
    message = jax.ShapeDtypeStruct((64, (HALO + sides) * COLS), BF)
    return pl.pallas_call(
        functools.partial(pack_kernel, sides),
        out_shape=(
            jax.ShapeDtypeStruct((64, ROWS * COLS), BF),
            message,
            message,
            jax.ShapeDtypeStruct((64, sides * COLS), BF),
        ),
        in_specs=[pl.BlockSpec(memory_space=pltpu.HBM)] * 2,
        scratch_shapes=[
            pltpu.VMEM((C1 * ROWS * 2, COLS), BF),
            pltpu.VMEM((C1 * ROWS * 2, COLS), BF),
            pltpu.VMEM((C1 * ROWS * 2, COLS), F32),
            pltpu.SemaphoreType.DMA((2,)),
        ],
        compiler_params=pltpu.CompilerParams(vmem_limit_bytes=VMEM_LIMIT),
        cost_estimate=pl.CostEstimate(flops=10**6, bytes_accessed=10**6, transcendentals=0),
        name="pack",
    )(flat(features), flat(cotangent))


def turn(main, side, by):
    lane = lanes_of(main.shape)
    a, b = pltpu.roll(main, (-by) % COLS, 1), pltpu.roll(side, (-by) % COLS, 1)
    crossed = lane >= COLS - by if by > 0 else lane < -by
    return jnp.where(crossed, b, a), jnp.where(crossed, a, b)


def pair_sum(value):
    lane = lanes_of(value.shape)
    other = jnp.where(lane % 2 == 0, pltpu.roll(value, COLS - 1, 1), pltpu.roll(value, 1, 1))
    return value + other


def dot(a, b):
    return jnp.dot(a, b, preferred_element_type=F32)


def dot_nt(a, b):
    return lax.dot_general(a, b, (((1,), (1,)), ((), ())), preferred_element_type=F32)


def block_kernel(
    counts,
    s_ref, even_ref, odd_ref, left_ref, right_ref, wo_ref, wg_ref, wc_ref, wq_ref,
    out_ref, gf_ref, gw_ref,
    ext_ref, side_ref, jst_ref, gst_ref, gsb_ref, pst_ref, psb_ref, qst_ref,
    pre_ref, prb_ref, ro_ref, rg_ref, rgb_ref, rq_ref, gp_ref, flat_ref, fa_ref, fb_ref, fc_ref,
):
    w, n = lax.axis_index("wide"), lax.axis_index("narrow")
    lane32 = lanes_of((C2, COLS))
    lane64 = lanes_of((64, COLS))
    flag = lambda is_there: jnp.where(is_there, 1.0, 0.0)
    has_left, has_right = flag(n > 0), flag(n < counts[1] - 1)
    has_above, has_below = flag(w > 0), flag(w < counts[0] - 1)

    odd = w % 2
    below = (HALO + ROWS) * COLS
    ext_ref[:, row(HALO, ROWS)] = s_ref[...]
    for ref, first in ((even_ref, below - below * odd), (odd_ref, below * odd)):
        ext_ref[:, pl.ds(pl.multiple_of(first, COLS), HALO * COLS)] = ref[:, row(0, HALO)]

    left = left_ref[...].astype(F32) * has_left
    right = right_ref[...].astype(F32) * has_right
    for r in range(EXT):
        at_right = pltpu.roll(right, (-HALO * r) % COLS, 1)
        at_left = pltpu.roll(left, (COLS - HALO - HALO * r) % COLS, 1)
        side_ref[:, row(r)] = jnp.where(
            lane64 < HALO, at_right, jnp.where(lane64 >= COLS - HALO, at_left, 0.0)
        ).astype(BF)

    half = [None, None]
    for r in range(EXT):
        both = [ref[0:32, row(r)].astype(F32) for ref in (ext_ref, side_ref)]
        if r % 2 == 0:
            half = both
        else:
            mean = []
            for first, second in zip(half, both):
                total = first + second
                mean.append((pair_sum(total[0:16] + total[16:32]) * 0.125).astype(BF).astype(F32))
            for d in range(3):
                a, b = mean if d == 1 else turn(mean[0], mean[1], 2 * (d - 1))
                pst_ref[d * 16 : d * 16 + 16, row(r // 2)] = a.astype(BF)
                psb_ref[d * 16 : d * 16 + 16, row(r // 2)] = b.astype(BF)
        if HALO - 1 <= r <= HALO + ROWS:
            at = r - HALO + 1
            for d in range(3):
                a = both[0] if d == 1 else turn(both[0], both[1], d - 1)[0]
                jst_ref[d * 64 : d * 64 + 32, row(at)] = a.astype(BF)

    pre_ref[...] = dot(wc_ref[...], pst_ref[...])
    prb_ref[...] = dot(wc_ref[...], psb_ref[...])

    for at in range(22):
        a0 = ext_ref[32:64, row(at + 1)].astype(F32)
        b0 = side_ref[32:64, row(at + 1)].astype(F32)
        for d in range(3):
            a, b = (a0, b0) if d == 1 else turn(a0, b0, d - 1)
            gst_ref[d * 32 : d * 32 + 32, row(at)] = a.astype(BF)
            gsb_ref[d * 32 : d * 32 + 32, row(at)] = b.astype(BF)
    rg_ref[...] = dot(wg_ref[...], gst_ref[...])
    for d in range(3):
        rgb_ref[d * 32 : d * 32 + 32, :] = dot(
            wg_ref[d * 64 + 32 : d * 64 + 64, :], gsb_ref[...]
        )

    for at in range(10):
        keep = has_above if at == 0 else has_below if at == 9 else 1.0
        keep_side = keep * jnp.where(lane32 < 64, has_right, has_left)
        act, grad = [], []
        for ref, joined_ref, base, size, kept in (
            (pre_ref, rg_ref, 32, 64, keep),
            (prb_ref, rgb_ref, 0, 32, keep_side),
        ):
            value = (
                ref[0:32, row(at)] + ref[32:64, row(at + 1)] + ref[64:96, row(at + 2)]
            )
            sig = 1.0 / (1.0 + jnp.exp(-value))
            act.append((value * sig * kept).astype(BF).astype(F32))
            total = jnp.zeros((C2, COLS), F32)
            for r in (2 * at, 2 * at + 1):
                for d in range(3):
                    lo = d * size + base
                    total = total + joined_ref[lo : lo + 32, row(r + d)]
            grad_act = pair_sum(total).astype(BF).astype(F32)
            grad_pre = grad_act * (sig * (1.0 + value * (1.0 - sig)))
            grad.append((grad_pre * kept).astype(BF).astype(F32))
        for d in range(3):
            a = act[0] if d == 1 else turn(act[0], act[1], d - 1)[0]
            a = a.astype(BF)
            for r in (2 * at - 1, 2 * at):
                if 0 <= r < 18:
                    jst_ref[d * 64 + 32 : d * 64 + 64, row(r)] = a
            q = grad[0] if d == 1 else turn(grad[0], grad[1], 2 * (d - 1))[0]
            qst_ref[d * 32 : d * 32 + 32, row(at)] = q.astype(BF)

    ro_ref[...] = dot(wo_ref[...], jst_ref[...])
    for y in range(ROWS):
        value = ro_ref[0:32, row(y)] + ro_ref[32:64, row(y + 1)] + ro_ref[64:96, row(y + 2)]
        for z in range(2):
            flat_ref[pl.ds(2 * y + z, C1, stride=2 * ROWS), :] = value[z * 16 : z * 16 + 16]
    out_ref[...] = flat_ref[...].astype(BF)

    rq_ref[...] = dot(wq_ref[...], qst_ref[...])
    for at in range(ROWS // 2):
        pooled = rq_ref[0:16, row(at)] + rq_ref[16:32, row(at + 1)] + rq_ref[32:48, row(at + 2)]
        pooled = pooled.astype(BF).astype(F32) * 0.125
        for y in (2 * at, 2 * at + 1):
            for z in range(2):
                total = pooled
                for d in range(3):
                    lo = d * 64 + z * 16
                    total = total + rg_ref[lo : lo + 16, row(y + 2 + d)]
                flat_ref[pl.ds(2 * y + z, C1, stride=2 * ROWS), :] = total
    gf_ref[...] = flat_ref[...].astype(BF)

    own = row(1, ROWS)
    fa_ref[0:16, :] = jst_ref[64:80, own]
    fa_ref[16:48, :] = jst_ref[96:128, own]
    fa_ref[48:64, :] = jst_ref[64:80, own]
    fa_ref[64:96, :] = jst_ref[96:128, own]
    fa_ref[96:128, :] = jnp.zeros((32, ROWS * COLS), BF)
    fb_ref[0:48, :] = jst_ref[80:128, own]
    fb_ref[48:96, :] = jst_ref[80:128, own]
    fb_ref[96:128, :] = jnp.zeros((32, ROWS * COLS), BF)
    fc_ref[0:96, :] = jnp.zeros((96, 8 * COLS), BF)
    fc_ref[96:128, :] = qst_ref[32:64, row(1, 8)]
    fine, coarse = {}, {}
    for ky in range(3):
        shifted = gst_ref[:, row(4 - ky, ROWS)]
        ra, rb = dot_nt(shifted, fa_ref[...]), dot_nt(shifted, fb_ref[...])
        rc = dot_nt(pst_ref[:, row(1 + ky, 8)], fc_ref[...])
        for kx in range(3):
            lo = (2 - kx) * 32
            fine[ky, 0, kx] = ra[lo + 16 : lo + 32]
            fine[ky, 1, kx] = ra[lo : lo + 16] + rb[lo + 16 : lo + 32]
            fine[ky, 2, kx] = rb[lo : lo + 16]
            coarse[ky, kx] = rc[kx * 16 : kx * 16 + 16] * 0.5
    lane16 = lanes_of((16, COLS))
    order = [(ky, kz, kx) for ky in range(3) for kz in range(3) for kx in range(3)]
    for i in range(16):
        value = jnp.zeros((16, COLS), F32)
        if i < 14:
            value = jnp.where(lane16 < 48, fine[order[i]], value)
        if i < 13:
            value = jnp.where((lane16 >= 48) & (lane16 < 96), fine[order[14 + i]], value)
        if i < 9:
            value = jnp.where(lane16 >= 96, coarse[i // 3, i % 3], value)
        gw_ref[i * 16 : i * 16 + 16, :] = value


def block(counts, operands):
    cells = (C1 * ROWS * 2, COLS)
    v = lambda rows_, lanes_, kind: pltpu.VMEM((rows_, lanes_ * COLS), kind)
    return pl.pallas_call(
        functools.partial(block_kernel, counts),
        out_shape=(
            jax.ShapeDtypeStruct(cells, BF),
            jax.ShapeDtypeStruct(cells, BF),
            jax.ShapeDtypeStruct((256, COLS), F32),
        ),
        scratch_shapes=[
            v(64, EXT, BF), v(64, EXT, BF),
            v(192, 18, BF),
            v(96, 22, BF), v(96, 22, BF),
            v(48, 12, BF), v(48, 12, BF),
            v(96, 10, BF),
            v(96, 12, F32), v(96, 12, F32),
            v(96, 18, F32),
            v(192, 22, F32), v(96, 22, F32),
            v(48, 10, F32),
            v(32, 8, BF),
            pltpu.VMEM(cells, F32),
            v(128, ROWS, BF), v(128, ROWS, BF), v(128, 8, BF),
        ],
        compiler_params=pltpu.CompilerParams(vmem_limit_bytes=VMEM_LIMIT),
        cost_estimate=pl.CostEstimate(flops=10**9, bytes_accessed=4 * 10**6, transcendentals=10**5),
        name="block",
    )(*operands)


def spread_kernel(fine_scale, coarse_scale, sum_ref, fine_ref, coarse_ref):
    for i in range(27):
        if i < 14:
            value = sum_ref[i * 16 : i * 16 + 16, :]
        else:
            value = pltpu.roll(sum_ref[(i - 14) * 16 : (i - 14) * 16 + 16, :], 80, 1)
        fine_ref[i * 16 : i * 16 + 16, :] = value[:, 0:48] * fine_scale
        ky, kz, kx = i // 9, i // 3 % 3, i % 3
        if kz == 1:
            at = (ky * 3 + kx) * 16
            value = pltpu.roll(sum_ref[at : at + 16, :], 32, 1)[:, 0:32] * coarse_scale
        else:
            value = jnp.zeros((16, 32), F32)
        coarse_ref[i * 16 : i * 16 + 16, :] = value


def spread(total, fine_scale, coarse_scale):
    return pl.pallas_call(
        functools.partial(spread_kernel, fine_scale, coarse_scale),
        out_shape=(
            jax.ShapeDtypeStruct((432, 48), F32),
            jax.ShapeDtypeStruct((432, 32), F32),
        ),
        compiler_params=pltpu.CompilerParams(vmem_limit_bytes=VMEM_LIMIT),
        name="spread",
    )(total)


def weight_matrices(coarse_weight, fine_weight):
    fine = jnp.transpose(fine_weight, (2, 3, 4, 0, 1))
    planes = []
    for zo in range(2):
        first, second = fine[:, 1 - zo], fine[:, 2 - zo]
        both = (first[..., C1:].astype(F32) + second[..., C1:].astype(F32)).astype(BF)
        planes.append(jnp.concatenate([first[..., :C1], second[..., :C1], both], -1))
    stacked = jnp.stack(planes, 1)
    wo = jnp.transpose(stacked, (0, 1, 3, 2, 4)).reshape(96, 192)
    wg = jnp.transpose(stacked[::-1, :, ::-1], (0, 4, 2, 1, 3)).reshape(192, 96)
    middle = coarse_weight[:, :, :, 1, :]
    wc = jnp.transpose(middle, (2, 0, 3, 1)).reshape(96, 48)
    wq = jnp.transpose(middle[:, :, ::-1, ::-1], (2, 1, 3, 0)).reshape(48, 96)
    return wo, wg, wc, wq


def shards(features, cotangent, coarse_weight, fine_weight):
    wide, narrow = lax.axis_size("wide"), lax.axis_size("narrow")
    matrices = weight_matrices(coarse_weight, fine_weight)
    sides = 1 if narrow == 2 else 2
    own, to_even, to_odd, strip = pack(features, cotangent, sides)
    swaps = lambda start: [
        pair for i in range(start, wide - 1, 2) for pair in ((i, i + 1), (i + 1, i))
    ]
    even = lax.ppermute(to_even, "wide", swaps(0))
    odd = lax.ppermute(to_odd, "wide", swaps(1))
    strip = strip + even[:, HALO * COLS :] + odd[:, HALO * COLS :]
    if sides == 1:
        left = right = lax.ppermute(strip, "narrow", [(0, 1), (1, 0)])
    else:
        right = lax.ppermute(strip[:, :COLS], "narrow", [(i + 1, i) for i in range(narrow - 1)])
        left = lax.ppermute(strip[:, COLS:], "narrow", [(i, i + 1) for i in range(narrow - 1)])
    output, grad_features, grads = block(
        (wide, narrow), (own, even, odd, left, right) + matrices
    )
    devices = wide * narrow
    share = -(-256 // devices)
    grads = jnp.pad(grads, ((0, share * devices - 256), (0, 0))).reshape(devices, share, COLS)
    both = ("wide", "narrow")
    parts = lax.all_to_all(grads, both, 0, 0, tiled=True)
    total = jnp.broadcast_to(jnp.sum(parts, 0, keepdims=True), parts.shape)
    total = lax.all_to_all(total, both, 0, 0, tiled=True)
    total = total.reshape(share * devices, COLS)[:256]
    all_cells = features.shape[1] * features.shape[2] * features.shape[3] * devices
    grad_fine, grad_coarse = spread(
        total, 1.0 / math.sqrt(all_cells), 1.0 / math.sqrt(all_cells // 8)
    )
    grad_fine = jnp.transpose(grad_fine.reshape(3, 3, 3, C1, C1 + C2), (3, 4, 0, 1, 2))
    grad_coarse = jnp.transpose(grad_coarse.reshape(3, 3, 3, C1, C2), (4, 3, 0, 1, 2))
    return (
        output.reshape(features.shape),
        grad_features.reshape(features.shape),
        grad_fine,
        grad_coarse,
    )


def solution(mesh):
    placed = P(None, "wide", None, "narrow")
    return jax.shard_map(
        shards,
        mesh=mesh,
        in_specs=(placed, placed, P(), P()),
        out_specs=(placed, placed, P(), P()),
        check_vma=False,
    )
```

```python
import functools
import math

import jax
import jax.numpy as jnp
from jax import lax
from jax.experimental import pallas as pl
from jax.experimental.pallas import tpu as pltpu
from jax.sharding import PartitionSpec as P

C1, C2 = 16, 32
ROWS, COLS = 16, 128
HALO = 4
EXT = ROWS + 2 * HALO
BF, F32 = jnp.bfloat16, jnp.float32
VMEM_LIMIT = 48 * 1024 * 1024


def lanes_of(shape):
    return lax.broadcasted_iota(jnp.int32, shape, len(shape) - 1)


def row(index, count=1):
    return slice(index * COLS, (index + count) * COLS)


def pack_kernel(sides, in_ref, s_ref, even_ref, odd_ref, strip_ref, wide_ref):
    lane = lanes_of((C1, COLS))
    place = lax.axis_index("narrow")
    odd = lax.axis_index("wide") % 2
    for a in range(2):
        wide_ref[...] = in_ref[a].astype(F32)
        for z in range(2):
            chans = slice(a * 32 + z * 16, a * 32 + z * 16 + 16)
            strips = [jnp.zeros((C1, COLS), F32) for _ in range(sides)]
            for y in range(ROWS):
                value = wide_ref[pl.ds(2 * y + z, C1, stride=2 * ROWS), :]
                s_ref[chans, row(y)] = value.astype(BF)
                start = HALO * (y + HALO)
                inside = (lane >= start) & (lane < start + HALO)
                for side in range(sides):
                    if sides == 2:
                        shift = start + HALO * side
                    else:
                        shift = start + HALO * (1 - place)
                    strips[side] = jnp.where(inside, pltpu.roll(value, shift, 1), strips[side])
            for side in range(sides):
                strip_ref[chans, row(side)] = strips[side].astype(BF)
                turned = pltpu.roll(strips[side], 64, 1)
                for ref, first in ((even_ref, 80 * odd), (odd_ref, 80 - 80 * odd)):
                    kept = (lane >= first) & (lane < first + 4 * HALO)
                    ref[chans, row(HALO + side)] = jnp.where(kept, turned, 0.0).astype(BF)
    last = (ROWS - HALO) * COLS
    for ref, first in ((even_ref, last - last * odd), (odd_ref, last * odd)):
        ref[:, row(0, HALO)] = s_ref[:, pl.ds(pl.multiple_of(first, COLS), HALO * COLS)]


def pack(features, cotangent, sides):
    flat = lambda a: a.reshape(C1 * ROWS * 2, COLS)
    message = jax.ShapeDtypeStruct((64, (HALO + sides) * COLS), BF)
    return pl.pallas_call(
        functools.partial(pack_kernel, sides),
        out_shape=(
            jax.ShapeDtypeStruct((64, ROWS * COLS), BF),
            message,
            message,
            jax.ShapeDtypeStruct((64, sides * COLS), BF),
        ),
        scratch_shapes=[pltpu.VMEM((C1 * ROWS * 2, COLS), F32)],
        compiler_params=pltpu.CompilerParams(vmem_limit_bytes=VMEM_LIMIT),
        cost_estimate=pl.CostEstimate(flops=10**6, bytes_accessed=10**6, transcendentals=0),
        name="pack",
    )(jnp.stack([flat(features), flat(cotangent)]))


def turn(main, side, by):
    lane = lanes_of(main.shape)
    a, b = pltpu.roll(main, (-by) % COLS, 1), pltpu.roll(side, (-by) % COLS, 1)
    crossed = lane >= COLS - by if by > 0 else lane < -by
    return jnp.where(crossed, b, a), jnp.where(crossed, a, b)


def pair_sum(value):
    lane = lanes_of(value.shape)
    other = jnp.where(lane % 2 == 0, pltpu.roll(value, COLS - 1, 1), pltpu.roll(value, 1, 1))
    return value + other


def dot(a, b):
    return jnp.dot(a, b, preferred_element_type=F32)


def dot_nt(a, b):
    return lax.dot_general(a, b, (((1,), (1,)), ((), ())), preferred_element_type=F32)


def block_kernel(
    counts,
    s_ref, even_ref, odd_ref, left_ref, right_ref, wo_ref, wg_ref, wc_ref, wq_ref,
    out_ref, gf_ref, gw_ref,
    ext_ref, side_ref, jst_ref, gst_ref, gsb_ref, pst_ref, psb_ref, qst_ref,
    pre_ref, prb_ref, ro_ref, rg_ref, rgb_ref, rq_ref, gp_ref, flat_ref, fa_ref, fb_ref, fc_ref,
):
    w, n = lax.axis_index("wide"), lax.axis_index("narrow")
    lane32 = lanes_of((C2, COLS))
    lane64 = lanes_of((64, COLS))
    flag = lambda is_there: jnp.where(is_there, 1.0, 0.0)
    has_left, has_right = flag(n > 0), flag(n < counts[1] - 1)
    has_above, has_below = flag(w > 0), flag(w < counts[0] - 1)

    odd = w % 2
    below = (HALO + ROWS) * COLS
    ext_ref[:, row(HALO, ROWS)] = s_ref[...]
    for ref, first in ((even_ref, below - below * odd), (odd_ref, below * odd)):
        ext_ref[:, pl.ds(pl.multiple_of(first, COLS), HALO * COLS)] = ref[:, row(0, HALO)]

    left = left_ref[...].astype(F32) * has_left
    right = right_ref[...].astype(F32) * has_right
    for r in range(EXT):
        at_right = pltpu.roll(right, (-HALO * r) % COLS, 1)
        at_left = pltpu.roll(left, (COLS - HALO - HALO * r) % COLS, 1)
        side_ref[:, row(r)] = jnp.where(
            lane64 < HALO, at_right, jnp.where(lane64 >= COLS - HALO, at_left, 0.0)
        ).astype(BF)

    half = [None, None]
    for r in range(EXT):
        both = [ref[0:32, row(r)].astype(F32) for ref in (ext_ref, side_ref)]
        if r % 2 == 0:
            half = both
        else:
            mean = []
            for first, second in zip(half, both):
                total = first + second
                mean.append((pair_sum(total[0:16] + total[16:32]) * 0.125).astype(BF).astype(F32))
            for d in range(3):
                a, b = mean if d == 1 else turn(mean[0], mean[1], 2 * (d - 1))
                pst_ref[d * 16 : d * 16 + 16, row(r // 2)] = a.astype(BF)
                psb_ref[d * 16 : d * 16 + 16, row(r // 2)] = b.astype(BF)
        if HALO - 1 <= r <= HALO + ROWS:
            at = r - HALO + 1
            for d in range(3):
                a = both[0] if d == 1 else turn(both[0], both[1], d - 1)[0]
                jst_ref[d * 64 : d * 64 + 32, row(at)] = a.astype(BF)

    pre_ref[...] = dot(wc_ref[...], pst_ref[...])
    prb_ref[...] = dot(wc_ref[...], psb_ref[...])

    for at in range(22):
        a0 = ext_ref[32:64, row(at + 1)].astype(F32)
        b0 = side_ref[32:64, row(at + 1)].astype(F32)
        for d in range(3):
            a, b = (a0, b0) if d == 1 else turn(a0, b0, d - 1)
            gst_ref[d * 32 : d * 32 + 32, row(at)] = a.astype(BF)
            gsb_ref[d * 32 : d * 32 + 32, row(at)] = b.astype(BF)
    rg_ref[...] = dot(wg_ref[...], gst_ref[...])
    for d in range(3):
        rgb_ref[d * 32 : d * 32 + 32, :] = dot(
            wg_ref[d * 64 + 32 : d * 64 + 64, :], gsb_ref[...]
        )

    for at in range(10):
        keep = has_above if at == 0 else has_below if at == 9 else 1.0
        keep_side = keep * jnp.where(lane32 < 64, has_right, has_left)
        act, grad = [], []
        for ref, joined_ref, base, size, kept in (
            (pre_ref, rg_ref, 32, 64, keep),
            (prb_ref, rgb_ref, 0, 32, keep_side),
        ):
            value = (
                ref[0:32, row(at)] + ref[32:64, row(at + 1)] + ref[64:96, row(at + 2)]
            )
            sig = 1.0 / (1.0 + jnp.exp(-value))
            act.append((value * sig * kept).astype(BF).astype(F32))
            total = jnp.zeros((C2, COLS), F32)
            for r in (2 * at, 2 * at + 1):
                for d in range(3):
                    lo = d * size + base
                    total = total + joined_ref[lo : lo + 32, row(r + d)]
            grad_act = pair_sum(total).astype(BF).astype(F32)
            grad_pre = grad_act * (sig * (1.0 + value * (1.0 - sig)))
            grad.append((grad_pre * kept).astype(BF).astype(F32))
        for d in range(3):
            a = act[0] if d == 1 else turn(act[0], act[1], d - 1)[0]
            a = a.astype(BF)
            for r in (2 * at - 1, 2 * at):
                if 0 <= r < 18:
                    jst_ref[d * 64 + 32 : d * 64 + 64, row(r)] = a
            q = grad[0] if d == 1 else turn(grad[0], grad[1], 2 * (d - 1))[0]
            qst_ref[d * 32 : d * 32 + 32, row(at)] = q.astype(BF)

    ro_ref[...] = dot(wo_ref[...], jst_ref[...])
    for y in range(ROWS):
        value = ro_ref[0:32, row(y)] + ro_ref[32:64, row(y + 1)] + ro_ref[64:96, row(y + 2)]
        for z in range(2):
            flat_ref[pl.ds(2 * y + z, C1, stride=2 * ROWS), :] = value[z * 16 : z * 16 + 16]
    out_ref[...] = flat_ref[...].astype(BF)

    rq_ref[...] = dot(wq_ref[...], qst_ref[...])
    for at in range(ROWS // 2):
        pooled = rq_ref[0:16, row(at)] + rq_ref[16:32, row(at + 1)] + rq_ref[32:48, row(at + 2)]
        pooled = pooled.astype(BF).astype(F32) * 0.125
        for y in (2 * at, 2 * at + 1):
            for z in range(2):
                total = pooled
                for d in range(3):
                    lo = d * 64 + z * 16
                    total = total + rg_ref[lo : lo + 16, row(y + 2 + d)]
                flat_ref[pl.ds(2 * y + z, C1, stride=2 * ROWS), :] = total
    gf_ref[...] = flat_ref[...].astype(BF)

    own = row(1, ROWS)
    fa_ref[0:16, :] = jst_ref[64:80, own]
    fa_ref[16:48, :] = jst_ref[96:128, own]
    fa_ref[48:64, :] = jst_ref[64:80, own]
    fa_ref[64:96, :] = jst_ref[96:128, own]
    fa_ref[96:128, :] = jnp.zeros((32, ROWS * COLS), BF)
    fb_ref[0:48, :] = jst_ref[80:128, own]
    fb_ref[48:96, :] = jst_ref[80:128, own]
    fb_ref[96:128, :] = jnp.zeros((32, ROWS * COLS), BF)
    fc_ref[0:96, :] = jnp.zeros((96, 8 * COLS), BF)
    fc_ref[96:128, :] = qst_ref[32:64, row(1, 8)]
    fine, coarse = {}, {}
    for ky in range(3):
        shifted = gst_ref[:, row(4 - ky, ROWS)]
        ra, rb = dot_nt(shifted, fa_ref[...]), dot_nt(shifted, fb_ref[...])
        rc = dot_nt(pst_ref[:, row(1 + ky, 8)], fc_ref[...])
        for kx in range(3):
            lo = (2 - kx) * 32
            fine[ky, 0, kx] = ra[lo + 16 : lo + 32]
            fine[ky, 1, kx] = ra[lo : lo + 16] + rb[lo + 16 : lo + 32]
            fine[ky, 2, kx] = rb[lo : lo + 16]
            coarse[ky, kx] = rc[kx * 16 : kx * 16 + 16] * 0.5
    lane16 = lanes_of((16, COLS))
    order = [(ky, kz, kx) for ky in range(3) for kz in range(3) for kx in range(3)]
    for i in range(16):
        value = jnp.zeros((16, COLS), F32)
        if i < 14:
            value = jnp.where(lane16 < 48, fine[order[i]], value)
        if i < 13:
            value = jnp.where((lane16 >= 48) & (lane16 < 96), fine[order[14 + i]], value)
        if i < 9:
            value = jnp.where(lane16 >= 96, coarse[i // 3, i % 3], value)
        gw_ref[i * 16 : i * 16 + 16, :] = value.astype(BF)


def block(counts, operands):
    cells = (C1 * ROWS * 2, COLS)
    v = lambda rows_, lanes_, kind: pltpu.VMEM((rows_, lanes_ * COLS), kind)
    return pl.pallas_call(
        functools.partial(block_kernel, counts),
        out_shape=(
            jax.ShapeDtypeStruct(cells, BF),
            jax.ShapeDtypeStruct(cells, BF),
            jax.ShapeDtypeStruct((256, COLS), BF),
        ),
        scratch_shapes=[
            v(64, EXT, BF), v(64, EXT, BF),
            v(192, 18, BF),
            v(96, 22, BF), v(96, 22, BF),
            v(48, 12, BF), v(48, 12, BF),
            v(96, 10, BF),
            v(96, 12, F32), v(96, 12, F32),
            v(96, 18, F32),
            v(192, 22, F32), v(96, 22, F32),
            v(48, 10, F32),
            v(32, 8, BF),
            pltpu.VMEM(cells, F32),
            v(128, ROWS, BF), v(128, ROWS, BF), v(128, 8, BF),
        ],
        compiler_params=pltpu.CompilerParams(vmem_limit_bytes=VMEM_LIMIT),
        cost_estimate=pl.CostEstimate(flops=10**9, bytes_accessed=4 * 10**6, transcendentals=10**5),
        name="block",
    )(*operands)


def add_kernel(parts_ref, copies_ref):
    total = parts_ref[0].astype(F32)
    for i in range(1, parts_ref.shape[0]):
        total = total + parts_ref[i].astype(F32)
    total = total.astype(BF)
    for i in range(parts_ref.shape[0]):
        copies_ref[i] = total


def add_up(parts):
    return pl.pallas_call(
        add_kernel,
        out_shape=jax.ShapeDtypeStruct(parts.shape, BF),
        compiler_params=pltpu.CompilerParams(vmem_limit_bytes=VMEM_LIMIT),
        name="add_up",
    )(parts)


def spread_kernel(fine_scale, coarse_scale, sum_ref, fine_ref, coarse_ref):
    for i in range(27):
        if i < 14:
            value = sum_ref[i * 16 : i * 16 + 16, :].astype(F32)
        else:
            at = (i - 14) * 16
            value = pltpu.roll(sum_ref[at : at + 16, :].astype(F32), 80, 1)
        fine_ref[i * 16 : i * 16 + 16, :] = value[:, 0:48] * fine_scale
        ky, kz, kx = i // 9, i // 3 % 3, i % 3
        if kz == 1:
            at = (ky * 3 + kx) * 16
            value = pltpu.roll(sum_ref[at : at + 16, :].astype(F32), 32, 1)[:, 0:32] * coarse_scale
        else:
            value = jnp.zeros((16, 32), F32)
        coarse_ref[i * 16 : i * 16 + 16, :] = value


def spread(total, fine_scale, coarse_scale):
    return pl.pallas_call(
        functools.partial(spread_kernel, fine_scale, coarse_scale),
        out_shape=(
            jax.ShapeDtypeStruct((432, 48), F32),
            jax.ShapeDtypeStruct((432, 32), F32),
        ),
        compiler_params=pltpu.CompilerParams(vmem_limit_bytes=VMEM_LIMIT),
        name="spread",
    )(total)


def weight_matrices(coarse_weight, fine_weight):
    fine = jnp.transpose(fine_weight, (2, 3, 4, 0, 1))
    planes = []
    for zo in range(2):
        first, second = fine[:, 1 - zo], fine[:, 2 - zo]
        both = (first[..., C1:].astype(F32) + second[..., C1:].astype(F32)).astype(BF)
        planes.append(jnp.concatenate([first[..., :C1], second[..., :C1], both], -1))
    stacked = jnp.stack(planes, 1)
    wo = jnp.transpose(stacked, (0, 1, 3, 2, 4)).reshape(96, 192)
    wg = jnp.transpose(stacked[::-1, :, ::-1], (0, 4, 2, 1, 3)).reshape(192, 96)
    middle = coarse_weight[:, :, :, 1, :]
    wc = jnp.transpose(middle, (2, 0, 3, 1)).reshape(96, 48)
    wq = jnp.transpose(middle[:, :, ::-1, ::-1], (2, 1, 3, 0)).reshape(48, 96)
    return wo, wg, wc, wq


def shards(features, cotangent, coarse_weight, fine_weight):
    wide, narrow = lax.axis_size("wide"), lax.axis_size("narrow")
    matrices = weight_matrices(coarse_weight, fine_weight)
    sides = 1 if narrow == 2 else 2
    own, to_even, to_odd, strip = pack(features, cotangent, sides)
    swaps = lambda start: [
        pair for i in range(start, wide - 1, 2) for pair in ((i, i + 1), (i + 1, i))
    ]
    even = lax.ppermute(to_even, "wide", swaps(0))
    odd = lax.ppermute(to_odd, "wide", swaps(1))
    strip = strip + even[:, HALO * COLS :] + odd[:, HALO * COLS :]
    if sides == 1:
        left = right = lax.ppermute(strip, "narrow", [(0, 1), (1, 0)])
    else:
        right = lax.ppermute(strip[:, :COLS], "narrow", [(i + 1, i) for i in range(narrow - 1)])
        left = lax.ppermute(strip[:, COLS:], "narrow", [(i, i + 1) for i in range(narrow - 1)])
    output, grad_features, grads = block(
        (wide, narrow), (own, even, odd, left, right) + matrices
    )
    devices = wide * narrow
    share = -(-256 // devices)
    grads = jnp.pad(grads, ((0, share * devices - 256), (0, 0))).reshape(devices, share, COLS)
    both = ("wide", "narrow")
    parts = lax.all_to_all(grads, both, 0, 0, tiled=True)
    total = lax.all_to_all(add_up(parts), both, 0, 0, tiled=True)
    total = total.reshape(share * devices, COLS)[:256]
    all_cells = features.shape[1] * features.shape[2] * features.shape[3] * devices
    grad_fine, grad_coarse = spread(
        total, 1.0 / math.sqrt(all_cells), 1.0 / math.sqrt(all_cells // 8)
    )
    grad_fine = jnp.transpose(grad_fine.reshape(3, 3, 3, C1, C1 + C2), (3, 4, 0, 1, 2))
    grad_coarse = jnp.transpose(grad_coarse.reshape(3, 3, 3, C1, C2), (4, 3, 0, 1, 2))
    return (
        output.reshape(features.shape),
        grad_features.reshape(features.shape),
        grad_fine,
        grad_coarse,
    )


def solution(mesh):
    placed = P(None, "wide", None, "narrow")
    return jax.shard_map(
        shards,
        mesh=mesh,
        in_specs=(placed, placed, P(), P()),
        out_specs=(placed, placed, P(), P()),
        check_vma=False,
    )
```

```python
import functools
import math

import jax
import jax.numpy as jnp
from jax import lax
from jax.experimental import pallas as pl
from jax.experimental.pallas import tpu as pltpu
from jax.sharding import PartitionSpec as P

C1, C2 = 16, 32
ROWS, COLS = 16, 128
HALO = 4
EXT = ROWS + 2 * HALO
BF, F32 = jnp.bfloat16, jnp.float32
WIDE = ("far", "near")
VMEM_LIMIT = 48 * 1024 * 1024


def lanes_of(shape):
    return lax.broadcasted_iota(jnp.int32, shape, len(shape) - 1)


def row(index, count=1):
    return slice(index * COLS, (index + count) * COLS)


def pack_kernel(sides, in_ref, s_ref, even_ref, odd_ref, strip_ref, wide_ref):
    lane = lanes_of((C1, COLS))
    place = lax.axis_index("narrow")
    odd = lax.axis_index(WIDE) % 2
    for a in range(2):
        wide_ref[...] = in_ref[a].astype(F32)
        for z in range(2):
            chans = slice(a * 32 + z * 16, a * 32 + z * 16 + 16)
            strips = [jnp.zeros((C1, COLS), F32) for _ in range(sides)]
            for y in range(ROWS):
                value = wide_ref[pl.ds(2 * y + z, C1, stride=2 * ROWS), :]
                s_ref[chans, row(y)] = value.astype(BF)
                start = HALO * (y + HALO)
                inside = (lane >= start) & (lane < start + HALO)
                for side in range(sides):
                    if sides == 2:
                        shift = start + HALO * side
                    else:
                        shift = start + HALO * (1 - place)
                    strips[side] = jnp.where(inside, pltpu.roll(value, shift, 1), strips[side])
            for side in range(sides):
                strip_ref[chans, row(side)] = strips[side].astype(BF)
                turned = pltpu.roll(strips[side], 64, 1)
                for ref, first in ((even_ref, 80 * odd), (odd_ref, 80 - 80 * odd)):
                    kept = (lane >= first) & (lane < first + 4 * HALO)
                    ref[chans, row(HALO + side)] = jnp.where(kept, turned, 0.0).astype(BF)
    last = (ROWS - HALO) * COLS
    for ref, first in ((even_ref, last - last * odd), (odd_ref, last * odd)):
        ref[:, row(0, HALO)] = s_ref[:, pl.ds(pl.multiple_of(first, COLS), HALO * COLS)]


def pack(features, cotangent, sides):
    flat = lambda a: a.reshape(C1 * ROWS * 2, COLS)
    message = jax.ShapeDtypeStruct((64, (HALO + sides) * COLS), BF)
    return pl.pallas_call(
        functools.partial(pack_kernel, sides),
        out_shape=(
            jax.ShapeDtypeStruct((64, ROWS * COLS), BF),
            message,
            message,
            jax.ShapeDtypeStruct((64, sides * COLS), BF),
        ),
        scratch_shapes=[pltpu.VMEM((C1 * ROWS * 2, COLS), F32)],
        compiler_params=pltpu.CompilerParams(vmem_limit_bytes=VMEM_LIMIT),
        cost_estimate=pl.CostEstimate(flops=10**6, bytes_accessed=10**6, transcendentals=0),
        name="pack",
    )(jnp.stack([flat(features), flat(cotangent)]))


def turn(main, side, by):
    lane = lanes_of(main.shape)
    a, b = pltpu.roll(main, (-by) % COLS, 1), pltpu.roll(side, (-by) % COLS, 1)
    crossed = lane >= COLS - by if by > 0 else lane < -by
    return jnp.where(crossed, b, a), jnp.where(crossed, a, b)


def pair_sum(value):
    lane = lanes_of(value.shape)
    other = jnp.where(lane % 2 == 0, pltpu.roll(value, COLS - 1, 1), pltpu.roll(value, 1, 1))
    return value + other


def dot(a, b):
    return jnp.dot(a, b, preferred_element_type=F32)


def dot_nt(a, b):
    return lax.dot_general(a, b, (((1,), (1,)), ((), ())), preferred_element_type=F32)


def block_kernel(
    counts,
    s_ref, even_ref, odd_ref, left_ref, right_ref, wo_ref, wg_ref, wc_ref, wq_ref,
    out_ref, gf_ref, gw_ref,
    ext_ref, side_ref, jst_ref, gst_ref, gsb_ref, pst_ref, psb_ref, qst_ref,
    pre_ref, prb_ref, ro_ref, rg_ref, rgb_ref, rq_ref, gp_ref, flat_ref, fa_ref, fb_ref, fc_ref,
):
    w, n = lax.axis_index(WIDE), lax.axis_index("narrow")
    lane32 = lanes_of((C2, COLS))
    lane64 = lanes_of((64, COLS))
    flag = lambda is_there: jnp.where(is_there, 1.0, 0.0)
    has_left, has_right = flag(n > 0), flag(n < counts[1] - 1)
    has_above, has_below = flag(w > 0), flag(w < counts[0] - 1)

    odd = w % 2
    below = (HALO + ROWS) * COLS
    ext_ref[:, row(HALO, ROWS)] = s_ref[...]
    for ref, first in ((even_ref, below - below * odd), (odd_ref, below * odd)):
        ext_ref[:, pl.ds(pl.multiple_of(first, COLS), HALO * COLS)] = ref[:, row(0, HALO)]

    left = left_ref[...].astype(F32) * has_left
    right = right_ref[...].astype(F32) * has_right
    for r in range(EXT):
        at_right = pltpu.roll(right, (-HALO * r) % COLS, 1)
        at_left = pltpu.roll(left, (COLS - HALO - HALO * r) % COLS, 1)
        side_ref[:, row(r)] = jnp.where(
            lane64 < HALO, at_right, jnp.where(lane64 >= COLS - HALO, at_left, 0.0)
        ).astype(BF)

    half = [None, None]
    for r in range(EXT):
        both = [ref[0:32, row(r)].astype(F32) for ref in (ext_ref, side_ref)]
        if r % 2 == 0:
            half = both
        else:
            mean = []
            for first, second in zip(half, both):
                total = first + second
                mean.append((pair_sum(total[0:16] + total[16:32]) * 0.125).astype(BF).astype(F32))
            for d in range(3):
                a, b = mean if d == 1 else turn(mean[0], mean[1], 2 * (d - 1))
                pst_ref[d * 16 : d * 16 + 16, row(r // 2)] = a.astype(BF)
                psb_ref[d * 16 : d * 16 + 16, row(r // 2)] = b.astype(BF)
        if HALO - 1 <= r <= HALO + ROWS:
            at = r - HALO + 1
            for d in range(3):
                a = both[0] if d == 1 else turn(both[0], both[1], d - 1)[0]
                jst_ref[d * 64 : d * 64 + 32, row(at)] = a.astype(BF)

    pre_ref[...] = dot(wc_ref[...], pst_ref[...])
    prb_ref[...] = dot(wc_ref[...], psb_ref[...])

    for at in range(22):
        a0 = ext_ref[32:64, row(at + 1)].astype(F32)
        b0 = side_ref[32:64, row(at + 1)].astype(F32)
        for d in range(3):
            a, b = (a0, b0) if d == 1 else turn(a0, b0, d - 1)
            gst_ref[d * 32 : d * 32 + 32, row(at)] = a.astype(BF)
            gsb_ref[d * 32 : d * 32 + 32, row(at)] = b.astype(BF)
    rg_ref[...] = dot(wg_ref[...], gst_ref[...])
    for d in range(3):
        rgb_ref[d * 32 : d * 32 + 32, :] = dot(
            wg_ref[d * 64 + 32 : d * 64 + 64, :], gsb_ref[...]
        )

    for at in range(10):
        keep = has_above if at == 0 else has_below if at == 9 else 1.0
        keep_side = keep * jnp.where(lane32 < 64, has_right, has_left)
        act, grad = [], []
        for ref, joined_ref, base, size, kept in (
            (pre_ref, rg_ref, 32, 64, keep),
            (prb_ref, rgb_ref, 0, 32, keep_side),
        ):
            value = (
                ref[0:32, row(at)] + ref[32:64, row(at + 1)] + ref[64:96, row(at + 2)]
            )
            sig = 1.0 / (1.0 + jnp.exp(-value))
            act.append((value * sig * kept).astype(BF).astype(F32))
            total = jnp.zeros((C2, COLS), F32)
            for r in (2 * at, 2 * at + 1):
                for d in range(3):
                    lo = d * size + base
                    total = total + joined_ref[lo : lo + 32, row(r + d)]
            grad_act = pair_sum(total).astype(BF).astype(F32)
            grad_pre = grad_act * (sig * (1.0 + value * (1.0 - sig)))
            grad.append((grad_pre * kept).astype(BF).astype(F32))
        for d in range(3):
            a = act[0] if d == 1 else turn(act[0], act[1], d - 1)[0]
            a = a.astype(BF)
            for r in (2 * at - 1, 2 * at):
                if 0 <= r < 18:
                    jst_ref[d * 64 + 32 : d * 64 + 64, row(r)] = a
            q = grad[0] if d == 1 else turn(grad[0], grad[1], 2 * (d - 1))[0]
            qst_ref[d * 32 : d * 32 + 32, row(at)] = q.astype(BF)

    ro_ref[...] = dot(wo_ref[...], jst_ref[...])
    for y in range(ROWS):
        value = ro_ref[0:32, row(y)] + ro_ref[32:64, row(y + 1)] + ro_ref[64:96, row(y + 2)]
        for z in range(2):
            flat_ref[pl.ds(2 * y + z, C1, stride=2 * ROWS), :] = value[z * 16 : z * 16 + 16]
    out_ref[...] = flat_ref[...].astype(BF)

    rq_ref[...] = dot(wq_ref[...], qst_ref[...])
    for at in range(ROWS // 2):
        pooled = rq_ref[0:16, row(at)] + rq_ref[16:32, row(at + 1)] + rq_ref[32:48, row(at + 2)]
        pooled = pooled.astype(BF).astype(F32) * 0.125
        for y in (2 * at, 2 * at + 1):
            for z in range(2):
                total = pooled
                for d in range(3):
                    lo = d * 64 + z * 16
                    total = total + rg_ref[lo : lo + 16, row(y + 2 + d)]
                flat_ref[pl.ds(2 * y + z, C1, stride=2 * ROWS), :] = total
    gf_ref[...] = flat_ref[...].astype(BF)

    own = row(1, ROWS)
    fa_ref[0:16, :] = jst_ref[64:80, own]
    fa_ref[16:48, :] = jst_ref[96:128, own]
    fa_ref[48:64, :] = jst_ref[64:80, own]
    fa_ref[64:96, :] = jst_ref[96:128, own]
    fa_ref[96:128, :] = jnp.zeros((32, ROWS * COLS), BF)
    fb_ref[0:48, :] = jst_ref[80:128, own]
    fb_ref[48:96, :] = jst_ref[80:128, own]
    fb_ref[96:128, :] = jnp.zeros((32, ROWS * COLS), BF)
    fc_ref[0:96, :] = jnp.zeros((96, 8 * COLS), BF)
    fc_ref[96:128, :] = qst_ref[32:64, row(1, 8)]
    fine, coarse = {}, {}
    for ky in range(3):
        shifted = gst_ref[:, row(4 - ky, ROWS)]
        ra, rb = dot_nt(shifted, fa_ref[...]), dot_nt(shifted, fb_ref[...])
        rc = dot_nt(pst_ref[:, row(1 + ky, 8)], fc_ref[...])
        for kx in range(3):
            lo = (2 - kx) * 32
            fine[ky, 0, kx] = ra[lo + 16 : lo + 32]
            fine[ky, 1, kx] = ra[lo : lo + 16] + rb[lo + 16 : lo + 32]
            fine[ky, 2, kx] = rb[lo : lo + 16]
            coarse[ky, kx] = rc[kx * 16 : kx * 16 + 16] * 0.5
    lane16 = lanes_of((16, COLS))
    order = [(ky, kz, kx) for ky in range(3) for kz in range(3) for kx in range(3)]
    for i in range(16):
        value = jnp.zeros((16, COLS), F32)
        if i < 14:
            value = jnp.where(lane16 < 48, fine[order[i]], value)
        if i < 13:
            value = jnp.where((lane16 >= 48) & (lane16 < 96), fine[order[14 + i]], value)
        if i < 9:
            value = jnp.where(lane16 >= 96, coarse[i // 3, i % 3], value)
        gw_ref[i * 16 : i * 16 + 16, :] = value.astype(BF)


def block(counts, operands):
    cells = (C1 * ROWS * 2, COLS)
    v = lambda rows_, lanes_, kind: pltpu.VMEM((rows_, lanes_ * COLS), kind)
    return pl.pallas_call(
        functools.partial(block_kernel, counts),
        out_shape=(
            jax.ShapeDtypeStruct(cells, BF),
            jax.ShapeDtypeStruct(cells, BF),
            jax.ShapeDtypeStruct((256, COLS), BF),
        ),
        scratch_shapes=[
            v(64, EXT, BF), v(64, EXT, BF),
            v(192, 18, BF),
            v(96, 22, BF), v(96, 22, BF),
            v(48, 12, BF), v(48, 12, BF),
            v(96, 10, BF),
            v(96, 12, F32), v(96, 12, F32),
            v(96, 18, F32),
            v(192, 22, F32), v(96, 22, F32),
            v(48, 10, F32),
            v(32, 8, BF),
            pltpu.VMEM(cells, F32),
            v(128, ROWS, BF), v(128, ROWS, BF), v(128, 8, BF),
        ],
        compiler_params=pltpu.CompilerParams(vmem_limit_bytes=VMEM_LIMIT),
        cost_estimate=pl.CostEstimate(flops=10**9, bytes_accessed=4 * 10**6, transcendentals=10**5),
        name="block",
    )(*operands)


def add_kernel(parts_ref, copies_ref):
    total = parts_ref[0].astype(F32)
    for i in range(1, parts_ref.shape[0]):
        total = total + parts_ref[i].astype(F32)
    total = total.astype(BF)
    for i in range(copies_ref.shape[0]):
        copies_ref[i] = total


def add_up(parts, copies):
    return pl.pallas_call(
        add_kernel,
        out_shape=jax.ShapeDtypeStruct((copies,) + parts.shape[1:], BF),
        compiler_params=pltpu.CompilerParams(vmem_limit_bytes=VMEM_LIMIT),
        name="add_up",
    )(parts)


def summed(grads):
    group, others = "far", ("near", "narrow")
    count, rest = lax.axis_size(group), lax.axis_size(others)
    length = grads.shape[0]
    share = -(-length // count)
    grads = jnp.pad(grads, ((0, share * count - length), (0, 0))).reshape(count, share, COLS)
    part = add_up(lax.all_to_all(grads, group, 0, 0, tiled=True), rest)
    part = add_up(lax.all_to_all(part, others, 0, 0, tiled=True), count)
    total = lax.all_to_all(part, group, 0, 0, tiled=True)
    return total.reshape(share * count, COLS)[:length]


def spread_kernel(fine_scale, coarse_scale, sum_ref, fine_ref, coarse_ref):
    for i in range(27):
        if i < 14:
            value = sum_ref[i * 16 : i * 16 + 16, :].astype(F32)
        else:
            at = (i - 14) * 16
            value = pltpu.roll(sum_ref[at : at + 16, :].astype(F32), 80, 1)
        fine_ref[i * 16 : i * 16 + 16, :] = value[:, 0:48] * fine_scale
        ky, kz, kx = i // 9, i // 3 % 3, i % 3
        if kz == 1:
            at = (ky * 3 + kx) * 16
            value = pltpu.roll(sum_ref[at : at + 16, :].astype(F32), 32, 1)[:, 0:32] * coarse_scale
        else:
            value = jnp.zeros((16, 32), F32)
        coarse_ref[i * 16 : i * 16 + 16, :] = value


def spread(total, fine_scale, coarse_scale):
    return pl.pallas_call(
        functools.partial(spread_kernel, fine_scale, coarse_scale),
        out_shape=(
            jax.ShapeDtypeStruct((432, 48), F32),
            jax.ShapeDtypeStruct((432, 32), F32),
        ),
        compiler_params=pltpu.CompilerParams(vmem_limit_bytes=VMEM_LIMIT),
        name="spread",
    )(total)


def weight_matrices(coarse_weight, fine_weight):
    fine = jnp.transpose(fine_weight, (2, 3, 4, 0, 1))
    planes = []
    for zo in range(2):
        first, second = fine[:, 1 - zo], fine[:, 2 - zo]
        both = (first[..., C1:].astype(F32) + second[..., C1:].astype(F32)).astype(BF)
        planes.append(jnp.concatenate([first[..., :C1], second[..., :C1], both], -1))
    stacked = jnp.stack(planes, 1)
    wo = jnp.transpose(stacked, (0, 1, 3, 2, 4)).reshape(96, 192)
    wg = jnp.transpose(stacked[::-1, :, ::-1], (0, 4, 2, 1, 3)).reshape(192, 96)
    middle = coarse_weight[:, :, :, 1, :]
    wc = jnp.transpose(middle, (2, 0, 3, 1)).reshape(96, 48)
    wq = jnp.transpose(middle[:, :, ::-1, ::-1], (2, 1, 3, 0)).reshape(48, 96)
    return wo, wg, wc, wq


def shards(features, cotangent, coarse_weight, fine_weight):
    wide, narrow = lax.axis_size(WIDE), lax.axis_size("narrow")
    matrices = weight_matrices(coarse_weight, fine_weight)
    sides = 1 if narrow == 2 else 2
    own, to_even, to_odd, strip = pack(features, cotangent, sides)
    swaps = lambda start: [
        pair for i in range(start, wide - 1, 2) for pair in ((i, i + 1), (i + 1, i))
    ]
    odd = lax.ppermute(to_odd, WIDE, swaps(1))
    even = lax.ppermute(to_even, WIDE, swaps(0))
    strip = strip + even[:, HALO * COLS :] + odd[:, HALO * COLS :]
    if sides == 1:
        left = right = lax.ppermute(strip, "narrow", [(0, 1), (1, 0)])
    else:
        right = lax.ppermute(strip[:, :COLS], "narrow", [(i + 1, i) for i in range(narrow - 1)])
        left = lax.ppermute(strip[:, COLS:], "narrow", [(i, i + 1) for i in range(narrow - 1)])
    output, grad_features, grads = block(
        (wide, narrow), (own, even, odd, left, right) + matrices
    )
    total = summed(grads)
    devices = wide * narrow
    all_cells = features.shape[1] * features.shape[2] * features.shape[3] * devices
    grad_fine, grad_coarse = spread(
        total, 1.0 / math.sqrt(all_cells), 1.0 / math.sqrt(all_cells // 8)
    )
    grad_fine = jnp.transpose(grad_fine.reshape(3, 3, 3, C1, C1 + C2), (3, 4, 0, 1, 2))
    grad_coarse = jnp.transpose(grad_coarse.reshape(3, 3, 3, C1, C2), (4, 3, 0, 1, 2))
    return (
        output.reshape(features.shape),
        grad_features.reshape(features.shape),
        grad_fine,
        grad_coarse,
    )


def solution(mesh):
    wide, narrow = mesh.shape["wide"], mesh.shape["narrow"]
    finer = jax.sharding.Mesh(mesh.devices.reshape(wide // 2, 2, narrow), WIDE + ("narrow",))
    placed = P(None, WIDE, None, "narrow")
    return jax.shard_map(
        shards,
        mesh=finer,
        in_specs=(placed, placed, P(), P()),
        out_specs=(placed, placed, P(), P()),
        check_vma=False,
    )
```

```python
import functools
import math

import jax
import jax.numpy as jnp
from jax import lax
from jax.experimental import pallas as pl
from jax.experimental.pallas import tpu as pltpu
from jax.sharding import PartitionSpec as P

C1, C2 = 16, 32
ROWS, COLS = 16, 128
HALO = 4
EXT = ROWS + 2 * HALO
BF, F32 = jnp.bfloat16, jnp.float32
VMEM_LIMIT = 48 * 1024 * 1024


def lanes_of(shape):
    return lax.broadcasted_iota(jnp.int32, shape, len(shape) - 1)


def row(index, count=1):
    return slice(index * COLS, (index + count) * COLS)


def pack_kernel(sides, in_ref, s_ref, even_ref, odd_ref, strip_ref, wide_ref):
    lane = lanes_of((C1, COLS))
    place = lax.axis_index("narrow")
    odd = lax.axis_index("wide") % 2
    for a in range(2):
        wide_ref[...] = in_ref[a].astype(F32)
        for z in range(2):
            chans = slice(a * 32 + z * 16, a * 32 + z * 16 + 16)
            strips = [jnp.zeros((C1, COLS), F32) for _ in range(sides)]
            for y in range(ROWS):
                value = wide_ref[pl.ds(2 * y + z, C1, stride=2 * ROWS), :]
                s_ref[chans, row(y)] = value.astype(BF)
                start = HALO * (y + HALO)
                inside = (lane >= start) & (lane < start + HALO)
                for side in range(sides):
                    if sides == 2:
                        shift = start + HALO * side
                    else:
                        shift = start + HALO * (1 - place)
                    strips[side] = jnp.where(inside, pltpu.roll(value, shift, 1), strips[side])
            for side in range(sides):
                strip_ref[chans, row(side)] = strips[side].astype(BF)
                turned = pltpu.roll(strips[side], 64, 1)
                for ref, first in ((even_ref, 80 * odd), (odd_ref, 80 - 80 * odd)):
                    kept = (lane >= first) & (lane < first + 4 * HALO)
                    ref[chans, row(HALO + side)] = jnp.where(kept, turned, 0.0).astype(BF)
    last = (ROWS - HALO) * COLS
    for ref, first in ((even_ref, last - last * odd), (odd_ref, last * odd)):
        ref[:, row(0, HALO)] = s_ref[:, pl.ds(pl.multiple_of(first, COLS), HALO * COLS)]


def pack(features, cotangent, sides):
    flat = lambda a: a.reshape(C1 * ROWS * 2, COLS)
    message = jax.ShapeDtypeStruct((64, (HALO + sides) * COLS), BF)
    return pl.pallas_call(
        functools.partial(pack_kernel, sides),
        out_shape=(
            jax.ShapeDtypeStruct((64, ROWS * COLS), BF),
            message,
            message,
            jax.ShapeDtypeStruct((64, sides * COLS), BF),
        ),
        scratch_shapes=[pltpu.VMEM((C1 * ROWS * 2, COLS), F32)],
        compiler_params=pltpu.CompilerParams(vmem_limit_bytes=VMEM_LIMIT),
        cost_estimate=pl.CostEstimate(flops=10**6, bytes_accessed=10**6, transcendentals=0),
        name="pack",
    )(jnp.stack([flat(features), flat(cotangent)]))


def turn(main, side, by):
    lane = lanes_of(main.shape)
    a, b = pltpu.roll(main, (-by) % COLS, 1), pltpu.roll(side, (-by) % COLS, 1)
    crossed = lane >= COLS - by if by > 0 else lane < -by
    return jnp.where(crossed, b, a), jnp.where(crossed, a, b)


def pair_sum(value):
    lane = lanes_of(value.shape)
    other = jnp.where(lane % 2 == 0, pltpu.roll(value, COLS - 1, 1), pltpu.roll(value, 1, 1))
    return value + other


def dot(a, b):
    return jnp.dot(a, b, preferred_element_type=F32)


def dot_nt(a, b):
    return lax.dot_general(a, b, (((1,), (1,)), ((), ())), preferred_element_type=F32)


def block_kernel(
    counts,
    s_ref, even_ref, odd_ref, left_ref, right_ref, wo_ref, wg_ref, wc_ref, wq_ref,
    out_ref, gf_ref, gw_ref,
    ext_ref, side_ref, jst_ref, gst_ref, gsb_ref, pst_ref, psb_ref, qst_ref,
    pre_ref, prb_ref, ro_ref, rg_ref, rgb_ref, rq_ref, gp_ref, flat_ref, fa_ref, fb_ref, fc_ref,
):
    w, n = lax.axis_index("wide"), lax.axis_index("narrow")
    lane32 = lanes_of((C2, COLS))
    lane64 = lanes_of((64, COLS))
    flag = lambda is_there: jnp.where(is_there, 1.0, 0.0)
    has_left, has_right = flag(n > 0), flag(n < counts[1] - 1)
    has_above, has_below = flag(w > 0), flag(w < counts[0] - 1)

    odd = w % 2
    below = (HALO + ROWS) * COLS
    ext_ref[:, row(HALO, ROWS)] = s_ref[...]
    for ref, first in ((even_ref, below - below * odd), (odd_ref, below * odd)):
        ext_ref[:, pl.ds(pl.multiple_of(first, COLS), HALO * COLS)] = ref[:, row(0, HALO)]

    left = left_ref[...].astype(F32) * has_left
    right = right_ref[...].astype(F32) * has_right
    for r in range(EXT):
        at_right = pltpu.roll(right, (-HALO * r) % COLS, 1)
        at_left = pltpu.roll(left, (COLS - HALO - HALO * r) % COLS, 1)
        side_ref[:, row(r)] = jnp.where(
            lane64 < HALO, at_right, jnp.where(lane64 >= COLS - HALO, at_left, 0.0)
        ).astype(BF)

    half = [None, None]
    for r in range(EXT):
        both = [ref[0:32, row(r)].astype(F32) for ref in (ext_ref, side_ref)]
        if r % 2 == 0:
            half = both
        else:
            mean = []
            for first, second in zip(half, both):
                total = first + second
                mean.append((pair_sum(total[0:16] + total[16:32]) * 0.125).astype(BF).astype(F32))
            for d in range(3):
                a, b = mean if d == 1 else turn(mean[0], mean[1], 2 * (d - 1))
                pst_ref[d * 16 : d * 16 + 16, row(r // 2)] = a.astype(BF)
                psb_ref[d * 16 : d * 16 + 16, row(r // 2)] = b.astype(BF)
        if HALO - 1 <= r <= HALO + ROWS:
            at = r - HALO + 1
            for d in range(3):
                a = both[0] if d == 1 else turn(both[0], both[1], d - 1)[0]
                jst_ref[d * 64 : d * 64 + 32, row(at)] = a.astype(BF)

    pre_ref[...] = dot(wc_ref[...], pst_ref[...])
    prb_ref[...] = dot(wc_ref[...], psb_ref[...])

    for at in range(22):
        a0 = ext_ref[32:64, row(at + 1)].astype(F32)
        b0 = side_ref[32:64, row(at + 1)].astype(F32)
        for d in range(3):
            a, b = (a0, b0) if d == 1 else turn(a0, b0, d - 1)
            gst_ref[d * 32 : d * 32 + 32, row(at)] = a.astype(BF)
            gsb_ref[d * 32 : d * 32 + 32, row(at)] = b.astype(BF)
    rg_ref[...] = dot(wg_ref[...], gst_ref[...])
    for d in range(3):
        rgb_ref[d * 32 : d * 32 + 32, :] = dot(
            wg_ref[d * 64 + 32 : d * 64 + 64, :], gsb_ref[...]
        )

    for at in range(10):
        keep = has_above if at == 0 else has_below if at == 9 else 1.0
        keep_side = keep * jnp.where(lane32 < 64, has_right, has_left)
        act, grad = [], []
        for ref, joined_ref, base, size, kept in (
            (pre_ref, rg_ref, 32, 64, keep),
            (prb_ref, rgb_ref, 0, 32, keep_side),
        ):
            value = (
                ref[0:32, row(at)] + ref[32:64, row(at + 1)] + ref[64:96, row(at + 2)]
            )
            sig = 1.0 / (1.0 + jnp.exp(-value))
            act.append((value * sig * kept).astype(BF).astype(F32))
            total = jnp.zeros((C2, COLS), F32)
            for r in (2 * at, 2 * at + 1):
                for d in range(3):
                    lo = d * size + base
                    total = total + joined_ref[lo : lo + 32, row(r + d)]
            grad_act = pair_sum(total).astype(BF).astype(F32)
            grad_pre = grad_act * (sig * (1.0 + value * (1.0 - sig)))
            grad.append((grad_pre * kept).astype(BF).astype(F32))
        for d in range(3):
            a = act[0] if d == 1 else turn(act[0], act[1], d - 1)[0]
            a = a.astype(BF)
            for r in (2 * at - 1, 2 * at):
                if 0 <= r < 18:
                    jst_ref[d * 64 + 32 : d * 64 + 64, row(r)] = a
            q = grad[0] if d == 1 else turn(grad[0], grad[1], 2 * (d - 1))[0]
            qst_ref[d * 32 : d * 32 + 32, row(at)] = q.astype(BF)

    ro_ref[...] = dot(wo_ref[...], jst_ref[...])
    for y in range(ROWS):
        value = ro_ref[0:32, row(y)] + ro_ref[32:64, row(y + 1)] + ro_ref[64:96, row(y + 2)]
        for z in range(2):
            flat_ref[pl.ds(2 * y + z, C1, stride=2 * ROWS), :] = value[z * 16 : z * 16 + 16]
    out_ref[...] = flat_ref[...].astype(BF)

    rq_ref[...] = dot(wq_ref[...], qst_ref[...])
    for at in range(ROWS // 2):
        pooled = rq_ref[0:16, row(at)] + rq_ref[16:32, row(at + 1)] + rq_ref[32:48, row(at + 2)]
        pooled = pooled.astype(BF).astype(F32) * 0.125
        for y in (2 * at, 2 * at + 1):
            for z in range(2):
                total = pooled
                for d in range(3):
                    lo = d * 64 + z * 16
                    total = total + rg_ref[lo : lo + 16, row(y + 2 + d)]
                flat_ref[pl.ds(2 * y + z, C1, stride=2 * ROWS), :] = total
    gf_ref[...] = flat_ref[...].astype(BF)

    own = row(1, ROWS)
    fa_ref[0:16, :] = jst_ref[64:80, own]
    fa_ref[16:48, :] = jst_ref[96:128, own]
    fa_ref[48:64, :] = jst_ref[64:80, own]
    fa_ref[64:96, :] = jst_ref[96:128, own]
    fa_ref[96:128, :] = jnp.zeros((32, ROWS * COLS), BF)
    fb_ref[0:48, :] = jst_ref[80:128, own]
    fb_ref[48:96, :] = jst_ref[80:128, own]
    fb_ref[96:128, :] = jnp.zeros((32, ROWS * COLS), BF)
    fc_ref[0:96, :] = jnp.zeros((96, 8 * COLS), BF)
    fc_ref[96:128, :] = qst_ref[32:64, row(1, 8)]
    fine, coarse = {}, {}
    for ky in range(3):
        shifted = gst_ref[:, row(4 - ky, ROWS)]
        ra, rb = dot_nt(shifted, fa_ref[...]), dot_nt(shifted, fb_ref[...])
        rc = dot_nt(pst_ref[:, row(1 + ky, 8)], fc_ref[...])
        for kx in range(3):
            lo = (2 - kx) * 32
            fine[ky, 0, kx] = ra[lo + 16 : lo + 32]
            fine[ky, 1, kx] = ra[lo : lo + 16] + rb[lo + 16 : lo + 32]
            fine[ky, 2, kx] = rb[lo : lo + 16]
            coarse[ky, kx] = rc[kx * 16 : kx * 16 + 16] * 0.5
    lane16 = lanes_of((16, COLS))
    order = [(ky, kz, kx) for ky in range(3) for kz in range(3) for kx in range(3)]
    for i in range(16):
        value = jnp.zeros((16, COLS), F32)
        if i < 14:
            value = jnp.where(lane16 < 48, fine[order[i]], value)
        if i < 13:
            value = jnp.where((lane16 >= 48) & (lane16 < 96), fine[order[14 + i]], value)
        if i < 9:
            value = jnp.where(lane16 >= 96, coarse[i // 3, i % 3], value)
        gw_ref[i * 16 : i * 16 + 16, :] = value.astype(BF)


def block(counts, operands):
    cells = (C1 * ROWS * 2, COLS)
    v = lambda rows_, lanes_, kind: pltpu.VMEM((rows_, lanes_ * COLS), kind)
    return pl.pallas_call(
        functools.partial(block_kernel, counts),
        out_shape=(
            jax.ShapeDtypeStruct(cells, BF),
            jax.ShapeDtypeStruct(cells, BF),
            jax.ShapeDtypeStruct((256, COLS), BF),
        ),
        scratch_shapes=[
            v(64, EXT, BF), v(64, EXT, BF),
            v(192, 18, BF),
            v(96, 22, BF), v(96, 22, BF),
            v(48, 12, BF), v(48, 12, BF),
            v(96, 10, BF),
            v(96, 12, F32), v(96, 12, F32),
            v(96, 18, F32),
            v(192, 22, F32), v(96, 22, F32),
            v(48, 10, F32),
            v(32, 8, BF),
            pltpu.VMEM(cells, F32),
            v(128, ROWS, BF), v(128, ROWS, BF), v(128, 8, BF),
        ],
        compiler_params=pltpu.CompilerParams(vmem_limit_bytes=VMEM_LIMIT),
        cost_estimate=pl.CostEstimate(flops=10**9, bytes_accessed=4 * 10**6, transcendentals=10**5),
        name="block",
    )(*operands)


def add_kernel(parts_ref, copies_ref):
    total = parts_ref[0].astype(F32)
    for i in range(1, parts_ref.shape[0]):
        total = total + parts_ref[i].astype(F32)
    total = total.astype(BF)
    for i in range(parts_ref.shape[0]):
        copies_ref[i] = total


def add_up(parts):
    return pl.pallas_call(
        add_kernel,
        out_shape=jax.ShapeDtypeStruct(parts.shape, BF),
        compiler_params=pltpu.CompilerParams(vmem_limit_bytes=VMEM_LIMIT),
        name="add_up",
    )(parts)


def spread_kernel(fine_scale, coarse_scale, sum_ref, fine_ref, coarse_ref):
    for i in range(27):
        if i < 14:
            value = sum_ref[i * 16 : i * 16 + 16, :].astype(F32)
        else:
            at = (i - 14) * 16
            value = pltpu.roll(sum_ref[at : at + 16, :].astype(F32), 80, 1)
        fine_ref[i * 16 : i * 16 + 16, :] = value[:, 0:48] * fine_scale
        ky, kz, kx = i // 9, i // 3 % 3, i % 3
        if kz == 1:
            at = (ky * 3 + kx) * 16
            value = pltpu.roll(sum_ref[at : at + 16, :].astype(F32), 32, 1)[:, 0:32] * coarse_scale
        else:
            value = jnp.zeros((16, 32), F32)
        coarse_ref[i * 16 : i * 16 + 16, :] = value


def spread(total, fine_scale, coarse_scale):
    return pl.pallas_call(
        functools.partial(spread_kernel, fine_scale, coarse_scale),
        out_shape=(
            jax.ShapeDtypeStruct((432, 48), F32),
            jax.ShapeDtypeStruct((432, 32), F32),
        ),
        compiler_params=pltpu.CompilerParams(vmem_limit_bytes=VMEM_LIMIT),
        name="spread",
    )(total)


def weight_matrices(coarse_weight, fine_weight):
    fine = jnp.transpose(fine_weight, (2, 3, 4, 0, 1))
    planes = []
    for zo in range(2):
        first, second = fine[:, 1 - zo], fine[:, 2 - zo]
        both = (first[..., C1:].astype(F32) + second[..., C1:].astype(F32)).astype(BF)
        planes.append(jnp.concatenate([first[..., :C1], second[..., :C1], both], -1))
    stacked = jnp.stack(planes, 1)
    wo = jnp.transpose(stacked, (0, 1, 3, 2, 4)).reshape(96, 192)
    wg = jnp.transpose(stacked[::-1, :, ::-1], (0, 4, 2, 1, 3)).reshape(192, 96)
    middle = coarse_weight[:, :, :, 1, :]
    wc = jnp.transpose(middle, (2, 0, 3, 1)).reshape(96, 48)
    wq = jnp.transpose(middle[:, :, ::-1, ::-1], (2, 1, 3, 0)).reshape(48, 96)
    return wo, wg, wc, wq


def shards(features, cotangent, coarse_weight, fine_weight):
    wide, narrow = lax.axis_size("wide"), lax.axis_size("narrow")
    matrices = weight_matrices(coarse_weight, fine_weight)
    sides = 1 if narrow == 2 else 2
    own, to_even, to_odd, strip = pack(features, cotangent, sides)
    swap = [pair for i in range(0, wide - 1, 2) for pair in ((i, i + 1), (i + 1, i))]
    relay = [pair for i in range(0, wide - 2, 2) for pair in ((i + 2, i), (i + 1, i + 3))]
    odd = lax.ppermute(lax.ppermute(to_odd, "wide", relay), "wide", swap)
    even = lax.ppermute(to_even, "wide", swap)
    strip = strip + even[:, HALO * COLS :] + odd[:, HALO * COLS :]
    if sides == 1:
        left = right = lax.ppermute(strip, "narrow", [(0, 1), (1, 0)])
    else:
        right = lax.ppermute(strip[:, :COLS], "narrow", [(i + 1, i) for i in range(narrow - 1)])
        left = lax.ppermute(strip[:, COLS:], "narrow", [(i, i + 1) for i in range(narrow - 1)])
    output, grad_features, grads = block(
        (wide, narrow), (own, even, odd, left, right) + matrices
    )
    devices = wide * narrow
    share = -(-256 // devices)
    grads = jnp.pad(grads, ((0, share * devices - 256), (0, 0))).reshape(devices, share, COLS)
    both = ("wide", "narrow")
    parts = lax.all_to_all(grads, both, 0, 0, tiled=True)
    total = lax.all_to_all(add_up(parts), both, 0, 0, tiled=True)
    total = total.reshape(share * devices, COLS)[:256]
    all_cells = features.shape[1] * features.shape[2] * features.shape[3] * devices
    grad_fine, grad_coarse = spread(
        total, 1.0 / math.sqrt(all_cells), 1.0 / math.sqrt(all_cells // 8)
    )
    grad_fine = jnp.transpose(grad_fine.reshape(3, 3, 3, C1, C1 + C2), (3, 4, 0, 1, 2))
    grad_coarse = jnp.transpose(grad_coarse.reshape(3, 3, 3, C1, C2), (4, 3, 0, 1, 2))
    return (
        output.reshape(features.shape),
        grad_features.reshape(features.shape),
        grad_fine,
        grad_coarse,
    )


def solution(mesh):
    placed = P(None, "wide", None, "narrow")
    return jax.shard_map(
        shards,
        mesh=mesh,
        in_specs=(placed, placed, P(), P()),
        out_specs=(placed, placed, P(), P()),
        check_vma=False,
    )
```

```python
import functools
import math

import jax
import jax.numpy as jnp
from jax import lax
from jax.experimental import pallas as pl
from jax.experimental.pallas import tpu as pltpu
from jax.sharding import PartitionSpec as P

C1, C2 = 16, 32
ROWS, COLS = 16, 128
HALO = 4
EXT = ROWS + 2 * HALO
BF, F32 = jnp.bfloat16, jnp.float32
VMEM_LIMIT = 48 * 1024 * 1024


def lanes_of(shape):
    return lax.broadcasted_iota(jnp.int32, shape, len(shape) - 1)


def row(index, count=1):
    return slice(index * COLS, (index + count) * COLS)


def pack_kernel(sides, in_ref, s_ref, even_ref, odd_ref, strip_ref, wide_ref):
    lane = lanes_of((C1, COLS))
    place = lax.axis_index("narrow")
    odd = lax.axis_index("wide") % 2
    for a in range(2):
        wide_ref[...] = in_ref[a].astype(F32)
        for z in range(2):
            chans = slice(a * 32 + z * 16, a * 32 + z * 16 + 16)
            strips = [jnp.zeros((C1, COLS), F32) for _ in range(sides)]
            for y in range(ROWS):
                value = wide_ref[pl.ds(2 * y + z, C1, stride=2 * ROWS), :]
                s_ref[chans, row(y)] = value.astype(BF)
                start = HALO * (y + HALO)
                inside = (lane >= start) & (lane < start + HALO)
                for side in range(sides):
                    if sides == 2:
                        shift = start + HALO * side
                    else:
                        shift = start + HALO * (1 - place)
                    strips[side] = jnp.where(inside, pltpu.roll(value, shift, 1), strips[side])
            for side in range(sides):
                strip_ref[chans, row(side)] = strips[side].astype(BF)
                turned = pltpu.roll(strips[side], 64, 1)
                for ref, first in ((even_ref, 80 * odd), (odd_ref, 80 - 80 * odd)):
                    kept = (lane >= first) & (lane < first + 4 * HALO)
                    ref[chans, row(HALO + side)] = jnp.where(kept, turned, 0.0).astype(BF)
    last = (ROWS - HALO) * COLS
    for ref, first in ((even_ref, last - last * odd), (odd_ref, last * odd)):
        ref[:, row(0, HALO)] = s_ref[:, pl.ds(pl.multiple_of(first, COLS), HALO * COLS)]


def pack(features, cotangent, sides):
    flat = lambda a: a.reshape(C1 * ROWS * 2, COLS)
    message = jax.ShapeDtypeStruct((64, (HALO + sides) * COLS), BF)
    return pl.pallas_call(
        functools.partial(pack_kernel, sides),
        out_shape=(
            jax.ShapeDtypeStruct((64, ROWS * COLS), BF),
            message,
            message,
            jax.ShapeDtypeStruct((64, sides * COLS), BF),
        ),
        scratch_shapes=[pltpu.VMEM((C1 * ROWS * 2, COLS), F32)],
        compiler_params=pltpu.CompilerParams(vmem_limit_bytes=VMEM_LIMIT),
        cost_estimate=pl.CostEstimate(flops=10**6, bytes_accessed=10**6, transcendentals=0),
        name="pack",
    )(jnp.stack([flat(features), flat(cotangent)]))


def turn(main, side, by):
    lane = lanes_of(main.shape)
    a, b = pltpu.roll(main, (-by) % COLS, 1), pltpu.roll(side, (-by) % COLS, 1)
    crossed = lane >= COLS - by if by > 0 else lane < -by
    return jnp.where(crossed, b, a), jnp.where(crossed, a, b)


def pair_sum(value):
    lane = lanes_of(value.shape)
    other = jnp.where(lane % 2 == 0, pltpu.roll(value, COLS - 1, 1), pltpu.roll(value, 1, 1))
    return value + other


def dot(a, b):
    return jnp.dot(a, b, preferred_element_type=F32)


def dot_nt(a, b):
    return lax.dot_general(a, b, (((1,), (1,)), ((), ())), preferred_element_type=F32)


def block_kernel(
    counts,
    s_ref, odd_ref, even_ref, left_ref, right_ref, wo_ref, wg_ref, wc_ref, wq_ref,
    out_ref, gf_ref, gw_ref,
    ext_ref, side_ref, jst_ref, gst_ref, gsb_ref, pst_ref, psb_ref, qst_ref,
    pre_ref, prb_ref, ro_ref, rg_ref, rgb_ref, rq_ref, gp_ref, flat_ref, fa_ref, fb_ref, fc_ref,
):
    w, n = lax.axis_index("wide"), lax.axis_index("narrow")
    lane32 = lanes_of((C2, COLS))
    lane64 = lanes_of((64, COLS))
    flag = lambda is_there: jnp.where(is_there, 1.0, 0.0)
    has_left, has_right = flag(n > 0), flag(n < counts[1] - 1)
    has_above, has_below = flag(w > 0), flag(w < counts[0] - 1)

    odd = w % 2
    below = (HALO + ROWS) * COLS
    ext_ref[:, row(HALO, ROWS)] = s_ref[...]
    for ref, first in ((even_ref, below - below * odd), (odd_ref, below * odd)):
        ext_ref[:, pl.ds(pl.multiple_of(first, COLS), HALO * COLS)] = ref[:, row(0, HALO)]

    left = left_ref[...].astype(F32) * has_left
    right = right_ref[...].astype(F32) * has_right
    for r in range(EXT):
        at_right = pltpu.roll(right, (-HALO * r) % COLS, 1)
        at_left = pltpu.roll(left, (COLS - HALO - HALO * r) % COLS, 1)
        side_ref[:, row(r)] = jnp.where(
            lane64 < HALO, at_right, jnp.where(lane64 >= COLS - HALO, at_left, 0.0)
        ).astype(BF)

    half = [None, None]
    for r in range(EXT):
        both = [ref[0:32, row(r)].astype(F32) for ref in (ext_ref, side_ref)]
        if r % 2 == 0:
            half = both
        else:
            mean = []
            for first, second in zip(half, both):
                total = first + second
                mean.append((pair_sum(total[0:16] + total[16:32]) * 0.125).astype(BF).astype(F32))
            for d in range(3):
                a, b = mean if d == 1 else turn(mean[0], mean[1], 2 * (d - 1))
                pst_ref[d * 16 : d * 16 + 16, row(r // 2)] = a.astype(BF)
                psb_ref[d * 16 : d * 16 + 16, row(r // 2)] = b.astype(BF)
        if HALO - 1 <= r <= HALO + ROWS:
            at = r - HALO + 1
            for d in range(3):
                a = both[0] if d == 1 else turn(both[0], both[1], d - 1)[0]
                jst_ref[d * 64 : d * 64 + 32, row(at)] = a.astype(BF)

    pre_ref[...] = dot(wc_ref[...], pst_ref[...])
    prb_ref[...] = dot(wc_ref[...], psb_ref[...])

    for at in range(22):
        a0 = ext_ref[32:64, row(at + 1)].astype(F32)
        b0 = side_ref[32:64, row(at + 1)].astype(F32)
        for d in range(3):
            a, b = (a0, b0) if d == 1 else turn(a0, b0, d - 1)
            gst_ref[d * 32 : d * 32 + 32, row(at)] = a.astype(BF)
            gsb_ref[d * 32 : d * 32 + 32, row(at)] = b.astype(BF)
    rg_ref[...] = dot(wg_ref[...], gst_ref[...])
    for d in range(3):
        rgb_ref[d * 32 : d * 32 + 32, :] = dot(
            wg_ref[d * 64 + 32 : d * 64 + 64, :], gsb_ref[...]
        )

    for at in range(10):
        keep = has_above if at == 0 else has_below if at == 9 else 1.0
        keep_side = keep * jnp.where(lane32 < 64, has_right, has_left)
        act, grad = [], []
        for ref, joined_ref, base, size, kept in (
            (pre_ref, rg_ref, 32, 64, keep),
            (prb_ref, rgb_ref, 0, 32, keep_side),
        ):
            value = (
                ref[0:32, row(at)] + ref[32:64, row(at + 1)] + ref[64:96, row(at + 2)]
            )
            sig = 1.0 / (1.0 + jnp.exp(-value))
            act.append((value * sig * kept).astype(BF).astype(F32))
            total = jnp.zeros((C2, COLS), F32)
            for r in (2 * at, 2 * at + 1):
                for d in range(3):
                    lo = d * size + base
                    total = total + joined_ref[lo : lo + 32, row(r + d)]
            grad_act = pair_sum(total).astype(BF).astype(F32)
            grad_pre = grad_act * (sig * (1.0 + value * (1.0 - sig)))
            grad.append((grad_pre * kept).astype(BF).astype(F32))
        for d in range(3):
            a = act[0] if d == 1 else turn(act[0], act[1], d - 1)[0]
            a = a.astype(BF)
            for r in (2 * at - 1, 2 * at):
                if 0 <= r < 18:
                    jst_ref[d * 64 + 32 : d * 64 + 64, row(r)] = a
            q = grad[0] if d == 1 else turn(grad[0], grad[1], 2 * (d - 1))[0]
            qst_ref[d * 32 : d * 32 + 32, row(at)] = q.astype(BF)

    ro_ref[...] = dot(wo_ref[...], jst_ref[...])
    for y in range(ROWS):
        value = ro_ref[0:32, row(y)] + ro_ref[32:64, row(y + 1)] + ro_ref[64:96, row(y + 2)]
        for z in range(2):
            flat_ref[pl.ds(2 * y + z, C1, stride=2 * ROWS), :] = value[z * 16 : z * 16 + 16]
    out_ref[...] = flat_ref[...].astype(BF)

    rq_ref[...] = dot(wq_ref[...], qst_ref[...])
    for at in range(ROWS // 2):
        pooled = rq_ref[0:16, row(at)] + rq_ref[16:32, row(at + 1)] + rq_ref[32:48, row(at + 2)]
        pooled = pooled.astype(BF).astype(F32) * 0.125
        for y in (2 * at, 2 * at + 1):
            for z in range(2):
                total = pooled
                for d in range(3):
                    lo = d * 64 + z * 16
                    total = total + rg_ref[lo : lo + 16, row(y + 2 + d)]
                flat_ref[pl.ds(2 * y + z, C1, stride=2 * ROWS), :] = total
    gf_ref[...] = flat_ref[...].astype(BF)

    own = row(1, ROWS)
    fa_ref[0:16, :] = jst_ref[64:80, own]
    fa_ref[16:48, :] = jst_ref[96:128, own]
    fa_ref[48:64, :] = jst_ref[64:80, own]
    fa_ref[64:96, :] = jst_ref[96:128, own]
    fa_ref[96:128, :] = jnp.zeros((32, ROWS * COLS), BF)
    fb_ref[0:48, :] = jst_ref[80:128, own]
    fb_ref[48:96, :] = jst_ref[80:128, own]
    fb_ref[96:128, :] = jnp.zeros((32, ROWS * COLS), BF)
    fc_ref[0:96, :] = jnp.zeros((96, 8 * COLS), BF)
    fc_ref[96:128, :] = qst_ref[32:64, row(1, 8)]
    fine, coarse = {}, {}
    for ky in range(3):
        shifted = gst_ref[:, row(4 - ky, ROWS)]
        ra, rb = dot_nt(shifted, fa_ref[...]), dot_nt(shifted, fb_ref[...])
        rc = dot_nt(pst_ref[:, row(1 + ky, 8)], fc_ref[...])
        for kx in range(3):
            lo = (2 - kx) * 32
            fine[ky, 0, kx] = ra[lo + 16 : lo + 32]
            fine[ky, 1, kx] = ra[lo : lo + 16] + rb[lo + 16 : lo + 32]
            fine[ky, 2, kx] = rb[lo : lo + 16]
            coarse[ky, kx] = rc[kx * 16 : kx * 16 + 16] * 0.5
    lane16 = lanes_of((16, COLS))
    order = [(ky, kz, kx) for ky in range(3) for kz in range(3) for kx in range(3)]
    for i in range(16):
        value = jnp.zeros((16, COLS), F32)
        if i < 14:
            value = jnp.where(lane16 < 48, fine[order[i]], value)
        if i < 13:
            value = jnp.where((lane16 >= 48) & (lane16 < 96), fine[order[14 + i]], value)
        if i < 9:
            value = jnp.where(lane16 >= 96, coarse[i // 3, i % 3], value)
        gw_ref[i * 16 : i * 16 + 16, :] = value.astype(BF)


def block(counts, operands):
    cells = (C1 * ROWS * 2, COLS)
    v = lambda rows_, lanes_, kind: pltpu.VMEM((rows_, lanes_ * COLS), kind)
    return pl.pallas_call(
        functools.partial(block_kernel, counts),
        out_shape=(
            jax.ShapeDtypeStruct(cells, BF),
            jax.ShapeDtypeStruct(cells, BF),
            jax.ShapeDtypeStruct((256, COLS), BF),
        ),
        scratch_shapes=[
            v(64, EXT, BF), v(64, EXT, BF),
            v(192, 18, BF),
            v(96, 22, BF), v(96, 22, BF),
            v(48, 12, BF), v(48, 12, BF),
            v(96, 10, BF),
            v(96, 12, F32), v(96, 12, F32),
            v(96, 18, F32),
            v(192, 22, F32), v(96, 22, F32),
            v(48, 10, F32),
            v(32, 8, BF),
            pltpu.VMEM(cells, F32),
            v(128, ROWS, BF), v(128, ROWS, BF), v(128, 8, BF),
        ],
        compiler_params=pltpu.CompilerParams(vmem_limit_bytes=VMEM_LIMIT),
        cost_estimate=pl.CostEstimate(flops=10**9, bytes_accessed=4 * 10**6, transcendentals=10**5),
        name="block",
    )(*operands)


def add_kernel(parts_ref, copies_ref):
    total = parts_ref[0].astype(F32)
    for i in range(1, parts_ref.shape[0]):
        total = total + parts_ref[i].astype(F32)
    total = total.astype(BF)
    for i in range(parts_ref.shape[0]):
        copies_ref[i] = total


def add_up(parts):
    return pl.pallas_call(
        add_kernel,
        out_shape=jax.ShapeDtypeStruct(parts.shape, BF),
        compiler_params=pltpu.CompilerParams(vmem_limit_bytes=VMEM_LIMIT),
        name="add_up",
    )(parts)


def spread_kernel(fine_scale, coarse_scale, sum_ref, fine_ref, coarse_ref):
    for i in range(27):
        if i < 14:
            value = sum_ref[i * 16 : i * 16 + 16, :].astype(F32)
        else:
            at = (i - 14) * 16
            value = pltpu.roll(sum_ref[at : at + 16, :].astype(F32), 80, 1)
        fine_ref[i * 16 : i * 16 + 16, :] = value[:, 0:48] * fine_scale
        ky, kz, kx = i // 9, i // 3 % 3, i % 3
        if kz == 1:
            at = (ky * 3 + kx) * 16
            value = pltpu.roll(sum_ref[at : at + 16, :].astype(F32), 32, 1)[:, 0:32] * coarse_scale
        else:
            value = jnp.zeros((16, 32), F32)
        coarse_ref[i * 16 : i * 16 + 16, :] = value


def spread(total, fine_scale, coarse_scale):
    return pl.pallas_call(
        functools.partial(spread_kernel, fine_scale, coarse_scale),
        out_shape=(
            jax.ShapeDtypeStruct((432, 48), F32),
            jax.ShapeDtypeStruct((432, 32), F32),
        ),
        compiler_params=pltpu.CompilerParams(vmem_limit_bytes=VMEM_LIMIT),
        name="spread",
    )(total)


def weight_matrices(coarse_weight, fine_weight):
    fine = jnp.transpose(fine_weight, (2, 3, 4, 0, 1))
    planes = []
    for zo in range(2):
        first, second = fine[:, 1 - zo], fine[:, 2 - zo]
        both = (first[..., C1:].astype(F32) + second[..., C1:].astype(F32)).astype(BF)
        planes.append(jnp.concatenate([first[..., :C1], second[..., :C1], both], -1))
    stacked = jnp.stack(planes, 1)
    wo = jnp.transpose(stacked, (0, 1, 3, 2, 4)).reshape(96, 192)
    wg = jnp.transpose(stacked[::-1, :, ::-1], (0, 4, 2, 1, 3)).reshape(192, 96)
    middle = coarse_weight[:, :, :, 1, :]
    wc = jnp.transpose(middle, (2, 0, 3, 1)).reshape(96, 48)
    wq = jnp.transpose(middle[:, :, ::-1, ::-1], (2, 1, 3, 0)).reshape(48, 96)
    return wo, wg, wc, wq


def shards(features, cotangent, coarse_weight, fine_weight):
    wide, narrow = lax.axis_size("wide"), lax.axis_size("narrow")
    matrices = weight_matrices(coarse_weight, fine_weight)
    sides = 1 if narrow == 2 else 2
    own, to_even, to_odd, strip = pack(features, cotangent, sides)
    swaps = lambda start: [
        pair for i in range(start, wide - 1, 2) for pair in ((i, i + 1), (i + 1, i))
    ]
    odd = lax.ppermute(to_odd, "wide", swaps(1))
    even = lax.ppermute(to_even, "wide", swaps(0))
    strip = strip + odd[:, HALO * COLS :] + even[:, HALO * COLS :]
    if sides == 1:
        left = right = lax.ppermute(strip, "narrow", [(0, 1), (1, 0)])
    else:
        right = lax.ppermute(strip[:, :COLS], "narrow", [(i + 1, i) for i in range(narrow - 1)])
        left = lax.ppermute(strip[:, COLS:], "narrow", [(i, i + 1) for i in range(narrow - 1)])
    output, grad_features, grads = block(
        (wide, narrow), (own, odd, even, left, right) + matrices
    )
    devices = wide * narrow
    share = -(-256 // devices)
    grads = jnp.pad(grads, ((0, share * devices - 256), (0, 0))).reshape(devices, share, COLS)
    both = ("wide", "narrow")
    parts = lax.all_to_all(grads, both, 0, 0, tiled=True)
    total = lax.all_to_all(add_up(parts), both, 0, 0, tiled=True)
    total = total.reshape(share * devices, COLS)[:256]
    all_cells = features.shape[1] * features.shape[2] * features.shape[3] * devices
    grad_fine, grad_coarse = spread(
        total, 1.0 / math.sqrt(all_cells), 1.0 / math.sqrt(all_cells // 8)
    )
    grad_fine = jnp.transpose(grad_fine.reshape(3, 3, 3, C1, C1 + C2), (3, 4, 0, 1, 2))
    grad_coarse = jnp.transpose(grad_coarse.reshape(3, 3, 3, C1, C2), (4, 3, 0, 1, 2))
    return (
        output.reshape(features.shape),
        grad_features.reshape(features.shape),
        grad_fine,
        grad_coarse,
    )


def solution(mesh):
    placed = P(None, "wide", None, "narrow")
    return jax.shard_map(
        shards,
        mesh=mesh,
        in_specs=(placed, placed, P(), P()),
        out_specs=(placed, placed, P(), P()),
        check_vma=False,
    )
```

```python
import functools
import math

import jax
import jax.numpy as jnp
from jax import lax
from jax.experimental import pallas as pl
from jax.experimental.pallas import tpu as pltpu
from jax.sharding import PartitionSpec as P

C1, C2 = 16, 32
ROWS, COLS = 16, 128
HALO = 4
BF, F32 = jnp.bfloat16, jnp.float32
VMEM_LIMIT = 48 * 1024 * 1024


def lanes_of(shape):
    return lax.broadcasted_iota(jnp.int32, shape, len(shape) - 1)


def row(index, count=1):
    return slice(index * COLS, (index + count) * COLS)


def pair_sum(value):
    lane = lanes_of(value.shape)
    other = jnp.where(lane % 2 == 0, pltpu.roll(value, COLS - 1, 1), pltpu.roll(value, 1, 1))
    return value + other


def pooled(first, second):
    total = first + second
    return (pair_sum(total[0:16] + total[16:32]) * 0.125).astype(BF)


def dot(a, b):
    return jnp.dot(a, b, preferred_element_type=F32)


def dot_nt(a, b):
    return lax.dot_general(a, b, (((1,), (1,)), ((), ())), preferred_element_type=F32)


def params():
    return pltpu.CompilerParams(vmem_limit_bytes=VMEM_LIMIT)


SLOTS = 5


def pack_kernel(sides, in_ref, s_ref, strip_ref, odd_ref, even_ref, wide_ref, base_ref):
    lane = lanes_of((C1, COLS))
    place = lax.axis_index("narrow")
    odd = lax.axis_index("wide") % 2
    strips = [[jnp.zeros((C1, COLS), F32) for _ in range(sides)] for _ in range(2)]
    for a in range(2):
        wide_ref[...] = in_ref[a].astype(F32)
        for z in range(2):
            chans = slice(a * 32 + z * 16, a * 32 + z * 16 + 16)
            for y in range(ROWS):
                value = wide_ref[pl.ds(2 * y + z, C1, stride=2 * ROWS), :]
                s_ref[chans, row(y)] = value.astype(BF)
                start = 64 * a + HALO * y
                inside = (lane >= start) & (lane < start + HALO)
                for side in range(sides):
                    if sides == 2:
                        shift = (start + HALO * side) % COLS
                    else:
                        shift = lax.rem(start + HALO * (1 - place), COLS)
                    strips[z][side] = jnp.where(inside, pltpu.roll(value, shift, 1), strips[z][side])
    for z in range(2):
        for side in range(sides):
            strip_ref[z * 16 : z * 16 + 16, row(side)] = strips[z][side].astype(BF)
    for to, near, pairs, cot in ((0, ROWS - 1, (6, 7), ROWS - 3), (1, 0, (0, 1), 0)):
        base_ref[to, :, row(0)] = s_ref[0:32, row(near)]
        for i, pair in enumerate(pairs):
            first, second = (s_ref[0:32, row(2 * pair + j)].astype(F32) for j in range(2))
            base_ref[to, i * 16 : i * 16 + 16, row(1)] = pooled(first, second)
        base_ref[to, :, row(2, 3)] = s_ref[32:64, row(cot, 3)]
    even_ref[:, row(0, SLOTS)] = base_ref[odd]
    odd_ref[:, row(0, SLOTS)] = base_ref[1 - odd]
    even_ref[:, row(SLOTS, sides)] = jnp.zeros((32, sides * COLS), BF)
    odd_ref[:, row(SLOTS, sides)] = jnp.zeros((32, sides * COLS), BF)


def pack(features, cotangent, sides):
    flat = lambda a: a.reshape(C1 * ROWS * 2, COLS)
    message = jax.ShapeDtypeStruct((32, (SLOTS + sides) * COLS), BF)
    return pl.pallas_call(
        functools.partial(pack_kernel, sides),
        out_shape=(
            jax.ShapeDtypeStruct((64, ROWS * COLS), BF),
            jax.ShapeDtypeStruct((32, sides * COLS), BF),
            message,
            message,
        ),
        scratch_shapes=[
            pltpu.VMEM((C1 * ROWS * 2, COLS), F32),
            pltpu.VMEM((2, 32, SLOTS * COLS), BF),
        ],
        compiler_params=params(),
        cost_estimate=pl.CostEstimate(flops=10**6, bytes_accessed=10**6, transcendentals=0),
        name="pack",
    )(jnp.stack([flat(features), flat(cotangent)]))


def beside(columns, at):
    lane = lanes_of(columns[0].shape)
    if len(columns) == 1:
        place = lax.axis_index("narrow")
        first = (COLS - HALO) * place
        turned = pltpu.roll(columns[0], lax.rem(COLS - at + first, COLS), 1)
        return jnp.where((lane >= first) & (lane < first + HALO), turned, 0.0)
    right = pltpu.roll(columns[0], (-at) % COLS, 1)
    left = pltpu.roll(columns[1], (COLS - HALO - at) % COLS, 1)
    return jnp.where(lane < HALO, right, jnp.where(lane >= COLS - HALO, left, 0.0))


def turn(main, side, by):
    lane = lanes_of(main.shape)
    a, b = pltpu.roll(main, (-by) % COLS, 1), pltpu.roll(side, (-by) % COLS, 1)
    crossed = lane >= COLS - by if by > 0 else lane < -by
    return jnp.where(crossed, b, a), jnp.where(crossed, a, b)


def put_pooled(main, side, main_ref, side_ref, at, side_at):
    main, side = main.astype(F32), side.astype(F32)
    for d in range(3):
        a, b = (main, side) if d == 1 else turn(main, side, 2 * (d - 1))
        main_ref[d * 16 : d * 16 + 16, row(at)] = a.astype(BF)
        side_ref[d * 16 : d * 16 + 16, row(side_at)] = b.astype(BF)


def put_cotangent(main, side, main_ref, side_ref, at, side_at):
    for d in range(3):
        a, b = (main, side) if d == 1 else turn(main, side, d - 1)
        main_ref[d * 32 : d * 32 + 32, row(at)] = a.astype(BF)
        side_ref[d * 32 : d * 32 + 32, row(side_at)] = b.astype(BF)


def put_features(main, side, ref, step, at):
    for d in range(3):
        a = main if d == 1 else turn(main, side, d - 1)[0]
        ref[d * step : d * step + 32, row(at)] = a.astype(BF)


def coarse_part(wg_ref, stack):
    return jnp.concatenate(
        [dot(wg_ref[d * 64 + 32 : d * 64 + 64, :], stack) for d in range(3)], 0
    )


def own_kernel(
    sides,
    s_ref, columns_ref, wc_ref, wg_ref,
    pst_ref, jf_ref, gst_ref, pre_ref, prb_ref, rg_ref, rgb_ref,
    psb_ref, gsb_ref,
):
    columns = [columns_ref[:, row(side)].astype(F32) for side in range(sides)]
    last = None
    for y in range(ROWS):
        main, side = s_ref[0:32, row(y)].astype(F32), beside(columns, HALO * y)
        put_features(main, side, jf_ref, 32, y)
        if y % 2 == 1:
            means = [pooled(a, b) for a, b in zip(last, (main, side))]
            put_pooled(*means, pst_ref, psb_ref, y // 2, y // 2)
        last = (main, side)
        main, side = s_ref[32:64, row(y)].astype(F32), beside(columns, 64 + HALO * y)
        put_cotangent(main, side, gst_ref, gsb_ref, y, y)
    pre_ref[...] = dot(wc_ref[...], pst_ref[...])
    prb_ref[...] = dot(wc_ref[...], psb_ref[...])
    rg_ref[...] = dot(wg_ref[...], gst_ref[...])
    rgb_ref[...] = coarse_part(wg_ref, gsb_ref[...])


def own_rows(s, columns, wc, wg, sides):
    half = ROWS // 2
    shape = lambda rows_, lanes_, kind: jax.ShapeDtypeStruct((rows_, lanes_ * COLS), kind)
    return pl.pallas_call(
        functools.partial(own_kernel, sides),
        out_shape=(
            shape(48, half, BF), shape(96, ROWS, BF), shape(96, ROWS, BF),
            shape(96, half, F32), shape(96, half, F32),
            shape(192, ROWS, F32), shape(96, ROWS, F32),
        ),
        scratch_shapes=[
            pltpu.VMEM((48, half * COLS), BF),
            pltpu.VMEM((96, ROWS * COLS), BF),
        ],
        compiler_params=params(),
        cost_estimate=pl.CostEstimate(flops=10**9, bytes_accessed=4 * 10**6, transcendentals=0),
        name="own_rows",
    )(s, columns, wc, wg)


def rest_kernel(
    counts, sides,
    odd_ref, even_ref, pst_own, jf_own, gst_own, pre_own, prb_own, rg_own, rgb_own,
    wo_ref, wg_ref, wc_ref, wq_ref,
    out_ref, gf_ref, gw_ref,
    halo_ref, jst_ref, gst_ref, gsb_ref, pst_ref, psb_ref, qst_ref,
    pre_ref, prb_ref, rg_ref, rgb_ref, ro_ref, rq_ref, flat_ref, fa_ref, fb_ref, fc_ref,
):
    w, n = lax.axis_index("wide"), lax.axis_index("narrow")
    lane32 = lanes_of((C2, COLS))
    flag = lambda is_there: jnp.where(is_there, 1.0, 0.0)
    has_left, has_right = flag(n > 0), flag(n < counts[1] - 1)
    has_above, has_below = flag(w > 0), flag(w < counts[0] - 1)

    odd = w % 2
    halo_ref[1 - odd] = even_ref[...]
    halo_ref[odd] = odd_ref[...]

    pst_ref[:, row(2, 8)] = pst_own[...]
    gst_ref[:, row(3, ROWS)] = gst_own[...]
    for d in range(3):
        jst_ref[d * 64 : d * 64 + 32, row(1, ROWS)] = jf_own[d * 32 : d * 32 + 32, :]
    for i in range(2):
        columns = [halo_ref[i, :, row(SLOTS + side)].astype(F32) for side in range(sides)]
        lane = HALO * (ROWS - HALO) if i == 0 else 0
        sides_f = [beside(columns, lane + HALO * r) for r in range(HALO)]
        near = HALO - 1 if i == 0 else 0
        put_features(halo_ref[i, :, row(0)].astype(F32), sides_f[near], jst_ref, 64, 17 * i)
        for j in range(2):
            main = halo_ref[i, j * 16 : j * 16 + 16, row(1)]
            side = pooled(sides_f[2 * j], sides_f[2 * j + 1])
            put_pooled(main, side, pst_ref, psb_ref, 10 * i + j, 2 * i + j)
        for j in range(3):
            main = halo_ref[i, :, row(2 + j)].astype(F32)
            side = beside(columns, 64 + lane + HALO * (j + 1 - i))
            put_cotangent(main, side, gst_ref, gsb_ref, 19 * i + j, 3 * i + j)
        pre_ref[:, row(2 * i, 2)] = dot(wc_ref[...], pst_ref[:, row(10 * i, 2)])
        rg_ref[:, row(3 * i, 3)] = dot(wg_ref[...], gst_ref[:, row(19 * i, 3)])
    prb_ref[...] = dot(wc_ref[...], psb_ref[...])
    rgb_ref[...] = coarse_part(wg_ref, gsb_ref[...])

    def part(own, halo, lo, size, at, edge, length):
        if at < edge:
            return halo[lo : lo + size, row(at)]
        if at < edge + length:
            return own[lo : lo + size, row(at - edge)]
        return halo[lo : lo + size, row(at - length)]

    for at in range(10):
        keep = has_above if at == 0 else has_below if at == 9 else 1.0
        keep_side = keep * jnp.where(lane32 < 64, has_right, has_left)
        act, grad = [], []
        for pre, joined, base, size, kept in (
            ((pre_own, pre_ref), (rg_own, rg_ref), 32, 64, keep),
            ((prb_own, prb_ref), (rgb_own, rgb_ref), 0, 32, keep_side),
        ):
            value = sum(part(*pre, d * 32, 32, at + d, 2, 8) for d in range(3))
            sig = 1.0 / (1.0 + jnp.exp(-value))
            act.append((value * sig * kept).astype(BF).astype(F32))
            total = sum(
                part(*joined, d * size + base, 32, r + d, 3, ROWS)
                for r in (2 * at, 2 * at + 1)
                for d in range(3)
            )
            grad_act = pair_sum(total).astype(BF).astype(F32)
            grad_pre = grad_act * (sig * (1.0 + value * (1.0 - sig)))
            grad.append((grad_pre * kept).astype(BF).astype(F32))
        for d in range(3):
            a = act[0] if d == 1 else turn(act[0], act[1], d - 1)[0]
            a = a.astype(BF)
            for r in (2 * at - 1, 2 * at):
                if 0 <= r < 18:
                    jst_ref[d * 64 + 32 : d * 64 + 64, row(r)] = a
            q = grad[0] if d == 1 else turn(grad[0], grad[1], 2 * (d - 1))[0]
            qst_ref[d * 32 : d * 32 + 32, row(at)] = q.astype(BF)

    ro_ref[...] = dot(wo_ref[...], jst_ref[...])
    for y in range(ROWS):
        value = ro_ref[0:32, row(y)] + ro_ref[32:64, row(y + 1)] + ro_ref[64:96, row(y + 2)]
        for z in range(2):
            flat_ref[pl.ds(2 * y + z, C1, stride=2 * ROWS), :] = value[z * 16 : z * 16 + 16]
    out_ref[...] = flat_ref[...].astype(BF)

    rq_ref[...] = dot(wq_ref[...], qst_ref[...])
    for at in range(ROWS // 2):
        coarse = rq_ref[0:16, row(at)] + rq_ref[16:32, row(at + 1)] + rq_ref[32:48, row(at + 2)]
        coarse = coarse.astype(BF).astype(F32) * 0.125
        for y in (2 * at, 2 * at + 1):
            for z in range(2):
                total = coarse
                for d in range(3):
                    total = total + part(rg_own, rg_ref, d * 64 + z * 16, 16, y + 2 + d, 3, ROWS)
                flat_ref[pl.ds(2 * y + z, C1, stride=2 * ROWS), :] = total
    gf_ref[...] = flat_ref[...].astype(BF)

    own = row(1, ROWS)
    fa_ref[0:16, :] = jst_ref[64:80, own]
    fa_ref[16:48, :] = jst_ref[96:128, own]
    fa_ref[48:64, :] = jst_ref[64:80, own]
    fa_ref[64:96, :] = jst_ref[96:128, own]
    fa_ref[96:128, :] = jnp.zeros((32, ROWS * COLS), BF)
    fb_ref[0:48, :] = jst_ref[80:128, own]
    fb_ref[48:96, :] = jst_ref[80:128, own]
    fb_ref[96:128, :] = jnp.zeros((32, ROWS * COLS), BF)
    fc_ref[0:96, :] = jnp.zeros((96, 8 * COLS), BF)
    fc_ref[96:128, :] = qst_ref[32:64, row(1, 8)]
    fine, coarse = {}, {}
    for ky in range(3):
        shifted = gst_ref[:, row(4 - ky, ROWS)]
        ra, rb = dot_nt(shifted, fa_ref[...]), dot_nt(shifted, fb_ref[...])
        rc = dot_nt(pst_ref[:, row(1 + ky, 8)], fc_ref[...])
        for kx in range(3):
            lo = (2 - kx) * 32
            fine[ky, 0, kx] = ra[lo + 16 : lo + 32]
            fine[ky, 1, kx] = ra[lo : lo + 16] + rb[lo + 16 : lo + 32]
            fine[ky, 2, kx] = rb[lo : lo + 16]
            coarse[ky, kx] = rc[kx * 16 : kx * 16 + 16] * 0.5
    lane16 = lanes_of((16, COLS))
    order = [(ky, kz, kx) for ky in range(3) for kz in range(3) for kx in range(3)]
    for i in range(16):
        value = jnp.zeros((16, COLS), F32)
        if i < 14:
            value = jnp.where(lane16 < 48, fine[order[i]], value)
        if i < 13:
            value = jnp.where((lane16 >= 48) & (lane16 < 96), fine[order[14 + i]], value)
        if i < 9:
            value = jnp.where(lane16 >= 96, coarse[i // 3, i % 3], value)
        gw_ref[i * 16 : i * 16 + 16, :] = value.astype(BF)


def rest(messages, own, matrices, counts, sides):
    cells = (C1 * ROWS * 2, COLS)
    v = lambda rows_, lanes_, kind: pltpu.VMEM((rows_, lanes_ * COLS), kind)
    return pl.pallas_call(
        functools.partial(rest_kernel, counts, sides),
        out_shape=(
            jax.ShapeDtypeStruct(cells, BF),
            jax.ShapeDtypeStruct(cells, BF),
            jax.ShapeDtypeStruct((256, COLS), BF),
        ),
        scratch_shapes=[
            pltpu.VMEM((2, 32, (SLOTS + sides) * COLS), BF),
            v(192, 18, BF),
            v(96, 22, BF), v(96, 6, BF),
            v(48, 12, BF), v(48, 4, BF),
            v(96, 10, BF),
            v(96, 4, F32), v(96, 4, F32),
            v(192, 6, F32), v(96, 6, F32),
            v(96, 18, F32),
            v(48, 10, F32),
            pltpu.VMEM(cells, F32),
            v(128, ROWS, BF), v(128, ROWS, BF), v(128, 8, BF),
        ],
        compiler_params=params(),
        cost_estimate=pl.CostEstimate(flops=10**9, bytes_accessed=4 * 10**6, transcendentals=10**5),
        name="rest",
    )(*messages, *own, *matrices)


def add_kernel(parts_ref, copies_ref):
    total = parts_ref[0].astype(F32)
    for i in range(1, parts_ref.shape[0]):
        total = total + parts_ref[i].astype(F32)
    total = total.astype(BF)
    for i in range(parts_ref.shape[0]):
        copies_ref[i] = total


def add_up(parts):
    return pl.pallas_call(
        add_kernel,
        out_shape=jax.ShapeDtypeStruct(parts.shape, BF),
        compiler_params=pltpu.CompilerParams(vmem_limit_bytes=VMEM_LIMIT),
        name="add_up",
    )(parts)


def spread_kernel(fine_scale, coarse_scale, sum_ref, fine_ref, coarse_ref):
    for i in range(27):
        if i < 14:
            value = sum_ref[i * 16 : i * 16 + 16, :].astype(F32)
        else:
            at = (i - 14) * 16
            value = pltpu.roll(sum_ref[at : at + 16, :].astype(F32), 80, 1)
        fine_ref[i * 16 : i * 16 + 16, :] = value[:, 0:48] * fine_scale
        ky, kz, kx = i // 9, i // 3 % 3, i % 3
        if kz == 1:
            at = (ky * 3 + kx) * 16
            value = pltpu.roll(sum_ref[at : at + 16, :].astype(F32), 32, 1)[:, 0:32] * coarse_scale
        else:
            value = jnp.zeros((16, 32), F32)
        coarse_ref[i * 16 : i * 16 + 16, :] = value


def spread(total, fine_scale, coarse_scale):
    return pl.pallas_call(
        functools.partial(spread_kernel, fine_scale, coarse_scale),
        out_shape=(
            jax.ShapeDtypeStruct((432, 48), F32),
            jax.ShapeDtypeStruct((432, 32), F32),
        ),
        compiler_params=pltpu.CompilerParams(vmem_limit_bytes=VMEM_LIMIT),
        name="spread",
    )(total)


def weight_matrices(coarse_weight, fine_weight):
    fine = jnp.transpose(fine_weight, (2, 3, 4, 0, 1))
    planes = []
    for zo in range(2):
        first, second = fine[:, 1 - zo], fine[:, 2 - zo]
        both = (first[..., C1:].astype(F32) + second[..., C1:].astype(F32)).astype(BF)
        planes.append(jnp.concatenate([first[..., :C1], second[..., :C1], both], -1))
    stacked = jnp.stack(planes, 1)
    wo = jnp.transpose(stacked, (0, 1, 3, 2, 4)).reshape(96, 192)
    wg = jnp.transpose(stacked[::-1, :, ::-1], (0, 4, 2, 1, 3)).reshape(192, 96)
    middle = coarse_weight[:, :, :, 1, :]
    wc = jnp.transpose(middle, (2, 0, 3, 1)).reshape(96, 48)
    wq = jnp.transpose(middle[:, :, ::-1, ::-1], (2, 1, 3, 0)).reshape(48, 96)
    return wo, wg, wc, wq


def shards(features, cotangent, coarse_weight, fine_weight):
    wide, narrow = lax.axis_size("wide"), lax.axis_size("narrow")
    wo, wg, wc, wq = weight_matrices(coarse_weight, fine_weight)
    sides = 1 if narrow == 2 else 2
    own, strip, to_odd, to_even = pack(features, cotangent, sides)
    if sides == 1:
        columns = lax.ppermute(strip, "narrow", [(0, 1), (1, 0)])
    else:
        right = lax.ppermute(strip[:, :COLS], "narrow", [(i + 1, i) for i in range(narrow - 1)])
        left = lax.ppermute(strip[:, COLS:], "narrow", [(i, i + 1) for i in range(narrow - 1)])
        columns = jnp.concatenate([right, left], 1)
    swaps = lambda start: [
        pair for i in range(start, wide - 1, 2) for pair in ((i, i + 1), (i + 1, i))
    ]
    with_columns = lambda message: lax.dynamic_update_slice(message, columns, (0, SLOTS * COLS))
    odd = lax.ppermute(with_columns(to_odd), "wide", swaps(1))
    even = lax.ppermute(with_columns(to_even), "wide", swaps(0))
    stacks = own_rows(own, columns, wc, wg, sides)
    output, grad_features, grads = rest((odd, even), stacks, (wo, wg, wc, wq), (wide, narrow), sides)
    devices = wide * narrow
    share = -(-256 // devices)
    grads = jnp.pad(grads, ((0, share * devices - 256), (0, 0))).reshape(devices, share, COLS)
    both = ("wide", "narrow")
    parts = lax.all_to_all(grads, both, 0, 0, tiled=True)
    total = lax.all_to_all(add_up(parts), both, 0, 0, tiled=True)
    total = total.reshape(share * devices, COLS)[:256]
    all_cells = features.shape[1] * features.shape[2] * features.shape[3] * devices
    grad_fine, grad_coarse = spread(
        total, 1.0 / math.sqrt(all_cells), 1.0 / math.sqrt(all_cells // 8)
    )
    grad_fine = jnp.transpose(grad_fine.reshape(3, 3, 3, C1, C1 + C2), (3, 4, 0, 1, 2))
    grad_coarse = jnp.transpose(grad_coarse.reshape(3, 3, 3, C1, C2), (4, 3, 0, 1, 2))
    return (
        output.reshape(features.shape),
        grad_features.reshape(features.shape),
        grad_fine,
        grad_coarse,
    )


def solution(mesh):
    placed = P(None, "wide", None, "narrow")
    return jax.shard_map(
        shards,
        mesh=mesh,
        in_specs=(placed, placed, P(), P()),
        out_specs=(placed, placed, P(), P()),
        check_vma=False,
    )
```

```python
import functools
import math

import jax
import jax.numpy as jnp
from jax import lax
from jax.experimental import pallas as pl
from jax.experimental.pallas import tpu as pltpu
from jax.sharding import PartitionSpec as P

C1, C2 = 16, 32
ROWS, COLS = 16, 128
HALO = 4
BF, F32 = jnp.bfloat16, jnp.float32
VMEM_LIMIT = 48 * 1024 * 1024


def lanes_of(shape):
    return lax.broadcasted_iota(jnp.int32, shape, len(shape) - 1)


def row(index, count=1):
    return slice(index * COLS, (index + count) * COLS)


def pair_sum(value):
    lane = lanes_of(value.shape)
    other = jnp.where(lane % 2 == 0, pltpu.roll(value, COLS - 1, 1), pltpu.roll(value, 1, 1))
    return value + other


def pooled(first, second):
    total = first + second
    return (pair_sum(total[0:16] + total[16:32]) * 0.125).astype(BF)


def dot(a, b):
    return jnp.dot(a, b, preferred_element_type=F32)


def dot_nt(a, b):
    return lax.dot_general(a, b, (((1,), (1,)), ((), ())), preferred_element_type=F32)


def params():
    return pltpu.CompilerParams(vmem_limit_bytes=VMEM_LIMIT)


SLOTS = 5


def pack_kernel(sides, in_ref, s_ref, strip_ref, odd_ref, even_ref, wide_ref, base_ref):
    lane = lanes_of((C1, COLS))
    place = lax.axis_index("narrow")
    odd = lax.axis_index("wide") % 2
    strips = [[jnp.zeros((C1, COLS), F32) for _ in range(sides)] for _ in range(2)]
    for a in range(2):
        wide_ref[...] = in_ref[a].astype(F32)
        for z in range(2):
            chans = slice(a * 32 + z * 16, a * 32 + z * 16 + 16)
            for y in range(ROWS):
                value = wide_ref[pl.ds(2 * y + z, C1, stride=2 * ROWS), :]
                s_ref[chans, row(y)] = value.astype(BF)
                start = 64 * a + HALO * y
                inside = (lane >= start) & (lane < start + HALO)
                for side in range(sides):
                    if sides == 2:
                        shift = (start + HALO * side) % COLS
                    else:
                        shift = lax.rem(start + HALO * (1 - place), COLS)
                    strips[z][side] = jnp.where(inside, pltpu.roll(value, shift, 1), strips[z][side])
    for z in range(2):
        for side in range(sides):
            strip_ref[z * 16 : z * 16 + 16, row(side)] = strips[z][side].astype(BF)
    for to, near, pairs, cot in ((0, ROWS - 1, (6, 7), ROWS - 3), (1, 0, (0, 1), 0)):
        base_ref[to, :, row(0)] = s_ref[0:32, row(near)]
        for i, pair in enumerate(pairs):
            first, second = (s_ref[0:32, row(2 * pair + j)].astype(F32) for j in range(2))
            base_ref[to, i * 16 : i * 16 + 16, row(1)] = pooled(first, second)
        base_ref[to, :, row(2, 3)] = s_ref[32:64, row(cot, 3)]
        for side in range(sides):
            for z in range(2):
                kept = lane % 64 >= 48 if to == 0 else lane % 64 < 16
                value = jnp.where(kept, strips[z][side], 0.0).astype(BF)
                base_ref[to, z * 16 : z * 16 + 16, row(SLOTS + side)] = value
    even_ref[...] = base_ref[odd]
    odd_ref[...] = base_ref[1 - odd]


def pack(features, cotangent, sides):
    flat = lambda a: a.reshape(C1 * ROWS * 2, COLS)
    message = jax.ShapeDtypeStruct((32, (SLOTS + sides) * COLS), BF)
    return pl.pallas_call(
        functools.partial(pack_kernel, sides),
        out_shape=(
            jax.ShapeDtypeStruct((64, ROWS * COLS), BF),
            jax.ShapeDtypeStruct((32, sides * COLS), BF),
            message,
            message,
        ),
        scratch_shapes=[
            pltpu.VMEM((C1 * ROWS * 2, COLS), F32),
            pltpu.VMEM((2, 32, (SLOTS + sides) * COLS), BF),
        ],
        compiler_params=params(),
        cost_estimate=pl.CostEstimate(flops=10**6, bytes_accessed=10**6, transcendentals=0),
        name="pack",
    )(jnp.stack([flat(features), flat(cotangent)]))


def beside(columns, at):
    lane = lanes_of(columns[0].shape)
    if len(columns) == 1:
        place = lax.axis_index("narrow")
        first = (COLS - HALO) * place
        turned = pltpu.roll(columns[0], lax.rem(COLS - at + first, COLS), 1)
        return jnp.where((lane >= first) & (lane < first + HALO), turned, 0.0)
    right = pltpu.roll(columns[0], (-at) % COLS, 1)
    left = pltpu.roll(columns[1], (COLS - HALO - at) % COLS, 1)
    return jnp.where(lane < HALO, right, jnp.where(lane >= COLS - HALO, left, 0.0))


def turn(main, side, by):
    lane = lanes_of(main.shape)
    a, b = pltpu.roll(main, (-by) % COLS, 1), pltpu.roll(side, (-by) % COLS, 1)
    crossed = lane >= COLS - by if by > 0 else lane < -by
    return jnp.where(crossed, b, a), jnp.where(crossed, a, b)


def put_pooled(main, side, main_ref, side_ref, at, side_at):
    main, side = main.astype(F32), side.astype(F32)
    for d in range(3):
        a, b = (main, side) if d == 1 else turn(main, side, 2 * (d - 1))
        main_ref[d * 16 : d * 16 + 16, row(at)] = a.astype(BF)
        side_ref[d * 16 : d * 16 + 16, row(side_at)] = b.astype(BF)


def put_cotangent(main, side, main_ref, side_ref, at, side_at):
    for d in range(3):
        a, b = (main, side) if d == 1 else turn(main, side, d - 1)
        main_ref[d * 32 : d * 32 + 32, row(at)] = a.astype(BF)
        side_ref[d * 32 : d * 32 + 32, row(side_at)] = b.astype(BF)


def put_features(main, side, ref, step, at):
    for d in range(3):
        a = main if d == 1 else turn(main, side, d - 1)[0]
        ref[d * step : d * step + 32, row(at)] = a.astype(BF)


def coarse_part(wg_ref, stack):
    return jnp.concatenate(
        [dot(wg_ref[d * 64 + 32 : d * 64 + 64, :], stack) for d in range(3)], 0
    )


def own_kernel(
    sides,
    s_ref, columns_ref, wc_ref, wg_ref,
    pst_ref, jf_ref, gst_ref, pre_ref, prb_ref, rg_ref, rgb_ref,
    psb_ref, gsb_ref,
):
    columns = [columns_ref[:, row(side)].astype(F32) for side in range(sides)]
    last = None
    for y in range(ROWS):
        main, side = s_ref[0:32, row(y)].astype(F32), beside(columns, HALO * y)
        put_features(main, side, jf_ref, 32, y)
        if y % 2 == 1:
            means = [pooled(a, b) for a, b in zip(last, (main, side))]
            put_pooled(*means, pst_ref, psb_ref, y // 2, y // 2)
        last = (main, side)
        main, side = s_ref[32:64, row(y)].astype(F32), beside(columns, 64 + HALO * y)
        put_cotangent(main, side, gst_ref, gsb_ref, y, y)
    pre_ref[...] = dot(wc_ref[...], pst_ref[...])
    prb_ref[...] = dot(wc_ref[...], psb_ref[...])
    rg_ref[...] = dot(wg_ref[...], gst_ref[...])
    rgb_ref[...] = coarse_part(wg_ref, gsb_ref[...])


def own_rows(s, columns, wc, wg, sides):
    half = ROWS // 2
    shape = lambda rows_, lanes_, kind: jax.ShapeDtypeStruct((rows_, lanes_ * COLS), kind)
    return pl.pallas_call(
        functools.partial(own_kernel, sides),
        out_shape=(
            shape(48, half, BF), shape(96, ROWS, BF), shape(96, ROWS, BF),
            shape(96, half, F32), shape(96, half, F32),
            shape(192, ROWS, F32), shape(96, ROWS, F32),
        ),
        scratch_shapes=[
            pltpu.VMEM((48, half * COLS), BF),
            pltpu.VMEM((96, ROWS * COLS), BF),
        ],
        compiler_params=params(),
        cost_estimate=pl.CostEstimate(flops=10**9, bytes_accessed=4 * 10**6, transcendentals=0),
        name="own_rows",
    )(s, columns, wc, wg)


def rest_kernel(
    counts, sides,
    odd_ref, even_ref, corners_ref, pst_own, jf_own, gst_own, pre_own, prb_own, rg_own, rgb_own,
    wo_ref, wg_ref, wc_ref, wq_ref,
    out_ref, gf_ref, gw_ref,
    halo_ref, jst_ref, gst_ref, gsb_ref, pst_ref, psb_ref, qst_ref,
    pre_ref, prb_ref, rg_ref, rgb_ref, ro_ref, rq_ref, flat_ref, fa_ref, fb_ref, fc_ref,
):
    w, n = lax.axis_index("wide"), lax.axis_index("narrow")
    lane32 = lanes_of((C2, COLS))
    flag = lambda is_there: jnp.where(is_there, 1.0, 0.0)
    has_left, has_right = flag(n > 0), flag(n < counts[1] - 1)
    has_above, has_below = flag(w > 0), flag(w < counts[0] - 1)

    odd = w % 2
    halo_ref[1 - odd] = even_ref[:, row(0, SLOTS)]
    halo_ref[odd] = odd_ref[:, row(0, SLOTS)]
    columns = [corners_ref[:, row(side)].astype(F32) for side in range(sides)]

    pst_ref[:, row(2, 8)] = pst_own[...]
    gst_ref[:, row(3, ROWS)] = gst_own[...]
    for d in range(3):
        jst_ref[d * 64 : d * 64 + 32, row(1, ROWS)] = jf_own[d * 32 : d * 32 + 32, :]
    for i in range(2):
        lane = HALO * (ROWS - HALO) if i == 0 else 0
        sides_f = [beside(columns, lane + HALO * r) for r in range(HALO)]
        near = HALO - 1 if i == 0 else 0
        put_features(halo_ref[i, :, row(0)].astype(F32), sides_f[near], jst_ref, 64, 17 * i)
        for j in range(2):
            main = halo_ref[i, j * 16 : j * 16 + 16, row(1)]
            side = pooled(sides_f[2 * j], sides_f[2 * j + 1])
            put_pooled(main, side, pst_ref, psb_ref, 10 * i + j, 2 * i + j)
        for j in range(3):
            main = halo_ref[i, :, row(2 + j)].astype(F32)
            side = beside(columns, 64 + lane + HALO * (j + 1 - i))
            put_cotangent(main, side, gst_ref, gsb_ref, 19 * i + j, 3 * i + j)
        pre_ref[:, row(2 * i, 2)] = dot(wc_ref[...], pst_ref[:, row(10 * i, 2)])
        rg_ref[:, row(3 * i, 3)] = dot(wg_ref[...], gst_ref[:, row(19 * i, 3)])
    prb_ref[...] = dot(wc_ref[...], psb_ref[...])
    rgb_ref[...] = coarse_part(wg_ref, gsb_ref[...])

    def part(own, halo, lo, size, at, edge, length):
        if at < edge:
            return halo[lo : lo + size, row(at)]
        if at < edge + length:
            return own[lo : lo + size, row(at - edge)]
        return halo[lo : lo + size, row(at - length)]

    for at in range(10):
        keep = has_above if at == 0 else has_below if at == 9 else 1.0
        keep_side = keep * jnp.where(lane32 < 64, has_right, has_left)
        act, grad = [], []
        for pre, joined, base, size, kept in (
            ((pre_own, pre_ref), (rg_own, rg_ref), 32, 64, keep),
            ((prb_own, prb_ref), (rgb_own, rgb_ref), 0, 32, keep_side),
        ):
            value = sum(part(*pre, d * 32, 32, at + d, 2, 8) for d in range(3))
            sig = 1.0 / (1.0 + jnp.exp(-value))
            act.append((value * sig * kept).astype(BF).astype(F32))
            total = sum(
                part(*joined, d * size + base, 32, r + d, 3, ROWS)
                for r in (2 * at, 2 * at + 1)
                for d in range(3)
            )
            grad_act = pair_sum(total).astype(BF).astype(F32)
            grad_pre = grad_act * (sig * (1.0 + value * (1.0 - sig)))
            grad.append((grad_pre * kept).astype(BF).astype(F32))
        for d in range(3):
            a = act[0] if d == 1 else turn(act[0], act[1], d - 1)[0]
            a = a.astype(BF)
            for r in (2 * at - 1, 2 * at):
                if 0 <= r < 18:
                    jst_ref[d * 64 + 32 : d * 64 + 64, row(r)] = a
            q = grad[0] if d == 1 else turn(grad[0], grad[1], 2 * (d - 1))[0]
            qst_ref[d * 32 : d * 32 + 32, row(at)] = q.astype(BF)

    ro_ref[...] = dot(wo_ref[...], jst_ref[...])
    for y in range(ROWS):
        value = ro_ref[0:32, row(y)] + ro_ref[32:64, row(y + 1)] + ro_ref[64:96, row(y + 2)]
        for z in range(2):
            flat_ref[pl.ds(2 * y + z, C1, stride=2 * ROWS), :] = value[z * 16 : z * 16 + 16]
    out_ref[...] = flat_ref[...].astype(BF)

    rq_ref[...] = dot(wq_ref[...], qst_ref[...])
    for at in range(ROWS // 2):
        coarse = rq_ref[0:16, row(at)] + rq_ref[16:32, row(at + 1)] + rq_ref[32:48, row(at + 2)]
        coarse = coarse.astype(BF).astype(F32) * 0.125
        for y in (2 * at, 2 * at + 1):
            for z in range(2):
                total = coarse
                for d in range(3):
                    total = total + part(rg_own, rg_ref, d * 64 + z * 16, 16, y + 2 + d, 3, ROWS)
                flat_ref[pl.ds(2 * y + z, C1, stride=2 * ROWS), :] = total
    gf_ref[...] = flat_ref[...].astype(BF)

    own = row(1, ROWS)
    fa_ref[0:16, :] = jst_ref[64:80, own]
    fa_ref[16:48, :] = jst_ref[96:128, own]
    fa_ref[48:64, :] = jst_ref[64:80, own]
    fa_ref[64:96, :] = jst_ref[96:128, own]
    fa_ref[96:128, :] = jnp.zeros((32, ROWS * COLS), BF)
    fb_ref[0:48, :] = jst_ref[80:128, own]
    fb_ref[48:96, :] = jst_ref[80:128, own]
    fb_ref[96:128, :] = jnp.zeros((32, ROWS * COLS), BF)
    fc_ref[0:96, :] = jnp.zeros((96, 8 * COLS), BF)
    fc_ref[96:128, :] = qst_ref[32:64, row(1, 8)]
    fine, coarse = {}, {}
    for ky in range(3):
        shifted = gst_ref[:, row(4 - ky, ROWS)]
        ra, rb = dot_nt(shifted, fa_ref[...]), dot_nt(shifted, fb_ref[...])
        rc = dot_nt(pst_ref[:, row(1 + ky, 8)], fc_ref[...])
        for kx in range(3):
            lo = (2 - kx) * 32
            fine[ky, 0, kx] = ra[lo + 16 : lo + 32]
            fine[ky, 1, kx] = ra[lo : lo + 16] + rb[lo + 16 : lo + 32]
            fine[ky, 2, kx] = rb[lo : lo + 16]
            coarse[ky, kx] = rc[kx * 16 : kx * 16 + 16] * 0.5
    lane16 = lanes_of((16, COLS))
    order = [(ky, kz, kx) for ky in range(3) for kz in range(3) for kx in range(3)]
    for i in range(16):
        value = jnp.zeros((16, COLS), F32)
        if i < 14:
            value = jnp.where(lane16 < 48, fine[order[i]], value)
        if i < 13:
            value = jnp.where((lane16 >= 48) & (lane16 < 96), fine[order[14 + i]], value)
        if i < 9:
            value = jnp.where(lane16 >= 96, coarse[i // 3, i % 3], value)
        gw_ref[i * 16 : i * 16 + 16, :] = value.astype(BF)


def rest(messages, own, matrices, counts, sides):
    cells = (C1 * ROWS * 2, COLS)
    v = lambda rows_, lanes_, kind: pltpu.VMEM((rows_, lanes_ * COLS), kind)
    return pl.pallas_call(
        functools.partial(rest_kernel, counts, sides),
        out_shape=(
            jax.ShapeDtypeStruct(cells, BF),
            jax.ShapeDtypeStruct(cells, BF),
            jax.ShapeDtypeStruct((256, COLS), BF),
        ),
        scratch_shapes=[
            pltpu.VMEM((2, 32, SLOTS * COLS), BF),
            v(192, 18, BF),
            v(96, 22, BF), v(96, 6, BF),
            v(48, 12, BF), v(48, 4, BF),
            v(96, 10, BF),
            v(96, 4, F32), v(96, 4, F32),
            v(192, 6, F32), v(96, 6, F32),
            v(96, 18, F32),
            v(48, 10, F32),
            pltpu.VMEM(cells, F32),
            v(128, ROWS, BF), v(128, ROWS, BF), v(128, 8, BF),
        ],
        compiler_params=params(),
        cost_estimate=pl.CostEstimate(flops=10**9, bytes_accessed=4 * 10**6, transcendentals=10**5),
        name="rest",
    )(*messages, *own, *matrices)


def add_kernel(parts_ref, copies_ref):
    total = parts_ref[0].astype(F32)
    for i in range(1, parts_ref.shape[0]):
        total = total + parts_ref[i].astype(F32)
    total = total.astype(BF)
    for i in range(parts_ref.shape[0]):
        copies_ref[i] = total


def add_up(parts):
    return pl.pallas_call(
        add_kernel,
        out_shape=jax.ShapeDtypeStruct(parts.shape, BF),
        compiler_params=pltpu.CompilerParams(vmem_limit_bytes=VMEM_LIMIT),
        name="add_up",
    )(parts)


def spread_kernel(fine_scale, coarse_scale, sum_ref, fine_ref, coarse_ref):
    for i in range(27):
        if i < 14:
            value = sum_ref[i * 16 : i * 16 + 16, :].astype(F32)
        else:
            at = (i - 14) * 16
            value = pltpu.roll(sum_ref[at : at + 16, :].astype(F32), 80, 1)
        fine_ref[i * 16 : i * 16 + 16, :] = value[:, 0:48] * fine_scale
        ky, kz, kx = i // 9, i // 3 % 3, i % 3
        if kz == 1:
            at = (ky * 3 + kx) * 16
            value = pltpu.roll(sum_ref[at : at + 16, :].astype(F32), 32, 1)[:, 0:32] * coarse_scale
        else:
            value = jnp.zeros((16, 32), F32)
        coarse_ref[i * 16 : i * 16 + 16, :] = value


def spread(total, fine_scale, coarse_scale):
    return pl.pallas_call(
        functools.partial(spread_kernel, fine_scale, coarse_scale),
        out_shape=(
            jax.ShapeDtypeStruct((432, 48), F32),
            jax.ShapeDtypeStruct((432, 32), F32),
        ),
        compiler_params=pltpu.CompilerParams(vmem_limit_bytes=VMEM_LIMIT),
        name="spread",
    )(total)


def matrices_kernel(
    fine_ref, coarse_ref, wo_ref, wg_ref, wc_ref, wq_ref, wide_ref, pieces_ref, blocks_ref
):
    lane = lanes_of((C1, COLS))
    wide_ref[:, 0:48] = fine_ref[...].astype(F32)
    for ky in range(3):
        for zo in range(2):
            tiles = [jnp.zeros((C1, COLS), F32) for _ in range(2)]
            for kx in range(3):
                at = ((ky * 3 + 1 - zo) * 3 + kx) * 16
                first, second = (wide_ref[at + i : at + i + 16, :] for i in (0, 48))
                both = (first + second).astype(BF).astype(F32)
                piece = jnp.where(lane < 32, pltpu.roll(second, 16, 1), pltpu.roll(both, 16, 1))
                piece = jnp.where(lane < 16, first, jnp.where(lane < 64, piece, 0.0))
                spot = (2 - kx) * 32 + zo * 16
                pieces_ref[2 - ky, spot : spot + 16, :] = piece
                tiles[kx // 2] = tiles[kx // 2] + (pltpu.roll(piece, 64, 1) if kx == 1 else piece)
            spot = ky * 32 + zo * 16
            wo_ref[spot : spot + 16, 0:128] = tiles[0].astype(BF)
            wo_ref[spot : spot + 16, 128:192] = tiles[1][:, 0:64].astype(BF)
    wide_ref[:, 0:32] = coarse_ref[...].astype(F32)
    for ky in range(3):
        total = jnp.zeros((C1, COLS), F32)
        for kx in range(3):
            at = ((ky * 3 + 1) * 3 + kx) * 16
            value = jnp.where(lane < 32, wide_ref[at : at + 16, :], 0.0)
            blocks_ref[ky, kx * 16 : kx * 16 + 16, :] = value
            spot = (2 - kx) * 32
            total = total + (pltpu.roll(value, spot, 1) if spot else value)
        wq_ref[(2 - ky) * 16 : (2 - ky) * 16 + 16, :] = total[:, 0:96].astype(BF)
    for d in range(3):
        wg_ref[d * 64 : d * 64 + 64, :] = jnp.transpose(pieces_ref[d])[0:64, 0:96].astype(BF)
        wc_ref[d * 32 : d * 32 + 32, :] = jnp.transpose(blocks_ref[d])[0:32, 0:48].astype(BF)


def weight_matrices(coarse_weight, fine_weight):
    fine = jnp.transpose(fine_weight, (2, 3, 4, 0, 1)).reshape(432, 48)
    coarse = jnp.transpose(coarse_weight, (2, 3, 4, 1, 0)).reshape(432, 32)
    shape = lambda *dims: jax.ShapeDtypeStruct(dims, BF)
    return pl.pallas_call(
        matrices_kernel,
        out_shape=(shape(96, 192), shape(192, 96), shape(96, 48), shape(48, 96)),
        scratch_shapes=[
            pltpu.VMEM((432, COLS), F32),
            pltpu.VMEM((3, COLS, COLS), F32),
            pltpu.VMEM((3, COLS, COLS), F32),
        ],
        compiler_params=params(),
        cost_estimate=pl.CostEstimate(flops=10**6, bytes_accessed=10**6, transcendentals=0),
        name="matrices",
    )(fine, coarse)


def beside_blocks(outer, narrow):
    if outer.shape[1] == COLS:
        return lax.ppermute(outer, "narrow", [(0, 1), (1, 0)])
    right = lax.ppermute(outer[:, :COLS], "narrow", [(i + 1, i) for i in range(narrow - 1)])
    left = lax.ppermute(outer[:, COLS:], "narrow", [(i, i + 1) for i in range(narrow - 1)])
    return jnp.concatenate([right, left], 1)


def shards(features, cotangent, coarse_weight, fine_weight):
    wide, narrow = lax.axis_size("wide"), lax.axis_size("narrow")
    sides = 1 if narrow == 2 else 2
    own, strip, to_odd, to_even = pack(features, cotangent, sides)
    swaps = lambda start: [
        pair for i in range(start, wide - 1, 2) for pair in ((i, i + 1), (i + 1, i))
    ]
    odd = lax.ppermute(to_odd, "wide", swaps(1))
    even = lax.ppermute(to_even, "wide", swaps(0))
    columns = beside_blocks(strip, narrow)
    wo, wg, wc, wq = weight_matrices(coarse_weight, fine_weight)
    corners = odd[:, SLOTS * COLS :] + even[:, SLOTS * COLS :]
    corners, columns = lax.optimization_barrier((corners, columns))
    corners = beside_blocks(corners, narrow)
    stacks = own_rows(own, columns, wc, wg, sides)
    output, grad_features, grads = rest((odd, even, corners), stacks, (wo, wg, wc, wq), (wide, narrow), sides)
    devices = wide * narrow
    share = -(-256 // devices)
    grads = jnp.pad(grads, ((0, share * devices - 256), (0, 0))).reshape(devices, share, COLS)
    both = ("wide", "narrow")
    parts = lax.all_to_all(grads, both, 0, 0, tiled=True)
    total = lax.all_to_all(add_up(parts), both, 0, 0, tiled=True)
    total = total.reshape(share * devices, COLS)[:256]
    all_cells = features.shape[1] * features.shape[2] * features.shape[3] * devices
    grad_fine, grad_coarse = spread(
        total, 1.0 / math.sqrt(all_cells), 1.0 / math.sqrt(all_cells // 8)
    )
    grad_fine = jnp.transpose(grad_fine.reshape(3, 3, 3, C1, C1 + C2), (3, 4, 0, 1, 2))
    grad_coarse = jnp.transpose(grad_coarse.reshape(3, 3, 3, C1, C2), (4, 3, 0, 1, 2))
    return (
        output.reshape(features.shape),
        grad_features.reshape(features.shape),
        grad_fine,
        grad_coarse,
    )


def solution(mesh):
    placed = P(None, "wide", None, "narrow")
    return jax.shard_map(
        shards,
        mesh=mesh,
        in_specs=(placed, placed, P(), P()),
        out_specs=(placed, placed, P(), P()),
        check_vma=False,
    )
```

```python
import functools
import math

import jax
import jax.numpy as jnp
from jax import lax
from jax.experimental import pallas as pl
from jax.experimental.pallas import tpu as pltpu
from jax.sharding import PartitionSpec as P

C1, C2 = 16, 32
ROWS, COLS = 16, 128
HALO = 4
BF, F32 = jnp.bfloat16, jnp.float32
VMEM_LIMIT = 48 * 1024 * 1024


def lanes_of(shape):
    return lax.broadcasted_iota(jnp.int32, shape, len(shape) - 1)


def row(index, count=1):
    return slice(index * COLS, (index + count) * COLS)


def pair_sum(value):
    lane = lanes_of(value.shape)
    other = jnp.where(lane % 2 == 0, pltpu.roll(value, COLS - 1, 1), pltpu.roll(value, 1, 1))
    return value + other


def pooled(first, second):
    total = first + second
    return (pair_sum(total[0:16] + total[16:32]) * 0.125).astype(BF)


def dot(a, b):
    return jnp.dot(a, b, preferred_element_type=F32)


def dot_nt(a, b):
    return lax.dot_general(a, b, (((1,), (1,)), ((), ())), preferred_element_type=F32)


def params():
    return pltpu.CompilerParams(vmem_limit_bytes=VMEM_LIMIT)


SLOTS = 5
CELLS = C1 * ROWS * 2
TAPS = 27 * C1


def pack_kernel(sides, in_ref, s_ref, strip_ref, odd_ref, even_ref, wide_ref, base_ref):
    lane = lanes_of((C1, COLS))
    place = lax.axis_index("narrow")
    odd = lax.axis_index("wide") % 2
    strips = [[jnp.zeros((C1, COLS), F32) for _ in range(sides)] for _ in range(2)]
    for a in range(2):
        wide_ref[...] = in_ref[a * CELLS : (a + 1) * CELLS, :].astype(F32)
        for z in range(2):
            chans = slice(a * 32 + z * 16, a * 32 + z * 16 + 16)
            for y in range(ROWS):
                value = wide_ref[pl.ds(2 * y + z, C1, stride=2 * ROWS), :]
                s_ref[chans, row(y)] = value.astype(BF)
                start = 64 * a + HALO * y
                inside = (lane >= start) & (lane < start + HALO)
                for side in range(sides):
                    if sides == 2:
                        shift = (start + HALO * side) % COLS
                    else:
                        shift = lax.rem(start + HALO * (1 - place), COLS)
                    strips[z][side] = jnp.where(inside, pltpu.roll(value, shift, 1), strips[z][side])
    for z in range(2):
        for side in range(sides):
            strip_ref[z * 16 : z * 16 + 16, row(side)] = strips[z][side].astype(BF)
    for to, near, pairs, cot in ((0, ROWS - 1, (6, 7), ROWS - 3), (1, 0, (0, 1), 0)):
        base_ref[to, :, row(0)] = s_ref[0:32, row(near)]
        for i, pair in enumerate(pairs):
            first, second = (s_ref[0:32, row(2 * pair + j)].astype(F32) for j in range(2))
            base_ref[to, i * 16 : i * 16 + 16, row(1)] = pooled(first, second)
        base_ref[to, :, row(2, 3)] = s_ref[32:64, row(cot, 3)]
        for side in range(sides):
            for z in range(2):
                kept = lane % 64 >= 48 if to == 0 else lane % 64 < 16
                value = jnp.where(kept, strips[z][side], 0.0).astype(BF)
                base_ref[to, z * 16 : z * 16 + 16, row(SLOTS + side)] = value
    even_ref[...] = base_ref[odd]
    odd_ref[...] = base_ref[1 - odd]


def stack(features, cotangent, coarse_weight, fine_weight):
    flat = lambda a: a.reshape(CELLS, COLS)
    fine = jnp.transpose(fine_weight, (2, 3, 4, 0, 1)).reshape(TAPS, 48)
    coarse = jnp.transpose(coarse_weight, (2, 3, 4, 1, 0)).reshape(TAPS, 32)
    weights = jnp.concatenate([fine, coarse, jnp.zeros((TAPS, 48), BF)], 1)
    return jnp.concatenate([flat(features), flat(cotangent), weights], 0)


def pack(stacked, sides):
    message = jax.ShapeDtypeStruct((32, (SLOTS + sides) * COLS), BF)
    return pl.pallas_call(
        functools.partial(pack_kernel, sides),
        out_shape=(
            jax.ShapeDtypeStruct((64, ROWS * COLS), BF),
            jax.ShapeDtypeStruct((32, sides * COLS), BF),
            message,
            message,
        ),
        scratch_shapes=[
            pltpu.VMEM((C1 * ROWS * 2, COLS), F32),
            pltpu.VMEM((2, 32, (SLOTS + sides) * COLS), BF),
        ],
        compiler_params=params(),
        cost_estimate=pl.CostEstimate(flops=10**6, bytes_accessed=10**6, transcendentals=0),
        name="pack",
    )(stacked)


def beside(columns, at):
    lane = lanes_of(columns[0].shape)
    if len(columns) == 1:
        place = lax.axis_index("narrow")
        first = (COLS - HALO) * place
        turned = pltpu.roll(columns[0], lax.rem(COLS - at + first, COLS), 1)
        return jnp.where((lane >= first) & (lane < first + HALO), turned, 0.0)
    right = pltpu.roll(columns[0], (-at) % COLS, 1)
    left = pltpu.roll(columns[1], (COLS - HALO - at) % COLS, 1)
    return jnp.where(lane < HALO, right, jnp.where(lane >= COLS - HALO, left, 0.0))


def turn(main, side, by):
    lane = lanes_of(main.shape)
    a, b = pltpu.roll(main, (-by) % COLS, 1), pltpu.roll(side, (-by) % COLS, 1)
    crossed = lane >= COLS - by if by > 0 else lane < -by
    return jnp.where(crossed, b, a), jnp.where(crossed, a, b)


def put_pooled(main, side, main_ref, side_ref, at, side_at):
    main, side = main.astype(F32), side.astype(F32)
    for d in range(3):
        a, b = (main, side) if d == 1 else turn(main, side, 2 * (d - 1))
        main_ref[d * 16 : d * 16 + 16, row(at)] = a.astype(BF)
        side_ref[d * 16 : d * 16 + 16, row(side_at)] = b.astype(BF)


def put_cotangent(main, side, main_ref, side_ref, at, side_at):
    for d in range(3):
        a, b = (main, side) if d == 1 else turn(main, side, d - 1)
        main_ref[d * 32 : d * 32 + 32, row(at)] = a.astype(BF)
        side_ref[d * 32 : d * 32 + 32, row(side_at)] = b.astype(BF)


def put_features(main, side, ref, step, at):
    for d in range(3):
        a = main if d == 1 else turn(main, side, d - 1)[0]
        ref[d * step : d * step + 32, row(at)] = a.astype(BF)


def coarse_part(wg_ref, stack):
    return jnp.concatenate(
        [dot(wg_ref[d * 64 + 32 : d * 64 + 64, :], stack) for d in range(3)], 0
    )


def own_kernel(
    sides,
    s_ref, columns_ref, wc_ref, wg_ref,
    pst_ref, jf_ref, gst_ref, pre_ref, prb_ref, rg_ref, rgb_ref,
    psb_ref, gsb_ref,
):
    columns = [columns_ref[:, row(side)].astype(F32) for side in range(sides)]
    last = None
    for y in range(ROWS):
        main, side = s_ref[0:32, row(y)].astype(F32), beside(columns, HALO * y)
        put_features(main, side, jf_ref, 32, y)
        if y % 2 == 1:
            means = [pooled(a, b) for a, b in zip(last, (main, side))]
            put_pooled(*means, pst_ref, psb_ref, y // 2, y // 2)
        last = (main, side)
        main, side = s_ref[32:64, row(y)].astype(F32), beside(columns, 64 + HALO * y)
        put_cotangent(main, side, gst_ref, gsb_ref, y, y)
    pre_ref[...] = dot(wc_ref[...], pst_ref[...])
    prb_ref[...] = dot(wc_ref[...], psb_ref[...])
    rg_ref[...] = dot(wg_ref[...], gst_ref[...])
    rgb_ref[...] = coarse_part(wg_ref, gsb_ref[...])


def own_rows(s, columns, wc, wg, sides):
    half = ROWS // 2
    shape = lambda rows_, lanes_, kind: jax.ShapeDtypeStruct((rows_, lanes_ * COLS), kind)
    return pl.pallas_call(
        functools.partial(own_kernel, sides),
        out_shape=(
            shape(48, half, BF), shape(96, ROWS, BF), shape(96, ROWS, BF),
            shape(96, half, F32), shape(96, half, F32),
            shape(192, ROWS, F32), shape(96, ROWS, F32),
        ),
        scratch_shapes=[
            pltpu.VMEM((48, half * COLS), BF),
            pltpu.VMEM((96, ROWS * COLS), BF),
        ],
        compiler_params=params(),
        cost_estimate=pl.CostEstimate(flops=10**9, bytes_accessed=4 * 10**6, transcendentals=0),
        name="own_rows",
    )(s, columns, wc, wg)


def rest_kernel(
    counts, sides,
    odd_ref, even_ref, corners_ref, pst_own, jf_own, gst_own, pre_own, prb_own, rg_own, rgb_own,
    wo_ref, wg_ref, wc_ref, wq_ref,
    out_ref, gf_ref, gw_ref,
    halo_ref, jst_ref, gst_ref, gsb_ref, pst_ref, psb_ref, qst_ref,
    pre_ref, prb_ref, rg_ref, rgb_ref, ro_ref, rq_ref, flat_ref, fa_ref, fb_ref, fc_ref,
):
    w, n = lax.axis_index("wide"), lax.axis_index("narrow")
    lane32 = lanes_of((C2, COLS))
    flag = lambda is_there: jnp.where(is_there, 1.0, 0.0)
    has_left, has_right = flag(n > 0), flag(n < counts[1] - 1)
    has_above, has_below = flag(w > 0), flag(w < counts[0] - 1)

    odd = w % 2
    halo_ref[1 - odd] = even_ref[:, row(0, SLOTS)]
    halo_ref[odd] = odd_ref[:, row(0, SLOTS)]
    columns = [corners_ref[:, row(side)].astype(F32) for side in range(sides)]

    pst_ref[:, row(2, 8)] = pst_own[...]
    gst_ref[:, row(3, ROWS)] = gst_own[...]
    for d in range(3):
        jst_ref[d * 64 : d * 64 + 32, row(1, ROWS)] = jf_own[d * 32 : d * 32 + 32, :]
    for i in range(2):
        lane = HALO * (ROWS - HALO) if i == 0 else 0
        sides_f = [beside(columns, lane + HALO * r) for r in range(HALO)]
        near = HALO - 1 if i == 0 else 0
        put_features(halo_ref[i, :, row(0)].astype(F32), sides_f[near], jst_ref, 64, 17 * i)
        for j in range(2):
            main = halo_ref[i, j * 16 : j * 16 + 16, row(1)]
            side = pooled(sides_f[2 * j], sides_f[2 * j + 1])
            put_pooled(main, side, pst_ref, psb_ref, 10 * i + j, 2 * i + j)
        for j in range(3):
            main = halo_ref[i, :, row(2 + j)].astype(F32)
            side = beside(columns, 64 + lane + HALO * (j + 1 - i))
            put_cotangent(main, side, gst_ref, gsb_ref, 19 * i + j, 3 * i + j)
        pre_ref[:, row(2 * i, 2)] = dot(wc_ref[...], pst_ref[:, row(10 * i, 2)])
        rg_ref[:, row(3 * i, 3)] = dot(wg_ref[...], gst_ref[:, row(19 * i, 3)])
    prb_ref[...] = dot(wc_ref[...], psb_ref[...])
    rgb_ref[...] = coarse_part(wg_ref, gsb_ref[...])

    def part(own, halo, lo, size, at, edge, length):
        if at < edge:
            return halo[lo : lo + size, row(at)]
        if at < edge + length:
            return own[lo : lo + size, row(at - edge)]
        return halo[lo : lo + size, row(at - length)]

    for at in range(10):
        keep = has_above if at == 0 else has_below if at == 9 else 1.0
        keep_side = keep * jnp.where(lane32 < 64, has_right, has_left)
        act, grad = [], []
        for pre, joined, base, size, kept in (
            ((pre_own, pre_ref), (rg_own, rg_ref), 32, 64, keep),
            ((prb_own, prb_ref), (rgb_own, rgb_ref), 0, 32, keep_side),
        ):
            value = sum(part(*pre, d * 32, 32, at + d, 2, 8) for d in range(3))
            sig = 1.0 / (1.0 + jnp.exp(-value))
            act.append((value * sig * kept).astype(BF).astype(F32))
            total = sum(
                part(*joined, d * size + base, 32, r + d, 3, ROWS)
                for r in (2 * at, 2 * at + 1)
                for d in range(3)
            )
            grad_act = pair_sum(total).astype(BF).astype(F32)
            grad_pre = grad_act * (sig * (1.0 + value * (1.0 - sig)))
            grad.append((grad_pre * kept).astype(BF).astype(F32))
        for d in range(3):
            a = act[0] if d == 1 else turn(act[0], act[1], d - 1)[0]
            a = a.astype(BF)
            for r in (2 * at - 1, 2 * at):
                if 0 <= r < 18:
                    jst_ref[d * 64 + 32 : d * 64 + 64, row(r)] = a
            q = grad[0] if d == 1 else turn(grad[0], grad[1], 2 * (d - 1))[0]
            qst_ref[d * 32 : d * 32 + 32, row(at)] = q.astype(BF)

    ro_ref[...] = dot(wo_ref[...], jst_ref[...])
    for y in range(ROWS):
        value = ro_ref[0:32, row(y)] + ro_ref[32:64, row(y + 1)] + ro_ref[64:96, row(y + 2)]
        for z in range(2):
            flat_ref[pl.ds(2 * y + z, C1, stride=2 * ROWS), :] = value[z * 16 : z * 16 + 16]
    out_ref[...] = flat_ref[...].astype(BF)

    rq_ref[...] = dot(wq_ref[...], qst_ref[...])
    for at in range(ROWS // 2):
        coarse = rq_ref[0:16, row(at)] + rq_ref[16:32, row(at + 1)] + rq_ref[32:48, row(at + 2)]
        coarse = coarse.astype(BF).astype(F32) * 0.125
        for y in (2 * at, 2 * at + 1):
            for z in range(2):
                total = coarse
                for d in range(3):
                    total = total + part(rg_own, rg_ref, d * 64 + z * 16, 16, y + 2 + d, 3, ROWS)
                flat_ref[pl.ds(2 * y + z, C1, stride=2 * ROWS), :] = total
    gf_ref[...] = flat_ref[...].astype(BF)

    own = row(1, ROWS)
    fa_ref[0:16, :] = jst_ref[64:80, own]
    fa_ref[16:48, :] = jst_ref[96:128, own]
    fa_ref[48:64, :] = jst_ref[64:80, own]
    fa_ref[64:96, :] = jst_ref[96:128, own]
    fa_ref[96:128, :] = jnp.zeros((32, ROWS * COLS), BF)
    fb_ref[0:48, :] = jst_ref[80:128, own]
    fb_ref[48:96, :] = jst_ref[80:128, own]
    fb_ref[96:128, :] = jnp.zeros((32, ROWS * COLS), BF)
    fc_ref[0:96, :] = jnp.zeros((96, 8 * COLS), BF)
    fc_ref[96:128, :] = qst_ref[32:64, row(1, 8)]
    fine, coarse = {}, {}
    for ky in range(3):
        shifted = gst_ref[:, row(4 - ky, ROWS)]
        ra, rb = dot_nt(shifted, fa_ref[...]), dot_nt(shifted, fb_ref[...])
        rc = dot_nt(pst_ref[:, row(1 + ky, 8)], fc_ref[...])
        for kx in range(3):
            lo = (2 - kx) * 32
            fine[ky, 0, kx] = ra[lo + 16 : lo + 32]
            fine[ky, 1, kx] = ra[lo : lo + 16] + rb[lo + 16 : lo + 32]
            fine[ky, 2, kx] = rb[lo : lo + 16]
            coarse[ky, kx] = rc[kx * 16 : kx * 16 + 16] * 0.5
    lane16 = lanes_of((16, COLS))
    order = [(ky, kz, kx) for ky in range(3) for kz in range(3) for kx in range(3)]
    for i in range(16):
        value = jnp.zeros((16, COLS), F32)
        if i < 14:
            value = jnp.where(lane16 < 48, fine[order[i]], value)
        if i < 13:
            value = jnp.where((lane16 >= 48) & (lane16 < 96), fine[order[14 + i]], value)
        if i < 9:
            value = jnp.where(lane16 >= 96, coarse[i // 3, i % 3], value)
        gw_ref[i * 16 : i * 16 + 16, :] = value.astype(BF)


def rest(messages, own, matrices, counts, sides):
    cells = (C1 * ROWS * 2, COLS)
    v = lambda rows_, lanes_, kind: pltpu.VMEM((rows_, lanes_ * COLS), kind)
    return pl.pallas_call(
        functools.partial(rest_kernel, counts, sides),
        out_shape=(
            jax.ShapeDtypeStruct(cells, BF),
            jax.ShapeDtypeStruct(cells, BF),
            jax.ShapeDtypeStruct((256, COLS), BF),
        ),
        scratch_shapes=[
            pltpu.VMEM((2, 32, SLOTS * COLS), BF),
            v(192, 18, BF),
            v(96, 22, BF), v(96, 6, BF),
            v(48, 12, BF), v(48, 4, BF),
            v(96, 10, BF),
            v(96, 4, F32), v(96, 4, F32),
            v(192, 6, F32), v(96, 6, F32),
            v(96, 18, F32),
            v(48, 10, F32),
            pltpu.VMEM(cells, F32),
            v(128, ROWS, BF), v(128, ROWS, BF), v(128, 8, BF),
        ],
        compiler_params=params(),
        cost_estimate=pl.CostEstimate(flops=10**9, bytes_accessed=4 * 10**6, transcendentals=10**5),
        name="rest",
    )(*messages, *own, *matrices)


def add_kernel(parts_ref, copies_ref):
    total = parts_ref[0].astype(F32)
    for i in range(1, parts_ref.shape[0]):
        total = total + parts_ref[i].astype(F32)
    total = total.astype(BF)
    for i in range(parts_ref.shape[0]):
        copies_ref[i] = total


def add_up(parts):
    return pl.pallas_call(
        add_kernel,
        out_shape=jax.ShapeDtypeStruct(parts.shape, BF),
        compiler_params=pltpu.CompilerParams(vmem_limit_bytes=VMEM_LIMIT),
        name="add_up",
    )(parts)


def spread_kernel(fine_scale, coarse_scale, sum_ref, fine_ref, coarse_ref):
    for i in range(27):
        if i < 14:
            value = sum_ref[i * 16 : i * 16 + 16, :].astype(F32)
        else:
            at = (i - 14) * 16
            value = pltpu.roll(sum_ref[at : at + 16, :].astype(F32), 80, 1)
        fine_ref[i * 16 : i * 16 + 16, :] = value[:, 0:48] * fine_scale
        ky, kz, kx = i // 9, i // 3 % 3, i % 3
        if kz == 1:
            at = (ky * 3 + kx) * 16
            value = pltpu.roll(sum_ref[at : at + 16, :].astype(F32), 32, 1)[:, 0:32] * coarse_scale
        else:
            value = jnp.zeros((16, 32), F32)
        coarse_ref[i * 16 : i * 16 + 16, :] = value


def spread(total, fine_scale, coarse_scale):
    return pl.pallas_call(
        functools.partial(spread_kernel, fine_scale, coarse_scale),
        out_shape=(
            jax.ShapeDtypeStruct((432, 48), F32),
            jax.ShapeDtypeStruct((432, 32), F32),
        ),
        compiler_params=pltpu.CompilerParams(vmem_limit_bytes=VMEM_LIMIT),
        name="spread",
    )(total)


def matrices_kernel(
    in_ref, wo_ref, wg_ref, wc_ref, wq_ref, wide_ref, pieces_ref, blocks_ref
):
    lane = lanes_of((C1, COLS))
    wide_ref[...] = in_ref[2 * CELLS : 2 * CELLS + TAPS, :].astype(F32)
    for ky in range(3):
        for zo in range(2):
            tiles = [jnp.zeros((C1, COLS), F32) for _ in range(2)]
            for kx in range(3):
                at = ((ky * 3 + 1 - zo) * 3 + kx) * 16
                first, second = (wide_ref[at + i : at + i + 16, :] for i in (0, 48))
                both = (first + second).astype(BF).astype(F32)
                piece = jnp.where(lane < 32, pltpu.roll(second, 16, 1), pltpu.roll(both, 16, 1))
                piece = jnp.where(lane < 16, first, jnp.where(lane < 64, piece, 0.0))
                spot = (2 - kx) * 32 + zo * 16
                pieces_ref[2 - ky, spot : spot + 16, :] = piece
                tiles[kx // 2] = tiles[kx // 2] + (pltpu.roll(piece, 64, 1) if kx == 1 else piece)
            spot = ky * 32 + zo * 16
            wo_ref[spot : spot + 16, 0:128] = tiles[0].astype(BF)
            wo_ref[spot : spot + 16, 128:192] = tiles[1][:, 0:64].astype(BF)
    for ky in range(3):
        total = jnp.zeros((C1, COLS), F32)
        for kx in range(3):
            at = ((ky * 3 + 1) * 3 + kx) * 16
            value = pltpu.roll(wide_ref[at : at + 16, :], 80, 1)
            value = jnp.where(lane < 32, value, 0.0)
            blocks_ref[ky, kx * 16 : kx * 16 + 16, :] = value
            spot = (2 - kx) * 32
            total = total + (pltpu.roll(value, spot, 1) if spot else value)
        wq_ref[(2 - ky) * 16 : (2 - ky) * 16 + 16, :] = total[:, 0:96].astype(BF)
    for d in range(3):
        wg_ref[d * 64 : d * 64 + 64, :] = jnp.transpose(pieces_ref[d])[0:64, 0:96].astype(BF)
        wc_ref[d * 32 : d * 32 + 32, :] = jnp.transpose(blocks_ref[d])[0:32, 0:48].astype(BF)


def weight_matrices(stacked):
    shape = lambda *dims: jax.ShapeDtypeStruct(dims, BF)
    return pl.pallas_call(
        matrices_kernel,
        out_shape=(shape(96, 192), shape(192, 96), shape(96, 48), shape(48, 96)),
        scratch_shapes=[
            pltpu.VMEM((TAPS, COLS), F32),
            pltpu.VMEM((3, COLS, COLS), F32),
            pltpu.VMEM((3, COLS, COLS), F32),
        ],
        compiler_params=params(),
        cost_estimate=pl.CostEstimate(flops=10**6, bytes_accessed=10**6, transcendentals=0),
        name="matrices",
    )(stacked)


def beside_blocks(outer, narrow):
    if outer.shape[1] == COLS:
        return lax.ppermute(outer, "narrow", [(0, 1), (1, 0)])
    right = lax.ppermute(outer[:, :COLS], "narrow", [(i + 1, i) for i in range(narrow - 1)])
    left = lax.ppermute(outer[:, COLS:], "narrow", [(i, i + 1) for i in range(narrow - 1)])
    return jnp.concatenate([right, left], 1)


def shards(features, cotangent, coarse_weight, fine_weight):
    wide, narrow = lax.axis_size("wide"), lax.axis_size("narrow")
    sides = 1 if narrow == 2 else 2
    stacked = stack(features, cotangent, coarse_weight, fine_weight)
    own, strip, to_odd, to_even = pack(stacked, sides)
    swaps = lambda start: [
        pair for i in range(start, wide - 1, 2) for pair in ((i, i + 1), (i + 1, i))
    ]
    odd = lax.ppermute(to_odd, "wide", swaps(1))
    even = lax.ppermute(to_even, "wide", swaps(0))
    columns = beside_blocks(strip, narrow)
    wo, wg, wc, wq = weight_matrices(stacked)
    corners = odd[:, SLOTS * COLS :] + even[:, SLOTS * COLS :]
    corners, columns = lax.optimization_barrier((corners, columns))
    corners = beside_blocks(corners, narrow)
    stacks = own_rows(own, columns, wc, wg, sides)
    output, grad_features, grads = rest((odd, even, corners), stacks, (wo, wg, wc, wq), (wide, narrow), sides)
    devices = wide * narrow
    share = -(-256 // devices)
    grads = jnp.pad(grads, ((0, share * devices - 256), (0, 0))).reshape(devices, share, COLS)
    both = ("wide", "narrow")
    parts = lax.all_to_all(grads, both, 0, 0, tiled=True)
    total = lax.all_to_all(add_up(parts), both, 0, 0, tiled=True)
    total = total.reshape(share * devices, COLS)[:256]
    all_cells = features.shape[1] * features.shape[2] * features.shape[3] * devices
    grad_fine, grad_coarse = spread(
        total, 1.0 / math.sqrt(all_cells), 1.0 / math.sqrt(all_cells // 8)
    )
    grad_fine = jnp.transpose(grad_fine.reshape(3, 3, 3, C1, C1 + C2), (3, 4, 0, 1, 2))
    grad_coarse = jnp.transpose(grad_coarse.reshape(3, 3, 3, C1, C2), (4, 3, 0, 1, 2))
    return (
        output.reshape(features.shape),
        grad_features.reshape(features.shape),
        grad_fine,
        grad_coarse,
    )


def solution(mesh):
    placed = P(None, "wide", None, "narrow")
    return jax.shard_map(
        shards,
        mesh=mesh,
        in_specs=(placed, placed, P(), P()),
        out_specs=(placed, placed, P(), P()),
        check_vma=False,
    )
```

```python
import functools
import math

import jax
import jax.numpy as jnp
from jax import lax
from jax.experimental import pallas as pl
from jax.experimental.pallas import tpu as pltpu
from jax.sharding import PartitionSpec as P

C1, C2 = 16, 32
ROWS, COLS = 16, 128
HALO = 4
BF, F32 = jnp.bfloat16, jnp.float32
VMEM_LIMIT = 48 * 1024 * 1024


def lanes_of(shape):
    return lax.broadcasted_iota(jnp.int32, shape, len(shape) - 1)


def row(index, count=1):
    return slice(index * COLS, (index + count) * COLS)


def pair_sum(value):
    lane = lanes_of(value.shape)
    other = jnp.where(lane % 2 == 0, pltpu.roll(value, COLS - 1, 1), pltpu.roll(value, 1, 1))
    return value + other


def pooled(first, second):
    total = first + second
    return (pair_sum(total[0:16] + total[16:32]) * 0.125).astype(BF)


def dot(a, b):
    return jnp.dot(a, b, preferred_element_type=F32)


def dot_nt(a, b):
    return lax.dot_general(a, b, (((1,), (1,)), ((), ())), preferred_element_type=F32)


def params():
    return pltpu.CompilerParams(vmem_limit_bytes=VMEM_LIMIT)


SLOTS = 5
CELLS = C1 * ROWS * 2
TAPS = 27 * C1


def pack_kernel(sides, in_ref, s_ref, strip_ref, odd_ref, even_ref, wide_ref, base_ref):
    lane = lanes_of((C1, COLS))
    place = lax.axis_index("narrow")
    odd = lax.axis_index("wide") % 2
    strips = [[jnp.zeros((C1, COLS), F32) for _ in range(sides)] for _ in range(2)]
    for a in range(2):
        wide_ref[...] = in_ref[a * CELLS : (a + 1) * CELLS, :].astype(F32)
        for z in range(2):
            chans = slice(a * 32 + z * 16, a * 32 + z * 16 + 16)
            for y in range(ROWS):
                value = wide_ref[pl.ds(2 * y + z, C1, stride=2 * ROWS), :]
                s_ref[chans, row(y)] = value.astype(BF)
                start = 64 * a + HALO * y
                inside = (lane >= start) & (lane < start + HALO)
                for side in range(sides):
                    if sides == 2:
                        shift = (start + HALO * side) % COLS
                    else:
                        shift = lax.rem(start + HALO * (1 - place), COLS)
                    strips[z][side] = jnp.where(inside, pltpu.roll(value, shift, 1), strips[z][side])
    for z in range(2):
        for side in range(sides):
            strip_ref[z * 16 : z * 16 + 16, row(side)] = strips[z][side].astype(BF)
    for to, near, pairs, cot in ((0, ROWS - 1, (6, 7), ROWS - 3), (1, 0, (0, 1), 0)):
        base_ref[to, :, row(0)] = s_ref[0:32, row(near)]
        for i, pair in enumerate(pairs):
            first, second = (s_ref[0:32, row(2 * pair + j)].astype(F32) for j in range(2))
            base_ref[to, i * 16 : i * 16 + 16, row(1)] = pooled(first, second)
        base_ref[to, :, row(2, 3)] = s_ref[32:64, row(cot, 3)]
        for side in range(sides):
            for z in range(2):
                kept = lane % 64 >= 48 if to == 0 else lane % 64 < 16
                value = jnp.where(kept, strips[z][side], 0.0).astype(BF)
                base_ref[to, z * 16 : z * 16 + 16, row(SLOTS + side)] = value
    even_ref[...] = base_ref[odd]
    odd_ref[...] = base_ref[1 - odd]


def stack(features, cotangent, coarse_weight, fine_weight):
    flat = lambda a: a.reshape(CELLS, COLS)
    fine = jnp.transpose(fine_weight, (2, 3, 4, 0, 1)).reshape(TAPS, 48)
    coarse = jnp.transpose(coarse_weight, (2, 3, 4, 1, 0)).reshape(TAPS, 32)
    weights = jnp.concatenate([fine, coarse, jnp.zeros((TAPS, 48), BF)], 1)
    return jnp.concatenate([flat(features), flat(cotangent), weights], 0)


def pack(stacked, sides):
    message = jax.ShapeDtypeStruct((32, (SLOTS + sides) * COLS), BF)
    return pl.pallas_call(
        functools.partial(pack_kernel, sides),
        out_shape=(
            jax.ShapeDtypeStruct((64, ROWS * COLS), BF),
            jax.ShapeDtypeStruct((32, sides * COLS), BF),
            message,
            message,
        ),
        scratch_shapes=[
            pltpu.VMEM((C1 * ROWS * 2, COLS), F32),
            pltpu.VMEM((2, 32, (SLOTS + sides) * COLS), BF),
        ],
        compiler_params=params(),
        cost_estimate=pl.CostEstimate(flops=10**6, bytes_accessed=10**6, transcendentals=0),
        name="pack",
    )(stacked)


def beside(columns, at):
    lane = lanes_of(columns[0].shape)
    if len(columns) == 1:
        place = lax.axis_index("narrow")
        first = (COLS - HALO) * place
        turned = pltpu.roll(columns[0], lax.rem(COLS - at + first, COLS), 1)
        return jnp.where((lane >= first) & (lane < first + HALO), turned, 0.0)
    right = pltpu.roll(columns[0], (-at) % COLS, 1)
    left = pltpu.roll(columns[1], (COLS - HALO - at) % COLS, 1)
    return jnp.where(lane < HALO, right, jnp.where(lane >= COLS - HALO, left, 0.0))


def turn(main, side, by):
    lane = lanes_of(main.shape)
    a, b = pltpu.roll(main, (-by) % COLS, 1), pltpu.roll(side, (-by) % COLS, 1)
    crossed = lane >= COLS - by if by > 0 else lane < -by
    return jnp.where(crossed, b, a), jnp.where(crossed, a, b)


def put_pooled(main, side, main_ref, side_ref, at, side_at):
    main, side = main.astype(F32), side.astype(F32)
    for d in range(3):
        a, b = (main, side) if d == 1 else turn(main, side, 2 * (d - 1))
        main_ref[d * 16 : d * 16 + 16, row(at)] = a.astype(BF)
        side_ref[d * 16 : d * 16 + 16, row(side_at)] = b.astype(BF)


def put_cotangent(main, side, main_ref, side_ref, at, side_at):
    for d in range(3):
        a, b = (main, side) if d == 1 else turn(main, side, d - 1)
        main_ref[d * 32 : d * 32 + 32, row(at)] = a.astype(BF)
        side_ref[d * 32 : d * 32 + 32, row(side_at)] = b.astype(BF)


def put_features(main, side, ref, step, at):
    for d in range(3):
        a = main if d == 1 else turn(main, side, d - 1)[0]
        ref[d * step : d * step + 32, row(at)] = a.astype(BF)


def coarse_row(values, totals, keeps):
    act, grad = [], []
    for value, total, kept in zip(values, totals, keeps):
        sig = 1.0 / (1.0 + jnp.exp(-value))
        act.append((value * sig * kept).astype(BF).astype(F32))
        grad_act = pair_sum(total).astype(BF).astype(F32)
        grad_pre = grad_act * (sig * (1.0 + value * (1.0 - sig)))
        grad.append((grad_pre * kept).astype(BF).astype(F32))
    acts = [act[0] if d == 1 else turn(act[0], act[1], d - 1)[0] for d in range(3)]
    grads = [grad[0] if d == 1 else turn(grad[0], grad[1], 2 * (d - 1))[0] for d in range(3)]
    return [a.astype(BF) for a in acts], [g.astype(BF) for g in grads]


def column_masks(count):
    n = lax.axis_index("narrow")
    flag = lambda is_there: jnp.where(is_there, 1.0, 0.0)
    return jnp.where(lanes_of((C2, COLS)) < 64, flag(n < count - 1), flag(n > 0))


INNER = range(1, ROWS // 2 - 1)


def own_kernel(
    counts, sides,
    s_ref, columns_ref, wo_ref, wc_ref, wg_ref,
    pst_ref, jst_ref, gst_ref, qst_ref, pre_ref, prb_ref, rg_ref, rgb_ref, ro_ref,
    psb_ref, gsb_ref,
):
    columns = [columns_ref[:, row(side)].astype(F32) for side in range(sides)]
    last = None
    for y in range(ROWS):
        main, side = s_ref[0:32, row(y)].astype(F32), beside(columns, HALO * y)
        put_features(main, side, jst_ref, 64, y)
        if y % 2 == 1:
            means = [pooled(a, b) for a, b in zip(last, (main, side))]
            put_pooled(*means, pst_ref, psb_ref, y // 2, y // 2)
        last = (main, side)
        main, side = s_ref[32:64, row(y)].astype(F32), beside(columns, 64 + HALO * y)
        put_cotangent(main, side, gst_ref, gsb_ref, y, y)
    pre_ref[...] = dot(wc_ref[...], pst_ref[...])
    prb_ref[...] = dot(wc_ref[...], psb_ref[...])
    rg_ref[...] = dot(wg_ref[...], gst_ref[...])
    rgb_ref[...] = dot(wg_ref[96:192, :], gsb_ref[...])
    there = column_masks(counts[1])
    for at in INNER:
        values = [
            sum(ref[d * 32 : d * 32 + 32, row(at + d - 1)] for d in range(3)) for ref in (pre_ref, prb_ref)
        ]
        totals = [
            sum(
                ref[lo + d * 32 : lo + d * 32 + 32, row(r + d - 1)]
                for r in (2 * at, 2 * at + 1)
                for d in range(3)
            )
            for ref, lo in ((rg_ref, 96), (rgb_ref, 0))
        ]
        acts, grads = coarse_row(values, totals, (1.0, there))
        for d in range(3):
            for r in (2 * at, 2 * at + 1):
                jst_ref[d * 64 + 32 : d * 64 + 64, row(r)] = acts[d]
            qst_ref[d * 32 : d * 32 + 32, row(at - 1)] = grads[d]
    for r in (0, 1, ROWS - 2, ROWS - 1):
        for d in range(3):
            jst_ref[d * 64 + 32 : d * 64 + 64, row(r)] = jnp.zeros((C2, COLS), BF)
    ro_ref[...] = dot(wo_ref[...], jst_ref[:, row(2, ROWS - 4)])


def own_rows(s, columns, wo, wc, wg, counts, sides):
    half = ROWS // 2
    shape = lambda rows_, lanes_, kind: jax.ShapeDtypeStruct((rows_, lanes_ * COLS), kind)
    return pl.pallas_call(
        functools.partial(own_kernel, counts, sides),
        out_shape=(
            shape(48, half, BF), shape(192, ROWS, BF), shape(96, ROWS, BF), shape(96, len(INNER), BF),
            shape(96, half, F32), shape(96, half, F32),
            shape(192, ROWS, F32), shape(96, ROWS, F32), shape(96, ROWS - 4, F32),
        ),
        scratch_shapes=[
            pltpu.VMEM((48, half * COLS), BF),
            pltpu.VMEM((96, ROWS * COLS), BF),
        ],
        compiler_params=params(),
        cost_estimate=pl.CostEstimate(flops=10**9, bytes_accessed=4 * 10**6, transcendentals=0),
        name="own_rows",
    )(s, columns, wo, wc, wg)


def rest_kernel(
    counts, sides,
    odd_ref, even_ref, corners_ref, pst_own, jst_own, gst_own, qst_own, pre_own, prb_own, rg_own, rgb_own, ro_own,
    wo_ref, wg_ref, wc_ref, wq_ref,
    out_ref, gf_ref, gw_ref,
    halo_ref, jst_ref, gst_ref, gsb_ref, pst_ref, psb_ref, qst_ref,
    pre_ref, prb_ref, rg_ref, rgb_ref, ro_ref, rq_ref, flat_ref, gl_ref, jl_ref, pl_ref, ql_ref,
):
    w = lax.axis_index("wide")
    there = column_masks(counts[1])
    flag = lambda is_there: jnp.where(is_there, 1.0, 0.0)
    has_above, has_below = flag(w > 0), flag(w < counts[0] - 1)

    odd = w % 2
    halo_ref[1 - odd] = even_ref[:, row(0, SLOTS)]
    halo_ref[odd] = odd_ref[:, row(0, SLOTS)]
    columns = [corners_ref[:, row(side)].astype(F32) for side in range(sides)]

    pst_ref[:, row(2, 8)] = pst_own[...]
    gst_ref[:, row(3, ROWS)] = gst_own[...]
    jst_ref[:, row(1, ROWS)] = jst_own[...]
    qst_ref[:, row(2, len(INNER))] = qst_own[...]
    for i in range(2):
        lane = HALO * (ROWS - HALO) if i == 0 else 0
        sides_f = [beside(columns, lane + HALO * r) for r in range(HALO)]
        near = HALO - 1 if i == 0 else 0
        put_features(halo_ref[i, :, row(0)].astype(F32), sides_f[near], jst_ref, 64, 17 * i)
        for j in range(2):
            main = halo_ref[i, j * 16 : j * 16 + 16, row(1)]
            side = pooled(sides_f[2 * j], sides_f[2 * j + 1])
            put_pooled(main, side, pst_ref, psb_ref, 10 * i + j, 2 * i + j)
        for j in range(3):
            main = halo_ref[i, :, row(2 + j)].astype(F32)
            side = beside(columns, 64 + lane + HALO * (j + 1 - i))
            put_cotangent(main, side, gst_ref, gsb_ref, 19 * i + j, 3 * i + j)
        pre_ref[:, row(2 * i, 2)] = dot(wc_ref[...], pst_ref[:, row(10 * i, 2)])
        rg_ref[:, row(3 * i, 3)] = dot(wg_ref[...], gst_ref[:, row(19 * i, 3)])
    prb_ref[...] = dot(wc_ref[...], psb_ref[...])
    rgb_ref[...] = dot(wg_ref[96:192, :], gsb_ref[...])

    def part(own, halo, lo, size, at, edge, length):
        if at < edge:
            return halo[lo : lo + size, row(at)]
        if at < edge + length:
            return own[lo : lo + size, row(at - edge)]
        return halo[lo : lo + size, row(at - length)]

    for at in (0, 1, 8, 9):
        keep = has_above if at == 0 else has_below if at == 9 else 1.0
        values = [
            sum(part(own, halo, d * 32, 32, at + d, 2, 8) for d in range(3))
            for own, halo in ((pre_own, pre_ref), (prb_own, prb_ref))
        ]
        totals = [
            sum(
                part(own, halo, lo + d * 32, 32, r + d, 3, ROWS)
                for r in (2 * at, 2 * at + 1)
                for d in range(3)
            )
            for own, halo, lo in ((rg_own, rg_ref, 96), (rgb_own, rgb_ref, 0))
        ]
        acts, grads = coarse_row(values, totals, (keep, keep * there))
        for d in range(3):
            for r in (2 * at - 1, 2 * at):
                if 0 <= r < 18:
                    jst_ref[d * 64 + 32 : d * 64 + 64, row(r)] = acts[d]
            qst_ref[d * 32 : d * 32 + 32, row(at)] = grads[d]

    for i in range(2):
        ro_ref[:, row(3 * i, 3)] = dot(wo_ref[...], jst_ref[:, row(15 * i, 3)])
    for y in range(ROWS):
        value = sum(part(ro_own, ro_ref, d * 32, 32, y + d, 3, ROWS - 4) for d in range(3))
        for z in range(2):
            flat_ref[pl.ds(2 * y + z, C1, stride=2 * ROWS), :] = value[z * 16 : z * 16 + 16]
    out_ref[...] = flat_ref[...].astype(BF)

    rq_ref[...] = dot(wq_ref[...], qst_ref[...])
    for at in range(ROWS // 2):
        coarse = rq_ref[0:16, row(at)] + rq_ref[16:32, row(at + 1)] + rq_ref[32:48, row(at + 2)]
        coarse = coarse.astype(BF).astype(F32) * 0.125
        for y in (2 * at, 2 * at + 1):
            for z in range(2):
                total = coarse
                for d in range(3):
                    total = total + part(rg_own, rg_ref, d * 32 + z * 16, 16, y + 2 + d, 3, ROWS)
                flat_ref[pl.ds(2 * y + z, C1, stride=2 * ROWS), :] = total
    gf_ref[...] = flat_ref[...].astype(BF)

    own = row(1, ROWS)
    for lo in (0, 48):
        jl_ref[lo : lo + 16, :] = jst_ref[64:80, own]
        jl_ref[lo + 16 : lo + 48, :] = jst_ref[96:128, own]
        jl_ref[128 + lo : 128 + lo + 48, :] = jst_ref[80:128, own]
    for lo in (96, 224):
        jl_ref[lo : lo + 32, :] = jnp.zeros((32, ROWS * COLS), BF)
    ql_ref[0:96, :] = jnp.zeros((96, 8 * COLS), BF)
    ql_ref[96:128, :] = qst_ref[32:64, row(1, 8)]
    for ky in range(3):
        gl_ref[ky * 96 : ky * 96 + 96, :] = gst_ref[:, row(4 - ky, ROWS)]
        pl_ref[ky * 48 : ky * 48 + 48, :] = pst_ref[:, row(1 + ky, 8)]
    rf = dot_nt(gl_ref[...], jl_ref[...])
    rc = dot_nt(pl_ref[...], ql_ref[...])
    fine, coarse = {}, {}
    for ky in range(3):
        for kx in range(3):
            lo = ky * 96 + (2 - kx) * 32
            fine[ky, 0, kx] = rf[lo + 16 : lo + 32, 0:128]
            fine[ky, 1, kx] = rf[lo : lo + 16, 0:128] + rf[lo + 16 : lo + 32, 128:256]
            fine[ky, 2, kx] = rf[lo : lo + 16, 128:256]
            coarse[ky, kx] = rc[ky * 48 + kx * 16 : ky * 48 + kx * 16 + 16] * 0.5
    lane16 = lanes_of((16, COLS))
    order = [(ky, kz, kx) for ky in range(3) for kz in range(3) for kx in range(3)]
    for i in range(16):
        value = jnp.zeros((16, COLS), F32)
        if i < 14:
            value = jnp.where(lane16 < 48, fine[order[i]], value)
        if i < 13:
            value = jnp.where((lane16 >= 48) & (lane16 < 96), fine[order[14 + i]], value)
        if i < 9:
            value = jnp.where(lane16 >= 96, coarse[i // 3, i % 3], value)
        gw_ref[i * 16 : i * 16 + 16, :] = value.astype(BF)


def rest(messages, own, matrices, counts, sides):
    cells = (C1 * ROWS * 2, COLS)
    v = lambda rows_, lanes_, kind: pltpu.VMEM((rows_, lanes_ * COLS), kind)
    return pl.pallas_call(
        functools.partial(rest_kernel, counts, sides),
        out_shape=(
            jax.ShapeDtypeStruct(cells, BF),
            jax.ShapeDtypeStruct(cells, BF),
            jax.ShapeDtypeStruct((256, COLS), BF),
        ),
        scratch_shapes=[
            pltpu.VMEM((2, 32, SLOTS * COLS), BF),
            v(192, 18, BF),
            v(96, 22, BF), v(96, 6, BF),
            v(48, 12, BF), v(48, 4, BF),
            v(96, 10, BF),
            v(96, 4, F32), v(96, 4, F32),
            v(192, 6, F32), v(96, 6, F32),
            v(96, 6, F32),
            v(48, 10, F32),
            pltpu.VMEM(cells, F32),
            v(288, ROWS, BF), v(256, ROWS, BF), v(144, 8, BF), v(128, 8, BF),
        ],
        compiler_params=params(),
        cost_estimate=pl.CostEstimate(flops=10**9, bytes_accessed=4 * 10**6, transcendentals=10**5),
        name="rest",
    )(*messages, *own, *matrices)


def add_kernel(parts_ref, copies_ref):
    total = parts_ref[0].astype(F32)
    for i in range(1, parts_ref.shape[0]):
        total = total + parts_ref[i].astype(F32)
    total = total.astype(BF)
    for i in range(parts_ref.shape[0]):
        copies_ref[i] = total


def add_up(parts):
    return pl.pallas_call(
        add_kernel,
        out_shape=jax.ShapeDtypeStruct(parts.shape, BF),
        compiler_params=pltpu.CompilerParams(vmem_limit_bytes=VMEM_LIMIT),
        name="add_up",
    )(parts)


def spread_kernel(fine_scale, coarse_scale, sum_ref, fine_ref, coarse_ref):
    for i in range(27):
        if i < 14:
            value = sum_ref[i * 16 : i * 16 + 16, :].astype(F32)
        else:
            at = (i - 14) * 16
            value = pltpu.roll(sum_ref[at : at + 16, :].astype(F32), 80, 1)
        fine_ref[i * 16 : i * 16 + 16, :] = value[:, 0:48] * fine_scale
        ky, kz, kx = i // 9, i // 3 % 3, i % 3
        if kz == 1:
            at = (ky * 3 + kx) * 16
            value = pltpu.roll(sum_ref[at : at + 16, :].astype(F32), 32, 1)[:, 0:32] * coarse_scale
        else:
            value = jnp.zeros((16, 32), F32)
        coarse_ref[i * 16 : i * 16 + 16, :] = value


def spread(total, fine_scale, coarse_scale):
    return pl.pallas_call(
        functools.partial(spread_kernel, fine_scale, coarse_scale),
        out_shape=(
            jax.ShapeDtypeStruct((432, 48), F32),
            jax.ShapeDtypeStruct((432, 32), F32),
        ),
        compiler_params=pltpu.CompilerParams(vmem_limit_bytes=VMEM_LIMIT),
        name="spread",
    )(total)


def matrices_kernel(
    in_ref, wo_ref, wg_ref, wc_ref, wq_ref, wide_ref, pieces_ref, blocks_ref
):
    lane = lanes_of((C1, COLS))
    wide_ref[...] = in_ref[2 * CELLS : 2 * CELLS + TAPS, :].astype(F32)
    for ky in range(3):
        for zo in range(2):
            tiles = [jnp.zeros((C1, COLS), F32) for _ in range(2)]
            for kx in range(3):
                at = ((ky * 3 + 1 - zo) * 3 + kx) * 16
                first, second = (wide_ref[at + i : at + i + 16, :] for i in (0, 48))
                both = (first + second).astype(BF).astype(F32)
                piece = jnp.where(lane < 32, pltpu.roll(second, 16, 1), pltpu.roll(both, 16, 1))
                piece = jnp.where(lane < 16, first, jnp.where(lane < 64, piece, 0.0))
                spot = (2 - kx) * 32 + zo * 16
                pieces_ref[2 - ky, spot : spot + 16, :] = piece
                tiles[kx // 2] = tiles[kx // 2] + (pltpu.roll(piece, 64, 1) if kx == 1 else piece)
            spot = ky * 32 + zo * 16
            wo_ref[spot : spot + 16, 0:128] = tiles[0].astype(BF)
            wo_ref[spot : spot + 16, 128:192] = tiles[1][:, 0:64].astype(BF)
    for ky in range(3):
        total = jnp.zeros((C1, COLS), F32)
        for kx in range(3):
            at = ((ky * 3 + 1) * 3 + kx) * 16
            value = pltpu.roll(wide_ref[at : at + 16, :], 80, 1)
            value = jnp.where(lane < 32, value, 0.0)
            blocks_ref[ky, kx * 16 : kx * 16 + 16, :] = value
            spot = (2 - kx) * 32
            total = total + (pltpu.roll(value, spot, 1) if spot else value)
        wq_ref[(2 - ky) * 16 : (2 - ky) * 16 + 16, :] = total[:, 0:96].astype(BF)
    for d in range(3):
        turned = jnp.transpose(pieces_ref[d])[0:64, 0:96].astype(BF)
        wg_ref[d * 32 : d * 32 + 32, :] = turned[0:32]
        wg_ref[96 + d * 32 : 96 + d * 32 + 32, :] = turned[32:64]
        wc_ref[d * 32 : d * 32 + 32, :] = jnp.transpose(blocks_ref[d])[0:32, 0:48].astype(BF)


def weight_matrices(stacked):
    shape = lambda *dims: jax.ShapeDtypeStruct(dims, BF)
    return pl.pallas_call(
        matrices_kernel,
        out_shape=(shape(96, 192), shape(192, 96), shape(96, 48), shape(48, 96)),
        scratch_shapes=[
            pltpu.VMEM((TAPS, COLS), F32),
            pltpu.VMEM((3, COLS, COLS), F32),
            pltpu.VMEM((3, COLS, COLS), F32),
        ],
        compiler_params=params(),
        cost_estimate=pl.CostEstimate(flops=10**6, bytes_accessed=10**6, transcendentals=0),
        name="matrices",
    )(stacked)


def beside_blocks(outer, narrow):
    if outer.shape[1] == COLS:
        return lax.ppermute(outer, "narrow", [(0, 1), (1, 0)])
    right = lax.ppermute(outer[:, :COLS], "narrow", [(i + 1, i) for i in range(narrow - 1)])
    left = lax.ppermute(outer[:, COLS:], "narrow", [(i, i + 1) for i in range(narrow - 1)])
    return jnp.concatenate([right, left], 1)


def shards(features, cotangent, coarse_weight, fine_weight):
    wide, narrow = lax.axis_size("wide"), lax.axis_size("narrow")
    sides = 1 if narrow == 2 else 2
    stacked = stack(features, cotangent, coarse_weight, fine_weight)
    own, strip, to_odd, to_even = pack(stacked, sides)
    swaps = lambda start: [
        pair for i in range(start, wide - 1, 2) for pair in ((i, i + 1), (i + 1, i))
    ]
    odd = lax.ppermute(to_odd, "wide", swaps(1))
    even = lax.ppermute(to_even, "wide", swaps(0))
    columns = beside_blocks(strip, narrow)
    wo, wg, wc, wq = weight_matrices(stacked)
    corners = odd[:, SLOTS * COLS :] + even[:, SLOTS * COLS :]
    columns, _ = lax.optimization_barrier((columns, corners))
    corners = beside_blocks(corners, narrow)
    stacks = own_rows(own, columns, wo, wc, wg, (wide, narrow), sides)
    output, grad_features, grads = rest((odd, even, corners), stacks, (wo, wg, wc, wq), (wide, narrow), sides)
    devices = wide * narrow
    share = -(-256 // devices)
    grads = jnp.pad(grads, ((0, share * devices - 256), (0, 0))).reshape(devices, share, COLS)
    both = ("wide", "narrow")
    parts = lax.all_to_all(grads, both, 0, 0, tiled=True)
    total = lax.all_to_all(add_up(parts), both, 0, 0, tiled=True)
    total = total.reshape(share * devices, COLS)[:256]
    all_cells = features.shape[1] * features.shape[2] * features.shape[3] * devices
    grad_fine, grad_coarse = spread(
        total, 1.0 / math.sqrt(all_cells), 1.0 / math.sqrt(all_cells // 8)
    )
    grad_fine = jnp.transpose(grad_fine.reshape(3, 3, 3, C1, C1 + C2), (3, 4, 0, 1, 2))
    grad_coarse = jnp.transpose(grad_coarse.reshape(3, 3, 3, C1, C2), (4, 3, 0, 1, 2))
    return (
        output.reshape(features.shape),
        grad_features.reshape(features.shape),
        grad_fine,
        grad_coarse,
    )


def solution(mesh):
    placed = P(None, "wide", None, "narrow")
    return jax.shard_map(
        shards,
        mesh=mesh,
        in_specs=(placed, placed, P(), P()),
        out_specs=(placed, placed, P(), P()),
        check_vma=False,
    )
```

```python
import functools
import math

import jax
import jax.numpy as jnp
from jax import lax
from jax.experimental import pallas as pl
from jax.experimental.pallas import tpu as pltpu
from jax.sharding import PartitionSpec as P

C1, C2 = 16, 32
ROWS, COLS = 16, 128
HALO = 4
BF, F32 = jnp.bfloat16, jnp.float32
VMEM_LIMIT = 48 * 1024 * 1024


def lanes_of(shape):
    return lax.broadcasted_iota(jnp.int32, shape, len(shape) - 1)


def row(index, count=1):
    return slice(index * COLS, (index + count) * COLS)


def pair_sum(value):
    lane = lanes_of(value.shape)
    other = jnp.where(lane % 2 == 0, pltpu.roll(value, COLS - 1, 1), pltpu.roll(value, 1, 1))
    return value + other


def pooled(first, second):
    total = first + second
    return (pair_sum(total[0:16] + total[16:32]) * 0.125).astype(BF)


def dot(a, b):
    return jnp.dot(a, b, preferred_element_type=F32)


def dot_nt(a, b):
    return lax.dot_general(a, b, (((1,), (1,)), ((), ())), preferred_element_type=F32)


def params():
    return pltpu.CompilerParams(vmem_limit_bytes=VMEM_LIMIT)


SLOTS = 5
CELLS = C1 * ROWS * 2
TAPS = 27 * C1


def pack_kernel(sides, in_ref, s_ref, strip_ref, odd_ref, even_ref, wide_ref, base_ref):
    lane = lanes_of((C1, COLS))
    place = lax.axis_index("narrow")
    odd = lax.axis_index("wide") % 2
    strips = [[jnp.zeros((C1, COLS), F32) for _ in range(sides)] for _ in range(2)]
    for a in range(2):
        wide_ref[...] = in_ref[a * CELLS : (a + 1) * CELLS, :].astype(F32)
        for z in range(2):
            chans = slice(a * 32 + z * 16, a * 32 + z * 16 + 16)
            for y in range(ROWS):
                value = wide_ref[pl.ds(2 * y + z, C1, stride=2 * ROWS), :]
                s_ref[chans, row(y)] = value.astype(BF)
                start = 64 * a + HALO * y
                inside = (lane >= start) & (lane < start + HALO)
                for side in range(sides):
                    if sides == 2:
                        shift = (start + HALO * side) % COLS
                    else:
                        shift = lax.rem(start + HALO * (1 - place), COLS)
                    strips[z][side] = jnp.where(inside, pltpu.roll(value, shift, 1), strips[z][side])
    for z in range(2):
        for side in range(sides):
            strip_ref[z * 16 : z * 16 + 16, row(side)] = strips[z][side].astype(BF)
    for to, near, pairs, cot in ((0, ROWS - 1, (6, 7), ROWS - 3), (1, 0, (0, 1), 0)):
        base_ref[to, :, row(0)] = s_ref[0:32, row(near)]
        for i, pair in enumerate(pairs):
            first, second = (s_ref[0:32, row(2 * pair + j)].astype(F32) for j in range(2))
            base_ref[to, i * 16 : i * 16 + 16, row(1)] = pooled(first, second)
        base_ref[to, :, row(2, 3)] = s_ref[32:64, row(cot, 3)]
        for side in range(sides):
            for z in range(2):
                kept = lane % 64 >= 48 if to == 0 else lane % 64 < 16
                value = jnp.where(kept, strips[z][side], 0.0).astype(BF)
                base_ref[to, z * 16 : z * 16 + 16, row(SLOTS + side)] = value
    even_ref[...] = base_ref[odd]
    odd_ref[...] = base_ref[1 - odd]


def stack(features, cotangent, coarse_weight, fine_weight):
    flat = lambda a: a.reshape(CELLS, COLS)
    fine = jnp.transpose(fine_weight, (2, 3, 4, 0, 1)).reshape(TAPS, 48)
    coarse = jnp.transpose(coarse_weight, (2, 3, 4, 1, 0)).reshape(TAPS, 32)
    weights = jnp.concatenate([fine, coarse, jnp.zeros((TAPS, 48), BF)], 1)
    return jnp.concatenate([flat(features), flat(cotangent), weights], 0)


def pack(stacked, sides):
    message = jax.ShapeDtypeStruct((32, (SLOTS + sides) * COLS), BF)
    return pl.pallas_call(
        functools.partial(pack_kernel, sides),
        out_shape=(
            jax.ShapeDtypeStruct((64, ROWS * COLS), BF),
            jax.ShapeDtypeStruct((32, sides * COLS), BF),
            message,
            message,
        ),
        scratch_shapes=[
            pltpu.VMEM((C1 * ROWS * 2, COLS), F32),
            pltpu.VMEM((2, 32, (SLOTS + sides) * COLS), BF),
        ],
        compiler_params=params(),
        cost_estimate=pl.CostEstimate(flops=10**6, bytes_accessed=10**6, transcendentals=0),
        name="pack",
    )(stacked)


def beside(columns, at):
    lane = lanes_of(columns[0].shape)
    if len(columns) == 1:
        place = lax.axis_index("narrow")
        first = (COLS - HALO) * place
        turned = pltpu.roll(columns[0], lax.rem(COLS - at + first, COLS), 1)
        return jnp.where((lane >= first) & (lane < first + HALO), turned, 0.0)
    right = pltpu.roll(columns[0], (-at) % COLS, 1)
    left = pltpu.roll(columns[1], (COLS - HALO - at) % COLS, 1)
    return jnp.where(lane < HALO, right, jnp.where(lane >= COLS - HALO, left, 0.0))


def turn(main, side, by):
    lane = lanes_of(main.shape)
    a, b = pltpu.roll(main, (-by) % COLS, 1), pltpu.roll(side, (-by) % COLS, 1)
    crossed = lane >= COLS - by if by > 0 else lane < -by
    return jnp.where(crossed, b, a), jnp.where(crossed, a, b)


def put_pooled(main, side, main_ref, side_ref, at, side_at):
    main, side = main.astype(F32), side.astype(F32)
    for d in range(3):
        a, b = (main, side) if d == 1 else turn(main, side, 2 * (d - 1))
        main_ref[d * 16 : d * 16 + 16, row(at)] = a.astype(BF)
        side_ref[d * 16 : d * 16 + 16, row(side_at)] = b.astype(BF)


def put_cotangent(main, side, main_ref, side_ref, at, side_at):
    for d in range(3):
        a, b = (main, side) if d == 1 else turn(main, side, d - 1)
        main_ref[d * 32 : d * 32 + 32, row(at)] = a.astype(BF)
        side_ref[d * 32 : d * 32 + 32, row(side_at)] = b.astype(BF)


def put_features(main, side, ref, step, at):
    for d in range(3):
        a = main if d == 1 else turn(main, side, d - 1)[0]
        ref[d * step : d * step + 32, row(at)] = a.astype(BF)


def coarse_row(values, totals, keeps):
    act, grad = [], []
    for value, total, kept in zip(values, totals, keeps):
        sig = 1.0 / (1.0 + jnp.exp(-value))
        act.append((value * sig * kept).astype(BF).astype(F32))
        grad_act = pair_sum(total).astype(BF).astype(F32)
        grad_pre = grad_act * (sig * (1.0 + value * (1.0 - sig)))
        grad.append((grad_pre * kept).astype(BF).astype(F32))
    acts = [act[0] if d == 1 else turn(act[0], act[1], d - 1)[0] for d in range(3)]
    grads = [grad[0] if d == 1 else turn(grad[0], grad[1], 2 * (d - 1))[0] for d in range(3)]
    return [a.astype(BF) for a in acts], [g.astype(BF) for g in grads]


def column_masks(count):
    n = lax.axis_index("narrow")
    flag = lambda is_there: jnp.where(is_there, 1.0, 0.0)
    return jnp.where(lanes_of((C2, COLS)) < 64, flag(n < count - 1), flag(n > 0))


INNER = range(1, ROWS // 2 - 1)


def own_kernel(
    counts, sides,
    s_ref, columns_ref, wo_ref, wc_ref, wg_ref,
    pst_ref, jst_ref, gst_ref, qst_ref, pre_ref, prb_ref, rg_ref, rgb_ref, ro_ref,
    psb_ref, gsb_ref,
):
    columns = [columns_ref[:, row(side)].astype(F32) for side in range(sides)]
    last = None
    for y in range(ROWS):
        main, side = s_ref[0:32, row(y)].astype(F32), beside(columns, HALO * y)
        put_features(main, side, jst_ref, 64, y)
        if y % 2 == 1:
            means = [pooled(a, b) for a, b in zip(last, (main, side))]
            put_pooled(*means, pst_ref, psb_ref, y // 2, y // 2)
        last = (main, side)
        main, side = s_ref[32:64, row(y)].astype(F32), beside(columns, 64 + HALO * y)
        put_cotangent(main, side, gst_ref, gsb_ref, y, y)
    pre_ref[...] = dot(wc_ref[...], pst_ref[...])
    prb_ref[...] = dot(wc_ref[...], psb_ref[...])
    rg_ref[...] = dot(wg_ref[...], gst_ref[...])
    rgb_ref[...] = dot(wg_ref[96:192, :], gsb_ref[...])
    there = column_masks(counts[1])
    for at in INNER:
        values = [
            sum(ref[d * 32 : d * 32 + 32, row(at + d - 1)] for d in range(3)) for ref in (pre_ref, prb_ref)
        ]
        totals = [
            sum(
                ref[lo + d * 32 : lo + d * 32 + 32, row(r + d - 1)]
                for r in (2 * at, 2 * at + 1)
                for d in range(3)
            )
            for ref, lo in ((rg_ref, 96), (rgb_ref, 0))
        ]
        acts, grads = coarse_row(values, totals, (1.0, there))
        for d in range(3):
            for r in (2 * at, 2 * at + 1):
                jst_ref[d * 64 + 32 : d * 64 + 64, row(r)] = acts[d]
            qst_ref[d * 32 : d * 32 + 32, row(at - 1)] = grads[d]
    for r in (0, 1, ROWS - 2, ROWS - 1):
        for d in range(3):
            jst_ref[d * 64 + 32 : d * 64 + 64, row(r)] = jnp.zeros((C2, COLS), BF)
    ro_ref[...] = dot(wo_ref[...], jst_ref[:, row(2, ROWS - 4)])


def own_rows(s, columns, wo, wc, wg, counts, sides):
    half = ROWS // 2
    shape = lambda rows_, lanes_, kind: jax.ShapeDtypeStruct((rows_, lanes_ * COLS), kind)
    return pl.pallas_call(
        functools.partial(own_kernel, counts, sides),
        out_shape=(
            shape(48, half, BF), shape(192, ROWS, BF), shape(96, ROWS, BF), shape(96, len(INNER), BF),
            shape(96, half, F32), shape(96, half, F32),
            shape(192, ROWS, F32), shape(96, ROWS, F32), shape(96, ROWS - 4, F32),
        ),
        scratch_shapes=[
            pltpu.VMEM((48, half * COLS), BF),
            pltpu.VMEM((96, ROWS * COLS), BF),
        ],
        compiler_params=params(),
        cost_estimate=pl.CostEstimate(flops=10**9, bytes_accessed=4 * 10**6, transcendentals=0),
        name="own_rows",
    )(s, columns, wo, wc, wg)


def put_joined(jst_ref, at, jl_ref, to):
    for lo in (0, 48):
        jl_ref[lo : lo + 16, to] = jst_ref[64:80, at]
        jl_ref[lo + 16 : lo + 48, to] = jst_ref[96:128, at]
        jl_ref[128 + lo : 128 + lo + 48, to] = jst_ref[80:128, at]
    for lo in (96, 224):
        jl_ref[lo : lo + 32, to] = jnp.zeros((32, to.stop - to.start), BF)


def inner_kernel(pst_ref, jst_ref, gst_ref, qst_ref, rf_ref, rc_ref, gl_ref, jl_ref, pl_ref, ql_ref):
    rows, coarse_rows = ROWS - 4, len(INNER)
    put_joined(jst_ref, row(2, rows), jl_ref, row(0, rows))
    ql_ref[0:96, :] = jnp.zeros((96, coarse_rows * COLS), BF)
    ql_ref[96:128, :] = qst_ref[32:64, :]
    for ky in range(3):
        gl_ref[ky * 96 : ky * 96 + 96, :] = gst_ref[:, row(3 - ky, rows)]
        pl_ref[ky * 48 : ky * 48 + 48, :] = pst_ref[:, row(ky, coarse_rows)]
    rf_ref[...] = dot_nt(gl_ref[...], jl_ref[...])
    rc_ref[...] = dot_nt(pl_ref[...], ql_ref[...])


def inner_sums(pst, jst, gst, qst):
    rows, coarse_rows = (ROWS - 4) * COLS, len(INNER) * COLS
    return pl.pallas_call(
        inner_kernel,
        out_shape=(jax.ShapeDtypeStruct((288, 256), F32), jax.ShapeDtypeStruct((144, COLS), F32)),
        scratch_shapes=[
            pltpu.VMEM((288, rows), BF),
            pltpu.VMEM((256, rows), BF),
            pltpu.VMEM((144, coarse_rows), BF),
            pltpu.VMEM((128, coarse_rows), BF),
        ],
        compiler_params=params(),
        cost_estimate=pl.CostEstimate(flops=10**9, bytes_accessed=4 * 10**6, transcendentals=0),
        name="inner_sums",
    )(pst, jst, gst, qst)


def rest_kernel(
    counts, sides,
    odd_ref, even_ref, corners_ref, pst_own, jst_own, gst_own, qst_own, pre_own, prb_own, rg_own, rgb_own, ro_own,
    rf_inner, rc_inner, wo_ref, wg_ref, wc_ref, wq_ref,
    out_hbm, gf_hbm, gw_ref,
    out_ref, gf_ref, sems, halo_ref, jst_ref, gst_ref, gsb_ref, pst_ref, psb_ref, qst_ref,
    pre_ref, prb_ref, rg_ref, rgb_ref, ro_ref, rq_ref, flat_ref, gl_ref, jl_ref, pl_ref, ql_ref,
):
    w = lax.axis_index("wide")
    there = column_masks(counts[1])
    flag = lambda is_there: jnp.where(is_there, 1.0, 0.0)
    has_above, has_below = flag(w > 0), flag(w < counts[0] - 1)

    odd = w % 2
    halo_ref[1 - odd] = even_ref[:, row(0, SLOTS)]
    halo_ref[odd] = odd_ref[:, row(0, SLOTS)]
    columns = [corners_ref[:, row(side)].astype(F32) for side in range(sides)]

    pst_ref[:, row(2, 8)] = pst_own[...]
    gst_ref[:, row(3, ROWS)] = gst_own[...]
    jst_ref[:, row(1, ROWS)] = jst_own[...]
    qst_ref[:, row(2, len(INNER))] = qst_own[...]
    for i in range(2):
        lane = HALO * (ROWS - HALO) if i == 0 else 0
        sides_f = [beside(columns, lane + HALO * r) for r in range(HALO)]
        near = HALO - 1 if i == 0 else 0
        put_features(halo_ref[i, :, row(0)].astype(F32), sides_f[near], jst_ref, 64, 17 * i)
        for j in range(2):
            main = halo_ref[i, j * 16 : j * 16 + 16, row(1)]
            side = pooled(sides_f[2 * j], sides_f[2 * j + 1])
            put_pooled(main, side, pst_ref, psb_ref, 10 * i + j, 2 * i + j)
        for j in range(3):
            main = halo_ref[i, :, row(2 + j)].astype(F32)
            side = beside(columns, 64 + lane + HALO * (j + 1 - i))
            put_cotangent(main, side, gst_ref, gsb_ref, 19 * i + j, 3 * i + j)
        pre_ref[:, row(2 * i, 2)] = dot(wc_ref[...], pst_ref[:, row(10 * i, 2)])
        rg_ref[:, row(3 * i, 3)] = dot(wg_ref[...], gst_ref[:, row(19 * i, 3)])
    prb_ref[...] = dot(wc_ref[...], psb_ref[...])
    rgb_ref[...] = dot(wg_ref[96:192, :], gsb_ref[...])

    def part(own, halo, lo, size, at, edge, length):
        if at < edge:
            return halo[lo : lo + size, row(at)]
        if at < edge + length:
            return own[lo : lo + size, row(at - edge)]
        return halo[lo : lo + size, row(at - length)]

    for at in (0, 1, 8, 9):
        keep = has_above if at == 0 else has_below if at == 9 else 1.0
        values = [
            sum(part(own, halo, d * 32, 32, at + d, 2, 8) for d in range(3))
            for own, halo in ((pre_own, pre_ref), (prb_own, prb_ref))
        ]
        totals = [
            sum(
                part(own, halo, lo + d * 32, 32, r + d, 3, ROWS)
                for r in (2 * at, 2 * at + 1)
                for d in range(3)
            )
            for own, halo, lo in ((rg_own, rg_ref, 96), (rgb_own, rgb_ref, 0))
        ]
        acts, grads = coarse_row(values, totals, (keep, keep * there))
        for d in range(3):
            for r in (2 * at - 1, 2 * at):
                if 0 <= r < 18:
                    jst_ref[d * 64 + 32 : d * 64 + 64, row(r)] = acts[d]
            qst_ref[d * 32 : d * 32 + 32, row(at)] = grads[d]

    for i in range(2):
        ro_ref[:, row(3 * i, 3)] = dot(wo_ref[...], jst_ref[:, row(15 * i, 3)])
    for y in range(ROWS):
        value = sum(part(ro_own, ro_ref, d * 32, 32, y + d, 3, ROWS - 4) for d in range(3))
        for z in range(2):
            flat_ref[pl.ds(2 * y + z, C1, stride=2 * ROWS), :] = value[z * 16 : z * 16 + 16]
    out_ref[...] = flat_ref[...].astype(BF)
    out_copy = pltpu.make_async_copy(out_ref, out_hbm, sems.at[0])
    out_copy.start()

    rq_ref[...] = dot(wq_ref[...], qst_ref[...])
    for at in range(ROWS // 2):
        coarse = rq_ref[0:16, row(at)] + rq_ref[16:32, row(at + 1)] + rq_ref[32:48, row(at + 2)]
        coarse = coarse.astype(BF).astype(F32) * 0.125
        for y in (2 * at, 2 * at + 1):
            for z in range(2):
                total = coarse
                for d in range(3):
                    total = total + part(rg_own, rg_ref, d * 32 + z * 16, 16, y + 2 + d, 3, ROWS)
                flat_ref[pl.ds(2 * y + z, C1, stride=2 * ROWS), :] = total
    gf_ref[...] = flat_ref[...].astype(BF)
    gf_copy = pltpu.make_async_copy(gf_ref, gf_hbm, sems.at[1])
    gf_copy.start()

    for i in range(2):
        at = row(1 + 14 * i, 2)
        put_joined(jst_ref, at, jl_ref, row(2 * i, 2))
        ql_ref[96:128, row(i)] = qst_ref[32:64, row(1 + 7 * i)]
        for ky in range(3):
            gl_ref[ky * 96 : ky * 96 + 96, row(2 * i, 2)] = gst_ref[:, row(14 * i + 4 - ky, 2)]
            pl_ref[ky * 48 : ky * 48 + 48, row(i)] = pst_ref[:, row(7 * i + 1 + ky)]
    ql_ref[0:96, :] = jnp.zeros((96, 2 * COLS), BF)
    rf = rf_inner[...] + dot_nt(gl_ref[...], jl_ref[...])
    rc = rc_inner[...] + dot_nt(pl_ref[...], ql_ref[...])
    fine, coarse = {}, {}
    for ky in range(3):
        for kx in range(3):
            lo = ky * 96 + (2 - kx) * 32
            fine[ky, 0, kx] = rf[lo + 16 : lo + 32, 0:128]
            fine[ky, 1, kx] = rf[lo : lo + 16, 0:128] + rf[lo + 16 : lo + 32, 128:256]
            fine[ky, 2, kx] = rf[lo : lo + 16, 128:256]
            coarse[ky, kx] = rc[ky * 48 + kx * 16 : ky * 48 + kx * 16 + 16] * 0.5
    lane16 = lanes_of((16, COLS))
    order = [(ky, kz, kx) for ky in range(3) for kz in range(3) for kx in range(3)]
    for i in range(16):
        value = jnp.zeros((16, COLS), F32)
        if i < 14:
            value = jnp.where(lane16 < 48, fine[order[i]], value)
        if i < 13:
            value = jnp.where((lane16 >= 48) & (lane16 < 96), fine[order[14 + i]], value)
        if i < 9:
            value = jnp.where(lane16 >= 96, coarse[i // 3, i % 3], value)
        gw_ref[i * 16 : i * 16 + 16, :] = value.astype(BF)
    out_copy.wait()
    gf_copy.wait()


def rest(messages, own, inner, matrices, counts, sides):
    cells = (C1 * ROWS * 2, COLS)
    v = lambda rows_, lanes_, kind: pltpu.VMEM((rows_, lanes_ * COLS), kind)
    return pl.pallas_call(
        functools.partial(rest_kernel, counts, sides),
        out_shape=(
            jax.ShapeDtypeStruct(cells, BF),
            jax.ShapeDtypeStruct(cells, BF),
            jax.ShapeDtypeStruct((256, COLS), BF),
        ),
        out_specs=(
            pl.BlockSpec(memory_space=pl.ANY),
            pl.BlockSpec(memory_space=pl.ANY),
            pl.BlockSpec(memory_space=pltpu.VMEM),
        ),
        scratch_shapes=[
            pltpu.VMEM(cells, BF), pltpu.VMEM(cells, BF), pltpu.SemaphoreType.DMA((2,)),
            pltpu.VMEM((2, 32, SLOTS * COLS), BF),
            v(192, 18, BF),
            v(96, 22, BF), v(96, 6, BF),
            v(48, 12, BF), v(48, 4, BF),
            v(96, 10, BF),
            v(96, 4, F32), v(96, 4, F32),
            v(192, 6, F32), v(96, 6, F32),
            v(96, 6, F32),
            v(48, 10, F32),
            pltpu.VMEM(cells, F32),
            v(288, 4, BF), v(256, 4, BF), v(144, 2, BF), v(128, 2, BF),
        ],
        compiler_params=params(),
        cost_estimate=pl.CostEstimate(flops=10**9, bytes_accessed=4 * 10**6, transcendentals=10**5),
        name="rest",
    )(*messages, *own, *inner, *matrices)


def add_kernel(parts_ref, copies_ref):
    total = parts_ref[0].astype(F32)
    for i in range(1, parts_ref.shape[0]):
        total = total + parts_ref[i].astype(F32)
    total = total.astype(BF)
    for i in range(parts_ref.shape[0]):
        copies_ref[i] = total


def add_up(parts):
    return pl.pallas_call(
        add_kernel,
        out_shape=jax.ShapeDtypeStruct(parts.shape, BF),
        compiler_params=pltpu.CompilerParams(vmem_limit_bytes=VMEM_LIMIT),
        name="add_up",
    )(parts)


def spread_kernel(fine_scale, coarse_scale, sum_ref, fine_ref, coarse_ref):
    for i in range(27):
        if i < 14:
            value = sum_ref[i * 16 : i * 16 + 16, :].astype(F32)
        else:
            at = (i - 14) * 16
            value = pltpu.roll(sum_ref[at : at + 16, :].astype(F32), 80, 1)
        fine_ref[i * 16 : i * 16 + 16, :] = value[:, 0:48] * fine_scale
        ky, kz, kx = i // 9, i // 3 % 3, i % 3
        if kz == 1:
            at = (ky * 3 + kx) * 16
            value = pltpu.roll(sum_ref[at : at + 16, :].astype(F32), 32, 1)[:, 0:32] * coarse_scale
        else:
            value = jnp.zeros((16, 32), F32)
        coarse_ref[i * 16 : i * 16 + 16, :] = value


def spread(total, fine_scale, coarse_scale):
    return pl.pallas_call(
        functools.partial(spread_kernel, fine_scale, coarse_scale),
        out_shape=(
            jax.ShapeDtypeStruct((432, 48), F32),
            jax.ShapeDtypeStruct((432, 32), F32),
        ),
        compiler_params=pltpu.CompilerParams(vmem_limit_bytes=VMEM_LIMIT),
        name="spread",
    )(total)


def matrices_kernel(
    in_ref, wo_ref, wg_ref, wc_ref, wq_ref, wide_ref, pieces_ref, blocks_ref
):
    lane = lanes_of((C1, COLS))
    wide_ref[...] = in_ref[2 * CELLS : 2 * CELLS + TAPS, :].astype(F32)
    for ky in range(3):
        for zo in range(2):
            tiles = [jnp.zeros((C1, COLS), F32) for _ in range(2)]
            for kx in range(3):
                at = ((ky * 3 + 1 - zo) * 3 + kx) * 16
                first, second = (wide_ref[at + i : at + i + 16, :] for i in (0, 48))
                both = (first + second).astype(BF).astype(F32)
                piece = jnp.where(lane < 32, pltpu.roll(second, 16, 1), pltpu.roll(both, 16, 1))
                piece = jnp.where(lane < 16, first, jnp.where(lane < 64, piece, 0.0))
                spot = (2 - kx) * 32 + zo * 16
                pieces_ref[2 - ky, spot : spot + 16, :] = piece
                tiles[kx // 2] = tiles[kx // 2] + (pltpu.roll(piece, 64, 1) if kx == 1 else piece)
            spot = ky * 32 + zo * 16
            wo_ref[spot : spot + 16, 0:128] = tiles[0].astype(BF)
            wo_ref[spot : spot + 16, 128:192] = tiles[1][:, 0:64].astype(BF)
    for ky in range(3):
        total = jnp.zeros((C1, COLS), F32)
        for kx in range(3):
            at = ((ky * 3 + 1) * 3 + kx) * 16
            value = pltpu.roll(wide_ref[at : at + 16, :], 80, 1)
            value = jnp.where(lane < 32, value, 0.0)
            blocks_ref[ky, kx * 16 : kx * 16 + 16, :] = value
            spot = (2 - kx) * 32
            total = total + (pltpu.roll(value, spot, 1) if spot else value)
        wq_ref[(2 - ky) * 16 : (2 - ky) * 16 + 16, :] = total[:, 0:96].astype(BF)
    for d in range(3):
        turned = jnp.transpose(pieces_ref[d])[0:64, 0:96].astype(BF)
        wg_ref[d * 32 : d * 32 + 32, :] = turned[0:32]
        wg_ref[96 + d * 32 : 96 + d * 32 + 32, :] = turned[32:64]
        wc_ref[d * 32 : d * 32 + 32, :] = jnp.transpose(blocks_ref[d])[0:32, 0:48].astype(BF)


def weight_matrices(stacked):
    shape = lambda *dims: jax.ShapeDtypeStruct(dims, BF)
    return pl.pallas_call(
        matrices_kernel,
        out_shape=(shape(96, 192), shape(192, 96), shape(96, 48), shape(48, 96)),
        scratch_shapes=[
            pltpu.VMEM((TAPS, COLS), F32),
            pltpu.VMEM((3, COLS, COLS), F32),
            pltpu.VMEM((3, COLS, COLS), F32),
        ],
        compiler_params=params(),
        cost_estimate=pl.CostEstimate(flops=10**6, bytes_accessed=10**6, transcendentals=0),
        name="matrices",
    )(stacked)


def beside_blocks(outer, narrow):
    if outer.shape[1] == COLS:
        return lax.ppermute(outer, "narrow", [(0, 1), (1, 0)])
    right = lax.ppermute(outer[:, :COLS], "narrow", [(i + 1, i) for i in range(narrow - 1)])
    left = lax.ppermute(outer[:, COLS:], "narrow", [(i, i + 1) for i in range(narrow - 1)])
    return jnp.concatenate([right, left], 1)


def shards(features, cotangent, coarse_weight, fine_weight):
    wide, narrow = lax.axis_size("wide"), lax.axis_size("narrow")
    sides = 1 if narrow == 2 else 2
    stacked = stack(features, cotangent, coarse_weight, fine_weight)
    own, strip, to_odd, to_even = pack(stacked, sides)
    swaps = lambda start: [
        pair for i in range(start, wide - 1, 2) for pair in ((i, i + 1), (i + 1, i))
    ]
    odd = lax.ppermute(to_odd, "wide", swaps(1))
    even = lax.ppermute(to_even, "wide", swaps(0))
    columns = beside_blocks(strip, narrow)
    wo, wg, wc, wq = weight_matrices(stacked)
    corners = odd[:, SLOTS * COLS :] + even[:, SLOTS * COLS :]
    stacks = own_rows(own, columns, wo, wc, wg, (wide, narrow), sides)
    inner, _ = lax.optimization_barrier((stacks[:4], corners))
    inner = inner_sums(*inner)
    corners = beside_blocks(corners, narrow)
    output, grad_features, grads = rest(
        (odd, even, corners), stacks, inner, (wo, wg, wc, wq), (wide, narrow), sides
    )
    devices = wide * narrow
    share = -(-256 // devices)
    grads = jnp.pad(grads, ((0, share * devices - 256), (0, 0))).reshape(devices, share, COLS)
    both = ("wide", "narrow")
    parts = lax.all_to_all(grads, both, 0, 0, tiled=True)
    total = lax.all_to_all(add_up(parts), both, 0, 0, tiled=True)
    total = total.reshape(share * devices, COLS)[:256]
    all_cells = features.shape[1] * features.shape[2] * features.shape[3] * devices
    grad_fine, grad_coarse = spread(
        total, 1.0 / math.sqrt(all_cells), 1.0 / math.sqrt(all_cells // 8)
    )
    grad_fine = jnp.transpose(grad_fine.reshape(3, 3, 3, C1, C1 + C2), (3, 4, 0, 1, 2))
    grad_coarse = jnp.transpose(grad_coarse.reshape(3, 3, 3, C1, C2), (4, 3, 0, 1, 2))
    return (
        output.reshape(features.shape),
        grad_features.reshape(features.shape),
        grad_fine,
        grad_coarse,
    )


def solution(mesh):
    placed = P(None, "wide", None, "narrow")
    return jax.shard_map(
        shards,
        mesh=mesh,
        in_specs=(placed, placed, P(), P()),
        out_specs=(placed, placed, P(), P()),
        check_vma=False,
    )
```

```python
import functools
import math

import jax
import jax.numpy as jnp
from jax import lax
from jax.experimental import pallas as pl
from jax.experimental.pallas import tpu as pltpu
from jax.sharding import PartitionSpec as P

C1, C2 = 16, 32
ROWS, COLS = 16, 128
HALO = 4
BF, F32 = jnp.bfloat16, jnp.float32
VMEM_LIMIT = 20 * 1024 * 1024


def lanes_of(shape):
    return lax.broadcasted_iota(jnp.int32, shape, len(shape) - 1)


def row(index, count=1):
    return slice(index * COLS, (index + count) * COLS)


def pair_sum(value):
    lane = lanes_of(value.shape)
    other = jnp.where(lane % 2 == 0, pltpu.roll(value, COLS - 1, 1), pltpu.roll(value, 1, 1))
    return value + other


def pooled(first, second):
    total = first + second
    return (pair_sum(total[0:16] + total[16:32]) * 0.125).astype(BF)


def dot(a, b):
    return jnp.dot(a, b, preferred_element_type=F32)


def dot_nt(a, b):
    return lax.dot_general(a, b, (((1,), (1,)), ((), ())), preferred_element_type=F32)


def params():
    return pltpu.CompilerParams(vmem_limit_bytes=VMEM_LIMIT)


SLOTS = 5
CELLS = C1 * ROWS * 2
TAPS = 27 * C1


def pack_kernel(sides, in_ref, s_ref, strip_ref, odd_ref, even_ref, wide_ref, base_ref):
    lane = lanes_of((C1, COLS))
    place = lax.axis_index("narrow")
    odd = lax.axis_index("wide") % 2
    strips = [[jnp.zeros((C1, COLS), F32) for _ in range(sides)] for _ in range(2)]
    for a in range(2):
        wide_ref[...] = in_ref[a * CELLS : (a + 1) * CELLS, :].astype(F32)
        for z in range(2):
            chans = slice(a * 32 + z * 16, a * 32 + z * 16 + 16)
            for y in range(ROWS):
                value = wide_ref[pl.ds(2 * y + z, C1, stride=2 * ROWS), :]
                s_ref[chans, row(y)] = value.astype(BF)
                start = 64 * a + HALO * y
                inside = (lane >= start) & (lane < start + HALO)
                for side in range(sides):
                    if sides == 2:
                        shift = (start + HALO * side) % COLS
                    else:
                        shift = lax.rem(start + HALO * (1 - place), COLS)
                    strips[z][side] = jnp.where(inside, pltpu.roll(value, shift, 1), strips[z][side])
    for z in range(2):
        for side in range(sides):
            strip_ref[z * 16 : z * 16 + 16, row(side)] = strips[z][side].astype(BF)
    for to, near, pairs, cot in ((0, ROWS - 1, (6, 7), ROWS - 3), (1, 0, (0, 1), 0)):
        base_ref[to, :, row(0)] = s_ref[0:32, row(near)]
        for i, pair in enumerate(pairs):
            first, second = (s_ref[0:32, row(2 * pair + j)].astype(F32) for j in range(2))
            base_ref[to, i * 16 : i * 16 + 16, row(1)] = pooled(first, second)
        base_ref[to, :, row(2, 3)] = s_ref[32:64, row(cot, 3)]
        for side in range(sides):
            for z in range(2):
                kept = lane % 64 >= 48 if to == 0 else lane % 64 < 16
                value = jnp.where(kept, strips[z][side], 0.0).astype(BF)
                base_ref[to, z * 16 : z * 16 + 16, row(SLOTS + side)] = value
    even_ref[...] = base_ref[odd]
    odd_ref[...] = base_ref[1 - odd]


def stack(features, cotangent, coarse_weight, fine_weight):
    flat = lambda a: a.reshape(CELLS, COLS)
    fine = jnp.transpose(fine_weight, (2, 3, 4, 0, 1)).reshape(TAPS, 48)
    coarse = jnp.transpose(coarse_weight, (2, 3, 4, 1, 0)).reshape(TAPS, 32)
    weights = jnp.concatenate([fine, coarse, jnp.zeros((TAPS, 48), BF)], 1)
    return jnp.concatenate([flat(features), flat(cotangent), weights], 0)


def pack(stacked, sides):
    message = jax.ShapeDtypeStruct((32, (SLOTS + sides) * COLS), BF)
    return pl.pallas_call(
        functools.partial(pack_kernel, sides),
        out_shape=(
            jax.ShapeDtypeStruct((64, ROWS * COLS), BF),
            jax.ShapeDtypeStruct((32, sides * COLS), BF),
            message,
            message,
        ),
        scratch_shapes=[
            pltpu.VMEM((C1 * ROWS * 2, COLS), F32),
            pltpu.VMEM((2, 32, (SLOTS + sides) * COLS), BF),
        ],
        compiler_params=params(),
        cost_estimate=pl.CostEstimate(flops=10**6, bytes_accessed=10**6, transcendentals=0),
        name="pack",
    )(stacked)


def beside(columns, at):
    lane = lanes_of(columns[0].shape)
    if len(columns) == 1:
        place = lax.axis_index("narrow")
        first = (COLS - HALO) * place
        turned = pltpu.roll(columns[0], lax.rem(COLS - at + first, COLS), 1)
        return jnp.where((lane >= first) & (lane < first + HALO), turned, 0.0)
    right = pltpu.roll(columns[0], (-at) % COLS, 1)
    left = pltpu.roll(columns[1], (COLS - HALO - at) % COLS, 1)
    return jnp.where(lane < HALO, right, jnp.where(lane >= COLS - HALO, left, 0.0))


def turn(main, side, by):
    lane = lanes_of(main.shape)
    a, b = pltpu.roll(main, (-by) % COLS, 1), pltpu.roll(side, (-by) % COLS, 1)
    crossed = lane >= COLS - by if by > 0 else lane < -by
    return jnp.where(crossed, b, a), jnp.where(crossed, a, b)


def put_pooled(main, side, main_ref, side_ref, at, side_at):
    main, side = main.astype(F32), side.astype(F32)
    for d in range(3):
        a, b = (main, side) if d == 1 else turn(main, side, 2 * (d - 1))
        main_ref[d * 16 : d * 16 + 16, row(at)] = a.astype(BF)
        side_ref[d * 16 : d * 16 + 16, row(side_at)] = b.astype(BF)


def put_cotangent(main, side, main_ref, side_ref, at, side_at):
    for d in range(3):
        a, b = (main, side) if d == 1 else turn(main, side, d - 1)
        main_ref[d * 32 : d * 32 + 32, row(at)] = a.astype(BF)
        side_ref[d * 32 : d * 32 + 32, row(side_at)] = b.astype(BF)


def put_features(main, side, ref, step, at):
    for d in range(3):
        a = main if d == 1 else turn(main, side, d - 1)[0]
        ref[d * step : d * step + 32, row(at)] = a.astype(BF)


def coarse_row(values, totals, keeps):
    act, grad = [], []
    for value, total, kept in zip(values, totals, keeps):
        sig = 1.0 / (1.0 + jnp.exp(-value))
        act.append((value * sig * kept).astype(BF).astype(F32))
        grad_act = pair_sum(total).astype(BF).astype(F32)
        grad_pre = grad_act * (sig * (1.0 + value * (1.0 - sig)))
        grad.append((grad_pre * kept).astype(BF).astype(F32))
    acts = [act[0] if d == 1 else turn(act[0], act[1], d - 1)[0] for d in range(3)]
    grads = [grad[0] if d == 1 else turn(grad[0], grad[1], 2 * (d - 1))[0] for d in range(3)]
    return [a.astype(BF) for a in acts], [g.astype(BF) for g in grads]


def column_masks(count):
    n = lax.axis_index("narrow")
    flag = lambda is_there: jnp.where(is_there, 1.0, 0.0)
    return jnp.where(lanes_of((C2, COLS)) < 64, flag(n < count - 1), flag(n > 0))


INNER = range(1, ROWS // 2 - 1)


def own_kernel(
    sides,
    s_ref, columns_ref, wc_ref, wg_ref,
    pst_ref, jf_ref, gst_ref, pre_ref, prb_ref, rg_ref, rgb_ref,
    psb_ref, gsb_ref,
):
    columns = [columns_ref[:, row(side)].astype(F32) for side in range(sides)]
    last = None
    for y in range(ROWS):
        main, side = s_ref[0:32, row(y)].astype(F32), beside(columns, HALO * y)
        put_features(main, side, jf_ref, 32, y)
        if y % 2 == 1:
            means = [pooled(a, b) for a, b in zip(last, (main, side))]
            put_pooled(*means, pst_ref, psb_ref, y // 2, y // 2)
        last = (main, side)
        main, side = s_ref[32:64, row(y)].astype(F32), beside(columns, 64 + HALO * y)
        put_cotangent(main, side, gst_ref, gsb_ref, y, y)
    pre_ref[...] = dot(wc_ref[...], pst_ref[...])
    prb_ref[...] = dot(wc_ref[...], psb_ref[...])
    rg_ref[...] = dot(wg_ref[...], gst_ref[...])
    rgb_ref[...] = dot(wg_ref[96:192, :], gsb_ref[...])


def shaped(rows_, lanes_, kind):
    return jax.ShapeDtypeStruct((rows_, lanes_ * COLS), kind)


def scratch(rows_, lanes_, kind):
    return pltpu.VMEM((rows_, lanes_ * COLS), kind)


def own_rows(s, columns, wc, wg, sides):
    half = ROWS // 2
    return pl.pallas_call(
        functools.partial(own_kernel, sides),
        out_shape=(
            shaped(48, half, BF), shaped(96, ROWS, BF), shaped(96, ROWS, BF),
            shaped(96, half, F32), shaped(96, half, F32),
            shaped(192, ROWS, F32), shaped(96, ROWS, F32),
        ),
        scratch_shapes=[scratch(48, half, BF), scratch(96, ROWS, BF)],
        compiler_params=params(),
        cost_estimate=pl.CostEstimate(flops=10**9, bytes_accessed=4 * 10**6, transcendentals=0),
        name="own_rows",
    )(s, columns, wc, wg)


def put_joined(jst_ref, at, jl_ref, to):
    for lo in (0, 48):
        jl_ref[lo : lo + 16, to] = jst_ref[64:80, at]
        jl_ref[lo + 16 : lo + 48, to] = jst_ref[96:128, at]
        jl_ref[128 + lo : 128 + lo + 48, to] = jst_ref[80:128, at]
    for lo in (96, 224):
        jl_ref[lo : lo + 32, to] = jnp.zeros((32, to.stop - to.start), BF)


def put_field(flat_ref, y, plane, value):
    flat_ref[pl.ds(2 * y + plane, C1, stride=2 * ROWS), :] = value


FINE = range(2 * INNER.start, 2 * INNER.stop)


def inner_kernel(
    count,
    pst_ref, jf_ref, gst_ref, pre_ref, prb_ref, rg_ref, rgb_ref, wo_ref, wq_ref,
    out_ref, gf_ref, ro_ref, rq_ref, rf_ref, rc_ref,
    jst_ref, qst_ref, gl_ref, jl_ref, pl_ref, ql_ref,
):
    rows, coarse_rows = len(FINE), len(INNER)
    there = column_masks(count)
    for d in range(3):
        jst_ref[d * 64 : d * 64 + 32, :] = jf_ref[d * 32 : d * 32 + 32, row(FINE.start, rows)]
    for at in INNER:
        values = [
            sum(ref[d * 32 : d * 32 + 32, row(at + d - 1)] for d in range(3)) for ref in (pre_ref, prb_ref)
        ]
        totals = [
            sum(
                ref[lo + d * 32 : lo + d * 32 + 32, row(r + d - 1)]
                for r in (2 * at, 2 * at + 1)
                for d in range(3)
            )
            for ref, lo in ((rg_ref, 96), (rgb_ref, 0))
        ]
        acts, grads = coarse_row(values, totals, (1.0, there))
        for d in range(3):
            for r in (2 * at, 2 * at + 1):
                jst_ref[d * 64 + 32 : d * 64 + 64, row(r - FINE.start)] = acts[d]
            qst_ref[d * 32 : d * 32 + 32, row(at - INNER.start)] = grads[d]
    ro_ref[...] = dot(wo_ref[...], jst_ref[...])
    rq_ref[...] = dot(wq_ref[...], qst_ref[...])

    put_joined(jst_ref, row(0, rows), jl_ref, row(0, rows))
    ql_ref[0:96, :] = jnp.zeros((96, coarse_rows * COLS), BF)
    ql_ref[96:128, :] = qst_ref[32:64, :]
    for ky in range(3):
        gl_ref[ky * 96 : ky * 96 + 96, :] = gst_ref[:, row(FINE.start + 1 - ky, rows)]
        pl_ref[ky * 48 : ky * 48 + 48, :] = pst_ref[:, row(INNER.start + ky - 1, coarse_rows)]
    rf_ref[...] = dot_nt(gl_ref[...], jl_ref[...])
    rc_ref[...] = dot_nt(pl_ref[...], ql_ref[...])

    for y in range(FINE.start + 1, FINE.stop - 1):
        value = sum(ro_ref[d * 32 : d * 32 + 32, row(y - 1 + d - FINE.start)] for d in range(3))
        for z in range(2):
            put_field(out_ref, y, z, value[z * 16 : z * 16 + 16])
    for at in range(INNER.start + 1, INNER.stop - 1):
        coarse = sum(rq_ref[d * 16 : d * 16 + 16, row(at - 1 + d - INNER.start)] for d in range(3))
        coarse = coarse.astype(BF).astype(F32) * 0.125
        for y in (2 * at, 2 * at + 1):
            for z in range(2):
                lo = z * 16
                value = sum(rg_ref[lo + d * 32 : lo + d * 32 + 16, row(y - 1 + d)] for d in range(3))
                put_field(gf_ref, y, z, value + coarse)


def inner_rows(own, wo, wq, count):
    rows, coarse_rows = len(FINE), len(INNER)
    return pl.pallas_call(
        functools.partial(inner_kernel, count),
        out_shape=(
            shaped(CELLS, 1, F32), shaped(CELLS, 1, F32),
            shaped(96, rows, F32), shaped(48, coarse_rows, F32),
            shaped(288, 2, F32), shaped(144, 1, F32),
        ),
        scratch_shapes=[
            scratch(192, rows, BF), scratch(96, coarse_rows, BF),
            scratch(288, rows, BF), scratch(256, rows, BF),
            scratch(144, coarse_rows, BF), scratch(128, coarse_rows, BF),
        ],
        compiler_params=params(),
        cost_estimate=pl.CostEstimate(flops=10**9, bytes_accessed=4 * 10**6, transcendentals=10**5),
        name="inner_rows",
    )(*own, wo, wq)


def rest_kernel(
    counts, sides,
    odd_ref, even_ref, corners_ref,
    pst_own, jf_own, gst_own, pre_own, prb_own, rg_own, rgb_own,
    out_inner, gf_inner, ro_inner, rq_inner, rf_inner, rc_inner,
    wo_ref, wg_ref, wc_ref, wq_ref,
    out_ref, gf_ref, gw_ref,
    halo_ref, jst_ref, gst_ref, gsb_ref, pst_ref, psb_ref, qst_ref,
    pre_ref, prb_ref, rg_ref, rgb_ref, ro_ref, rq_ref, gl_ref, jl_ref, pl_ref, ql_ref, flat_ref,
):
    w = lax.axis_index("wide")
    there = column_masks(counts[1])
    flag = lambda is_there: jnp.where(is_there, 1.0, 0.0)
    has_above, has_below = flag(w > 0), flag(w < counts[0] - 1)

    odd = w % 2
    halo_ref[1 - odd] = even_ref[:, row(0, SLOTS)]
    halo_ref[odd] = odd_ref[:, row(0, SLOTS)]
    columns = [corners_ref[:, row(side)].astype(F32) for side in range(sides)]

    for i in range(2):
        lane = HALO * (ROWS - HALO) if i == 0 else 0
        for j in range(3):
            main = halo_ref[i, :, row(2 + j)].astype(F32)
            side = beside(columns, 64 + lane + HALO * (j + 1 - i))
            put_cotangent(main, side, gst_ref, gsb_ref, 9 * i + j, 3 * i + j)
        gst_ref[:, row(3 + 3 * i, 3)] = gst_own[:, row(13 * i, 3)]
        rg_ref[:, row(3 * i, 3)] = dot(wg_ref[...], gst_ref[:, row(9 * i, 3)])
    rgb_ref[...] = dot(wg_ref[96:192, :], gsb_ref[...])
    for i in range(2):
        lane = HALO * (ROWS - HALO) if i == 0 else 0
        sides_f = [beside(columns, lane + HALO * r) for r in range(HALO)]
        near = HALO - 1 if i == 0 else 0
        for j in range(2):
            main = halo_ref[i, j * 16 : j * 16 + 16, row(1)]
            side = pooled(sides_f[2 * j], sides_f[2 * j + 1])
            put_pooled(main, side, pst_ref, psb_ref, 6 * i + j, 2 * i + j)
        pst_ref[:, row(2 + 2 * i, 2)] = pst_own[:, row(6 * i, 2)]
        pre_ref[:, row(2 * i, 2)] = dot(wc_ref[...], pst_ref[:, row(6 * i, 2)])
        put_features(halo_ref[i, :, row(0)].astype(F32), sides_f[near], jst_ref, 64, 5 * i)
        for d in range(3):
            jst_ref[d * 64 : d * 64 + 32, row(1 + 2 * i, 2)] = jf_own[d * 32 : d * 32 + 32, row(14 * i, 2)]
    prb_ref[...] = dot(wc_ref[...], psb_ref[...])

    def part(own, halo, lo, size, at, edge, length):
        if at < edge:
            return halo[lo : lo + size, row(at)]
        if at < edge + length:
            return own[lo : lo + size, row(at - edge)]
        return halo[lo : lo + size, row(at - length)]

    for k, at in enumerate((0, 1, 8, 9)):
        keep = has_above if at == 0 else has_below if at == 9 else 1.0
        values = [
            sum(part(own, halo, d * 32, 32, at + d, 2, 8) for d in range(3))
            for own, halo in ((pre_own, pre_ref), (prb_own, prb_ref))
        ]
        totals = [
            sum(
                part(own, halo, lo + d * 32, 32, r + d, 3, ROWS)
                for r in (2 * at, 2 * at + 1)
                for d in range(3)
            )
            for own, halo, lo in ((rg_own, rg_ref, 96), (rgb_own, rgb_ref, 0))
        ]
        acts, grads = coarse_row(values, totals, (keep, keep * there))
        for d in range(3):
            for r in ((0,), (1, 2), (3, 4), (5,))[k]:
                jst_ref[d * 64 + 32 : d * 64 + 64, row(r)] = acts[d]
            qst_ref[d * 32 : d * 32 + 32, row(k)] = grads[d]

    put_joined(jst_ref, row(1, 4), jl_ref, row(0, 4))
    ql_ref[0:96, :] = jnp.zeros((96, 2 * COLS), BF)
    ql_ref[96:128, :] = qst_ref[32:64, row(1, 2)]
    for i in range(2):
        for ky in range(3):
            gl_ref[ky * 96 : ky * 96 + 96, row(2 * i, 2)] = gst_ref[:, row(4 + 4 * i - ky, 2)]
            pl_ref[ky * 48 : ky * 48 + 48, row(i)] = pst_ref[:, row(1 + 3 * i + ky)]
    rf = rf_inner[...] + dot_nt(gl_ref[...], jl_ref[...])
    rc = rc_inner[...] + dot_nt(pl_ref[...], ql_ref[...])
    ro_ref[...] = dot(wo_ref[...], jst_ref[...])
    rq_ref[...] = dot(wq_ref[...], qst_ref[...])
    fine, coarse = {}, {}
    for ky in range(3):
        for kx in range(3):
            lo = ky * 96 + (2 - kx) * 32
            fine[ky, 0, kx] = rf[lo + 16 : lo + 32, 0:128]
            fine[ky, 1, kx] = rf[lo : lo + 16, 0:128] + rf[lo + 16 : lo + 32, 128:256]
            fine[ky, 2, kx] = rf[lo : lo + 16, 128:256]
            coarse[ky, kx] = rc[ky * 48 + kx * 16 : ky * 48 + kx * 16 + 16] * 0.5
    lane16 = lanes_of((16, COLS))
    order = [(ky, kz, kx) for ky in range(3) for kz in range(3) for kx in range(3)]
    for i in range(16):
        value = jnp.zeros((16, COLS), F32)
        if i < 14:
            value = jnp.where(lane16 < 48, fine[order[i]], value)
        if i < 13:
            value = jnp.where((lane16 >= 48) & (lane16 < 96), fine[order[14 + i]], value)
        if i < 9:
            value = jnp.where(lane16 >= 96, coarse[i // 3, i % 3], value)
        gw_ref[i * 16 : i * 16 + 16, :] = value.astype(BF)

    flat_ref[0] = out_inner[...]
    flat_ref[1] = gf_inner[...]
    for y in (0, 1, 2, 13, 14, 15):
        value = sum(part(ro_inner, ro_ref, d * 32, 32, y + d, 3, len(FINE)) for d in range(3))
        for z in range(2):
            put_field(flat_ref.at[0], y, z, value[z * 16 : z * 16 + 16])
    out_ref[...] = flat_ref[0].astype(BF)

    for at in (0, 1, 6, 7):
        coarse = sum(part(rq_inner, rq_ref, d * 16, 16, at + d, 2, len(INNER)) for d in range(3))
        coarse = coarse.astype(BF).astype(F32) * 0.125
        for y in (2 * at, 2 * at + 1):
            for z in range(2):
                lo = z * 16
                value = sum(part(rg_own, rg_ref, lo + d * 32, 16, y + 2 + d, 3, ROWS) for d in range(3))
                put_field(flat_ref.at[1], y, z, value + coarse)
    gf_ref[...] = flat_ref[1].astype(BF)


def rest(messages, own, inner, matrices, counts, sides):
    return pl.pallas_call(
        functools.partial(rest_kernel, counts, sides),
        out_shape=(
            pltpu.VMEM((CELLS, COLS), BF),
            pltpu.VMEM((CELLS, COLS), BF),
            jax.ShapeDtypeStruct((256, COLS), BF),
        ),
        scratch_shapes=[
            pltpu.VMEM((2, 32, SLOTS * COLS), BF),
            scratch(192, 6, BF),
            scratch(96, 12, BF), scratch(96, 6, BF),
            scratch(48, 8, BF), scratch(48, 4, BF),
            scratch(96, 4, BF),
            scratch(96, 4, F32), scratch(96, 4, F32),
            scratch(192, 6, F32), scratch(96, 6, F32),
            scratch(96, 6, F32),
            scratch(48, 4, F32),
            scratch(288, 4, BF), scratch(256, 4, BF), scratch(144, 2, BF), scratch(128, 2, BF),
            pltpu.VMEM((2, CELLS, COLS), F32),
        ],
        compiler_params=params(),
        cost_estimate=pl.CostEstimate(flops=10**9, bytes_accessed=4 * 10**6, transcendentals=10**5),
        name="rest",
    )(*messages, *own, *inner, *matrices)


def add_kernel(parts_ref, copies_ref):
    total = parts_ref[0].astype(F32)
    for i in range(1, parts_ref.shape[0]):
        total = total + parts_ref[i].astype(F32)
    total = total.astype(BF)
    for i in range(parts_ref.shape[0]):
        copies_ref[i] = total


def add_up(parts):
    return pl.pallas_call(
        add_kernel,
        out_shape=jax.ShapeDtypeStruct(parts.shape, BF),
        compiler_params=pltpu.CompilerParams(vmem_limit_bytes=VMEM_LIMIT),
        name="add_up",
    )(parts)


def spread_kernel(
    fine_scale, coarse_scale, sum_ref, out_ref, gf_ref, out_hbm, gf_hbm, fine_ref, coarse_ref, sems
):
    copies = [
        pltpu.make_async_copy(ref, hbm, sems.at[i])
        for i, (ref, hbm) in enumerate(((out_ref, out_hbm), (gf_ref, gf_hbm)))
    ]
    for copy in copies:
        copy.start()
    for i in range(27):
        if i < 14:
            value = sum_ref[i * 16 : i * 16 + 16, :].astype(F32)
        else:
            at = (i - 14) * 16
            value = pltpu.roll(sum_ref[at : at + 16, :].astype(F32), 80, 1)
        fine_ref[i * 16 : i * 16 + 16, :] = value[:, 0:48] * fine_scale
        ky, kz, kx = i // 9, i // 3 % 3, i % 3
        if kz == 1:
            at = (ky * 3 + kx) * 16
            value = pltpu.roll(sum_ref[at : at + 16, :].astype(F32), 32, 1)[:, 0:32] * coarse_scale
        else:
            value = jnp.zeros((16, 32), F32)
        coarse_ref[i * 16 : i * 16 + 16, :] = value
    for copy in copies:
        copy.wait()


def spread(total, output, grad_features, fine_scale, coarse_scale):
    vmem, anywhere = pl.BlockSpec(memory_space=pltpu.VMEM), pl.BlockSpec(memory_space=pl.ANY)
    return pl.pallas_call(
        functools.partial(spread_kernel, fine_scale, coarse_scale),
        in_specs=[vmem] * 3,
        out_specs=(anywhere, anywhere, vmem, vmem),
        out_shape=(
            jax.ShapeDtypeStruct((CELLS, COLS), BF),
            jax.ShapeDtypeStruct((CELLS, COLS), BF),
            jax.ShapeDtypeStruct((TAPS, 48), F32),
            jax.ShapeDtypeStruct((TAPS, 32), F32),
        ),
        scratch_shapes=[pltpu.SemaphoreType.DMA((2,))],
        compiler_params=params(),
        name="spread",
    )(total, output, grad_features)


def matrices_kernel(
    in_ref, wo_ref, wg_ref, wc_ref, wq_ref, wide_ref, pieces_ref, blocks_ref
):
    lane = lanes_of((C1, COLS))
    wide_ref[...] = in_ref[2 * CELLS : 2 * CELLS + TAPS, :].astype(F32)
    for ky in range(3):
        for zo in range(2):
            tiles = [jnp.zeros((C1, COLS), F32) for _ in range(2)]
            for kx in range(3):
                at = ((ky * 3 + 1 - zo) * 3 + kx) * 16
                first, second = (wide_ref[at + i : at + i + 16, :] for i in (0, 48))
                both = (first + second).astype(BF).astype(F32)
                piece = jnp.where(lane < 32, pltpu.roll(second, 16, 1), pltpu.roll(both, 16, 1))
                piece = jnp.where(lane < 16, first, jnp.where(lane < 64, piece, 0.0))
                spot = (2 - kx) * 32 + zo * 16
                pieces_ref[2 - ky, spot : spot + 16, :] = piece
                tiles[kx // 2] = tiles[kx // 2] + (pltpu.roll(piece, 64, 1) if kx == 1 else piece)
            spot = ky * 32 + zo * 16
            wo_ref[spot : spot + 16, 0:128] = tiles[0].astype(BF)
            wo_ref[spot : spot + 16, 128:192] = tiles[1][:, 0:64].astype(BF)
    for ky in range(3):
        total = jnp.zeros((C1, COLS), F32)
        for kx in range(3):
            at = ((ky * 3 + 1) * 3 + kx) * 16
            value = pltpu.roll(wide_ref[at : at + 16, :], 80, 1)
            value = jnp.where(lane < 32, value, 0.0)
            blocks_ref[ky, kx * 16 : kx * 16 + 16, :] = value
            spot = (2 - kx) * 32
            total = total + (pltpu.roll(value, spot, 1) if spot else value)
        wq_ref[(2 - ky) * 16 : (2 - ky) * 16 + 16, :] = total[:, 0:96].astype(BF)
    for d in range(3):
        turned = jnp.transpose(pieces_ref[d])[0:64, 0:96].astype(BF)
        wg_ref[d * 32 : d * 32 + 32, :] = turned[0:32]
        wg_ref[96 + d * 32 : 96 + d * 32 + 32, :] = turned[32:64]
        wc_ref[d * 32 : d * 32 + 32, :] = jnp.transpose(blocks_ref[d])[0:32, 0:48].astype(BF)


def weight_matrices(stacked):
    shape = lambda *dims: jax.ShapeDtypeStruct(dims, BF)
    return pl.pallas_call(
        matrices_kernel,
        out_shape=(shape(96, 192), shape(192, 96), shape(96, 48), shape(48, 96)),
        scratch_shapes=[
            pltpu.VMEM((TAPS, COLS), F32),
            pltpu.VMEM((3, COLS, COLS), F32),
            pltpu.VMEM((3, COLS, COLS), F32),
        ],
        compiler_params=params(),
        cost_estimate=pl.CostEstimate(flops=10**6, bytes_accessed=10**6, transcendentals=0),
        name="matrices",
    )(stacked)


def beside_blocks(outer, narrow):
    if outer.shape[1] == COLS:
        return lax.ppermute(outer, "narrow", [(0, 1), (1, 0)])
    right = lax.ppermute(outer[:, :COLS], "narrow", [(i + 1, i) for i in range(narrow - 1)])
    left = lax.ppermute(outer[:, COLS:], "narrow", [(i, i + 1) for i in range(narrow - 1)])
    return jnp.concatenate([right, left], 1)


def shards(features, cotangent, coarse_weight, fine_weight):
    wide, narrow = lax.axis_size("wide"), lax.axis_size("narrow")
    sides = 1 if narrow == 2 else 2
    stacked = stack(features, cotangent, coarse_weight, fine_weight)
    own, strip, to_odd, to_even = pack(stacked, sides)
    swaps = lambda start: [
        pair for i in range(start, wide - 1, 2) for pair in ((i, i + 1), (i + 1, i))
    ]
    odd = lax.ppermute(to_odd, "wide", swaps(1))
    even = lax.ppermute(to_even, "wide", swaps(0))
    columns = beside_blocks(strip, narrow)
    wo, wg, wc, wq = weight_matrices(stacked)
    corners = odd[:, SLOTS * COLS :] + even[:, SLOTS * COLS :]
    stacks = own_rows(own, columns, wc, wg, sides)
    stacks, _ = lax.optimization_barrier((stacks, corners))
    inner = inner_rows(stacks, wo, wq, narrow)
    corners = beside_blocks(corners, narrow)
    output, grad_features, grads = rest(
        (odd, even, corners), stacks, inner, (wo, wg, wc, wq), (wide, narrow), sides
    )
    devices = wide * narrow
    share = -(-256 // devices)
    grads = jnp.pad(grads, ((0, share * devices - 256), (0, 0))).reshape(devices, share, COLS)
    both = ("wide", "narrow")
    parts = lax.all_to_all(grads, both, 0, 0, tiled=True)
    total = lax.all_to_all(add_up(parts), both, 0, 0, tiled=True)
    total = total.reshape(share * devices, COLS)[:256]
    all_cells = features.shape[1] * features.shape[2] * features.shape[3] * devices
    output, grad_features, grad_fine, grad_coarse = spread(
        total, output, grad_features, 1.0 / math.sqrt(all_cells), 1.0 / math.sqrt(all_cells // 8)
    )
    grad_fine = jnp.transpose(grad_fine.reshape(3, 3, 3, C1, C1 + C2), (3, 4, 0, 1, 2))
    grad_coarse = jnp.transpose(grad_coarse.reshape(3, 3, 3, C1, C2), (4, 3, 0, 1, 2))
    return (
        output.reshape(features.shape),
        grad_features.reshape(features.shape),
        grad_fine,
        grad_coarse,
    )


def solution(mesh):
    placed = P(None, "wide", None, "narrow")
    return jax.shard_map(
        shards,
        mesh=mesh,
        in_specs=(placed, placed, P(), P()),
        out_specs=(placed, placed, P(), P()),
        check_vma=False,
    )
```

```python
import functools
import math

import jax
import jax.numpy as jnp
from jax import lax
from jax.experimental import pallas as pl
from jax.experimental.pallas import tpu as pltpu
from jax.sharding import PartitionSpec as P

C1, C2 = 16, 32
ROWS, COLS = 16, 128
HALO = 4
BF, F32 = jnp.bfloat16, jnp.float32
VMEM_LIMIT = 20 * 1024 * 1024


def lanes_of(shape):
    return lax.broadcasted_iota(jnp.int32, shape, len(shape) - 1)


def row(index, count=1):
    return slice(index * COLS, (index + count) * COLS)


def pair_sum(value):
    lane = lanes_of(value.shape)
    other = jnp.where(lane % 2 == 0, pltpu.roll(value, COLS - 1, 1), pltpu.roll(value, 1, 1))
    return value + other


def pooled(first, second):
    total = first + second
    return (pair_sum(total[0:16] + total[16:32]) * 0.125).astype(BF)


def dot(a, b):
    return jnp.dot(a, b, preferred_element_type=F32)


def dot_nt(a, b):
    return lax.dot_general(a, b, (((1,), (1,)), ((), ())), preferred_element_type=F32)


def params():
    return pltpu.CompilerParams(vmem_limit_bytes=VMEM_LIMIT)


SLOTS = 5
CELLS = C1 * ROWS * 2
TAPS = 27 * C1


def chunks(pairs, sems, pieces):
    copies = []
    for i, (source, target) in enumerate(pairs):
        rows = source.shape[0] // pieces
        copies.append([
            pltpu.make_async_copy(
                source.at[pl.ds(j * rows, rows)], target.at[pl.ds(j * rows, rows)], sems.at[i, j]
            )
            for j in range(pieces)
        ])
    return copies


def start(copies):
    for copy in copies:
        copy.start()


def wait(copies):
    for copy in copies:
        copy.wait()


def pack_kernel(
    sides, f_hbm, g_hbm, s_ref, strip_ref, odd_ref, even_ref, f_ref, g_ref, wide_ref, base_ref, sems
):
    arrivals = chunks(((f_hbm, f_ref), (g_hbm, g_ref)), sems, 4)
    for copies in arrivals:
        start(copies)
    lane = lanes_of((C1, COLS))
    place = lax.axis_index("narrow")
    odd = lax.axis_index("wide") % 2
    strips = [[jnp.zeros((C1, COLS), F32) for _ in range(sides)] for _ in range(2)]
    for a in range(2):
        wait(arrivals[a])
        wide_ref[...] = (f_ref, g_ref)[a][...].astype(F32)
        for z in range(2):
            chans = slice(a * 32 + z * 16, a * 32 + z * 16 + 16)
            for y in range(ROWS):
                value = wide_ref[pl.ds(2 * y + z, C1, stride=2 * ROWS), :]
                s_ref[chans, row(y)] = value.astype(BF)
                first = 64 * a + HALO * y
                inside = (lane >= first) & (lane < first + HALO)
                for side in range(sides):
                    if sides == 2:
                        shift = (first + HALO * side) % COLS
                    else:
                        shift = lax.rem(first + HALO * (1 - place), COLS)
                    strips[z][side] = jnp.where(inside, pltpu.roll(value, shift, 1), strips[z][side])
    for z in range(2):
        for side in range(sides):
            strip_ref[z * 16 : z * 16 + 16, row(side)] = strips[z][side].astype(BF)
    for to, near, pairs, cot in ((0, ROWS - 1, (6, 7), ROWS - 3), (1, 0, (0, 1), 0)):
        base_ref[to, :, row(0)] = s_ref[0:32, row(near)]
        for i, pair in enumerate(pairs):
            first, second = (s_ref[0:32, row(2 * pair + j)].astype(F32) for j in range(2))
            base_ref[to, i * 16 : i * 16 + 16, row(1)] = pooled(first, second)
        base_ref[to, :, row(2, 3)] = s_ref[32:64, row(cot, 3)]
        for side in range(sides):
            for z in range(2):
                kept = lane % 64 >= 48 if to == 0 else lane % 64 < 16
                value = jnp.where(kept, strips[z][side], 0.0).astype(BF)
                base_ref[to, z * 16 : z * 16 + 16, row(SLOTS + side)] = value
    even_ref[...] = base_ref[odd]
    odd_ref[...] = base_ref[1 - odd]


def kept_in_hbm(array):
    return pltpu.with_memory_space_constraint(array, pltpu.HBM)


def pack(features, cotangent, sides):
    flat = lambda a: kept_in_hbm(a.reshape(CELLS, COLS))
    message = jax.ShapeDtypeStruct((32, (SLOTS + sides) * COLS), BF)
    return pl.pallas_call(
        functools.partial(pack_kernel, sides),
        in_specs=[pl.BlockSpec(memory_space=pltpu.HBM)] * 2,
        out_shape=(
            jax.ShapeDtypeStruct((64, ROWS * COLS), BF),
            jax.ShapeDtypeStruct((32, sides * COLS), BF),
            message,
            message,
        ),
        scratch_shapes=[
            pltpu.VMEM((CELLS, COLS), BF),
            pltpu.VMEM((CELLS, COLS), BF),
            pltpu.VMEM((CELLS, COLS), F32),
            pltpu.VMEM((2, 32, (SLOTS + sides) * COLS), BF),
            pltpu.SemaphoreType.DMA((2, 4)),
        ],
        compiler_params=params(),
        cost_estimate=pl.CostEstimate(flops=10**6, bytes_accessed=10**6, transcendentals=0),
        name="pack",
    )(flat(features), flat(cotangent))


def beside(columns, at):
    lane = lanes_of(columns[0].shape)
    if len(columns) == 1:
        place = lax.axis_index("narrow")
        first = (COLS - HALO) * place
        turned = pltpu.roll(columns[0], lax.rem(COLS - at + first, COLS), 1)
        return jnp.where((lane >= first) & (lane < first + HALO), turned, 0.0)
    right = pltpu.roll(columns[0], (-at) % COLS, 1)
    left = pltpu.roll(columns[1], (COLS - HALO - at) % COLS, 1)
    return jnp.where(lane < HALO, right, jnp.where(lane >= COLS - HALO, left, 0.0))


def turn(main, side, by):
    lane = lanes_of(main.shape)
    a, b = pltpu.roll(main, (-by) % COLS, 1), pltpu.roll(side, (-by) % COLS, 1)
    crossed = lane >= COLS - by if by > 0 else lane < -by
    return jnp.where(crossed, b, a), jnp.where(crossed, a, b)


def put_pooled(main, side, main_ref, side_ref, at, side_at):
    main, side = main.astype(F32), side.astype(F32)
    for d in range(3):
        a, b = (main, side) if d == 1 else turn(main, side, 2 * (d - 1))
        main_ref[d * 16 : d * 16 + 16, row(at)] = a.astype(BF)
        side_ref[d * 16 : d * 16 + 16, row(side_at)] = b.astype(BF)


def put_cotangent(main, side, main_ref, side_ref, at, side_at):
    for d in range(3):
        a, b = (main, side) if d == 1 else turn(main, side, d - 1)
        main_ref[d * 32 : d * 32 + 32, row(at)] = a.astype(BF)
        side_ref[d * 32 : d * 32 + 32, row(side_at)] = b.astype(BF)


def put_features(main, side, ref, step, at):
    for d in range(3):
        a = main if d == 1 else turn(main, side, d - 1)[0]
        ref[d * step : d * step + 32, row(at)] = a.astype(BF)


def coarse_row(values, totals, keeps):
    act, grad = [], []
    for value, total, kept in zip(values, totals, keeps):
        sig = 1.0 / (1.0 + jnp.exp(-value))
        act.append((value * sig * kept).astype(BF).astype(F32))
        grad_act = pair_sum(total).astype(BF).astype(F32)
        grad_pre = grad_act * (sig * (1.0 + value * (1.0 - sig)))
        grad.append((grad_pre * kept).astype(BF).astype(F32))
    acts = [act[0] if d == 1 else turn(act[0], act[1], d - 1)[0] for d in range(3)]
    grads = [grad[0] if d == 1 else turn(grad[0], grad[1], 2 * (d - 1))[0] for d in range(3)]
    return [a.astype(BF) for a in acts], [g.astype(BF) for g in grads]


def column_masks(count):
    n = lax.axis_index("narrow")
    flag = lambda is_there: jnp.where(is_there, 1.0, 0.0)
    return jnp.where(lanes_of((C2, COLS)) < 64, flag(n < count - 1), flag(n > 0))


INNER = range(1, ROWS // 2 - 1)


def own_kernel(
    sides,
    s_ref, columns_ref, wc_ref, wg_ref,
    pst_ref, jf_ref, gst_ref, pre_ref, prb_ref, rg_ref, rgb_ref,
    psb_ref, gsb_ref,
):
    columns = [columns_ref[:, row(side)].astype(F32) for side in range(sides)]
    last = None
    for y in range(ROWS):
        main, side = s_ref[0:32, row(y)].astype(F32), beside(columns, HALO * y)
        put_features(main, side, jf_ref, 32, y)
        if y % 2 == 1:
            means = [pooled(a, b) for a, b in zip(last, (main, side))]
            put_pooled(*means, pst_ref, psb_ref, y // 2, y // 2)
        last = (main, side)
        main, side = s_ref[32:64, row(y)].astype(F32), beside(columns, 64 + HALO * y)
        put_cotangent(main, side, gst_ref, gsb_ref, y, y)
    pre_ref[...] = dot(wc_ref[...], pst_ref[...])
    prb_ref[...] = dot(wc_ref[...], psb_ref[...])
    rg_ref[...] = dot(wg_ref[...], gst_ref[...])
    rgb_ref[...] = dot(wg_ref[96:192, :], gsb_ref[...])


def shaped(rows_, lanes_, kind):
    return jax.ShapeDtypeStruct((rows_, lanes_ * COLS), kind)


def scratch(rows_, lanes_, kind):
    return pltpu.VMEM((rows_, lanes_ * COLS), kind)


def own_rows(s, columns, wc, wg, sides):
    half = ROWS // 2
    return pl.pallas_call(
        functools.partial(own_kernel, sides),
        out_shape=(
            shaped(48, half, BF), shaped(96, ROWS, BF), shaped(96, ROWS, BF),
            shaped(96, half, F32), shaped(96, half, F32),
            shaped(192, ROWS, F32), shaped(96, ROWS, F32),
        ),
        scratch_shapes=[scratch(48, half, BF), scratch(96, ROWS, BF)],
        compiler_params=params(),
        cost_estimate=pl.CostEstimate(flops=10**9, bytes_accessed=4 * 10**6, transcendentals=0),
        name="own_rows",
    )(s, columns, wc, wg)


def put_joined(jst_ref, at, jl_ref, to):
    for lo in (0, 48):
        jl_ref[lo : lo + 16, to] = jst_ref[64:80, at]
        jl_ref[lo + 16 : lo + 48, to] = jst_ref[96:128, at]
        jl_ref[128 + lo : 128 + lo + 48, to] = jst_ref[80:128, at]
    for lo in (96, 224):
        jl_ref[lo : lo + 32, to] = jnp.zeros((32, to.stop - to.start), BF)


def put_field(flat_ref, y, plane, value):
    flat_ref[pl.ds(2 * y + plane, C1, stride=2 * ROWS), :] = value


FINE = range(2 * INNER.start, 2 * INNER.stop)


def inner_kernel(
    count,
    pst_ref, jf_ref, gst_ref, pre_ref, prb_ref, rg_ref, rgb_ref, wo_ref, wq_ref,
    out_ref, gf_ref, ro_ref, rq_ref, rf_ref, rc_ref,
    jst_ref, qst_ref, gl_ref, jl_ref, pl_ref, ql_ref,
):
    rows, coarse_rows = len(FINE), len(INNER)
    there = column_masks(count)
    for d in range(3):
        jst_ref[d * 64 : d * 64 + 32, :] = jf_ref[d * 32 : d * 32 + 32, row(FINE.start, rows)]
    for at in INNER:
        values = [
            sum(ref[d * 32 : d * 32 + 32, row(at + d - 1)] for d in range(3)) for ref in (pre_ref, prb_ref)
        ]
        totals = [
            sum(
                ref[lo + d * 32 : lo + d * 32 + 32, row(r + d - 1)]
                for r in (2 * at, 2 * at + 1)
                for d in range(3)
            )
            for ref, lo in ((rg_ref, 96), (rgb_ref, 0))
        ]
        acts, grads = coarse_row(values, totals, (1.0, there))
        for d in range(3):
            for r in (2 * at, 2 * at + 1):
                jst_ref[d * 64 + 32 : d * 64 + 64, row(r - FINE.start)] = acts[d]
            qst_ref[d * 32 : d * 32 + 32, row(at - INNER.start)] = grads[d]
    ro_ref[...] = dot(wo_ref[...], jst_ref[...])
    rq_ref[...] = dot(wq_ref[...], qst_ref[...])

    put_joined(jst_ref, row(0, rows), jl_ref, row(0, rows))
    ql_ref[0:96, :] = jnp.zeros((96, coarse_rows * COLS), BF)
    ql_ref[96:128, :] = qst_ref[32:64, :]
    for ky in range(3):
        gl_ref[ky * 96 : ky * 96 + 96, :] = gst_ref[:, row(FINE.start + 1 - ky, rows)]
        pl_ref[ky * 48 : ky * 48 + 48, :] = pst_ref[:, row(INNER.start + ky - 1, coarse_rows)]
    rf_ref[...] = dot_nt(gl_ref[...], jl_ref[...])
    rc_ref[...] = dot_nt(pl_ref[...], ql_ref[...])

    for y in range(FINE.start + 1, FINE.stop - 1):
        value = sum(ro_ref[d * 32 : d * 32 + 32, row(y - 1 + d - FINE.start)] for d in range(3))
        for z in range(2):
            put_field(out_ref, y, z, value[z * 16 : z * 16 + 16])
    for at in range(INNER.start + 1, INNER.stop - 1):
        coarse = sum(rq_ref[d * 16 : d * 16 + 16, row(at - 1 + d - INNER.start)] for d in range(3))
        coarse = coarse.astype(BF).astype(F32) * 0.125
        for y in (2 * at, 2 * at + 1):
            for z in range(2):
                lo = z * 16
                value = sum(rg_ref[lo + d * 32 : lo + d * 32 + 16, row(y - 1 + d)] for d in range(3))
                put_field(gf_ref, y, z, value + coarse)


def inner_rows(own, wo, wq, count):
    rows, coarse_rows = len(FINE), len(INNER)
    return pl.pallas_call(
        functools.partial(inner_kernel, count),
        out_shape=(
            shaped(CELLS, 1, F32), shaped(CELLS, 1, F32),
            shaped(96, rows, F32), shaped(48, coarse_rows, F32),
            shaped(288, 2, F32), shaped(144, 1, F32),
        ),
        scratch_shapes=[
            scratch(192, rows, BF), scratch(96, coarse_rows, BF),
            scratch(288, rows, BF), scratch(256, rows, BF),
            scratch(144, coarse_rows, BF), scratch(128, coarse_rows, BF),
        ],
        compiler_params=params(),
        cost_estimate=pl.CostEstimate(flops=10**9, bytes_accessed=4 * 10**6, transcendentals=10**5),
        name="inner_rows",
    )(*own, wo, wq)


def rest_kernel(
    counts, sides,
    odd_ref, even_ref, corners_ref,
    pst_own, jf_own, gst_own, pre_own, prb_own, rg_own, rgb_own,
    out_inner, gf_inner, ro_inner, rq_inner, rf_inner, rc_inner,
    wo_ref, wg_ref, wc_ref, wq_ref,
    out_ref, gf_ref, gw_ref,
    halo_ref, jst_ref, gst_ref, gsb_ref, pst_ref, psb_ref, qst_ref,
    pre_ref, prb_ref, rg_ref, rgb_ref, ro_ref, rq_ref, gl_ref, jl_ref, pl_ref, ql_ref, flat_ref,
):
    w = lax.axis_index("wide")
    there = column_masks(counts[1])
    flag = lambda is_there: jnp.where(is_there, 1.0, 0.0)
    has_above, has_below = flag(w > 0), flag(w < counts[0] - 1)

    odd = w % 2
    halo_ref[1 - odd] = even_ref[:, row(0, SLOTS)]
    halo_ref[odd] = odd_ref[:, row(0, SLOTS)]
    columns = [corners_ref[:, row(side)].astype(F32) for side in range(sides)]

    for i in range(2):
        lane = HALO * (ROWS - HALO) if i == 0 else 0
        for j in range(3):
            main = halo_ref[i, :, row(2 + j)].astype(F32)
            side = beside(columns, 64 + lane + HALO * (j + 1 - i))
            put_cotangent(main, side, gst_ref, gsb_ref, 9 * i + j, 3 * i + j)
        gst_ref[:, row(3 + 3 * i, 3)] = gst_own[:, row(13 * i, 3)]
        rg_ref[:, row(3 * i, 3)] = dot(wg_ref[...], gst_ref[:, row(9 * i, 3)])
    rgb_ref[...] = dot(wg_ref[96:192, :], gsb_ref[...])
    for i in range(2):
        lane = HALO * (ROWS - HALO) if i == 0 else 0
        sides_f = [beside(columns, lane + HALO * r) for r in range(HALO)]
        near = HALO - 1 if i == 0 else 0
        for j in range(2):
            main = halo_ref[i, j * 16 : j * 16 + 16, row(1)]
            side = pooled(sides_f[2 * j], sides_f[2 * j + 1])
            put_pooled(main, side, pst_ref, psb_ref, 6 * i + j, 2 * i + j)
        pst_ref[:, row(2 + 2 * i, 2)] = pst_own[:, row(6 * i, 2)]
        pre_ref[:, row(2 * i, 2)] = dot(wc_ref[...], pst_ref[:, row(6 * i, 2)])
        put_features(halo_ref[i, :, row(0)].astype(F32), sides_f[near], jst_ref, 64, 5 * i)
        for d in range(3):
            jst_ref[d * 64 : d * 64 + 32, row(1 + 2 * i, 2)] = jf_own[d * 32 : d * 32 + 32, row(14 * i, 2)]
    prb_ref[...] = dot(wc_ref[...], psb_ref[...])

    def part(own, halo, lo, size, at, edge, length):
        if at < edge:
            return halo[lo : lo + size, row(at)]
        if at < edge + length:
            return own[lo : lo + size, row(at - edge)]
        return halo[lo : lo + size, row(at - length)]

    for k, at in enumerate((0, 1, 8, 9)):
        keep = has_above if at == 0 else has_below if at == 9 else 1.0
        values = [
            sum(part(own, halo, d * 32, 32, at + d, 2, 8) for d in range(3))
            for own, halo in ((pre_own, pre_ref), (prb_own, prb_ref))
        ]
        totals = [
            sum(
                part(own, halo, lo + d * 32, 32, r + d, 3, ROWS)
                for r in (2 * at, 2 * at + 1)
                for d in range(3)
            )
            for own, halo, lo in ((rg_own, rg_ref, 96), (rgb_own, rgb_ref, 0))
        ]
        acts, grads = coarse_row(values, totals, (keep, keep * there))
        for d in range(3):
            for r in ((0,), (1, 2), (3, 4), (5,))[k]:
                jst_ref[d * 64 + 32 : d * 64 + 64, row(r)] = acts[d]
            qst_ref[d * 32 : d * 32 + 32, row(k)] = grads[d]

    put_joined(jst_ref, row(1, 4), jl_ref, row(0, 4))
    ql_ref[0:96, :] = jnp.zeros((96, 2 * COLS), BF)
    ql_ref[96:128, :] = qst_ref[32:64, row(1, 2)]
    for i in range(2):
        for ky in range(3):
            gl_ref[ky * 96 : ky * 96 + 96, row(2 * i, 2)] = gst_ref[:, row(4 + 4 * i - ky, 2)]
            pl_ref[ky * 48 : ky * 48 + 48, row(i)] = pst_ref[:, row(1 + 3 * i + ky)]
    rf = rf_inner[...] + dot_nt(gl_ref[...], jl_ref[...])
    rc = rc_inner[...] + dot_nt(pl_ref[...], ql_ref[...])
    ro_ref[...] = dot(wo_ref[...], jst_ref[...])
    rq_ref[...] = dot(wq_ref[...], qst_ref[...])
    fine, coarse = {}, {}
    for ky in range(3):
        for kx in range(3):
            lo = ky * 96 + (2 - kx) * 32
            fine[ky, 0, kx] = rf[lo + 16 : lo + 32, 0:128]
            fine[ky, 1, kx] = rf[lo : lo + 16, 0:128] + rf[lo + 16 : lo + 32, 128:256]
            fine[ky, 2, kx] = rf[lo : lo + 16, 128:256]
            coarse[ky, kx] = rc[ky * 48 + kx * 16 : ky * 48 + kx * 16 + 16] * 0.5
    lane16 = lanes_of((16, COLS))
    order = [(ky, kz, kx) for ky in range(3) for kz in range(3) for kx in range(3)]
    for i in range(16):
        value = jnp.zeros((16, COLS), F32)
        if i < 14:
            value = jnp.where(lane16 < 48, fine[order[i]], value)
        if i < 13:
            value = jnp.where((lane16 >= 48) & (lane16 < 96), fine[order[14 + i]], value)
        if i < 9:
            value = jnp.where(lane16 >= 96, coarse[i // 3, i % 3], value)
        gw_ref[i * 16 : i * 16 + 16, :] = value.astype(BF)

    flat_ref[0] = out_inner[...]
    flat_ref[1] = gf_inner[...]
    for y in (0, 1, 2, 13, 14, 15):
        value = sum(part(ro_inner, ro_ref, d * 32, 32, y + d, 3, len(FINE)) for d in range(3))
        for z in range(2):
            put_field(flat_ref.at[0], y, z, value[z * 16 : z * 16 + 16])
    out_ref[...] = flat_ref[0].astype(BF)

    for at in (0, 1, 6, 7):
        coarse = sum(part(rq_inner, rq_ref, d * 16, 16, at + d, 2, len(INNER)) for d in range(3))
        coarse = coarse.astype(BF).astype(F32) * 0.125
        for y in (2 * at, 2 * at + 1):
            for z in range(2):
                lo = z * 16
                value = sum(part(rg_own, rg_ref, lo + d * 32, 16, y + 2 + d, 3, ROWS) for d in range(3))
                put_field(flat_ref.at[1], y, z, value + coarse)
    gf_ref[...] = flat_ref[1].astype(BF)


def rest(messages, own, inner, matrices, counts, sides):
    return pl.pallas_call(
        functools.partial(rest_kernel, counts, sides),
        out_shape=(
            pltpu.VMEM((CELLS, COLS), BF),
            pltpu.VMEM((CELLS, COLS), BF),
            jax.ShapeDtypeStruct((256, COLS), BF),
        ),
        scratch_shapes=[
            pltpu.VMEM((2, 32, SLOTS * COLS), BF),
            scratch(192, 6, BF),
            scratch(96, 12, BF), scratch(96, 6, BF),
            scratch(48, 8, BF), scratch(48, 4, BF),
            scratch(96, 4, BF),
            scratch(96, 4, F32), scratch(96, 4, F32),
            scratch(192, 6, F32), scratch(96, 6, F32),
            scratch(96, 6, F32),
            scratch(48, 4, F32),
            scratch(288, 4, BF), scratch(256, 4, BF), scratch(144, 2, BF), scratch(128, 2, BF),
            pltpu.VMEM((2, CELLS, COLS), F32),
        ],
        compiler_params=params(),
        cost_estimate=pl.CostEstimate(flops=10**9, bytes_accessed=4 * 10**6, transcendentals=10**5),
        name="rest",
    )(*messages, *own, *inner, *matrices)


def add_kernel(parts_ref, copies_ref):
    total = parts_ref[0].astype(F32)
    for i in range(1, parts_ref.shape[0]):
        total = total + parts_ref[i].astype(F32)
    total = total.astype(BF)
    for i in range(parts_ref.shape[0]):
        copies_ref[i] = total


def add_up(parts):
    return pl.pallas_call(
        add_kernel,
        out_shape=jax.ShapeDtypeStruct(parts.shape, BF),
        compiler_params=pltpu.CompilerParams(vmem_limit_bytes=VMEM_LIMIT),
        name="add_up",
    )(parts)


def spread_kernel(
    fine_scale, coarse_scale,
    sum_ref, out_ref, gf_ref,
    out_hbm, gf_hbm, fine_hbm, coarse_hbm,
    fine_ref, coarse_ref, field_sems, weight_sems,
):
    fields = chunks(((out_ref, out_hbm), (gf_ref, gf_hbm)), field_sems, 4)
    weights = chunks(((fine_ref, fine_hbm), (coarse_ref, coarse_hbm)), weight_sems, 3)
    for copies in fields:
        start(copies)
    for i in range(27):
        at = (i if i < 14 else i - 14) * 16
        value = sum_ref[at : at + 16, :].astype(F32)
        if i >= 14:
            value = pltpu.roll(value, 80, 1)
        fine_ref[i * 16 : i * 16 + 16, :] = value[:, 0:48] * fine_scale
        ky, kz, kx = i // 9, i // 3 % 3, i % 3
        if kz == 1:
            at = (ky * 3 + kx) * 16
            value = pltpu.roll(sum_ref[at : at + 16, :].astype(F32), 32, 1)[:, 0:32] * coarse_scale
        else:
            value = jnp.zeros((16, 32), F32)
        coarse_ref[i * 16 : i * 16 + 16, :] = value
        if i % 9 == 8:
            weights[0][ky].start()
            weights[1][ky].start()
    for copies in fields + weights:
        wait(copies)


def spread(total, output, grad_features, fine_scale, coarse_scale):
    return pl.pallas_call(
        functools.partial(spread_kernel, fine_scale, coarse_scale),
        in_specs=[pl.BlockSpec(memory_space=pltpu.VMEM)] * 3,
        out_specs=(pl.BlockSpec(memory_space=pl.ANY),) * 4,
        out_shape=(
            jax.ShapeDtypeStruct((CELLS, COLS), BF),
            jax.ShapeDtypeStruct((CELLS, COLS), BF),
            jax.ShapeDtypeStruct((TAPS, 48), F32),
            jax.ShapeDtypeStruct((TAPS, 32), F32),
        ),
        scratch_shapes=[
            pltpu.VMEM((TAPS, 48), F32),
            pltpu.VMEM((TAPS, 32), F32),
            pltpu.SemaphoreType.DMA((2, 4)),
            pltpu.SemaphoreType.DMA((2, 3)),
        ],
        compiler_params=params(),
        name="spread",
    )(total, output, grad_features)


def matrices_kernel(
    fine_hbm, coarse_hbm, wo_ref, wg_ref, wc_ref, wq_ref,
    fine_ref, coarse_ref, wide_ref, pieces_ref, blocks_ref, sems,
):
    fine_copies, coarse_copies = chunks(((fine_hbm, fine_ref), (coarse_hbm, coarse_ref)), sems, 3)
    start(fine_copies)
    start(coarse_copies)
    lane = lanes_of((C1, COLS))
    wait(fine_copies)
    wide_ref[:, 0:48] = fine_ref[...].astype(F32)
    for ky in range(3):
        for zo in range(2):
            tiles = [jnp.zeros((C1, COLS), F32) for _ in range(2)]
            for kx in range(3):
                at = ((ky * 3 + 1 - zo) * 3 + kx) * 16
                first, second = (wide_ref[at + i : at + i + 16, :] for i in (0, 48))
                both = (first + second).astype(BF).astype(F32)
                piece = jnp.where(lane < 32, pltpu.roll(second, 16, 1), pltpu.roll(both, 16, 1))
                piece = jnp.where(lane < 16, first, jnp.where(lane < 64, piece, 0.0))
                spot = (2 - kx) * 32 + zo * 16
                pieces_ref[2 - ky, spot : spot + 16, :] = piece
                tiles[kx // 2] = tiles[kx // 2] + (pltpu.roll(piece, 64, 1) if kx == 1 else piece)
            spot = ky * 32 + zo * 16
            wo_ref[spot : spot + 16, 0:128] = tiles[0].astype(BF)
            wo_ref[spot : spot + 16, 128:192] = tiles[1][:, 0:64].astype(BF)
    wait(coarse_copies)
    wide_ref[:, 0:32] = coarse_ref[...].astype(F32)
    for ky in range(3):
        total = jnp.zeros((C1, COLS), F32)
        for kx in range(3):
            at = ((ky * 3 + 1) * 3 + kx) * 16
            value = jnp.where(lane < 32, wide_ref[at : at + 16, :], 0.0)
            blocks_ref[ky, kx * 16 : kx * 16 + 16, :] = value
            spot = (2 - kx) * 32
            total = total + (pltpu.roll(value, spot, 1) if spot else value)
        wq_ref[(2 - ky) * 16 : (2 - ky) * 16 + 16, :] = total[:, 0:96].astype(BF)
    for d in range(3):
        turned = jnp.transpose(pieces_ref[d])[0:64, 0:96].astype(BF)
        wg_ref[d * 32 : d * 32 + 32, :] = turned[0:32]
        wg_ref[96 + d * 32 : 96 + d * 32 + 32, :] = turned[32:64]
        wc_ref[d * 32 : d * 32 + 32, :] = jnp.transpose(blocks_ref[d])[0:32, 0:48].astype(BF)


def weight_matrices(coarse_weight, fine_weight):
    fine = jnp.transpose(fine_weight, (2, 3, 4, 0, 1)).reshape(TAPS, 48)
    coarse = jnp.transpose(coarse_weight, (2, 3, 4, 1, 0)).reshape(TAPS, 32)
    shape = lambda *dims: jax.ShapeDtypeStruct(dims, BF)
    return pl.pallas_call(
        matrices_kernel,
        in_specs=[pl.BlockSpec(memory_space=pltpu.HBM)] * 2,
        out_shape=(shape(96, 192), shape(192, 96), shape(96, 48), shape(48, 96)),
        scratch_shapes=[
            pltpu.VMEM((TAPS, 48), BF),
            pltpu.VMEM((TAPS, 32), BF),
            pltpu.VMEM((TAPS, COLS), F32),
            pltpu.VMEM((3, COLS, COLS), F32),
            pltpu.VMEM((3, COLS, COLS), F32),
            pltpu.SemaphoreType.DMA((2, 3)),
        ],
        compiler_params=params(),
        cost_estimate=pl.CostEstimate(flops=10**6, bytes_accessed=10**6, transcendentals=0),
        name="matrices",
    )(kept_in_hbm(fine), kept_in_hbm(coarse))


def beside_blocks(outer, narrow):
    if outer.shape[1] == COLS:
        return lax.ppermute(outer, "narrow", [(0, 1), (1, 0)])
    right = lax.ppermute(outer[:, :COLS], "narrow", [(i + 1, i) for i in range(narrow - 1)])
    left = lax.ppermute(outer[:, COLS:], "narrow", [(i, i + 1) for i in range(narrow - 1)])
    return jnp.concatenate([right, left], 1)


def shards(features, cotangent, coarse_weight, fine_weight):
    wide, narrow = lax.axis_size("wide"), lax.axis_size("narrow")
    sides = 1 if narrow == 2 else 2
    own, strip, to_odd, to_even = pack(features, cotangent, sides)
    swaps = lambda start: [
        pair for i in range(start, wide - 1, 2) for pair in ((i, i + 1), (i + 1, i))
    ]
    odd = lax.ppermute(to_odd, "wide", swaps(1))
    even = lax.ppermute(to_even, "wide", swaps(0))
    columns = beside_blocks(strip, narrow)
    wo, wg, wc, wq = weight_matrices(coarse_weight, fine_weight)
    corners = odd[:, SLOTS * COLS :] + even[:, SLOTS * COLS :]
    stacks = own_rows(own, columns, wc, wg, sides)
    stacks, _ = lax.optimization_barrier((stacks, corners))
    inner = inner_rows(stacks, wo, wq, narrow)
    corners = beside_blocks(corners, narrow)
    output, grad_features, grads = rest(
        (odd, even, corners), stacks, inner, (wo, wg, wc, wq), (wide, narrow), sides
    )
    devices = wide * narrow
    share = -(-256 // devices)
    grads = jnp.pad(grads, ((0, share * devices - 256), (0, 0))).reshape(devices, share, COLS)
    both = ("wide", "narrow")
    parts = lax.all_to_all(grads, both, 0, 0, tiled=True)
    total = lax.all_to_all(add_up(parts), both, 0, 0, tiled=True)
    total = total.reshape(share * devices, COLS)[:256]
    all_cells = features.shape[1] * features.shape[2] * features.shape[3] * devices
    output, grad_features, grad_fine, grad_coarse = spread(
        total, output, grad_features, 1.0 / math.sqrt(all_cells), 1.0 / math.sqrt(all_cells // 8)
    )
    grad_fine = jnp.transpose(grad_fine.reshape(3, 3, 3, C1, C1 + C2), (3, 4, 0, 1, 2))
    grad_coarse = jnp.transpose(grad_coarse.reshape(3, 3, 3, C1, C2), (4, 3, 0, 1, 2))
    return (
        output.reshape(features.shape),
        grad_features.reshape(features.shape),
        grad_fine,
        grad_coarse,
    )


def solution(mesh):
    placed = P(None, "wide", None, "narrow")
    return jax.shard_map(
        shards,
        mesh=mesh,
        in_specs=(placed, placed, P(), P()),
        out_specs=(placed, placed, P(), P()),
        check_vma=False,
    )
```

```python
import functools
import math

import jax
import jax.numpy as jnp
from jax import lax
from jax.experimental import pallas as pl
from jax.experimental.pallas import tpu as pltpu
from jax.sharding import PartitionSpec as P

C1, C2 = 16, 32
ROWS, COLS = 16, 128
HALO = 4
BF, F32 = jnp.bfloat16, jnp.float32
VMEM_LIMIT = 20 * 1024 * 1024


def lanes_of(shape):
    return lax.broadcasted_iota(jnp.int32, shape, len(shape) - 1)


def row(index, count=1):
    return slice(index * COLS, (index + count) * COLS)


def pair_sum(value):
    lane = lanes_of(value.shape)
    other = jnp.where(lane % 2 == 0, pltpu.roll(value, COLS - 1, 1), pltpu.roll(value, 1, 1))
    return value + other


def pooled(first, second):
    total = first + second
    return (pair_sum(total[0:16] + total[16:32]) * 0.125).astype(BF)


def dot(a, b):
    return jnp.dot(a, b, preferred_element_type=F32)


def dot_nt(a, b):
    return lax.dot_general(a, b, (((1,), (1,)), ((), ())), preferred_element_type=F32)


def params():
    return pltpu.CompilerParams(vmem_limit_bytes=VMEM_LIMIT)


SLOTS = 5
CELLS = C1 * ROWS * 2
TAPS = 27 * C1


def chunks(pairs, sems, pieces):
    copies = []
    for i, (source, target) in enumerate(pairs):
        rows = source.shape[0] // pieces
        copies.append([
            pltpu.make_async_copy(
                source.at[pl.ds(j * rows, rows)], target.at[pl.ds(j * rows, rows)], sems.at[i, j]
            )
            for j in range(pieces)
        ])
    return copies


def start(copies):
    for copy in copies:
        copy.start()


def wait(copies):
    for copy in copies:
        copy.wait()


def pack_kernel(
    sides, f_hbm, g_hbm, s_ref, strip_ref, odd_ref, even_ref, f_ref, g_ref, wide_ref, base_ref, sems
):
    arrivals = chunks(((f_hbm, f_ref), (g_hbm, g_ref)), sems, 4)
    for copies in arrivals:
        start(copies)
    lane = lanes_of((C1, COLS))
    place = lax.axis_index("narrow")
    odd = lax.axis_index("wide") % 2
    strips = [[jnp.zeros((C1, COLS), F32) for _ in range(sides)] for _ in range(2)]
    for a in range(2):
        wait(arrivals[a])
        wide_ref[...] = (f_ref, g_ref)[a][...].astype(F32)
        for z in range(2):
            chans = slice(a * 32 + z * 16, a * 32 + z * 16 + 16)
            for y in range(ROWS):
                value = wide_ref[pl.ds(2 * y + z, C1, stride=2 * ROWS), :]
                s_ref[chans, row(y)] = value.astype(BF)
                first = 64 * a + HALO * y
                inside = (lane >= first) & (lane < first + HALO)
                for side in range(sides):
                    if sides == 2:
                        shift = (first + HALO * side) % COLS
                    else:
                        shift = lax.rem(first + HALO * (1 - place), COLS)
                    strips[z][side] = jnp.where(inside, pltpu.roll(value, shift, 1), strips[z][side])
    for z in range(2):
        for side in range(sides):
            strip_ref[z * 16 : z * 16 + 16, row(side)] = strips[z][side].astype(BF)
    for to, near, pairs, cot in ((0, ROWS - 1, (6, 7), ROWS - 3), (1, 0, (0, 1), 0)):
        base_ref[to, :, row(0)] = s_ref[0:32, row(near)]
        for i, pair in enumerate(pairs):
            first, second = (s_ref[0:32, row(2 * pair + j)].astype(F32) for j in range(2))
            base_ref[to, i * 16 : i * 16 + 16, row(1)] = pooled(first, second)
        base_ref[to, :, row(2, 3)] = s_ref[32:64, row(cot, 3)]
        for side in range(sides):
            for z in range(2):
                kept = lane % 64 >= 48 if to == 0 else lane % 64 < 16
                value = jnp.where(kept, strips[z][side], 0.0).astype(BF)
                base_ref[to, z * 16 : z * 16 + 16, row(SLOTS + side)] = value
    even_ref[...] = base_ref[odd]
    odd_ref[...] = base_ref[1 - odd]


def kept_in_hbm(array):
    return pltpu.with_memory_space_constraint(array, pltpu.HBM)


def pack(features, cotangent, sides):
    flat = lambda a: kept_in_hbm(a.reshape(CELLS, COLS))
    message = jax.ShapeDtypeStruct((32, (SLOTS + sides) * COLS), BF)
    return pl.pallas_call(
        functools.partial(pack_kernel, sides),
        in_specs=[pl.BlockSpec(memory_space=pltpu.HBM)] * 2,
        out_shape=(
            jax.ShapeDtypeStruct((64, ROWS * COLS), BF),
            jax.ShapeDtypeStruct((32, sides * COLS), BF),
            message,
            message,
        ),
        scratch_shapes=[
            pltpu.VMEM((CELLS, COLS), BF),
            pltpu.VMEM((CELLS, COLS), BF),
            pltpu.VMEM((CELLS, COLS), F32),
            pltpu.VMEM((2, 32, (SLOTS + sides) * COLS), BF),
            pltpu.SemaphoreType.DMA((2, 4)),
        ],
        compiler_params=params(),
        cost_estimate=pl.CostEstimate(flops=10**6, bytes_accessed=10**6, transcendentals=0),
        name="pack",
    )(flat(features), flat(cotangent))


def beside(columns, at):
    lane = lanes_of(columns[0].shape)
    if len(columns) == 1:
        place = lax.axis_index("narrow")
        first = (COLS - HALO) * place
        turned = pltpu.roll(columns[0], lax.rem(COLS - at + first, COLS), 1)
        return jnp.where((lane >= first) & (lane < first + HALO), turned, 0.0)
    right = pltpu.roll(columns[0], (-at) % COLS, 1)
    left = pltpu.roll(columns[1], (COLS - HALO - at) % COLS, 1)
    return jnp.where(lane < HALO, right, jnp.where(lane >= COLS - HALO, left, 0.0))


def turn(main, side, by):
    lane = lanes_of(main.shape)
    a, b = pltpu.roll(main, (-by) % COLS, 1), pltpu.roll(side, (-by) % COLS, 1)
    crossed = lane >= COLS - by if by > 0 else lane < -by
    return jnp.where(crossed, b, a), jnp.where(crossed, a, b)


def put_pooled(main, side, main_ref, side_ref, at, side_at):
    main, side = main.astype(F32), side.astype(F32)
    for d in range(3):
        a, b = (main, side) if d == 1 else turn(main, side, 2 * (d - 1))
        main_ref[d * 16 : d * 16 + 16, row(at)] = a.astype(BF)
        side_ref[d * 16 : d * 16 + 16, row(side_at)] = b.astype(BF)


def put_cotangent(main, side, main_ref, side_ref, at, side_at):
    for d in range(3):
        a, b = (main, side) if d == 1 else turn(main, side, d - 1)
        main_ref[d * 32 : d * 32 + 32, row(at)] = a.astype(BF)
        side_ref[d * 32 : d * 32 + 32, row(side_at)] = b.astype(BF)


def put_features(main, side, ref, step, at):
    for d in range(3):
        a = main if d == 1 else turn(main, side, d - 1)[0]
        ref[d * step : d * step + 32, row(at)] = a.astype(BF)


def coarse_row(values, totals, keeps):
    act, grad = [], []
    for value, total, kept in zip(values, totals, keeps):
        sig = 1.0 / (1.0 + jnp.exp(-value))
        act.append((value * sig * kept).astype(BF).astype(F32))
        grad_act = pair_sum(total).astype(BF).astype(F32)
        grad_pre = grad_act * (sig * (1.0 + value * (1.0 - sig)))
        grad.append((grad_pre * kept).astype(BF).astype(F32))
    acts = [act[0] if d == 1 else turn(act[0], act[1], d - 1)[0] for d in range(3)]
    grads = [grad[0] if d == 1 else turn(grad[0], grad[1], 2 * (d - 1))[0] for d in range(3)]
    return [a.astype(BF) for a in acts], [g.astype(BF) for g in grads]


def column_masks(count):
    n = lax.axis_index("narrow")
    flag = lambda is_there: jnp.where(is_there, 1.0, 0.0)
    return jnp.where(lanes_of((C2, COLS)) < 64, flag(n < count - 1), flag(n > 0))


INNER = range(1, ROWS // 2 - 1)


def own_kernel(
    sides,
    s_ref, columns_ref, wc_ref, wg_ref,
    pst_ref, jf_ref, gst_ref, pre_ref, prb_ref, rg_ref, rgb_ref,
    psb_ref, gsb_ref,
):
    columns = [columns_ref[:, row(side)].astype(F32) for side in range(sides)]
    last = None
    for y in range(ROWS):
        main, side = s_ref[0:32, row(y)].astype(F32), beside(columns, HALO * y)
        put_features(main, side, jf_ref, 32, y)
        if y % 2 == 1:
            means = [pooled(a, b) for a, b in zip(last, (main, side))]
            put_pooled(*means, pst_ref, psb_ref, y // 2, y // 2)
        last = (main, side)
        main, side = s_ref[32:64, row(y)].astype(F32), beside(columns, 64 + HALO * y)
        put_cotangent(main, side, gst_ref, gsb_ref, y, y)
    pre_ref[...] = dot(wc_ref[...], pst_ref[...])
    prb_ref[...] = dot(wc_ref[...], psb_ref[...])
    rg_ref[...] = dot(wg_ref[...], gst_ref[...])
    rgb_ref[...] = dot(wg_ref[96:192, :], gsb_ref[...])


def shaped(rows_, lanes_, kind):
    return jax.ShapeDtypeStruct((rows_, lanes_ * COLS), kind)


def scratch(rows_, lanes_, kind):
    return pltpu.VMEM((rows_, lanes_ * COLS), kind)


def own_rows(s, columns, wc, wg, sides):
    half = ROWS // 2
    return pl.pallas_call(
        functools.partial(own_kernel, sides),
        out_shape=(
            shaped(48, half, BF), shaped(96, ROWS, BF), shaped(96, ROWS, BF),
            shaped(96, half, F32), shaped(96, half, F32),
            shaped(192, ROWS, F32), shaped(96, ROWS, F32),
        ),
        scratch_shapes=[scratch(48, half, BF), scratch(96, ROWS, BF)],
        compiler_params=params(),
        cost_estimate=pl.CostEstimate(flops=10**9, bytes_accessed=4 * 10**6, transcendentals=0),
        name="own_rows",
    )(s, columns, wc, wg)


def put_joined(jst_ref, at, jl_ref, to):
    for lo in (0, 48):
        jl_ref[lo : lo + 16, to] = jst_ref[64:80, at]
        jl_ref[lo + 16 : lo + 48, to] = jst_ref[96:128, at]
        jl_ref[128 + lo : 128 + lo + 48, to] = jst_ref[80:128, at]
    for lo in (96, 224):
        jl_ref[lo : lo + 32, to] = jnp.zeros((32, to.stop - to.start), BF)


def put_field(flat_ref, y, plane, value):
    flat_ref[pl.ds(2 * y + plane, C1, stride=2 * ROWS), :] = value


FINE = range(2 * INNER.start, 2 * INNER.stop)


def inner_kernel(
    count,
    pst_ref, jf_ref, gst_ref, pre_ref, prb_ref, rg_ref, rgb_ref, wo_ref, wq_ref,
    out_ref, gf_ref, ro_ref, rq_ref, rf_ref, rc_ref,
    jst_ref, qst_ref, gl_ref, jl_ref, pl_ref, ql_ref,
):
    rows, coarse_rows = len(FINE), len(INNER)
    there = column_masks(count)
    for d in range(3):
        jst_ref[d * 64 : d * 64 + 32, :] = jf_ref[d * 32 : d * 32 + 32, row(FINE.start, rows)]
    for at in INNER:
        values = [
            sum(ref[d * 32 : d * 32 + 32, row(at + d - 1)] for d in range(3)) for ref in (pre_ref, prb_ref)
        ]
        totals = [
            sum(
                ref[lo + d * 32 : lo + d * 32 + 32, row(r + d - 1)]
                for r in (2 * at, 2 * at + 1)
                for d in range(3)
            )
            for ref, lo in ((rg_ref, 96), (rgb_ref, 0))
        ]
        acts, grads = coarse_row(values, totals, (1.0, there))
        for d in range(3):
            for r in (2 * at, 2 * at + 1):
                jst_ref[d * 64 + 32 : d * 64 + 64, row(r - FINE.start)] = acts[d]
            qst_ref[d * 32 : d * 32 + 32, row(at - INNER.start)] = grads[d]
    ro_ref[...] = dot(wo_ref[...], jst_ref[...])
    rq_ref[...] = dot(wq_ref[...], qst_ref[...])

    put_joined(jst_ref, row(0, rows), jl_ref, row(0, rows))
    ql_ref[0:96, :] = jnp.zeros((96, coarse_rows * COLS), BF)
    ql_ref[96:128, :] = qst_ref[32:64, :]
    for ky in range(3):
        gl_ref[ky * 96 : ky * 96 + 96, :] = gst_ref[:, row(FINE.start + 1 - ky, rows)]
        pl_ref[ky * 48 : ky * 48 + 48, :] = pst_ref[:, row(INNER.start + ky - 1, coarse_rows)]
    rf_ref[...] = dot_nt(gl_ref[...], jl_ref[...])
    rc_ref[...] = dot_nt(pl_ref[...], ql_ref[...])

    for y in range(FINE.start + 1, FINE.stop - 1):
        value = sum(ro_ref[d * 32 : d * 32 + 32, row(y - 1 + d - FINE.start)] for d in range(3))
        for z in range(2):
            put_field(out_ref, y, z, value[z * 16 : z * 16 + 16])
    for at in range(INNER.start + 1, INNER.stop - 1):
        coarse = sum(rq_ref[d * 16 : d * 16 + 16, row(at - 1 + d - INNER.start)] for d in range(3))
        coarse = coarse.astype(BF).astype(F32) * 0.125
        for y in (2 * at, 2 * at + 1):
            for z in range(2):
                lo = z * 16
                value = sum(rg_ref[lo + d * 32 : lo + d * 32 + 16, row(y - 1 + d)] for d in range(3))
                put_field(gf_ref, y, z, value + coarse)


def inner_rows(own, wo, wq, count):
    rows, coarse_rows = len(FINE), len(INNER)
    return pl.pallas_call(
        functools.partial(inner_kernel, count),
        out_shape=(
            shaped(CELLS, 1, F32), shaped(CELLS, 1, F32),
            shaped(96, rows, F32), shaped(48, coarse_rows, F32),
            shaped(288, 2, F32), shaped(144, 1, F32),
        ),
        scratch_shapes=[
            scratch(192, rows, BF), scratch(96, coarse_rows, BF),
            scratch(288, rows, BF), scratch(256, rows, BF),
            scratch(144, coarse_rows, BF), scratch(128, coarse_rows, BF),
        ],
        compiler_params=params(),
        cost_estimate=pl.CostEstimate(flops=10**9, bytes_accessed=4 * 10**6, transcendentals=10**5),
        name="inner_rows",
    )(*own, wo, wq)


def rest_kernel(
    counts, sides,
    odd_ref, even_ref, corners_ref,
    pst_own, jf_own, gst_own, pre_own, prb_own, rg_own, rgb_own,
    out_inner, gf_inner, ro_inner, rq_inner, rf_inner, rc_inner,
    wo_ref, wg_ref, wc_ref, wq_ref,
    out_ref, gf_ref, gw_ref,
    halo_ref, jst_ref, gst_ref, gsb_ref, pst_ref, psb_ref, qst_ref,
    pre_ref, prb_ref, rg_ref, rgb_ref, ro_ref, rq_ref, gl_ref, jl_ref, pl_ref, ql_ref, flat_ref,
):
    w = lax.axis_index("wide")
    there = column_masks(counts[1])
    flag = lambda is_there: jnp.where(is_there, 1.0, 0.0)
    has_above, has_below = flag(w > 0), flag(w < counts[0] - 1)

    odd = w % 2
    halo_ref[1 - odd] = even_ref[:, row(0, SLOTS)]
    halo_ref[odd] = odd_ref[:, row(0, SLOTS)]
    columns = [corners_ref[:, row(side)].astype(F32) for side in range(sides)]

    for i in range(2):
        lane = HALO * (ROWS - HALO) if i == 0 else 0
        for j in range(3):
            main = halo_ref[i, :, row(2 + j)].astype(F32)
            side = beside(columns, 64 + lane + HALO * (j + 1 - i))
            put_cotangent(main, side, gst_ref, gsb_ref, 9 * i + j, 3 * i + j)
        gst_ref[:, row(3 + 3 * i, 3)] = gst_own[:, row(13 * i, 3)]
        rg_ref[:, row(3 * i, 3)] = dot(wg_ref[...], gst_ref[:, row(9 * i, 3)])
    rgb_ref[...] = dot(wg_ref[96:192, :], gsb_ref[...])
    for i in range(2):
        lane = HALO * (ROWS - HALO) if i == 0 else 0
        sides_f = [beside(columns, lane + HALO * r) for r in range(HALO)]
        near = HALO - 1 if i == 0 else 0
        for j in range(2):
            main = halo_ref[i, j * 16 : j * 16 + 16, row(1)]
            side = pooled(sides_f[2 * j], sides_f[2 * j + 1])
            put_pooled(main, side, pst_ref, psb_ref, 6 * i + j, 2 * i + j)
        pst_ref[:, row(2 + 2 * i, 2)] = pst_own[:, row(6 * i, 2)]
        pre_ref[:, row(2 * i, 2)] = dot(wc_ref[...], pst_ref[:, row(6 * i, 2)])
        put_features(halo_ref[i, :, row(0)].astype(F32), sides_f[near], jst_ref, 64, 5 * i)
        for d in range(3):
            jst_ref[d * 64 : d * 64 + 32, row(1 + 2 * i, 2)] = jf_own[d * 32 : d * 32 + 32, row(14 * i, 2)]
    prb_ref[...] = dot(wc_ref[...], psb_ref[...])

    def part(own, halo, lo, size, at, edge, length):
        if at < edge:
            return halo[lo : lo + size, row(at)]
        if at < edge + length:
            return own[lo : lo + size, row(at - edge)]
        return halo[lo : lo + size, row(at - length)]

    for k, at in enumerate((0, 1, 8, 9)):
        keep = has_above if at == 0 else has_below if at == 9 else 1.0
        values = [
            sum(part(own, halo, d * 32, 32, at + d, 2, 8) for d in range(3))
            for own, halo in ((pre_own, pre_ref), (prb_own, prb_ref))
        ]
        totals = [
            sum(
                part(own, halo, lo + d * 32, 32, r + d, 3, ROWS)
                for r in (2 * at, 2 * at + 1)
                for d in range(3)
            )
            for own, halo, lo in ((rg_own, rg_ref, 96), (rgb_own, rgb_ref, 0))
        ]
        acts, grads = coarse_row(values, totals, (keep, keep * there))
        for d in range(3):
            for r in ((0,), (1, 2), (3, 4), (5,))[k]:
                jst_ref[d * 64 + 32 : d * 64 + 64, row(r)] = acts[d]
            qst_ref[d * 32 : d * 32 + 32, row(k)] = grads[d]

    put_joined(jst_ref, row(1, 4), jl_ref, row(0, 4))
    ql_ref[0:96, :] = jnp.zeros((96, 2 * COLS), BF)
    ql_ref[96:128, :] = qst_ref[32:64, row(1, 2)]
    for i in range(2):
        for ky in range(3):
            gl_ref[ky * 96 : ky * 96 + 96, row(2 * i, 2)] = gst_ref[:, row(4 + 4 * i - ky, 2)]
            pl_ref[ky * 48 : ky * 48 + 48, row(i)] = pst_ref[:, row(1 + 3 * i + ky)]
    rf = rf_inner[...] + dot_nt(gl_ref[...], jl_ref[...])
    rc = rc_inner[...] + dot_nt(pl_ref[...], ql_ref[...])
    ro_ref[...] = dot(wo_ref[...], jst_ref[...])
    rq_ref[...] = dot(wq_ref[...], qst_ref[...])
    fine, coarse = {}, {}
    for ky in range(3):
        for kx in range(3):
            lo = ky * 96 + (2 - kx) * 32
            fine[ky, 0, kx] = rf[lo + 16 : lo + 32, 0:128]
            fine[ky, 1, kx] = rf[lo : lo + 16, 0:128] + rf[lo + 16 : lo + 32, 128:256]
            fine[ky, 2, kx] = rf[lo : lo + 16, 128:256]
            coarse[ky, kx] = rc[ky * 48 + kx * 16 : ky * 48 + kx * 16 + 16] * 0.5
    lane16 = lanes_of((16, COLS))
    order = [(ky, kz, kx) for ky in range(3) for kz in range(3) for kx in range(3)]
    for i in range(16):
        value = jnp.zeros((16, COLS), F32)
        if i < 14:
            value = jnp.where(lane16 < 48, fine[order[i]], value)
        if i < 13:
            value = jnp.where((lane16 >= 48) & (lane16 < 96), fine[order[14 + i]], value)
        if i < 9:
            value = jnp.where(lane16 >= 96, coarse[i // 3, i % 3], value)
        gw_ref[i * 16 : i * 16 + 16, :] = value.astype(BF)

    flat_ref[0] = out_inner[...]
    flat_ref[1] = gf_inner[...]
    for y in (0, 1, 2, 13, 14, 15):
        value = sum(part(ro_inner, ro_ref, d * 32, 32, y + d, 3, len(FINE)) for d in range(3))
        for z in range(2):
            put_field(flat_ref.at[0], y, z, value[z * 16 : z * 16 + 16])
    out_ref[...] = flat_ref[0].astype(BF)

    for at in (0, 1, 6, 7):
        coarse = sum(part(rq_inner, rq_ref, d * 16, 16, at + d, 2, len(INNER)) for d in range(3))
        coarse = coarse.astype(BF).astype(F32) * 0.125
        for y in (2 * at, 2 * at + 1):
            for z in range(2):
                lo = z * 16
                value = sum(part(rg_own, rg_ref, lo + d * 32, 16, y + 2 + d, 3, ROWS) for d in range(3))
                put_field(flat_ref.at[1], y, z, value + coarse)
    gf_ref[...] = flat_ref[1].astype(BF)


def rest(messages, own, inner, matrices, counts, sides):
    return pl.pallas_call(
        functools.partial(rest_kernel, counts, sides),
        out_shape=(
            pltpu.VMEM((CELLS, COLS), BF),
            pltpu.VMEM((CELLS, COLS), BF),
            jax.ShapeDtypeStruct((256, COLS), BF),
        ),
        scratch_shapes=[
            pltpu.VMEM((2, 32, SLOTS * COLS), BF),
            scratch(192, 6, BF),
            scratch(96, 12, BF), scratch(96, 6, BF),
            scratch(48, 8, BF), scratch(48, 4, BF),
            scratch(96, 4, BF),
            scratch(96, 4, F32), scratch(96, 4, F32),
            scratch(192, 6, F32), scratch(96, 6, F32),
            scratch(96, 6, F32),
            scratch(48, 4, F32),
            scratch(288, 4, BF), scratch(256, 4, BF), scratch(144, 2, BF), scratch(128, 2, BF),
            pltpu.VMEM((2, CELLS, COLS), F32),
        ],
        compiler_params=params(),
        cost_estimate=pl.CostEstimate(flops=10**9, bytes_accessed=4 * 10**6, transcendentals=10**5),
        name="rest",
    )(*messages, *own, *inner, *matrices)


def add_kernel(parts_ref, copies_ref):
    total = parts_ref[0].astype(F32)
    for i in range(1, parts_ref.shape[0]):
        total = total + parts_ref[i].astype(F32)
    total = total.astype(BF)
    for i in range(parts_ref.shape[0]):
        copies_ref[i] = total


def add_up(parts):
    return pl.pallas_call(
        add_kernel,
        out_shape=jax.ShapeDtypeStruct(parts.shape, BF),
        compiler_params=pltpu.CompilerParams(vmem_limit_bytes=VMEM_LIMIT),
        name="add_up",
    )(parts)


def spread_kernel(
    fine_scale, coarse_scale,
    sum_ref, out_ref, gf_ref,
    out_hbm, gf_hbm, fine_hbm, coarse_hbm,
    fine_ref, coarse_ref, field_sems, weight_sems,
):
    fields = chunks(((out_ref, out_hbm), (gf_ref, gf_hbm)), field_sems, 4)
    weights = chunks(((fine_ref, fine_hbm), (coarse_ref, coarse_hbm)), weight_sems, 3)
    for copies in fields:
        start(copies)
    for i in range(27):
        at = (i if i < 14 else i - 14) * 16
        value = sum_ref[at : at + 16, :].astype(F32)
        if i >= 14:
            value = pltpu.roll(value, 80, 1)
        fine_ref[i * 16 : i * 16 + 16, :] = value[:, 0:48] * fine_scale
        ky, kz, kx = i // 9, i // 3 % 3, i % 3
        if kz == 1:
            at = (ky * 3 + kx) * 16
            value = pltpu.roll(sum_ref[at : at + 16, :].astype(F32), 32, 1)[:, 0:32] * coarse_scale
        else:
            value = jnp.zeros((16, 32), F32)
        coarse_ref[i * 16 : i * 16 + 16, :] = value
        if i % 9 == 8:
            weights[0][ky].start()
            weights[1][ky].start()
    for copies in fields + weights:
        wait(copies)


def spread(total, output, grad_features, fine_scale, coarse_scale):
    return pl.pallas_call(
        functools.partial(spread_kernel, fine_scale, coarse_scale),
        in_specs=[pl.BlockSpec(memory_space=pltpu.VMEM)] * 3,
        out_specs=(pl.BlockSpec(memory_space=pl.ANY),) * 4,
        out_shape=(
            jax.ShapeDtypeStruct((CELLS, COLS), BF),
            jax.ShapeDtypeStruct((CELLS, COLS), BF),
            jax.ShapeDtypeStruct((TAPS, 48), F32),
            jax.ShapeDtypeStruct((TAPS, 32), F32),
        ),
        scratch_shapes=[
            pltpu.VMEM((TAPS, 48), F32),
            pltpu.VMEM((TAPS, 32), F32),
            pltpu.SemaphoreType.DMA((2, 4)),
            pltpu.SemaphoreType.DMA((2, 3)),
        ],
        compiler_params=params(),
        name="spread",
    )(total, output, grad_features)


def matrices_kernel(
    fine_hbm, coarse_hbm, wo_ref, wg_ref, wc_ref, wq_ref,
    fine_ref, coarse_ref, wide_ref, pieces_ref, blocks_ref, sems,
):
    fine_copies, coarse_copies = chunks(((fine_hbm, fine_ref), (coarse_hbm, coarse_ref)), sems, 3)
    start(fine_copies)
    start(coarse_copies)
    lane = lanes_of((C1, COLS))
    wait(fine_copies)
    wide_ref[:, 0:48] = fine_ref[...].astype(F32)
    for ky in range(3):
        for zo in range(2):
            tiles = [jnp.zeros((C1, COLS), F32) for _ in range(2)]
            for kx in range(3):
                at = ((ky * 3 + 1 - zo) * 3 + kx) * 16
                first, second = (wide_ref[at + i : at + i + 16, :] for i in (0, 48))
                both = (first + second).astype(BF).astype(F32)
                piece = jnp.where(lane < 32, pltpu.roll(second, 16, 1), pltpu.roll(both, 16, 1))
                piece = jnp.where(lane < 16, first, jnp.where(lane < 64, piece, 0.0))
                spot = (2 - kx) * 32 + zo * 16
                pieces_ref[2 - ky, spot : spot + 16, :] = piece
                tiles[kx // 2] = tiles[kx // 2] + (pltpu.roll(piece, 64, 1) if kx == 1 else piece)
            spot = ky * 32 + zo * 16
            wo_ref[spot : spot + 16, 0:128] = tiles[0].astype(BF)
            wo_ref[spot : spot + 16, 128:192] = tiles[1][:, 0:64].astype(BF)
    wait(coarse_copies)
    wide_ref[:, 0:32] = coarse_ref[...].astype(F32)
    for ky in range(3):
        total = jnp.zeros((C1, COLS), F32)
        for kx in range(3):
            at = ((ky * 3 + 1) * 3 + kx) * 16
            value = jnp.where(lane < 32, wide_ref[at : at + 16, :], 0.0)
            blocks_ref[ky, kx * 16 : kx * 16 + 16, :] = value
            spot = (2 - kx) * 32
            total = total + (pltpu.roll(value, spot, 1) if spot else value)
        wq_ref[(2 - ky) * 16 : (2 - ky) * 16 + 16, :] = total[:, 0:96].astype(BF)
    for d in range(3):
        turned = jnp.transpose(pieces_ref[d])[0:64, 0:96].astype(BF)
        wg_ref[d * 32 : d * 32 + 32, :] = turned[0:32]
        wg_ref[96 + d * 32 : 96 + d * 32 + 32, :] = turned[32:64]
        wc_ref[d * 32 : d * 32 + 32, :] = jnp.transpose(blocks_ref[d])[0:32, 0:48].astype(BF)


def weight_matrices(coarse_weight, fine_weight):
    fine = jnp.transpose(fine_weight, (2, 3, 4, 0, 1)).reshape(TAPS, 48)
    coarse = jnp.transpose(coarse_weight, (2, 3, 4, 1, 0)).reshape(TAPS, 32)
    shape = lambda *dims: jax.ShapeDtypeStruct(dims, BF)
    return pl.pallas_call(
        matrices_kernel,
        in_specs=[pl.BlockSpec(memory_space=pltpu.HBM)] * 2,
        out_shape=(shape(96, 192), shape(192, 96), shape(96, 48), shape(48, 96)),
        scratch_shapes=[
            pltpu.VMEM((TAPS, 48), BF),
            pltpu.VMEM((TAPS, 32), BF),
            pltpu.VMEM((TAPS, COLS), F32),
            pltpu.VMEM((3, COLS, COLS), F32),
            pltpu.VMEM((3, COLS, COLS), F32),
            pltpu.SemaphoreType.DMA((2, 3)),
        ],
        compiler_params=params(),
        cost_estimate=pl.CostEstimate(flops=10**6, bytes_accessed=10**6, transcendentals=0),
        name="matrices",
    )(kept_in_hbm(fine), kept_in_hbm(coarse))


def beside_blocks(outer, narrow):
    if outer.shape[1] == COLS:
        return lax.ppermute(outer, "narrow", [(0, 1), (1, 0)])
    right = lax.ppermute(outer[:, :COLS], "narrow", [(i + 1, i) for i in range(narrow - 1)])
    left = lax.ppermute(outer[:, COLS:], "narrow", [(i, i + 1) for i in range(narrow - 1)])
    return jnp.concatenate([right, left], 1)


def shards(features, cotangent, coarse_weight, fine_weight):
    wide, narrow = lax.axis_size("wide"), lax.axis_size("narrow")
    sides = 1 if narrow == 2 else 2
    own, strip, to_odd, to_even = pack(features, cotangent, sides)
    swaps = lambda start: [
        pair for i in range(start, wide - 1, 2) for pair in ((i, i + 1), (i + 1, i))
    ]
    odd = lax.ppermute(to_odd, "wide", swaps(1))
    even = lax.ppermute(to_even, "wide", swaps(0))
    columns = beside_blocks(strip, narrow)
    wo, wg, wc, wq = weight_matrices(coarse_weight, fine_weight)
    corners = odd[:, SLOTS * COLS :] + even[:, SLOTS * COLS :]
    columns, _ = lax.optimization_barrier((columns, corners))
    stacks = own_rows(own, columns, wc, wg, sides)
    inner = inner_rows(stacks, wo, wq, narrow)
    corners = beside_blocks(corners, narrow)
    output, grad_features, grads = rest(
        (odd, even, corners), stacks, inner, (wo, wg, wc, wq), (wide, narrow), sides
    )
    devices = wide * narrow
    share = -(-256 // devices)
    grads = jnp.pad(grads, ((0, share * devices - 256), (0, 0))).reshape(devices, share, COLS)
    both = ("wide", "narrow")
    parts = lax.all_to_all(grads, both, 0, 0, tiled=True)
    total = lax.all_to_all(add_up(parts), both, 0, 0, tiled=True)
    total = total.reshape(share * devices, COLS)[:256]
    all_cells = features.shape[1] * features.shape[2] * features.shape[3] * devices
    output, grad_features, grad_fine, grad_coarse = spread(
        total, output, grad_features, 1.0 / math.sqrt(all_cells), 1.0 / math.sqrt(all_cells // 8)
    )
    grad_fine = jnp.transpose(grad_fine.reshape(3, 3, 3, C1, C1 + C2), (3, 4, 0, 1, 2))
    grad_coarse = jnp.transpose(grad_coarse.reshape(3, 3, 3, C1, C2), (4, 3, 0, 1, 2))
    return (
        output.reshape(features.shape),
        grad_features.reshape(features.shape),
        grad_fine,
        grad_coarse,
    )


def solution(mesh):
    placed = P(None, "wide", None, "narrow")
    return jax.shard_map(
        shards,
        mesh=mesh,
        in_specs=(placed, placed, P(), P()),
        out_specs=(placed, placed, P(), P()),
        check_vma=False,
    )
```

```python
import functools
import math

import jax
import jax.numpy as jnp
from jax import lax
from jax.experimental import pallas as pl
from jax.experimental.pallas import tpu as pltpu
from jax.sharding import PartitionSpec as P

C1, C2 = 16, 32
ROWS, COLS = 16, 128
HALO = 4
BF, F32 = jnp.bfloat16, jnp.float32
VMEM_LIMIT = 20 * 1024 * 1024


def lanes_of(shape):
    return lax.broadcasted_iota(jnp.int32, shape, len(shape) - 1)


def row(index, count=1):
    return slice(index * COLS, (index + count) * COLS)


def pair_sum(value):
    lane = lanes_of(value.shape)
    other = jnp.where(lane % 2 == 0, pltpu.roll(value, COLS - 1, 1), pltpu.roll(value, 1, 1))
    return value + other


def pooled(first, second):
    total = first + second
    return (pair_sum(total[0:16] + total[16:32]) * 0.125).astype(BF)


def dot(a, b):
    return jnp.dot(a, b, preferred_element_type=F32)


def dot_nt(a, b):
    return lax.dot_general(a, b, (((1,), (1,)), ((), ())), preferred_element_type=F32)


def params():
    return pltpu.CompilerParams(vmem_limit_bytes=VMEM_LIMIT)


SLOTS = 5
CELLS = C1 * ROWS * 2
TAPS = 27 * C1


def chunks(pairs, sems, pieces):
    copies = []
    for i, (source, target) in enumerate(pairs):
        rows = source.shape[0] // pieces
        copies.append([
            pltpu.make_async_copy(
                source.at[pl.ds(j * rows, rows)], target.at[pl.ds(j * rows, rows)], sems.at[i, j]
            )
            for j in range(pieces)
        ])
    return copies


def start(copies):
    for copy in copies:
        copy.start()


def wait(copies):
    for copy in copies:
        copy.wait()


def pack_kernel(
    sides, f_hbm, g_hbm, s_ref, strip_ref, odd_ref, even_ref, f_ref, g_ref, wide_ref, base_ref, sems
):
    arrivals = chunks(((f_hbm, f_ref), (g_hbm, g_ref)), sems, 4)
    for copies in arrivals:
        start(copies)
    lane = lanes_of((C1, COLS))
    place = lax.axis_index("narrow")
    odd = lax.axis_index("wide") % 2
    strips = [[jnp.zeros((C1, COLS), F32) for _ in range(sides)] for _ in range(2)]
    for a in range(2):
        wait(arrivals[a])
        wide_ref[...] = (f_ref, g_ref)[a][...].astype(F32)
        for z in range(2):
            chans = slice(a * 32 + z * 16, a * 32 + z * 16 + 16)
            for y in range(ROWS):
                value = wide_ref[pl.ds(2 * y + z, C1, stride=2 * ROWS), :]
                s_ref[chans, row(y)] = value.astype(BF)
                first = 64 * a + HALO * y
                inside = (lane >= first) & (lane < first + HALO)
                for side in range(sides):
                    if sides == 2:
                        shift = (first + HALO * side) % COLS
                    else:
                        shift = lax.rem(first + HALO * (1 - place), COLS)
                    strips[z][side] = jnp.where(inside, pltpu.roll(value, shift, 1), strips[z][side])
    for z in range(2):
        for side in range(sides):
            strip_ref[z * 16 : z * 16 + 16, row(side)] = strips[z][side].astype(BF)
    for to, near, pairs, cot in ((0, ROWS - 1, (6, 7), ROWS - 3), (1, 0, (0, 1), 0)):
        base_ref[to, :, row(0)] = s_ref[0:32, row(near)]
        for i, pair in enumerate(pairs):
            first, second = (s_ref[0:32, row(2 * pair + j)].astype(F32) for j in range(2))
            base_ref[to, i * 16 : i * 16 + 16, row(1)] = pooled(first, second)
        base_ref[to, :, row(2, 3)] = s_ref[32:64, row(cot, 3)]
        for side in range(sides):
            for z in range(2):
                kept = lane % 64 >= 48 if to == 0 else lane % 64 < 16
                value = jnp.where(kept, strips[z][side], 0.0).astype(BF)
                base_ref[to, z * 16 : z * 16 + 16, row(SLOTS + side)] = value
    even_ref[...] = base_ref[odd]
    odd_ref[...] = base_ref[1 - odd]


def kept_in_hbm(array):
    return pltpu.with_memory_space_constraint(array, pltpu.HBM)


def pack(features, cotangent, sides):
    flat = lambda a: kept_in_hbm(a.reshape(CELLS, COLS))
    message = jax.ShapeDtypeStruct((32, (SLOTS + sides) * COLS), BF)
    return pl.pallas_call(
        functools.partial(pack_kernel, sides),
        in_specs=[pl.BlockSpec(memory_space=pltpu.HBM)] * 2,
        out_shape=(
            jax.ShapeDtypeStruct((64, ROWS * COLS), BF),
            jax.ShapeDtypeStruct((32, sides * COLS), BF),
            message,
            message,
        ),
        scratch_shapes=[
            pltpu.VMEM((CELLS, COLS), BF),
            pltpu.VMEM((CELLS, COLS), BF),
            pltpu.VMEM((CELLS, COLS), F32),
            pltpu.VMEM((2, 32, (SLOTS + sides) * COLS), BF),
            pltpu.SemaphoreType.DMA((2, 4)),
        ],
        compiler_params=params(),
        cost_estimate=pl.CostEstimate(flops=10**6, bytes_accessed=10**6, transcendentals=0),
        name="pack",
    )(flat(features), flat(cotangent))


def beside(columns, at):
    lane = lanes_of(columns[0].shape)
    if len(columns) == 1:
        place = lax.axis_index("narrow")
        first = (COLS - HALO) * place
        turned = pltpu.roll(columns[0], lax.rem(COLS - at + first, COLS), 1)
        return jnp.where((lane >= first) & (lane < first + HALO), turned, 0.0)
    right = pltpu.roll(columns[0], (-at) % COLS, 1)
    left = pltpu.roll(columns[1], (COLS - HALO - at) % COLS, 1)
    return jnp.where(lane < HALO, right, jnp.where(lane >= COLS - HALO, left, 0.0))


def turn(main, side, by):
    lane = lanes_of(main.shape)
    a, b = pltpu.roll(main, (-by) % COLS, 1), pltpu.roll(side, (-by) % COLS, 1)
    crossed = lane >= COLS - by if by > 0 else lane < -by
    return jnp.where(crossed, b, a), jnp.where(crossed, a, b)


def put_pooled(main, side, main_ref, side_ref, at, side_at):
    main, side = main.astype(F32), side.astype(F32)
    for d in range(3):
        a, b = (main, side) if d == 1 else turn(main, side, 2 * (d - 1))
        main_ref[d * 16 : d * 16 + 16, row(at)] = a.astype(BF)
        side_ref[d * 16 : d * 16 + 16, row(side_at)] = b.astype(BF)


def put_cotangent(main, side, main_ref, side_ref, at, side_at):
    for d in range(3):
        a, b = (main, side) if d == 1 else turn(main, side, d - 1)
        main_ref[d * 32 : d * 32 + 32, row(at)] = a.astype(BF)
        side_ref[d * 32 : d * 32 + 32, row(side_at)] = b.astype(BF)


def put_features(main, side, ref, step, at):
    for d in range(3):
        a = main if d == 1 else turn(main, side, d - 1)[0]
        ref[d * step : d * step + 32, row(at)] = a.astype(BF)


def coarse_row(values, totals, keeps):
    act, grad = [], []
    for value, total, kept in zip(values, totals, keeps):
        sig = 1.0 / (1.0 + jnp.exp(-value))
        act.append((value * sig * kept).astype(BF).astype(F32))
        grad_act = pair_sum(total).astype(BF).astype(F32)
        grad_pre = grad_act * (sig * (1.0 + value * (1.0 - sig)))
        grad.append((grad_pre * kept).astype(BF).astype(F32))
    acts = [act[0] if d == 1 else turn(act[0], act[1], d - 1)[0] for d in range(3)]
    grads = [grad[0] if d == 1 else turn(grad[0], grad[1], 2 * (d - 1))[0] for d in range(3)]
    return [a.astype(BF) for a in acts], [g.astype(BF) for g in grads]


def column_masks(count):
    n = lax.axis_index("narrow")
    flag = lambda is_there: jnp.where(is_there, 1.0, 0.0)
    return jnp.where(lanes_of((C2, COLS)) < 64, flag(n < count - 1), flag(n > 0))


INNER = range(1, ROWS // 2 - 1)


def own_kernel(
    sides,
    s_ref, columns_ref, wc_ref, wg_ref,
    pst_ref, jf_ref, gst_ref, pre_ref, prb_ref, rg_ref, rgb_ref,
    psb_ref, gsb_ref,
):
    columns = [columns_ref[:, row(side)].astype(F32) for side in range(sides)]
    last = None
    for y in range(ROWS):
        main, side = s_ref[0:32, row(y)].astype(F32), beside(columns, HALO * y)
        put_features(main, side, jf_ref, 32, y)
        if y % 2 == 1:
            means = [pooled(a, b) for a, b in zip(last, (main, side))]
            put_pooled(*means, pst_ref, psb_ref, y // 2, y // 2)
        last = (main, side)
        main, side = s_ref[32:64, row(y)].astype(F32), beside(columns, 64 + HALO * y)
        put_cotangent(main, side, gst_ref, gsb_ref, y, y)
    pre_ref[...] = dot(wc_ref[...], pst_ref[...])
    prb_ref[...] = dot(wc_ref[...], psb_ref[...])
    rg_ref[...] = dot(wg_ref[...], gst_ref[...])
    rgb_ref[...] = dot(wg_ref[96:192, :], gsb_ref[...])


def shaped(rows_, lanes_, kind):
    return jax.ShapeDtypeStruct((rows_, lanes_ * COLS), kind)


def scratch(rows_, lanes_, kind):
    return pltpu.VMEM((rows_, lanes_ * COLS), kind)


def own_rows(s, columns, wc, wg, sides):
    half = ROWS // 2
    return pl.pallas_call(
        functools.partial(own_kernel, sides),
        out_shape=(
            shaped(48, half, BF), shaped(96, ROWS, BF), shaped(96, ROWS, BF),
            shaped(96, half, F32), shaped(96, half, F32),
            shaped(192, ROWS, F32), shaped(96, ROWS, F32),
        ),
        scratch_shapes=[scratch(48, half, BF), scratch(96, ROWS, BF)],
        compiler_params=params(),
        cost_estimate=pl.CostEstimate(flops=10**9, bytes_accessed=4 * 10**6, transcendentals=0),
        name="own_rows",
    )(s, columns, wc, wg)


def put_joined(jst_ref, at, jl_ref, to):
    for lo in (0, 48):
        jl_ref[lo : lo + 16, to] = jst_ref[64:80, at]
        jl_ref[lo + 16 : lo + 48, to] = jst_ref[96:128, at]
        jl_ref[128 + lo : 128 + lo + 48, to] = jst_ref[80:128, at]
    for lo in (96, 224):
        jl_ref[lo : lo + 32, to] = jnp.zeros((32, to.stop - to.start), BF)


def put_field(flat_ref, y, plane, value):
    flat_ref[pl.ds(2 * y + plane, C1, stride=2 * ROWS), :] = value


FINE = range(2 * INNER.start, 2 * INNER.stop)


def inner_kernel(
    count,
    pst_ref, jf_ref, gst_ref, pre_ref, prb_ref, rg_ref, rgb_ref, wo_ref, wq_ref,
    out_ref, gf_ref, ro_ref, rq_ref, rf_ref, rc_ref,
    jst_ref, qst_ref, gl_ref, jl_ref, pl_ref, ql_ref,
):
    rows, coarse_rows = len(FINE), len(INNER)
    there = column_masks(count)
    for d in range(3):
        jst_ref[d * 64 : d * 64 + 32, :] = jf_ref[d * 32 : d * 32 + 32, row(FINE.start, rows)]
    for at in INNER:
        values = [
            sum(ref[d * 32 : d * 32 + 32, row(at + d - 1)] for d in range(3)) for ref in (pre_ref, prb_ref)
        ]
        totals = [
            sum(
                ref[lo + d * 32 : lo + d * 32 + 32, row(r + d - 1)]
                for r in (2 * at, 2 * at + 1)
                for d in range(3)
            )
            for ref, lo in ((rg_ref, 96), (rgb_ref, 0))
        ]
        acts, grads = coarse_row(values, totals, (1.0, there))
        for d in range(3):
            for r in (2 * at, 2 * at + 1):
                jst_ref[d * 64 + 32 : d * 64 + 64, row(r - FINE.start)] = acts[d]
            qst_ref[d * 32 : d * 32 + 32, row(at - INNER.start)] = grads[d]
    ro_ref[...] = dot(wo_ref[...], jst_ref[...])
    rq_ref[...] = dot(wq_ref[...], qst_ref[...])

    put_joined(jst_ref, row(0, rows), jl_ref, row(0, rows))
    ql_ref[0:96, :] = jnp.zeros((96, coarse_rows * COLS), BF)
    ql_ref[96:128, :] = qst_ref[32:64, :]
    for ky in range(3):
        gl_ref[ky * 96 : ky * 96 + 96, :] = gst_ref[:, row(FINE.start + 1 - ky, rows)]
        pl_ref[ky * 48 : ky * 48 + 48, :] = pst_ref[:, row(INNER.start + ky - 1, coarse_rows)]
    rf_ref[...] = dot_nt(gl_ref[...], jl_ref[...])
    rc_ref[...] = dot_nt(pl_ref[...], ql_ref[...])

    for y in range(FINE.start + 1, FINE.stop - 1):
        value = sum(ro_ref[d * 32 : d * 32 + 32, row(y - 1 + d - FINE.start)] for d in range(3))
        for z in range(2):
            put_field(out_ref, y, z, value[z * 16 : z * 16 + 16])
    for at in range(INNER.start + 1, INNER.stop - 1):
        coarse = sum(rq_ref[d * 16 : d * 16 + 16, row(at - 1 + d - INNER.start)] for d in range(3))
        coarse = coarse.astype(BF).astype(F32) * 0.125
        for y in (2 * at, 2 * at + 1):
            for z in range(2):
                lo = z * 16
                value = sum(rg_ref[lo + d * 32 : lo + d * 32 + 16, row(y - 1 + d)] for d in range(3))
                put_field(gf_ref, y, z, value + coarse)


def inner_rows(own, wo, wq, count):
    rows, coarse_rows = len(FINE), len(INNER)
    return pl.pallas_call(
        functools.partial(inner_kernel, count),
        out_shape=(
            shaped(CELLS, 1, F32), shaped(CELLS, 1, F32),
            shaped(96, rows, F32), shaped(48, coarse_rows, F32),
            shaped(288, 2, F32), shaped(144, 1, F32),
        ),
        scratch_shapes=[
            scratch(192, rows, BF), scratch(96, coarse_rows, BF),
            scratch(288, rows, BF), scratch(256, rows, BF),
            scratch(144, coarse_rows, BF), scratch(128, coarse_rows, BF),
        ],
        compiler_params=params(),
        cost_estimate=pl.CostEstimate(flops=10**9, bytes_accessed=4 * 10**6, transcendentals=10**5),
        name="inner_rows",
    )(*own, wo, wq)


def rest_kernel(
    counts, sides,
    odd_ref, even_ref, corners_ref,
    pst_own, jf_own, gst_own, pre_own, prb_own, rg_own, rgb_own,
    out_inner, gf_inner, ro_inner, rq_inner, rf_inner, rc_inner,
    wo_ref, wg_ref, wc_ref, wq_ref,
    out_ref, gf_ref, gw_ref,
    halo_ref, jst_ref, gst_ref, gsb_ref, pst_ref, psb_ref, qst_ref,
    pre_ref, prb_ref, rg_ref, rgb_ref, ro_ref, rq_ref, gl_ref, jl_ref, pl_ref, ql_ref, flat_ref,
):
    w = lax.axis_index("wide")
    there = column_masks(counts[1])
    flag = lambda is_there: jnp.where(is_there, 1.0, 0.0)
    has_above, has_below = flag(w > 0), flag(w < counts[0] - 1)

    odd = w % 2
    halo_ref[1 - odd] = even_ref[:, row(0, SLOTS)]
    halo_ref[odd] = odd_ref[:, row(0, SLOTS)]
    columns = [corners_ref[:, row(side)].astype(F32) for side in range(sides)]

    for i in range(2):
        lane = HALO * (ROWS - HALO) if i == 0 else 0
        for j in range(3):
            main = halo_ref[i, :, row(2 + j)].astype(F32)
            side = beside(columns, 64 + lane + HALO * (j + 1 - i))
            put_cotangent(main, side, gst_ref, gsb_ref, 9 * i + j, 3 * i + j)
        gst_ref[:, row(3 + 3 * i, 3)] = gst_own[:, row(13 * i, 3)]
        rg_ref[:, row(3 * i, 3)] = dot(wg_ref[...], gst_ref[:, row(9 * i, 3)])
    rgb_ref[...] = dot(wg_ref[96:192, :], gsb_ref[...])
    for i in range(2):
        lane = HALO * (ROWS - HALO) if i == 0 else 0
        sides_f = [beside(columns, lane + HALO * r) for r in range(HALO)]
        near = HALO - 1 if i == 0 else 0
        for j in range(2):
            main = halo_ref[i, j * 16 : j * 16 + 16, row(1)]
            side = pooled(sides_f[2 * j], sides_f[2 * j + 1])
            put_pooled(main, side, pst_ref, psb_ref, 6 * i + j, 2 * i + j)
        pst_ref[:, row(2 + 2 * i, 2)] = pst_own[:, row(6 * i, 2)]
        pre_ref[:, row(2 * i, 2)] = dot(wc_ref[...], pst_ref[:, row(6 * i, 2)])
        put_features(halo_ref[i, :, row(0)].astype(F32), sides_f[near], jst_ref, 64, 5 * i)
        for d in range(3):
            jst_ref[d * 64 : d * 64 + 32, row(1 + 2 * i, 2)] = jf_own[d * 32 : d * 32 + 32, row(14 * i, 2)]
    prb_ref[...] = dot(wc_ref[...], psb_ref[...])

    def part(own, halo, lo, size, at, edge, length):
        if at < edge:
            return halo[lo : lo + size, row(at)]
        if at < edge + length:
            return own[lo : lo + size, row(at - edge)]
        return halo[lo : lo + size, row(at - length)]

    for k, at in enumerate((0, 1, 8, 9)):
        keep = has_above if at == 0 else has_below if at == 9 else 1.0
        values = [
            sum(part(own, halo, d * 32, 32, at + d, 2, 8) for d in range(3))
            for own, halo in ((pre_own, pre_ref), (prb_own, prb_ref))
        ]
        totals = [
            sum(
                part(own, halo, lo + d * 32, 32, r + d, 3, ROWS)
                for r in (2 * at, 2 * at + 1)
                for d in range(3)
            )
            for own, halo, lo in ((rg_own, rg_ref, 96), (rgb_own, rgb_ref, 0))
        ]
        acts, grads = coarse_row(values, totals, (keep, keep * there))
        for d in range(3):
            for r in ((0,), (1, 2), (3, 4), (5,))[k]:
                jst_ref[d * 64 + 32 : d * 64 + 64, row(r)] = acts[d]
            qst_ref[d * 32 : d * 32 + 32, row(k)] = grads[d]

    put_joined(jst_ref, row(1, 4), jl_ref, row(0, 4))
    ql_ref[0:96, :] = jnp.zeros((96, 2 * COLS), BF)
    ql_ref[96:128, :] = qst_ref[32:64, row(1, 2)]
    for i in range(2):
        for ky in range(3):
            gl_ref[ky * 96 : ky * 96 + 96, row(2 * i, 2)] = gst_ref[:, row(4 + 4 * i - ky, 2)]
            pl_ref[ky * 48 : ky * 48 + 48, row(i)] = pst_ref[:, row(1 + 3 * i + ky)]
    rf = rf_inner[...] + dot_nt(gl_ref[...], jl_ref[...])
    rc = rc_inner[...] + dot_nt(pl_ref[...], ql_ref[...])
    ro_ref[...] = dot(wo_ref[...], jst_ref[...])
    rq_ref[...] = dot(wq_ref[...], qst_ref[...])
    fine, coarse = {}, {}
    for ky in range(3):
        for kx in range(3):
            lo = ky * 96 + (2 - kx) * 32
            fine[ky, 0, kx] = rf[lo + 16 : lo + 32, 0:128]
            fine[ky, 1, kx] = rf[lo : lo + 16, 0:128] + rf[lo + 16 : lo + 32, 128:256]
            fine[ky, 2, kx] = rf[lo : lo + 16, 128:256]
            coarse[ky, kx] = rc[ky * 48 + kx * 16 : ky * 48 + kx * 16 + 16] * 0.5
    lane16 = lanes_of((16, COLS))
    order = [(ky, kz, kx) for ky in range(3) for kz in range(3) for kx in range(3)]
    for i in range(16):
        value = jnp.zeros((16, COLS), F32)
        if i < 14:
            value = jnp.where(lane16 < 48, fine[order[i]], value)
        if i < 13:
            value = jnp.where((lane16 >= 48) & (lane16 < 96), fine[order[14 + i]], value)
        if i < 9:
            value = jnp.where(lane16 >= 96, coarse[i // 3, i % 3], value)
        gw_ref[i * 16 : i * 16 + 16, :] = value.astype(BF)

    flat_ref[0] = out_inner[...]
    flat_ref[1] = gf_inner[...]
    for y in (0, 1, 2, 13, 14, 15):
        value = sum(part(ro_inner, ro_ref, d * 32, 32, y + d, 3, len(FINE)) for d in range(3))
        for z in range(2):
            put_field(flat_ref.at[0], y, z, value[z * 16 : z * 16 + 16])
    out_ref[...] = flat_ref[0].astype(BF)

    for at in (0, 1, 6, 7):
        coarse = sum(part(rq_inner, rq_ref, d * 16, 16, at + d, 2, len(INNER)) for d in range(3))
        coarse = coarse.astype(BF).astype(F32) * 0.125
        for y in (2 * at, 2 * at + 1):
            for z in range(2):
                lo = z * 16
                value = sum(part(rg_own, rg_ref, lo + d * 32, 16, y + 2 + d, 3, ROWS) for d in range(3))
                put_field(flat_ref.at[1], y, z, value + coarse)
    gf_ref[...] = flat_ref[1].astype(BF)


def rest(messages, own, inner, matrices, counts, sides):
    return pl.pallas_call(
        functools.partial(rest_kernel, counts, sides),
        out_shape=(
            pltpu.VMEM((CELLS, COLS), BF),
            pltpu.VMEM((CELLS, COLS), BF),
            jax.ShapeDtypeStruct((256, COLS), BF),
        ),
        scratch_shapes=[
            pltpu.VMEM((2, 32, SLOTS * COLS), BF),
            scratch(192, 6, BF),
            scratch(96, 12, BF), scratch(96, 6, BF),
            scratch(48, 8, BF), scratch(48, 4, BF),
            scratch(96, 4, BF),
            scratch(96, 4, F32), scratch(96, 4, F32),
            scratch(192, 6, F32), scratch(96, 6, F32),
            scratch(96, 6, F32),
            scratch(48, 4, F32),
            scratch(288, 4, BF), scratch(256, 4, BF), scratch(144, 2, BF), scratch(128, 2, BF),
            pltpu.VMEM((2, CELLS, COLS), F32),
        ],
        compiler_params=params(),
        cost_estimate=pl.CostEstimate(flops=10**9, bytes_accessed=4 * 10**6, transcendentals=10**5),
        name="rest",
    )(*messages, *own, *inner, *matrices)


def add_kernel(parts_ref, total_ref):
    total = parts_ref[0].astype(F32)
    for i in range(1, parts_ref.shape[0]):
        total = total + parts_ref[i].astype(F32)
    total_ref[...] = total.astype(BF)


def add_up(parts):
    return pl.pallas_call(
        add_kernel,
        out_shape=jax.ShapeDtypeStruct(parts.shape[1:], BF),
        compiler_params=pltpu.CompilerParams(vmem_limit_bytes=VMEM_LIMIT),
        name="add_up",
    )(parts)


def spread_kernel(
    fine_scale, coarse_scale,
    sum_ref, out_ref, gf_ref,
    out_hbm, gf_hbm, fine_hbm, coarse_hbm,
    fine_ref, coarse_ref, field_sems, weight_sems,
):
    fields = chunks(((out_ref, out_hbm), (gf_ref, gf_hbm)), field_sems, 4)
    weights = chunks(((fine_ref, fine_hbm), (coarse_ref, coarse_hbm)), weight_sems, 3)
    for copies in fields:
        start(copies)
    for i in range(27):
        at = (i if i < 14 else i - 14) * 16
        value = sum_ref[at : at + 16, :].astype(F32)
        if i >= 14:
            value = pltpu.roll(value, 80, 1)
        fine_ref[i * 16 : i * 16 + 16, :] = value[:, 0:48] * fine_scale
        ky, kz, kx = i // 9, i // 3 % 3, i % 3
        if kz == 1:
            at = (ky * 3 + kx) * 16
            value = pltpu.roll(sum_ref[at : at + 16, :].astype(F32), 32, 1)[:, 0:32] * coarse_scale
        else:
            value = jnp.zeros((16, 32), F32)
        coarse_ref[i * 16 : i * 16 + 16, :] = value
        if i % 9 == 8:
            weights[0][ky].start()
            weights[1][ky].start()
    for copies in fields + weights:
        wait(copies)


def spread(total, output, grad_features, fine_scale, coarse_scale):
    return pl.pallas_call(
        functools.partial(spread_kernel, fine_scale, coarse_scale),
        in_specs=[pl.BlockSpec(memory_space=pltpu.VMEM)] * 3,
        out_specs=(pl.BlockSpec(memory_space=pl.ANY),) * 4,
        out_shape=(
            jax.ShapeDtypeStruct((CELLS, COLS), BF),
            jax.ShapeDtypeStruct((CELLS, COLS), BF),
            jax.ShapeDtypeStruct((TAPS, 48), F32),
            jax.ShapeDtypeStruct((TAPS, 32), F32),
        ),
        scratch_shapes=[
            pltpu.VMEM((TAPS, 48), F32),
            pltpu.VMEM((TAPS, 32), F32),
            pltpu.SemaphoreType.DMA((2, 4)),
            pltpu.SemaphoreType.DMA((2, 3)),
        ],
        compiler_params=params(),
        name="spread",
    )(total, output, grad_features)


def matrices_kernel(
    fine_hbm, coarse_hbm, wo_ref, wg_ref, wc_ref, wq_ref,
    fine_ref, coarse_ref, wide_ref, pieces_ref, blocks_ref, sems,
):
    fine_copies, coarse_copies = chunks(((fine_hbm, fine_ref), (coarse_hbm, coarse_ref)), sems, 3)
    start(fine_copies)
    start(coarse_copies)
    lane = lanes_of((C1, COLS))
    wait(fine_copies)
    wide_ref[:, 0:48] = fine_ref[...].astype(F32)
    for ky in range(3):
        for zo in range(2):
            tiles = [jnp.zeros((C1, COLS), F32) for _ in range(2)]
            for kx in range(3):
                at = ((ky * 3 + 1 - zo) * 3 + kx) * 16
                first, second = (wide_ref[at + i : at + i + 16, :] for i in (0, 48))
                both = (first + second).astype(BF).astype(F32)
                piece = jnp.where(lane < 32, pltpu.roll(second, 16, 1), pltpu.roll(both, 16, 1))
                piece = jnp.where(lane < 16, first, jnp.where(lane < 64, piece, 0.0))
                spot = (2 - kx) * 32 + zo * 16
                pieces_ref[2 - ky, spot : spot + 16, :] = piece
                tiles[kx // 2] = tiles[kx // 2] + (pltpu.roll(piece, 64, 1) if kx == 1 else piece)
            spot = ky * 32 + zo * 16
            wo_ref[spot : spot + 16, 0:128] = tiles[0].astype(BF)
            wo_ref[spot : spot + 16, 128:192] = tiles[1][:, 0:64].astype(BF)
    wait(coarse_copies)
    wide_ref[:, 0:32] = coarse_ref[...].astype(F32)
    for ky in range(3):
        total = jnp.zeros((C1, COLS), F32)
        for kx in range(3):
            at = ((ky * 3 + 1) * 3 + kx) * 16
            value = jnp.where(lane < 32, wide_ref[at : at + 16, :], 0.0)
            blocks_ref[ky, kx * 16 : kx * 16 + 16, :] = value
            spot = (2 - kx) * 32
            total = total + (pltpu.roll(value, spot, 1) if spot else value)
        wq_ref[(2 - ky) * 16 : (2 - ky) * 16 + 16, :] = total[:, 0:96].astype(BF)
    for d in range(3):
        turned = jnp.transpose(pieces_ref[d])[0:64, 0:96].astype(BF)
        wg_ref[d * 32 : d * 32 + 32, :] = turned[0:32]
        wg_ref[96 + d * 32 : 96 + d * 32 + 32, :] = turned[32:64]
        wc_ref[d * 32 : d * 32 + 32, :] = jnp.transpose(blocks_ref[d])[0:32, 0:48].astype(BF)


def weight_matrices(coarse_weight, fine_weight):
    fine = jnp.transpose(fine_weight, (2, 3, 4, 0, 1)).reshape(TAPS, 48)
    coarse = jnp.transpose(coarse_weight, (2, 3, 4, 1, 0)).reshape(TAPS, 32)
    shape = lambda *dims: jax.ShapeDtypeStruct(dims, BF)
    return pl.pallas_call(
        matrices_kernel,
        in_specs=[pl.BlockSpec(memory_space=pltpu.HBM)] * 2,
        out_shape=(shape(96, 192), shape(192, 96), shape(96, 48), shape(48, 96)),
        scratch_shapes=[
            pltpu.VMEM((TAPS, 48), BF),
            pltpu.VMEM((TAPS, 32), BF),
            pltpu.VMEM((TAPS, COLS), F32),
            pltpu.VMEM((3, COLS, COLS), F32),
            pltpu.VMEM((3, COLS, COLS), F32),
            pltpu.SemaphoreType.DMA((2, 3)),
        ],
        compiler_params=params(),
        cost_estimate=pl.CostEstimate(flops=10**6, bytes_accessed=10**6, transcendentals=0),
        name="matrices",
    )(kept_in_hbm(fine), kept_in_hbm(coarse))


def beside_blocks(outer, narrow):
    if outer.shape[1] == COLS:
        return lax.ppermute(outer, "narrow", [(0, 1), (1, 0)])
    right = lax.ppermute(outer[:, :COLS], "narrow", [(i + 1, i) for i in range(narrow - 1)])
    left = lax.ppermute(outer[:, COLS:], "narrow", [(i, i + 1) for i in range(narrow - 1)])
    return jnp.concatenate([right, left], 1)


def shards(features, cotangent, coarse_weight, fine_weight):
    wide, narrow = lax.axis_size("wide"), lax.axis_size("narrow")
    sides = 1 if narrow == 2 else 2
    own, strip, to_odd, to_even = pack(features, cotangent, sides)
    swaps = lambda start: [
        pair for i in range(start, wide - 1, 2) for pair in ((i, i + 1), (i + 1, i))
    ]
    odd = lax.ppermute(to_odd, "wide", swaps(1))
    even = lax.ppermute(to_even, "wide", swaps(0))
    columns = beside_blocks(strip, narrow)
    wo, wg, wc, wq = weight_matrices(coarse_weight, fine_weight)
    corners = odd[:, SLOTS * COLS :] + even[:, SLOTS * COLS :]
    columns, _ = lax.optimization_barrier((columns, corners))
    stacks = own_rows(own, columns, wc, wg, sides)
    inner = inner_rows(stacks, wo, wq, narrow)
    corners = beside_blocks(corners, narrow)
    output, grad_features, grads = rest(
        (odd, even, corners), stacks, inner, (wo, wg, wc, wq), (wide, narrow), sides
    )
    devices = wide * narrow
    share = -(-256 // devices)
    grads = jnp.pad(grads, ((0, share * devices - 256), (0, 0))).reshape(devices, share, COLS)
    both = ("wide", "narrow")
    parts = lax.all_to_all(grads, both, 0, 0, tiled=True)
    total = lax.all_gather(add_up(parts), both, axis=0, tiled=True)
    total = total.reshape(share * devices, COLS)[:256]
    all_cells = features.shape[1] * features.shape[2] * features.shape[3] * devices
    output, grad_features, grad_fine, grad_coarse = spread(
        total, output, grad_features, 1.0 / math.sqrt(all_cells), 1.0 / math.sqrt(all_cells // 8)
    )
    grad_fine = jnp.transpose(grad_fine.reshape(3, 3, 3, C1, C1 + C2), (3, 4, 0, 1, 2))
    grad_coarse = jnp.transpose(grad_coarse.reshape(3, 3, 3, C1, C2), (4, 3, 0, 1, 2))
    return (
        output.reshape(features.shape),
        grad_features.reshape(features.shape),
        grad_fine,
        grad_coarse,
    )


def solution(mesh):
    placed = P(None, "wide", None, "narrow")
    return jax.shard_map(
        shards,
        mesh=mesh,
        in_specs=(placed, placed, P(), P()),
        out_specs=(placed, placed, P(), P()),
        check_vma=False,
    )
```

```python
import functools
import math

import jax
import jax.numpy as jnp
from jax import lax
from jax.experimental import pallas as pl
from jax.experimental.pallas import tpu as pltpu
from jax.sharding import PartitionSpec as P

C1, C2 = 16, 32
ROWS, COLS = 16, 128
HALO = 4
BF, F32 = jnp.bfloat16, jnp.float32
VMEM_LIMIT = 20 * 1024 * 1024


def lanes_of(shape):
    return lax.broadcasted_iota(jnp.int32, shape, len(shape) - 1)


def row(index, count=1):
    return slice(index * COLS, (index + count) * COLS)


def pair_sum(value):
    lane = lanes_of(value.shape)
    other = jnp.where(lane % 2 == 0, pltpu.roll(value, COLS - 1, 1), pltpu.roll(value, 1, 1))
    return value + other


def pooled(first, second):
    total = first + second
    return (pair_sum(total[0:16] + total[16:32]) * 0.125).astype(BF)


def dot(a, b):
    return jnp.dot(a, b, preferred_element_type=F32)


def dot_nt(a, b):
    return lax.dot_general(a, b, (((1,), (1,)), ((), ())), preferred_element_type=F32)


def params():
    return pltpu.CompilerParams(vmem_limit_bytes=VMEM_LIMIT)


SLOTS = 5
CELLS = C1 * ROWS * 2
TAPS = 27 * C1


def chunks(pairs, sems, pieces):
    copies = []
    for i, (source, target) in enumerate(pairs):
        rows = source.shape[0] // pieces
        copies.append([
            pltpu.make_async_copy(
                source.at[pl.ds(j * rows, rows)], target.at[pl.ds(j * rows, rows)], sems.at[i, j]
            )
            for j in range(pieces)
        ])
    return copies


def start(copies):
    for copy in copies:
        copy.start()


def wait(copies):
    for copy in copies:
        copy.wait()


def pack_kernel(
    sides, f_hbm, g_hbm, s_ref, strip_ref, odd_ref, even_ref, f_ref, g_ref, wide_ref, base_ref, sems
):
    arrivals = chunks(((f_hbm, f_ref), (g_hbm, g_ref)), sems, 4)
    for copies in arrivals:
        start(copies)
    lane = lanes_of((C1, COLS))
    place = lax.axis_index("narrow")
    odd = lax.axis_index("wide") % 2
    strips = [[jnp.zeros((C1, COLS), F32) for _ in range(sides)] for _ in range(2)]
    for a in range(2):
        wait(arrivals[a])
        wide_ref[...] = (f_ref, g_ref)[a][...].astype(F32)
        for z in range(2):
            chans = slice(a * 32 + z * 16, a * 32 + z * 16 + 16)
            for y in range(ROWS):
                value = wide_ref[pl.ds(2 * y + z, C1, stride=2 * ROWS), :]
                s_ref[chans, row(y)] = value.astype(BF)
                first = 64 * a + HALO * y
                inside = (lane >= first) & (lane < first + HALO)
                for side in range(sides):
                    if sides == 2:
                        shift = (first + HALO * side) % COLS
                    else:
                        shift = lax.rem(first + HALO * (1 - place), COLS)
                    strips[z][side] = jnp.where(inside, pltpu.roll(value, shift, 1), strips[z][side])
    for z in range(2):
        for side in range(sides):
            strip_ref[z * 16 : z * 16 + 16, row(side)] = strips[z][side].astype(BF)
    for to, near, pairs, cot in ((0, ROWS - 1, (6, 7), ROWS - 3), (1, 0, (0, 1), 0)):
        base_ref[to, :, row(0)] = s_ref[0:32, row(near)]
        for i, pair in enumerate(pairs):
            first, second = (s_ref[0:32, row(2 * pair + j)].astype(F32) for j in range(2))
            base_ref[to, i * 16 : i * 16 + 16, row(1)] = pooled(first, second)
        base_ref[to, :, row(2, 3)] = s_ref[32:64, row(cot, 3)]
    even_ref[:, row(0, SLOTS)] = base_ref[odd]
    odd_ref[:, row(0, SLOTS)] = base_ref[1 - odd]
    even_ref[:, row(SLOTS, sides)] = jnp.zeros((32, sides * COLS), BF)
    odd_ref[:, row(SLOTS, sides)] = jnp.zeros((32, sides * COLS), BF)


def kept_in_hbm(array):
    return pltpu.with_memory_space_constraint(array, pltpu.HBM)


def pack(features, cotangent, sides):
    flat = lambda a: kept_in_hbm(a.reshape(CELLS, COLS))
    message = jax.ShapeDtypeStruct((32, (SLOTS + sides) * COLS), BF)
    return pl.pallas_call(
        functools.partial(pack_kernel, sides),
        in_specs=[pl.BlockSpec(memory_space=pltpu.HBM)] * 2,
        out_shape=(
            jax.ShapeDtypeStruct((64, ROWS * COLS), BF),
            jax.ShapeDtypeStruct((32, sides * COLS), BF),
            message,
            message,
        ),
        scratch_shapes=[
            pltpu.VMEM((CELLS, COLS), BF),
            pltpu.VMEM((CELLS, COLS), BF),
            pltpu.VMEM((CELLS, COLS), F32),
            pltpu.VMEM((2, 32, SLOTS * COLS), BF),
            pltpu.SemaphoreType.DMA((2, 4)),
        ],
        compiler_params=params(),
        cost_estimate=pl.CostEstimate(flops=10**6, bytes_accessed=10**6, transcendentals=0),
        name="pack",
    )(flat(features), flat(cotangent))


def beside(columns, at):
    lane = lanes_of(columns[0].shape)
    if len(columns) == 1:
        place = lax.axis_index("narrow")
        first = (COLS - HALO) * place
        turned = pltpu.roll(columns[0], lax.rem(COLS - at + first, COLS), 1)
        return jnp.where((lane >= first) & (lane < first + HALO), turned, 0.0)
    right = pltpu.roll(columns[0], (-at) % COLS, 1)
    left = pltpu.roll(columns[1], (COLS - HALO - at) % COLS, 1)
    return jnp.where(lane < HALO, right, jnp.where(lane >= COLS - HALO, left, 0.0))


def turn(main, side, by):
    lane = lanes_of(main.shape)
    a, b = pltpu.roll(main, (-by) % COLS, 1), pltpu.roll(side, (-by) % COLS, 1)
    crossed = lane >= COLS - by if by > 0 else lane < -by
    return jnp.where(crossed, b, a), jnp.where(crossed, a, b)


def put_pooled(main, side, main_ref, side_ref, at, side_at):
    main, side = main.astype(F32), side.astype(F32)
    for d in range(3):
        a, b = (main, side) if d == 1 else turn(main, side, 2 * (d - 1))
        main_ref[d * 16 : d * 16 + 16, row(at)] = a.astype(BF)
        side_ref[d * 16 : d * 16 + 16, row(side_at)] = b.astype(BF)


def put_cotangent(main, side, main_ref, side_ref, at, side_at):
    for d in range(3):
        a, b = (main, side) if d == 1 else turn(main, side, d - 1)
        main_ref[d * 32 : d * 32 + 32, row(at)] = a.astype(BF)
        side_ref[d * 32 : d * 32 + 32, row(side_at)] = b.astype(BF)


def put_features(main, side, ref, step, at):
    for d in range(3):
        a = main if d == 1 else turn(main, side, d - 1)[0]
        ref[d * step : d * step + 32, row(at)] = a.astype(BF)


def coarse_row(values, totals, keeps):
    act, grad = [], []
    for value, total, kept in zip(values, totals, keeps):
        sig = 1.0 / (1.0 + jnp.exp(-value))
        act.append((value * sig * kept).astype(BF).astype(F32))
        grad_act = pair_sum(total).astype(BF).astype(F32)
        grad_pre = grad_act * (sig * (1.0 + value * (1.0 - sig)))
        grad.append((grad_pre * kept).astype(BF).astype(F32))
    acts = [act[0] if d == 1 else turn(act[0], act[1], d - 1)[0] for d in range(3)]
    grads = [grad[0] if d == 1 else turn(grad[0], grad[1], 2 * (d - 1))[0] for d in range(3)]
    return [a.astype(BF) for a in acts], [g.astype(BF) for g in grads]


def column_masks(count):
    n = lax.axis_index("narrow")
    flag = lambda is_there: jnp.where(is_there, 1.0, 0.0)
    return jnp.where(lanes_of((C2, COLS)) < 64, flag(n < count - 1), flag(n > 0))


INNER = range(1, ROWS // 2 - 1)


def own_kernel(
    sides,
    s_ref, columns_ref, wc_ref, wg_ref,
    pst_ref, jf_ref, gst_ref, pre_ref, prb_ref, rg_ref, rgb_ref,
    psb_ref, gsb_ref,
):
    columns = [columns_ref[:, row(side)].astype(F32) for side in range(sides)]
    last = None
    for y in range(ROWS):
        main, side = s_ref[0:32, row(y)].astype(F32), beside(columns, HALO * y)
        put_features(main, side, jf_ref, 32, y)
        if y % 2 == 1:
            means = [pooled(a, b) for a, b in zip(last, (main, side))]
            put_pooled(*means, pst_ref, psb_ref, y // 2, y // 2)
        last = (main, side)
        main, side = s_ref[32:64, row(y)].astype(F32), beside(columns, 64 + HALO * y)
        put_cotangent(main, side, gst_ref, gsb_ref, y, y)
    pre_ref[...] = dot(wc_ref[...], pst_ref[...])
    prb_ref[...] = dot(wc_ref[...], psb_ref[...])
    rg_ref[...] = dot(wg_ref[...], gst_ref[...])
    rgb_ref[...] = dot(wg_ref[96:192, :], gsb_ref[...])


def shaped(rows_, lanes_, kind):
    return jax.ShapeDtypeStruct((rows_, lanes_ * COLS), kind)


def scratch(rows_, lanes_, kind):
    return pltpu.VMEM((rows_, lanes_ * COLS), kind)


def own_rows(s, columns, wc, wg, sides):
    half = ROWS // 2
    return pl.pallas_call(
        functools.partial(own_kernel, sides),
        out_shape=(
            shaped(48, half, BF), shaped(96, ROWS, BF), shaped(96, ROWS, BF),
            shaped(96, half, F32), shaped(96, half, F32),
            shaped(192, ROWS, F32), shaped(96, ROWS, F32),
        ),
        scratch_shapes=[scratch(48, half, BF), scratch(96, ROWS, BF)],
        compiler_params=params(),
        cost_estimate=pl.CostEstimate(flops=10**9, bytes_accessed=4 * 10**6, transcendentals=0),
        name="own_rows",
    )(s, columns, wc, wg)


def put_joined(jst_ref, at, jl_ref, to):
    for lo in (0, 48):
        jl_ref[lo : lo + 16, to] = jst_ref[64:80, at]
        jl_ref[lo + 16 : lo + 48, to] = jst_ref[96:128, at]
        jl_ref[128 + lo : 128 + lo + 48, to] = jst_ref[80:128, at]
    for lo in (96, 224):
        jl_ref[lo : lo + 32, to] = jnp.zeros((32, to.stop - to.start), BF)


def put_field(flat_ref, y, plane, value):
    flat_ref[pl.ds(2 * y + plane, C1, stride=2 * ROWS), :] = value


FINE = range(2 * INNER.start, 2 * INNER.stop)


def inner_kernel(
    count,
    pst_ref, jf_ref, gst_ref, pre_ref, prb_ref, rg_ref, rgb_ref, wo_ref, wq_ref,
    out_ref, gf_ref, ro_ref, rq_ref, rf_ref, rc_ref,
    jst_ref, qst_ref, gl_ref, jl_ref, pl_ref, ql_ref,
):
    rows, coarse_rows = len(FINE), len(INNER)
    there = column_masks(count)
    for d in range(3):
        jst_ref[d * 64 : d * 64 + 32, :] = jf_ref[d * 32 : d * 32 + 32, row(FINE.start, rows)]
    for at in INNER:
        values = [
            sum(ref[d * 32 : d * 32 + 32, row(at + d - 1)] for d in range(3)) for ref in (pre_ref, prb_ref)
        ]
        totals = [
            sum(
                ref[lo + d * 32 : lo + d * 32 + 32, row(r + d - 1)]
                for r in (2 * at, 2 * at + 1)
                for d in range(3)
            )
            for ref, lo in ((rg_ref, 96), (rgb_ref, 0))
        ]
        acts, grads = coarse_row(values, totals, (1.0, there))
        for d in range(3):
            for r in (2 * at, 2 * at + 1):
                jst_ref[d * 64 + 32 : d * 64 + 64, row(r - FINE.start)] = acts[d]
            qst_ref[d * 32 : d * 32 + 32, row(at - INNER.start)] = grads[d]
    ro_ref[...] = dot(wo_ref[...], jst_ref[...])
    rq_ref[...] = dot(wq_ref[...], qst_ref[...])

    put_joined(jst_ref, row(0, rows), jl_ref, row(0, rows))
    ql_ref[0:96, :] = jnp.zeros((96, coarse_rows * COLS), BF)
    ql_ref[96:128, :] = qst_ref[32:64, :]
    for ky in range(3):
        gl_ref[ky * 96 : ky * 96 + 96, :] = gst_ref[:, row(FINE.start + 1 - ky, rows)]
        pl_ref[ky * 48 : ky * 48 + 48, :] = pst_ref[:, row(INNER.start + ky - 1, coarse_rows)]
    rf_ref[...] = dot_nt(gl_ref[...], jl_ref[...])
    rc_ref[...] = dot_nt(pl_ref[...], ql_ref[...])

    for y in range(FINE.start + 1, FINE.stop - 1):
        value = sum(ro_ref[d * 32 : d * 32 + 32, row(y - 1 + d - FINE.start)] for d in range(3))
        for z in range(2):
            put_field(out_ref, y, z, value[z * 16 : z * 16 + 16])
    for at in range(INNER.start + 1, INNER.stop - 1):
        coarse = sum(rq_ref[d * 16 : d * 16 + 16, row(at - 1 + d - INNER.start)] for d in range(3))
        coarse = coarse.astype(BF).astype(F32) * 0.125
        for y in (2 * at, 2 * at + 1):
            for z in range(2):
                lo = z * 16
                value = sum(rg_ref[lo + d * 32 : lo + d * 32 + 16, row(y - 1 + d)] for d in range(3))
                put_field(gf_ref, y, z, value + coarse)


def inner_rows(own, wo, wq, count):
    rows, coarse_rows = len(FINE), len(INNER)
    return pl.pallas_call(
        functools.partial(inner_kernel, count),
        out_shape=(
            shaped(CELLS, 1, F32), shaped(CELLS, 1, F32),
            shaped(96, rows, F32), shaped(48, coarse_rows, F32),
            shaped(288, 2, F32), shaped(144, 1, F32),
        ),
        scratch_shapes=[
            scratch(192, rows, BF), scratch(96, coarse_rows, BF),
            scratch(288, rows, BF), scratch(256, rows, BF),
            scratch(144, coarse_rows, BF), scratch(128, coarse_rows, BF),
        ],
        compiler_params=params(),
        cost_estimate=pl.CostEstimate(flops=10**9, bytes_accessed=4 * 10**6, transcendentals=10**5),
        name="inner_rows",
    )(*own, wo, wq)


def rest_kernel(
    counts, sides,
    even_ref, odd_ref,
    pst_own, jf_own, gst_own, pre_own, prb_own, rg_own, rgb_own,
    out_inner, gf_inner, ro_inner, rq_inner, rf_inner, rc_inner,
    wo_ref, wg_ref, wc_ref, wq_ref,
    out_ref, gf_ref, gw_ref,
    halo_ref, jst_ref, gst_ref, gsb_ref, pst_ref, psb_ref, qst_ref,
    pre_ref, prb_ref, rg_ref, rgb_ref, ro_ref, rq_ref, gl_ref, jl_ref, pl_ref, ql_ref, flat_ref,
):
    w = lax.axis_index("wide")
    there = column_masks(counts[1])
    flag = lambda is_there: jnp.where(is_there, 1.0, 0.0)
    has_above, has_below = flag(w > 0), flag(w < counts[0] - 1)

    odd = w % 2
    halo_ref[1 - odd] = even_ref[...]
    halo_ref[odd] = odd_ref[...]
    columns = [
        [halo_ref[i, :, row(SLOTS + side)].astype(F32) for side in range(sides)] for i in range(2)
    ]

    for i in range(2):
        lane = HALO * (ROWS - HALO) if i == 0 else 0
        for j in range(3):
            main = halo_ref[i, :, row(2 + j)].astype(F32)
            side = beside(columns[i], 64 + lane + HALO * (j + 1 - i))
            put_cotangent(main, side, gst_ref, gsb_ref, 9 * i + j, 3 * i + j)
        gst_ref[:, row(3 + 3 * i, 3)] = gst_own[:, row(13 * i, 3)]
        rg_ref[:, row(3 * i, 3)] = dot(wg_ref[...], gst_ref[:, row(9 * i, 3)])
    rgb_ref[...] = dot(wg_ref[96:192, :], gsb_ref[...])
    for i in range(2):
        lane = HALO * (ROWS - HALO) if i == 0 else 0
        sides_f = [beside(columns[i], lane + HALO * r) for r in range(HALO)]
        near = HALO - 1 if i == 0 else 0
        for j in range(2):
            main = halo_ref[i, j * 16 : j * 16 + 16, row(1)]
            side = pooled(sides_f[2 * j], sides_f[2 * j + 1])
            put_pooled(main, side, pst_ref, psb_ref, 6 * i + j, 2 * i + j)
        pst_ref[:, row(2 + 2 * i, 2)] = pst_own[:, row(6 * i, 2)]
        pre_ref[:, row(2 * i, 2)] = dot(wc_ref[...], pst_ref[:, row(6 * i, 2)])
        put_features(halo_ref[i, :, row(0)].astype(F32), sides_f[near], jst_ref, 64, 5 * i)
        for d in range(3):
            jst_ref[d * 64 : d * 64 + 32, row(1 + 2 * i, 2)] = jf_own[d * 32 : d * 32 + 32, row(14 * i, 2)]
    prb_ref[...] = dot(wc_ref[...], psb_ref[...])

    def part(own, halo, lo, size, at, edge, length):
        if at < edge:
            return halo[lo : lo + size, row(at)]
        if at < edge + length:
            return own[lo : lo + size, row(at - edge)]
        return halo[lo : lo + size, row(at - length)]

    for k, at in enumerate((0, 1, 8, 9)):
        keep = has_above if at == 0 else has_below if at == 9 else 1.0
        values = [
            sum(part(own, halo, d * 32, 32, at + d, 2, 8) for d in range(3))
            for own, halo in ((pre_own, pre_ref), (prb_own, prb_ref))
        ]
        totals = [
            sum(
                part(own, halo, lo + d * 32, 32, r + d, 3, ROWS)
                for r in (2 * at, 2 * at + 1)
                for d in range(3)
            )
            for own, halo, lo in ((rg_own, rg_ref, 96), (rgb_own, rgb_ref, 0))
        ]
        acts, grads = coarse_row(values, totals, (keep, keep * there))
        for d in range(3):
            for r in ((0,), (1, 2), (3, 4), (5,))[k]:
                jst_ref[d * 64 + 32 : d * 64 + 64, row(r)] = acts[d]
            qst_ref[d * 32 : d * 32 + 32, row(k)] = grads[d]

    put_joined(jst_ref, row(1, 4), jl_ref, row(0, 4))
    ql_ref[0:96, :] = jnp.zeros((96, 2 * COLS), BF)
    ql_ref[96:128, :] = qst_ref[32:64, row(1, 2)]
    for i in range(2):
        for ky in range(3):
            gl_ref[ky * 96 : ky * 96 + 96, row(2 * i, 2)] = gst_ref[:, row(4 + 4 * i - ky, 2)]
            pl_ref[ky * 48 : ky * 48 + 48, row(i)] = pst_ref[:, row(1 + 3 * i + ky)]
    rf = rf_inner[...] + dot_nt(gl_ref[...], jl_ref[...])
    rc = rc_inner[...] + dot_nt(pl_ref[...], ql_ref[...])
    ro_ref[...] = dot(wo_ref[...], jst_ref[...])
    rq_ref[...] = dot(wq_ref[...], qst_ref[...])
    fine, coarse = {}, {}
    for ky in range(3):
        for kx in range(3):
            lo = ky * 96 + (2 - kx) * 32
            fine[ky, 0, kx] = rf[lo + 16 : lo + 32, 0:128]
            fine[ky, 1, kx] = rf[lo : lo + 16, 0:128] + rf[lo + 16 : lo + 32, 128:256]
            fine[ky, 2, kx] = rf[lo : lo + 16, 128:256]
            coarse[ky, kx] = rc[ky * 48 + kx * 16 : ky * 48 + kx * 16 + 16] * 0.5
    lane16 = lanes_of((16, COLS))
    order = [(ky, kz, kx) for ky in range(3) for kz in range(3) for kx in range(3)]
    for i in range(16):
        value = jnp.zeros((16, COLS), F32)
        if i < 14:
            value = jnp.where(lane16 < 48, fine[order[i]], value)
        if i < 13:
            value = jnp.where((lane16 >= 48) & (lane16 < 96), fine[order[14 + i]], value)
        if i < 9:
            value = jnp.where(lane16 >= 96, coarse[i // 3, i % 3], value)
        gw_ref[i * 16 : i * 16 + 16, :] = value.astype(BF)

    flat_ref[0] = out_inner[...]
    flat_ref[1] = gf_inner[...]
    for y in (0, 1, 2, 13, 14, 15):
        value = sum(part(ro_inner, ro_ref, d * 32, 32, y + d, 3, len(FINE)) for d in range(3))
        for z in range(2):
            put_field(flat_ref.at[0], y, z, value[z * 16 : z * 16 + 16])
    out_ref[...] = flat_ref[0].astype(BF)

    for at in (0, 1, 6, 7):
        coarse = sum(part(rq_inner, rq_ref, d * 16, 16, at + d, 2, len(INNER)) for d in range(3))
        coarse = coarse.astype(BF).astype(F32) * 0.125
        for y in (2 * at, 2 * at + 1):
            for z in range(2):
                lo = z * 16
                value = sum(part(rg_own, rg_ref, lo + d * 32, 16, y + 2 + d, 3, ROWS) for d in range(3))
                put_field(flat_ref.at[1], y, z, value + coarse)
    gf_ref[...] = flat_ref[1].astype(BF)


def rest(messages, own, inner, matrices, counts, sides):
    return pl.pallas_call(
        functools.partial(rest_kernel, counts, sides),
        out_shape=(
            pltpu.VMEM((CELLS, COLS), BF),
            pltpu.VMEM((CELLS, COLS), BF),
            jax.ShapeDtypeStruct((256, COLS), BF),
        ),
        scratch_shapes=[
            pltpu.VMEM((2, 32, (SLOTS + sides) * COLS), BF),
            scratch(192, 6, BF),
            scratch(96, 12, BF), scratch(96, 6, BF),
            scratch(48, 8, BF), scratch(48, 4, BF),
            scratch(96, 4, BF),
            scratch(96, 4, F32), scratch(96, 4, F32),
            scratch(192, 6, F32), scratch(96, 6, F32),
            scratch(96, 6, F32),
            scratch(48, 4, F32),
            scratch(288, 4, BF), scratch(256, 4, BF), scratch(144, 2, BF), scratch(128, 2, BF),
            pltpu.VMEM((2, CELLS, COLS), F32),
        ],
        compiler_params=params(),
        cost_estimate=pl.CostEstimate(flops=10**9, bytes_accessed=4 * 10**6, transcendentals=10**5),
        name="rest",
    )(*messages, *own, *inner, *matrices)


def add_kernel(parts_ref, copies_ref):
    total = parts_ref[0].astype(F32)
    for i in range(1, parts_ref.shape[0]):
        total = total + parts_ref[i].astype(F32)
    total = total.astype(BF)
    for i in range(parts_ref.shape[0]):
        copies_ref[i] = total


def add_up(parts):
    return pl.pallas_call(
        add_kernel,
        out_shape=jax.ShapeDtypeStruct(parts.shape, BF),
        compiler_params=pltpu.CompilerParams(vmem_limit_bytes=VMEM_LIMIT),
        name="add_up",
    )(parts)


def spread_kernel(
    fine_scale, coarse_scale,
    sum_ref, out_ref, gf_ref,
    out_hbm, gf_hbm, fine_hbm, coarse_hbm,
    fine_ref, coarse_ref, field_sems, weight_sems,
):
    fields = chunks(((out_ref, out_hbm), (gf_ref, gf_hbm)), field_sems, 4)
    weights = chunks(((fine_ref, fine_hbm), (coarse_ref, coarse_hbm)), weight_sems, 3)
    for copies in fields:
        start(copies)
    for i in range(27):
        at = (i if i < 14 else i - 14) * 16
        value = sum_ref[at : at + 16, :].astype(F32)
        if i >= 14:
            value = pltpu.roll(value, 80, 1)
        fine_ref[i * 16 : i * 16 + 16, :] = value[:, 0:48] * fine_scale
        ky, kz, kx = i // 9, i // 3 % 3, i % 3
        if kz == 1:
            at = (ky * 3 + kx) * 16
            value = pltpu.roll(sum_ref[at : at + 16, :].astype(F32), 32, 1)[:, 0:32] * coarse_scale
        else:
            value = jnp.zeros((16, 32), F32)
        coarse_ref[i * 16 : i * 16 + 16, :] = value
        if i % 9 == 8:
            weights[0][ky].start()
            weights[1][ky].start()
    for copies in fields + weights:
        wait(copies)


def spread(total, output, grad_features, fine_scale, coarse_scale):
    return pl.pallas_call(
        functools.partial(spread_kernel, fine_scale, coarse_scale),
        in_specs=[pl.BlockSpec(memory_space=pltpu.VMEM)] * 3,
        out_specs=(pl.BlockSpec(memory_space=pl.ANY),) * 4,
        out_shape=(
            jax.ShapeDtypeStruct((CELLS, COLS), BF),
            jax.ShapeDtypeStruct((CELLS, COLS), BF),
            jax.ShapeDtypeStruct((TAPS, 48), F32),
            jax.ShapeDtypeStruct((TAPS, 32), F32),
        ),
        scratch_shapes=[
            pltpu.VMEM((TAPS, 48), F32),
            pltpu.VMEM((TAPS, 32), F32),
            pltpu.SemaphoreType.DMA((2, 4)),
            pltpu.SemaphoreType.DMA((2, 3)),
        ],
        compiler_params=params(),
        name="spread",
    )(total, output, grad_features)


def matrices_kernel(
    fine_hbm, coarse_hbm, wo_ref, wg_ref, wc_ref, wq_ref,
    fine_ref, coarse_ref, wide_ref, pieces_ref, blocks_ref, sems,
):
    fine_copies, coarse_copies = chunks(((fine_hbm, fine_ref), (coarse_hbm, coarse_ref)), sems, 3)
    start(fine_copies)
    start(coarse_copies)
    lane = lanes_of((C1, COLS))
    wait(fine_copies)
    wide_ref[:, 0:48] = fine_ref[...].astype(F32)
    for ky in range(3):
        for zo in range(2):
            tiles = [jnp.zeros((C1, COLS), F32) for _ in range(2)]
            for kx in range(3):
                at = ((ky * 3 + 1 - zo) * 3 + kx) * 16
                first, second = (wide_ref[at + i : at + i + 16, :] for i in (0, 48))
                both = (first + second).astype(BF).astype(F32)
                piece = jnp.where(lane < 32, pltpu.roll(second, 16, 1), pltpu.roll(both, 16, 1))
                piece = jnp.where(lane < 16, first, jnp.where(lane < 64, piece, 0.0))
                spot = (2 - kx) * 32 + zo * 16
                pieces_ref[2 - ky, spot : spot + 16, :] = piece
                tiles[kx // 2] = tiles[kx // 2] + (pltpu.roll(piece, 64, 1) if kx == 1 else piece)
            spot = ky * 32 + zo * 16
            wo_ref[spot : spot + 16, 0:128] = tiles[0].astype(BF)
            wo_ref[spot : spot + 16, 128:192] = tiles[1][:, 0:64].astype(BF)
    wait(coarse_copies)
    wide_ref[:, 0:32] = coarse_ref[...].astype(F32)
    for ky in range(3):
        total = jnp.zeros((C1, COLS), F32)
        for kx in range(3):
            at = ((ky * 3 + 1) * 3 + kx) * 16
            value = jnp.where(lane < 32, wide_ref[at : at + 16, :], 0.0)
            blocks_ref[ky, kx * 16 : kx * 16 + 16, :] = value
            spot = (2 - kx) * 32
            total = total + (pltpu.roll(value, spot, 1) if spot else value)
        wq_ref[(2 - ky) * 16 : (2 - ky) * 16 + 16, :] = total[:, 0:96].astype(BF)
    for d in range(3):
        turned = jnp.transpose(pieces_ref[d])[0:64, 0:96].astype(BF)
        wg_ref[d * 32 : d * 32 + 32, :] = turned[0:32]
        wg_ref[96 + d * 32 : 96 + d * 32 + 32, :] = turned[32:64]
        wc_ref[d * 32 : d * 32 + 32, :] = jnp.transpose(blocks_ref[d])[0:32, 0:48].astype(BF)


def weight_matrices(coarse_weight, fine_weight):
    fine = jnp.transpose(fine_weight, (2, 3, 4, 0, 1)).reshape(TAPS, 48)
    coarse = jnp.transpose(coarse_weight, (2, 3, 4, 1, 0)).reshape(TAPS, 32)
    shape = lambda *dims: jax.ShapeDtypeStruct(dims, BF)
    return pl.pallas_call(
        matrices_kernel,
        in_specs=[pl.BlockSpec(memory_space=pltpu.HBM)] * 2,
        out_shape=(shape(96, 192), shape(192, 96), shape(96, 48), shape(48, 96)),
        scratch_shapes=[
            pltpu.VMEM((TAPS, 48), BF),
            pltpu.VMEM((TAPS, 32), BF),
            pltpu.VMEM((TAPS, COLS), F32),
            pltpu.VMEM((3, COLS, COLS), F32),
            pltpu.VMEM((3, COLS, COLS), F32),
            pltpu.SemaphoreType.DMA((2, 3)),
        ],
        compiler_params=params(),
        cost_estimate=pl.CostEstimate(flops=10**6, bytes_accessed=10**6, transcendentals=0),
        name="matrices",
    )(kept_in_hbm(fine), kept_in_hbm(coarse))


def beside_blocks(outer, narrow):
    if outer.shape[1] == COLS:
        return lax.ppermute(outer, "narrow", [(0, 1), (1, 0)])
    right = lax.ppermute(outer[:, :COLS], "narrow", [(i + 1, i) for i in range(narrow - 1)])
    left = lax.ppermute(outer[:, COLS:], "narrow", [(i, i + 1) for i in range(narrow - 1)])
    return jnp.concatenate([right, left], 1)


def shards(features, cotangent, coarse_weight, fine_weight):
    wide, narrow = lax.axis_size("wide"), lax.axis_size("narrow")
    sides = 1 if narrow == 2 else 2
    own, strip, to_odd, to_even = pack(features, cotangent, sides)
    swaps = lambda start: [
        pair for i in range(start, wide - 1, 2) for pair in ((i, i + 1), (i + 1, i))
    ]
    columns = beside_blocks(strip, narrow)
    wo, wg, wc, wq = weight_matrices(coarse_weight, fine_weight)
    with_columns = lambda message: lax.dynamic_update_slice(message, columns, (0, SLOTS * COLS))
    odd = lax.ppermute(with_columns(to_odd), "wide", swaps(1))
    even = lax.ppermute(with_columns(to_even), "wide", swaps(0))
    stacks = own_rows(own, columns, wc, wg, sides)
    inner = inner_rows(stacks, wo, wq, narrow)
    output, grad_features, grads = rest(
        (even, odd), stacks, inner, (wo, wg, wc, wq), (wide, narrow), sides
    )
    devices = wide * narrow
    share = -(-256 // devices)
    grads = jnp.pad(grads, ((0, share * devices - 256), (0, 0))).reshape(devices, share, COLS)
    both = ("wide", "narrow")
    parts = lax.all_to_all(grads, both, 0, 0, tiled=True)
    total = lax.all_to_all(add_up(parts), both, 0, 0, tiled=True)
    total = total.reshape(share * devices, COLS)[:256]
    all_cells = features.shape[1] * features.shape[2] * features.shape[3] * devices
    output, grad_features, grad_fine, grad_coarse = spread(
        total, output, grad_features, 1.0 / math.sqrt(all_cells), 1.0 / math.sqrt(all_cells // 8)
    )
    grad_fine = jnp.transpose(grad_fine.reshape(3, 3, 3, C1, C1 + C2), (3, 4, 0, 1, 2))
    grad_coarse = jnp.transpose(grad_coarse.reshape(3, 3, 3, C1, C2), (4, 3, 0, 1, 2))
    return (
        output.reshape(features.shape),
        grad_features.reshape(features.shape),
        grad_fine,
        grad_coarse,
    )


def solution(mesh):
    placed = P(None, "wide", None, "narrow")
    return jax.shard_map(
        shards,
        mesh=mesh,
        in_specs=(placed, placed, P(), P()),
        out_specs=(placed, placed, P(), P()),
        check_vma=False,
    )
```

```python
import functools
import math

import jax
import jax.numpy as jnp
from jax import lax
from jax.experimental import pallas as pl
from jax.experimental.pallas import tpu as pltpu
from jax.sharding import PartitionSpec as P

C1, C2 = 16, 32
ROWS, COLS = 16, 128
HALO = 4
BF, F32 = jnp.bfloat16, jnp.float32
VMEM_LIMIT = 20 * 1024 * 1024


def lanes_of(shape):
    return lax.broadcasted_iota(jnp.int32, shape, len(shape) - 1)


def row(index, count=1):
    return slice(index * COLS, (index + count) * COLS)


def pair_sum(value):
    lane = lanes_of(value.shape)
    other = jnp.where(lane % 2 == 0, pltpu.roll(value, COLS - 1, 1), pltpu.roll(value, 1, 1))
    return value + other


def pooled(first, second):
    total = first + second
    return (pair_sum(total[0:16] + total[16:32]) * 0.125).astype(BF)


def dot(a, b):
    return jnp.dot(a, b, preferred_element_type=F32)


def dot_nt(a, b):
    return lax.dot_general(a, b, (((1,), (1,)), ((), ())), preferred_element_type=F32)


def params():
    return pltpu.CompilerParams(vmem_limit_bytes=VMEM_LIMIT)


SLOTS = 5
CELLS = C1 * ROWS * 2
TAPS = 27 * C1


def chunks(pairs, sems, pieces):
    copies = []
    for i, (source, target) in enumerate(pairs):
        rows = source.shape[0] // pieces
        copies.append([
            pltpu.make_async_copy(
                source.at[pl.ds(j * rows, rows)], target.at[pl.ds(j * rows, rows)], sems.at[i, j]
            )
            for j in range(pieces)
        ])
    return copies


def start(copies):
    for copy in copies:
        copy.start()


def wait(copies):
    for copy in copies:
        copy.wait()


def pack_kernel(
    sides, f_hbm, g_hbm, s_ref, strip_ref, odd_ref, even_ref, f_ref, g_ref, wide_ref, base_ref, sems
):
    arrivals = chunks(((f_hbm, f_ref), (g_hbm, g_ref)), sems, 4)
    for copies in arrivals:
        start(copies)
    lane = lanes_of((C1, COLS))
    place = lax.axis_index("narrow")
    odd = lax.axis_index("wide") % 2
    strips = [[jnp.zeros((C1, COLS), F32) for _ in range(sides)] for _ in range(2)]
    for a in range(2):
        wait(arrivals[a])
        wide_ref[...] = (f_ref, g_ref)[a][...].astype(F32)
        for z in range(2):
            chans = slice(a * 32 + z * 16, a * 32 + z * 16 + 16)
            for y in range(ROWS):
                value = wide_ref[pl.ds(2 * y + z, C1, stride=2 * ROWS), :]
                s_ref[chans, row(y)] = value.astype(BF)
                first = 64 * a + HALO * y
                inside = (lane >= first) & (lane < first + HALO)
                for side in range(sides):
                    if sides == 2:
                        shift = (first + HALO * side) % COLS
                    else:
                        shift = lax.rem(first + HALO * (1 - place), COLS)
                    strips[z][side] = jnp.where(inside, pltpu.roll(value, shift, 1), strips[z][side])
    for z in range(2):
        for side in range(sides):
            strip_ref[z * 16 : z * 16 + 16, row(side)] = strips[z][side].astype(BF)
    for to, near, pairs, cot in ((0, ROWS - 1, (6, 7), ROWS - 3), (1, 0, (0, 1), 0)):
        base_ref[to, :, row(0)] = s_ref[0:32, row(near)]
        for i, pair in enumerate(pairs):
            first, second = (s_ref[0:32, row(2 * pair + j)].astype(F32) for j in range(2))
            base_ref[to, i * 16 : i * 16 + 16, row(1)] = pooled(first, second)
        base_ref[to, :, row(2, 3)] = s_ref[32:64, row(cot, 3)]
    even_ref[:, row(0, SLOTS)] = base_ref[odd]
    odd_ref[:, row(0, SLOTS)] = base_ref[1 - odd]
    even_ref[:, row(SLOTS, sides)] = jnp.zeros((32, sides * COLS), BF)
    odd_ref[:, row(SLOTS, sides)] = jnp.zeros((32, sides * COLS), BF)


def kept_in_hbm(array):
    return pltpu.with_memory_space_constraint(array, pltpu.HBM)


def pack(features, cotangent, sides):
    flat = lambda a: kept_in_hbm(a.reshape(CELLS, COLS))
    message = jax.ShapeDtypeStruct((32, (SLOTS + sides) * COLS), BF)
    return pl.pallas_call(
        functools.partial(pack_kernel, sides),
        in_specs=[pl.BlockSpec(memory_space=pltpu.HBM)] * 2,
        out_shape=(
            jax.ShapeDtypeStruct((64, ROWS * COLS), BF),
            jax.ShapeDtypeStruct((32, sides * COLS), BF),
            message,
            message,
        ),
        scratch_shapes=[
            pltpu.VMEM((CELLS, COLS), BF),
            pltpu.VMEM((CELLS, COLS), BF),
            pltpu.VMEM((CELLS, COLS), F32),
            pltpu.VMEM((2, 32, SLOTS * COLS), BF),
            pltpu.SemaphoreType.DMA((2, 4)),
        ],
        compiler_params=params(),
        cost_estimate=pl.CostEstimate(flops=10**6, bytes_accessed=10**6, transcendentals=0),
        name="pack",
    )(flat(features), flat(cotangent))


def beside(columns, at):
    lane = lanes_of(columns[0].shape)
    if len(columns) == 1:
        place = lax.axis_index("narrow")
        first = (COLS - HALO) * place
        turned = pltpu.roll(columns[0], lax.rem(COLS - at + first, COLS), 1)
        return jnp.where((lane >= first) & (lane < first + HALO), turned, 0.0)
    right = pltpu.roll(columns[0], (-at) % COLS, 1)
    left = pltpu.roll(columns[1], (COLS - HALO - at) % COLS, 1)
    return jnp.where(lane < HALO, right, jnp.where(lane >= COLS - HALO, left, 0.0))


def turn(main, side, by):
    lane = lanes_of(main.shape)
    a, b = pltpu.roll(main, (-by) % COLS, 1), pltpu.roll(side, (-by) % COLS, 1)
    crossed = lane >= COLS - by if by > 0 else lane < -by
    return jnp.where(crossed, b, a), jnp.where(crossed, a, b)


def put_pooled(main, side, main_ref, side_ref, at, side_at):
    main, side = main.astype(F32), side.astype(F32)
    for d in range(3):
        a, b = (main, side) if d == 1 else turn(main, side, 2 * (d - 1))
        main_ref[d * 16 : d * 16 + 16, row(at)] = a.astype(BF)
        side_ref[d * 16 : d * 16 + 16, row(side_at)] = b.astype(BF)


def put_cotangent(main, side, main_ref, side_ref, at, side_at):
    for d in range(3):
        a, b = (main, side) if d == 1 else turn(main, side, d - 1)
        main_ref[d * 32 : d * 32 + 32, row(at)] = a.astype(BF)
        side_ref[d * 32 : d * 32 + 32, row(side_at)] = b.astype(BF)


def put_features(main, side, ref, step, at):
    for d in range(3):
        a = main if d == 1 else turn(main, side, d - 1)[0]
        ref[d * step : d * step + 32, row(at)] = a.astype(BF)


def coarse_row(values, totals, keeps):
    act, grad = [], []
    for value, total, kept in zip(values, totals, keeps):
        sig = 1.0 / (1.0 + jnp.exp(-value))
        act.append((value * sig * kept).astype(BF).astype(F32))
        grad_act = pair_sum(total).astype(BF).astype(F32)
        grad_pre = grad_act * (sig * (1.0 + value * (1.0 - sig)))
        grad.append((grad_pre * kept).astype(BF).astype(F32))
    acts = [act[0] if d == 1 else turn(act[0], act[1], d - 1)[0] for d in range(3)]
    grads = [grad[0] if d == 1 else turn(grad[0], grad[1], 2 * (d - 1))[0] for d in range(3)]
    return [a.astype(BF) for a in acts], [g.astype(BF) for g in grads]


def column_masks(count):
    n = lax.axis_index("narrow")
    flag = lambda is_there: jnp.where(is_there, 1.0, 0.0)
    return jnp.where(lanes_of((C2, COLS)) < 64, flag(n < count - 1), flag(n > 0))


INNER = range(1, ROWS // 2 - 1)


def own_kernel(
    sides,
    s_ref, columns_ref, wc_ref, wg_ref,
    pst_ref, jf_ref, gst_ref, pre_ref, prb_ref, rg_ref, rgb_ref,
    psb_ref, gsb_ref,
):
    columns = [columns_ref[:, row(side)].astype(F32) for side in range(sides)]
    last = None
    for y in range(ROWS):
        main, side = s_ref[0:32, row(y)].astype(F32), beside(columns, HALO * y)
        put_features(main, side, jf_ref, 32, y)
        if y % 2 == 1:
            means = [pooled(a, b) for a, b in zip(last, (main, side))]
            put_pooled(*means, pst_ref, psb_ref, y // 2, y // 2)
        last = (main, side)
        main, side = s_ref[32:64, row(y)].astype(F32), beside(columns, 64 + HALO * y)
        put_cotangent(main, side, gst_ref, gsb_ref, y, y)
    pre_ref[...] = dot(wc_ref[...], pst_ref[...])
    prb_ref[...] = dot(wc_ref[...], psb_ref[...])
    rg_ref[...] = dot(wg_ref[...], gst_ref[...])
    rgb_ref[...] = dot(wg_ref[96:192, :], gsb_ref[...])


def shaped(rows_, lanes_, kind):
    return jax.ShapeDtypeStruct((rows_, lanes_ * COLS), kind)


def scratch(rows_, lanes_, kind):
    return pltpu.VMEM((rows_, lanes_ * COLS), kind)


def own_rows(s, columns, wc, wg, sides):
    half = ROWS // 2
    return pl.pallas_call(
        functools.partial(own_kernel, sides),
        out_shape=(
            shaped(48, half, BF), shaped(96, ROWS, BF), shaped(96, ROWS, BF),
            shaped(96, half, F32), shaped(96, half, F32),
            shaped(192, ROWS, F32), shaped(96, ROWS, F32),
        ),
        scratch_shapes=[scratch(48, half, BF), scratch(96, ROWS, BF)],
        compiler_params=params(),
        cost_estimate=pl.CostEstimate(flops=10**9, bytes_accessed=4 * 10**6, transcendentals=0),
        name="own_rows",
    )(s, columns, wc, wg)


def put_joined(jst_ref, at, jl_ref, to):
    for lo in (0, 48):
        jl_ref[lo : lo + 16, to] = jst_ref[64:80, at]
        jl_ref[lo + 16 : lo + 48, to] = jst_ref[96:128, at]
        jl_ref[128 + lo : 128 + lo + 48, to] = jst_ref[80:128, at]
    for lo in (96, 224):
        jl_ref[lo : lo + 32, to] = jnp.zeros((32, to.stop - to.start), BF)


def put_field(flat_ref, y, plane, value):
    flat_ref[pl.ds(2 * y + plane, C1, stride=2 * ROWS), :] = value


FINE = range(2 * INNER.start, 2 * INNER.stop)


def inner_kernel(
    count,
    pst_ref, jf_ref, gst_ref, pre_ref, prb_ref, rg_ref, rgb_ref, wo_ref, wq_ref,
    out_ref, gf_ref, ro_ref, rq_ref, rf_ref, rc_ref,
    jst_ref, qst_ref, gl_ref, jl_ref, pl_ref, ql_ref,
):
    rows, coarse_rows = len(FINE), len(INNER)
    there = column_masks(count)
    for d in range(3):
        jst_ref[d * 64 : d * 64 + 32, :] = jf_ref[d * 32 : d * 32 + 32, row(FINE.start, rows)]
    for at in INNER:
        values = [
            sum(ref[d * 32 : d * 32 + 32, row(at + d - 1)] for d in range(3)) for ref in (pre_ref, prb_ref)
        ]
        totals = [
            sum(
                ref[lo + d * 32 : lo + d * 32 + 32, row(r + d - 1)]
                for r in (2 * at, 2 * at + 1)
                for d in range(3)
            )
            for ref, lo in ((rg_ref, 96), (rgb_ref, 0))
        ]
        acts, grads = coarse_row(values, totals, (1.0, there))
        for d in range(3):
            for r in (2 * at, 2 * at + 1):
                jst_ref[d * 64 + 32 : d * 64 + 64, row(r - FINE.start)] = acts[d]
            qst_ref[d * 32 : d * 32 + 32, row(at - INNER.start)] = grads[d]
    ro_ref[...] = dot(wo_ref[...], jst_ref[...])
    rq_ref[...] = dot(wq_ref[...], qst_ref[...])

    put_joined(jst_ref, row(0, rows), jl_ref, row(0, rows))
    ql_ref[0:96, :] = jnp.zeros((96, coarse_rows * COLS), BF)
    ql_ref[96:128, :] = qst_ref[32:64, :]
    for ky in range(3):
        gl_ref[ky * 96 : ky * 96 + 96, :] = gst_ref[:, row(FINE.start + 1 - ky, rows)]
        pl_ref[ky * 48 : ky * 48 + 48, :] = pst_ref[:, row(INNER.start + ky - 1, coarse_rows)]
    rf_ref[...] = dot_nt(gl_ref[...], jl_ref[...])
    rc_ref[...] = dot_nt(pl_ref[...], ql_ref[...])

    for y in range(FINE.start + 1, FINE.stop - 1):
        value = sum(ro_ref[d * 32 : d * 32 + 32, row(y - 1 + d - FINE.start)] for d in range(3))
        for z in range(2):
            put_field(out_ref, y, z, value[z * 16 : z * 16 + 16])
    for at in range(INNER.start + 1, INNER.stop - 1):
        coarse = sum(rq_ref[d * 16 : d * 16 + 16, row(at - 1 + d - INNER.start)] for d in range(3))
        coarse = coarse.astype(BF).astype(F32) * 0.125
        for y in (2 * at, 2 * at + 1):
            for z in range(2):
                lo = z * 16
                value = sum(rg_ref[lo + d * 32 : lo + d * 32 + 16, row(y - 1 + d)] for d in range(3))
                put_field(gf_ref, y, z, value + coarse)


def inner_rows(own, wo, wq, count):
    rows, coarse_rows = len(FINE), len(INNER)
    return pl.pallas_call(
        functools.partial(inner_kernel, count),
        out_shape=(
            shaped(CELLS, 1, F32), shaped(CELLS, 1, F32),
            shaped(96, rows, F32), shaped(48, coarse_rows, F32),
            shaped(288, 2, F32), shaped(144, 1, F32),
        ),
        scratch_shapes=[
            scratch(192, rows, BF), scratch(96, coarse_rows, BF),
            scratch(288, rows, BF), scratch(256, rows, BF),
            scratch(144, coarse_rows, BF), scratch(128, coarse_rows, BF),
        ],
        compiler_params=params(),
        cost_estimate=pl.CostEstimate(flops=10**9, bytes_accessed=4 * 10**6, transcendentals=10**5),
        name="inner_rows",
    )(*own, wo, wq)


def rest_kernel(
    counts, sides,
    even_ref, odd_ref,
    pst_own, jf_own, gst_own, pre_own, prb_own, rg_own, rgb_own,
    out_inner, gf_inner, ro_inner, rq_inner, rf_inner, rc_inner,
    wo_ref, wg_ref, wc_ref, wq_ref,
    out_ref, gf_ref, gw_ref,
    halo_ref, jst_ref, gst_ref, gsb_ref, pst_ref, psb_ref, qst_ref,
    pre_ref, prb_ref, rg_ref, rgb_ref, ro_ref, rq_ref, gl_ref, jl_ref, pl_ref, ql_ref, flat_ref,
):
    w = lax.axis_index("wide")
    there = column_masks(counts[1])
    flag = lambda is_there: jnp.where(is_there, 1.0, 0.0)
    has_above, has_below = flag(w > 0), flag(w < counts[0] - 1)

    odd = w % 2
    halo_ref[1 - odd] = even_ref[...]
    inside = flag((w > 0) & (w < counts[0] - 1))
    halo_ref[odd] = (odd_ref[...].astype(F32) * inside).astype(BF)
    columns = [
        [halo_ref[i, :, row(SLOTS + side)].astype(F32) for side in range(sides)] for i in range(2)
    ]

    for i in range(2):
        lane = HALO * (ROWS - HALO) if i == 0 else 0
        for j in range(3):
            main = halo_ref[i, :, row(2 + j)].astype(F32)
            side = beside(columns[i], 64 + lane + HALO * (j + 1 - i))
            put_cotangent(main, side, gst_ref, gsb_ref, 9 * i + j, 3 * i + j)
        gst_ref[:, row(3 + 3 * i, 3)] = gst_own[:, row(13 * i, 3)]
        rg_ref[:, row(3 * i, 3)] = dot(wg_ref[...], gst_ref[:, row(9 * i, 3)])
    rgb_ref[...] = dot(wg_ref[96:192, :], gsb_ref[...])
    for i in range(2):
        lane = HALO * (ROWS - HALO) if i == 0 else 0
        sides_f = [beside(columns[i], lane + HALO * r) for r in range(HALO)]
        near = HALO - 1 if i == 0 else 0
        for j in range(2):
            main = halo_ref[i, j * 16 : j * 16 + 16, row(1)]
            side = pooled(sides_f[2 * j], sides_f[2 * j + 1])
            put_pooled(main, side, pst_ref, psb_ref, 6 * i + j, 2 * i + j)
        pst_ref[:, row(2 + 2 * i, 2)] = pst_own[:, row(6 * i, 2)]
        pre_ref[:, row(2 * i, 2)] = dot(wc_ref[...], pst_ref[:, row(6 * i, 2)])
        put_features(halo_ref[i, :, row(0)].astype(F32), sides_f[near], jst_ref, 64, 5 * i)
        for d in range(3):
            jst_ref[d * 64 : d * 64 + 32, row(1 + 2 * i, 2)] = jf_own[d * 32 : d * 32 + 32, row(14 * i, 2)]
    prb_ref[...] = dot(wc_ref[...], psb_ref[...])

    def part(own, halo, lo, size, at, edge, length):
        if at < edge:
            return halo[lo : lo + size, row(at)]
        if at < edge + length:
            return own[lo : lo + size, row(at - edge)]
        return halo[lo : lo + size, row(at - length)]

    for k, at in enumerate((0, 1, 8, 9)):
        keep = has_above if at == 0 else has_below if at == 9 else 1.0
        values = [
            sum(part(own, halo, d * 32, 32, at + d, 2, 8) for d in range(3))
            for own, halo in ((pre_own, pre_ref), (prb_own, prb_ref))
        ]
        totals = [
            sum(
                part(own, halo, lo + d * 32, 32, r + d, 3, ROWS)
                for r in (2 * at, 2 * at + 1)
                for d in range(3)
            )
            for own, halo, lo in ((rg_own, rg_ref, 96), (rgb_own, rgb_ref, 0))
        ]
        acts, grads = coarse_row(values, totals, (keep, keep * there))
        for d in range(3):
            for r in ((0,), (1, 2), (3, 4), (5,))[k]:
                jst_ref[d * 64 + 32 : d * 64 + 64, row(r)] = acts[d]
            qst_ref[d * 32 : d * 32 + 32, row(k)] = grads[d]

    put_joined(jst_ref, row(1, 4), jl_ref, row(0, 4))
    ql_ref[0:96, :] = jnp.zeros((96, 2 * COLS), BF)
    ql_ref[96:128, :] = qst_ref[32:64, row(1, 2)]
    for i in range(2):
        for ky in range(3):
            gl_ref[ky * 96 : ky * 96 + 96, row(2 * i, 2)] = gst_ref[:, row(4 + 4 * i - ky, 2)]
            pl_ref[ky * 48 : ky * 48 + 48, row(i)] = pst_ref[:, row(1 + 3 * i + ky)]
    rf = rf_inner[...] + dot_nt(gl_ref[...], jl_ref[...])
    rc = rc_inner[...] + dot_nt(pl_ref[...], ql_ref[...])
    ro_ref[...] = dot(wo_ref[...], jst_ref[...])
    rq_ref[...] = dot(wq_ref[...], qst_ref[...])
    fine, coarse = {}, {}
    for ky in range(3):
        for kx in range(3):
            lo = ky * 96 + (2 - kx) * 32
            fine[ky, 0, kx] = rf[lo + 16 : lo + 32, 0:128]
            fine[ky, 1, kx] = rf[lo : lo + 16, 0:128] + rf[lo + 16 : lo + 32, 128:256]
            fine[ky, 2, kx] = rf[lo : lo + 16, 128:256]
            coarse[ky, kx] = rc[ky * 48 + kx * 16 : ky * 48 + kx * 16 + 16] * 0.5
    lane16 = lanes_of((16, COLS))
    order = [(ky, kz, kx) for ky in range(3) for kz in range(3) for kx in range(3)]
    for i in range(16):
        value = jnp.zeros((16, COLS), F32)
        if i < 14:
            value = jnp.where(lane16 < 48, fine[order[i]], value)
        if i < 13:
            value = jnp.where((lane16 >= 48) & (lane16 < 96), fine[order[14 + i]], value)
        if i < 9:
            value = jnp.where(lane16 >= 96, coarse[i // 3, i % 3], value)
        gw_ref[i * 16 : i * 16 + 16, :] = value.astype(BF)

    flat_ref[0] = out_inner[...]
    flat_ref[1] = gf_inner[...]
    for y in (0, 1, 2, 13, 14, 15):
        value = sum(part(ro_inner, ro_ref, d * 32, 32, y + d, 3, len(FINE)) for d in range(3))
        for z in range(2):
            put_field(flat_ref.at[0], y, z, value[z * 16 : z * 16 + 16])
    out_ref[...] = flat_ref[0].astype(BF)

    for at in (0, 1, 6, 7):
        coarse = sum(part(rq_inner, rq_ref, d * 16, 16, at + d, 2, len(INNER)) for d in range(3))
        coarse = coarse.astype(BF).astype(F32) * 0.125
        for y in (2 * at, 2 * at + 1):
            for z in range(2):
                lo = z * 16
                value = sum(part(rg_own, rg_ref, lo + d * 32, 16, y + 2 + d, 3, ROWS) for d in range(3))
                put_field(flat_ref.at[1], y, z, value + coarse)
    gf_ref[...] = flat_ref[1].astype(BF)


def rest(messages, own, inner, matrices, counts, sides):
    return pl.pallas_call(
        functools.partial(rest_kernel, counts, sides),
        out_shape=(
            pltpu.VMEM((CELLS, COLS), BF),
            pltpu.VMEM((CELLS, COLS), BF),
            jax.ShapeDtypeStruct((256, COLS), BF),
        ),
        scratch_shapes=[
            pltpu.VMEM((2, 32, (SLOTS + sides) * COLS), BF),
            scratch(192, 6, BF),
            scratch(96, 12, BF), scratch(96, 6, BF),
            scratch(48, 8, BF), scratch(48, 4, BF),
            scratch(96, 4, BF),
            scratch(96, 4, F32), scratch(96, 4, F32),
            scratch(192, 6, F32), scratch(96, 6, F32),
            scratch(96, 6, F32),
            scratch(48, 4, F32),
            scratch(288, 4, BF), scratch(256, 4, BF), scratch(144, 2, BF), scratch(128, 2, BF),
            pltpu.VMEM((2, CELLS, COLS), F32),
        ],
        compiler_params=params(),
        cost_estimate=pl.CostEstimate(flops=10**9, bytes_accessed=4 * 10**6, transcendentals=10**5),
        name="rest",
    )(*messages, *own, *inner, *matrices)


def add_kernel(parts_ref, copies_ref):
    total = parts_ref[0].astype(F32)
    for i in range(1, parts_ref.shape[0]):
        total = total + parts_ref[i].astype(F32)
    total = total.astype(BF)
    for i in range(parts_ref.shape[0]):
        copies_ref[i] = total


def add_up(parts):
    return pl.pallas_call(
        add_kernel,
        out_shape=jax.ShapeDtypeStruct(parts.shape, BF),
        compiler_params=pltpu.CompilerParams(vmem_limit_bytes=VMEM_LIMIT),
        name="add_up",
    )(parts)


def spread_kernel(
    fine_scale, coarse_scale,
    sum_ref, out_ref, gf_ref,
    out_hbm, gf_hbm, fine_hbm, coarse_hbm,
    fine_ref, coarse_ref, field_sems, weight_sems,
):
    fields = chunks(((out_ref, out_hbm), (gf_ref, gf_hbm)), field_sems, 4)
    weights = chunks(((fine_ref, fine_hbm), (coarse_ref, coarse_hbm)), weight_sems, 3)
    for copies in fields:
        start(copies)
    for i in range(27):
        at = (i if i < 14 else i - 14) * 16
        value = sum_ref[at : at + 16, :].astype(F32)
        if i >= 14:
            value = pltpu.roll(value, 80, 1)
        fine_ref[i * 16 : i * 16 + 16, :] = value[:, 0:48] * fine_scale
        ky, kz, kx = i // 9, i // 3 % 3, i % 3
        if kz == 1:
            at = (ky * 3 + kx) * 16
            value = pltpu.roll(sum_ref[at : at + 16, :].astype(F32), 32, 1)[:, 0:32] * coarse_scale
        else:
            value = jnp.zeros((16, 32), F32)
        coarse_ref[i * 16 : i * 16 + 16, :] = value
        if i % 9 == 8:
            weights[0][ky].start()
            weights[1][ky].start()
    for copies in fields + weights:
        wait(copies)


def spread(total, output, grad_features, fine_scale, coarse_scale):
    return pl.pallas_call(
        functools.partial(spread_kernel, fine_scale, coarse_scale),
        in_specs=[pl.BlockSpec(memory_space=pltpu.VMEM)] * 3,
        out_specs=(pl.BlockSpec(memory_space=pl.ANY),) * 4,
        out_shape=(
            jax.ShapeDtypeStruct((CELLS, COLS), BF),
            jax.ShapeDtypeStruct((CELLS, COLS), BF),
            jax.ShapeDtypeStruct((TAPS, 48), F32),
            jax.ShapeDtypeStruct((TAPS, 32), F32),
        ),
        scratch_shapes=[
            pltpu.VMEM((TAPS, 48), F32),
            pltpu.VMEM((TAPS, 32), F32),
            pltpu.SemaphoreType.DMA((2, 4)),
            pltpu.SemaphoreType.DMA((2, 3)),
        ],
        compiler_params=params(),
        name="spread",
    )(total, output, grad_features)


def matrices_kernel(
    fine_hbm, coarse_hbm, wo_ref, wg_ref, wc_ref, wq_ref,
    fine_ref, coarse_ref, wide_ref, pieces_ref, blocks_ref, sems,
):
    fine_copies, coarse_copies = chunks(((fine_hbm, fine_ref), (coarse_hbm, coarse_ref)), sems, 3)
    start(fine_copies)
    start(coarse_copies)
    lane = lanes_of((C1, COLS))
    wait(fine_copies)
    wide_ref[:, 0:48] = fine_ref[...].astype(F32)
    for ky in range(3):
        for zo in range(2):
            tiles = [jnp.zeros((C1, COLS), F32) for _ in range(2)]
            for kx in range(3):
                at = ((ky * 3 + 1 - zo) * 3 + kx) * 16
                first, second = (wide_ref[at + i : at + i + 16, :] for i in (0, 48))
                both = (first + second).astype(BF).astype(F32)
                piece = jnp.where(lane < 32, pltpu.roll(second, 16, 1), pltpu.roll(both, 16, 1))
                piece = jnp.where(lane < 16, first, jnp.where(lane < 64, piece, 0.0))
                spot = (2 - kx) * 32 + zo * 16
                pieces_ref[2 - ky, spot : spot + 16, :] = piece
                tiles[kx // 2] = tiles[kx // 2] + (pltpu.roll(piece, 64, 1) if kx == 1 else piece)
            spot = ky * 32 + zo * 16
            wo_ref[spot : spot + 16, 0:128] = tiles[0].astype(BF)
            wo_ref[spot : spot + 16, 128:192] = tiles[1][:, 0:64].astype(BF)
    wait(coarse_copies)
    wide_ref[:, 0:32] = coarse_ref[...].astype(F32)
    for ky in range(3):
        total = jnp.zeros((C1, COLS), F32)
        for kx in range(3):
            at = ((ky * 3 + 1) * 3 + kx) * 16
            value = jnp.where(lane < 32, wide_ref[at : at + 16, :], 0.0)
            blocks_ref[ky, kx * 16 : kx * 16 + 16, :] = value
            spot = (2 - kx) * 32
            total = total + (pltpu.roll(value, spot, 1) if spot else value)
        wq_ref[(2 - ky) * 16 : (2 - ky) * 16 + 16, :] = total[:, 0:96].astype(BF)
    for d in range(3):
        turned = jnp.transpose(pieces_ref[d])[0:64, 0:96].astype(BF)
        wg_ref[d * 32 : d * 32 + 32, :] = turned[0:32]
        wg_ref[96 + d * 32 : 96 + d * 32 + 32, :] = turned[32:64]
        wc_ref[d * 32 : d * 32 + 32, :] = jnp.transpose(blocks_ref[d])[0:32, 0:48].astype(BF)


def weight_matrices(coarse_weight, fine_weight):
    fine = jnp.transpose(fine_weight, (2, 3, 4, 0, 1)).reshape(TAPS, 48)
    coarse = jnp.transpose(coarse_weight, (2, 3, 4, 1, 0)).reshape(TAPS, 32)
    shape = lambda *dims: jax.ShapeDtypeStruct(dims, BF)
    return pl.pallas_call(
        matrices_kernel,
        in_specs=[pl.BlockSpec(memory_space=pltpu.HBM)] * 2,
        out_shape=(shape(96, 192), shape(192, 96), shape(96, 48), shape(48, 96)),
        scratch_shapes=[
            pltpu.VMEM((TAPS, 48), BF),
            pltpu.VMEM((TAPS, 32), BF),
            pltpu.VMEM((TAPS, COLS), F32),
            pltpu.VMEM((3, COLS, COLS), F32),
            pltpu.VMEM((3, COLS, COLS), F32),
            pltpu.SemaphoreType.DMA((2, 3)),
        ],
        compiler_params=params(),
        cost_estimate=pl.CostEstimate(flops=10**6, bytes_accessed=10**6, transcendentals=0),
        name="matrices",
    )(kept_in_hbm(fine), kept_in_hbm(coarse))


def beside_blocks(outer, narrow):
    if outer.shape[1] == COLS:
        return lax.ppermute(outer, "narrow", [(0, 1), (1, 0)])
    right = lax.ppermute(outer[:, :COLS], "narrow", [(i + 1, i) for i in range(narrow - 1)])
    left = lax.ppermute(outer[:, COLS:], "narrow", [(i, i + 1) for i in range(narrow - 1)])
    return jnp.concatenate([right, left], 1)


def shards(features, cotangent, coarse_weight, fine_weight):
    wide, narrow = lax.axis_size("wide"), lax.axis_size("narrow")
    sides = 1 if narrow == 2 else 2
    own, strip, to_odd, to_even = pack(features, cotangent, sides)
    swaps = lambda start: [
        pair
        for i in range(start, wide, 2)
        for pair in ((i, (i + 1) % wide), ((i + 1) % wide, i))
    ]
    columns = beside_blocks(strip, narrow)
    wo, wg, wc, wq = weight_matrices(coarse_weight, fine_weight)
    with_columns = lambda message: lax.dynamic_update_slice(message, columns, (0, SLOTS * COLS))
    odd = lax.ppermute(with_columns(to_odd), "wide", swaps(1))
    even = lax.ppermute(with_columns(to_even), "wide", swaps(0))
    stacks = own_rows(own, columns, wc, wg, sides)
    inner = inner_rows(stacks, wo, wq, narrow)
    output, grad_features, grads = rest(
        (even, odd), stacks, inner, (wo, wg, wc, wq), (wide, narrow), sides
    )
    devices = wide * narrow
    share = -(-256 // devices)
    grads = jnp.pad(grads, ((0, share * devices - 256), (0, 0))).reshape(devices, share, COLS)
    both = ("wide", "narrow")
    parts = lax.all_to_all(grads, both, 0, 0, tiled=True)
    total = lax.all_to_all(add_up(parts), both, 0, 0, tiled=True)
    total = total.reshape(share * devices, COLS)[:256]
    all_cells = features.shape[1] * features.shape[2] * features.shape[3] * devices
    output, grad_features, grad_fine, grad_coarse = spread(
        total, output, grad_features, 1.0 / math.sqrt(all_cells), 1.0 / math.sqrt(all_cells // 8)
    )
    grad_fine = jnp.transpose(grad_fine.reshape(3, 3, 3, C1, C1 + C2), (3, 4, 0, 1, 2))
    grad_coarse = jnp.transpose(grad_coarse.reshape(3, 3, 3, C1, C2), (4, 3, 0, 1, 2))
    return (
        output.reshape(features.shape),
        grad_features.reshape(features.shape),
        grad_fine,
        grad_coarse,
    )


def solution(mesh):
    placed = P(None, "wide", None, "narrow")
    return jax.shard_map(
        shards,
        mesh=mesh,
        in_specs=(placed, placed, P(), P()),
        out_specs=(placed, placed, P(), P()),
        check_vma=False,
    )
```

```python
import functools
import math

import jax
import jax.numpy as jnp
from jax import lax
from jax.experimental import pallas as pl
from jax.experimental.pallas import tpu as pltpu
from jax.sharding import PartitionSpec as P

C1, C2 = 16, 32
ROWS, COLS = 16, 128
HALO = 4
BF, F32 = jnp.bfloat16, jnp.float32
VMEM_LIMIT = 20 * 1024 * 1024


def lanes_of(shape):
    return lax.broadcasted_iota(jnp.int32, shape, len(shape) - 1)


def row(index, count=1):
    return slice(index * COLS, (index + count) * COLS)


def pair_sum(value):
    lane = lanes_of(value.shape)
    other = jnp.where(lane % 2 == 0, pltpu.roll(value, COLS - 1, 1), pltpu.roll(value, 1, 1))
    return value + other


def pooled(first, second):
    total = first + second
    return (pair_sum(total[0:16] + total[16:32]) * 0.125).astype(BF)


def dot(a, b):
    return jnp.dot(a, b, preferred_element_type=F32)


def dot_nt(a, b):
    return lax.dot_general(a, b, (((1,), (1,)), ((), ())), preferred_element_type=F32)


def params():
    return pltpu.CompilerParams(vmem_limit_bytes=VMEM_LIMIT)


SLOTS = 5
CELLS = C1 * ROWS * 2
TAPS = 27 * C1


def chunks(pairs, sems, pieces):
    copies = []
    for i, (source, target) in enumerate(pairs):
        rows = source.shape[0] // pieces
        copies.append([
            pltpu.make_async_copy(
                source.at[pl.ds(j * rows, rows)], target.at[pl.ds(j * rows, rows)], sems.at[i, j]
            )
            for j in range(pieces)
        ])
    return copies


def start(copies):
    for copy in copies:
        copy.start()


def wait(copies):
    for copy in copies:
        copy.wait()


def pack_kernel(
    sides, f_hbm, g_hbm, s_ref, strip_ref, odd_ref, even_ref, f_ref, g_ref, wide_ref, base_ref, sems
):
    arrivals = chunks(((f_hbm, f_ref), (g_hbm, g_ref)), sems, 4)
    for copies in arrivals:
        start(copies)
    lane = lanes_of((C1, COLS))
    place = lax.axis_index("narrow")
    odd = lax.axis_index("wide") % 2
    strips = [[jnp.zeros((C1, COLS), F32) for _ in range(sides)] for _ in range(2)]
    for a in range(2):
        wait(arrivals[a])
        wide_ref[...] = (f_ref, g_ref)[a][...].astype(F32)
        for z in range(2):
            chans = slice(a * 32 + z * 16, a * 32 + z * 16 + 16)
            for y in range(ROWS):
                value = wide_ref[pl.ds(2 * y + z, C1, stride=2 * ROWS), :]
                s_ref[chans, row(y)] = value.astype(BF)
                first = 64 * a + HALO * y
                inside = (lane >= first) & (lane < first + HALO)
                for side in range(sides):
                    if sides == 2:
                        shift = (first + HALO * side) % COLS
                    else:
                        shift = lax.rem(first + HALO * (1 - place), COLS)
                    strips[z][side] = jnp.where(inside, pltpu.roll(value, shift, 1), strips[z][side])
    for z in range(2):
        for side in range(sides):
            strip_ref[z * 16 : z * 16 + 16, row(side)] = strips[z][side].astype(BF)
    for to, near, pairs, cot in ((0, ROWS - 1, (6, 7), ROWS - 3), (1, 0, (0, 1), 0)):
        base_ref[to, :, row(0)] = s_ref[0:32, row(near)]
        for i, pair in enumerate(pairs):
            first, second = (s_ref[0:32, row(2 * pair + j)].astype(F32) for j in range(2))
            base_ref[to, i * 16 : i * 16 + 16, row(1)] = pooled(first, second)
        base_ref[to, :, row(2, 3)] = s_ref[32:64, row(cot, 3)]
    even_ref[:, row(0, SLOTS)] = base_ref[odd]
    odd_ref[:, row(0, SLOTS)] = base_ref[1 - odd]
    even_ref[:, row(SLOTS, sides)] = jnp.zeros((32, sides * COLS), BF)
    odd_ref[:, row(SLOTS, sides)] = jnp.zeros((32, sides * COLS), BF)


def kept_in_hbm(array):
    return pltpu.with_memory_space_constraint(array, pltpu.HBM)


def pack(features, cotangent, sides):
    flat = lambda a: kept_in_hbm(a.reshape(CELLS, COLS))
    message = jax.ShapeDtypeStruct((32, (SLOTS + sides) * COLS), BF)
    return pl.pallas_call(
        functools.partial(pack_kernel, sides),
        in_specs=[pl.BlockSpec(memory_space=pltpu.HBM)] * 2,
        out_shape=(
            jax.ShapeDtypeStruct((64, ROWS * COLS), BF),
            jax.ShapeDtypeStruct((32, sides * COLS), BF),
            message,
            message,
        ),
        scratch_shapes=[
            pltpu.VMEM((CELLS, COLS), BF),
            pltpu.VMEM((CELLS, COLS), BF),
            pltpu.VMEM((CELLS, COLS), F32),
            pltpu.VMEM((2, 32, SLOTS * COLS), BF),
            pltpu.SemaphoreType.DMA((2, 4)),
        ],
        compiler_params=params(),
        cost_estimate=pl.CostEstimate(flops=10**6, bytes_accessed=10**6, transcendentals=0),
        name="pack",
    )(flat(features), flat(cotangent))


def beside(columns, at):
    lane = lanes_of(columns[0].shape)
    if len(columns) == 1:
        place = lax.axis_index("narrow")
        first = (COLS - HALO) * place
        turned = pltpu.roll(columns[0], lax.rem(COLS - at + first, COLS), 1)
        return jnp.where((lane >= first) & (lane < first + HALO), turned, 0.0)
    right = pltpu.roll(columns[0], (-at) % COLS, 1)
    left = pltpu.roll(columns[1], (COLS - HALO - at) % COLS, 1)
    return jnp.where(lane < HALO, right, jnp.where(lane >= COLS - HALO, left, 0.0))


def turn(main, side, by):
    lane = lanes_of(main.shape)
    a, b = pltpu.roll(main, (-by) % COLS, 1), pltpu.roll(side, (-by) % COLS, 1)
    crossed = lane >= COLS - by if by > 0 else lane < -by
    return jnp.where(crossed, b, a), jnp.where(crossed, a, b)


def put_pooled(main, side, main_ref, side_ref, at, side_at):
    main, side = main.astype(F32), side.astype(F32)
    for d in range(3):
        a, b = (main, side) if d == 1 else turn(main, side, 2 * (d - 1))
        main_ref[d * 16 : d * 16 + 16, row(at)] = a.astype(BF)
        side_ref[d * 16 : d * 16 + 16, row(side_at)] = b.astype(BF)


def put_cotangent(main, side, main_ref, side_ref, at, side_at):
    for d in range(3):
        a, b = (main, side) if d == 1 else turn(main, side, d - 1)
        main_ref[d * 32 : d * 32 + 32, row(at)] = a.astype(BF)
        side_ref[d * 32 : d * 32 + 32, row(side_at)] = b.astype(BF)


def put_features(main, side, ref, step, at):
    for d in range(3):
        a = main if d == 1 else turn(main, side, d - 1)[0]
        ref[d * step : d * step + 32, row(at)] = a.astype(BF)


def coarse_row(values, totals, keeps):
    act, grad = [], []
    for value, total, kept in zip(values, totals, keeps):
        sig = 1.0 / (1.0 + jnp.exp(-value))
        act.append((value * sig * kept).astype(BF).astype(F32))
        grad_act = pair_sum(total).astype(BF).astype(F32)
        grad_pre = grad_act * (sig * (1.0 + value * (1.0 - sig)))
        grad.append((grad_pre * kept).astype(BF).astype(F32))
    acts = [act[0] if d == 1 else turn(act[0], act[1], d - 1)[0] for d in range(3)]
    grads = [grad[0] if d == 1 else turn(grad[0], grad[1], 2 * (d - 1))[0] for d in range(3)]
    return [a.astype(BF) for a in acts], [g.astype(BF) for g in grads]


def column_masks(count):
    n = lax.axis_index("narrow")
    flag = lambda is_there: jnp.where(is_there, 1.0, 0.0)
    return jnp.where(lanes_of((C2, COLS)) < 64, flag(n < count - 1), flag(n > 0))


INNER = range(1, ROWS // 2 - 1)


def own_kernel(
    sides,
    s_ref, columns_ref, wc_ref, wg_ref,
    pst_ref, jf_ref, gst_ref, pre_ref, prb_ref, rg_ref, rgb_ref,
    psb_ref, gsb_ref,
):
    columns = [columns_ref[:, row(side)].astype(F32) for side in range(sides)]
    last = None
    for y in range(ROWS):
        main, side = s_ref[0:32, row(y)].astype(F32), beside(columns, HALO * y)
        put_features(main, side, jf_ref, 32, y)
        if y % 2 == 1:
            means = [pooled(a, b) for a, b in zip(last, (main, side))]
            put_pooled(*means, pst_ref, psb_ref, y // 2, y // 2)
        last = (main, side)
        main, side = s_ref[32:64, row(y)].astype(F32), beside(columns, 64 + HALO * y)
        put_cotangent(main, side, gst_ref, gsb_ref, y, y)
    pre_ref[...] = dot(wc_ref[...], pst_ref[...])
    prb_ref[...] = dot(wc_ref[...], psb_ref[...])
    rg_ref[...] = dot(wg_ref[...], gst_ref[...])
    rgb_ref[...] = dot(wg_ref[96:192, :], gsb_ref[...])


def shaped(rows_, lanes_, kind):
    return jax.ShapeDtypeStruct((rows_, lanes_ * COLS), kind)


def scratch(rows_, lanes_, kind):
    return pltpu.VMEM((rows_, lanes_ * COLS), kind)


def own_rows(s, columns, wc, wg, sides):
    half = ROWS // 2
    return pl.pallas_call(
        functools.partial(own_kernel, sides),
        out_shape=(
            shaped(48, half, BF), shaped(96, ROWS, BF), shaped(96, ROWS, BF),
            shaped(96, half, F32), shaped(96, half, F32),
            shaped(192, ROWS, F32), shaped(96, ROWS, F32),
        ),
        scratch_shapes=[scratch(48, half, BF), scratch(96, ROWS, BF)],
        compiler_params=params(),
        cost_estimate=pl.CostEstimate(flops=10**9, bytes_accessed=4 * 10**6, transcendentals=0),
        name="own_rows",
    )(s, columns, wc, wg)


def put_joined(jst_ref, at, jl_ref, to):
    for lo in (0, 48):
        jl_ref[lo : lo + 16, to] = jst_ref[64:80, at]
        jl_ref[lo + 16 : lo + 48, to] = jst_ref[96:128, at]
        jl_ref[128 + lo : 128 + lo + 48, to] = jst_ref[80:128, at]
    for lo in (96, 224):
        jl_ref[lo : lo + 32, to] = jnp.zeros((32, to.stop - to.start), BF)


def put_field(flat_ref, y, plane, value):
    flat_ref[pl.ds(2 * y + plane, C1, stride=2 * ROWS), :] = value


FINE = range(2 * INNER.start, 2 * INNER.stop)


def inner_kernel(
    count,
    pst_ref, jf_ref, gst_ref, pre_ref, prb_ref, rg_ref, rgb_ref, wo_ref, wq_ref,
    out_ref, gf_ref, ro_ref, rq_ref, rf_ref, rc_ref,
    jst_ref, qst_ref, gl_ref, jl_ref, pl_ref, ql_ref,
):
    rows, coarse_rows = len(FINE), len(INNER)
    there = column_masks(count)
    for d in range(3):
        jst_ref[d * 64 : d * 64 + 32, :] = jf_ref[d * 32 : d * 32 + 32, row(FINE.start, rows)]
    for at in INNER:
        values = [
            sum(ref[d * 32 : d * 32 + 32, row(at + d - 1)] for d in range(3)) for ref in (pre_ref, prb_ref)
        ]
        totals = [
            sum(
                ref[lo + d * 32 : lo + d * 32 + 32, row(r + d - 1)]
                for r in (2 * at, 2 * at + 1)
                for d in range(3)
            )
            for ref, lo in ((rg_ref, 96), (rgb_ref, 0))
        ]
        acts, grads = coarse_row(values, totals, (1.0, there))
        for d in range(3):
            for r in (2 * at, 2 * at + 1):
                jst_ref[d * 64 + 32 : d * 64 + 64, row(r - FINE.start)] = acts[d]
            qst_ref[d * 32 : d * 32 + 32, row(at - INNER.start)] = grads[d]
    ro_ref[...] = dot(wo_ref[...], jst_ref[...])
    rq_ref[...] = dot(wq_ref[...], qst_ref[...])

    put_joined(jst_ref, row(0, rows), jl_ref, row(0, rows))
    ql_ref[0:96, :] = jnp.zeros((96, coarse_rows * COLS), BF)
    ql_ref[96:128, :] = qst_ref[32:64, :]
    for ky in range(3):
        gl_ref[ky * 96 : ky * 96 + 96, :] = gst_ref[:, row(FINE.start + 1 - ky, rows)]
        pl_ref[ky * 48 : ky * 48 + 48, :] = pst_ref[:, row(INNER.start + ky - 1, coarse_rows)]
    rf_ref[...] = dot_nt(gl_ref[...], jl_ref[...])
    rc_ref[...] = dot_nt(pl_ref[...], ql_ref[...])

    for y in range(FINE.start + 1, FINE.stop - 1):
        value = sum(ro_ref[d * 32 : d * 32 + 32, row(y - 1 + d - FINE.start)] for d in range(3))
        for z in range(2):
            put_field(out_ref, y, z, value[z * 16 : z * 16 + 16])
    for at in range(INNER.start + 1, INNER.stop - 1):
        coarse = sum(rq_ref[d * 16 : d * 16 + 16, row(at - 1 + d - INNER.start)] for d in range(3))
        coarse = coarse.astype(BF).astype(F32) * 0.125
        for y in (2 * at, 2 * at + 1):
            for z in range(2):
                lo = z * 16
                value = sum(rg_ref[lo + d * 32 : lo + d * 32 + 16, row(y - 1 + d)] for d in range(3))
                put_field(gf_ref, y, z, value + coarse)


def inner_rows(own, wo, wq, count):
    rows, coarse_rows = len(FINE), len(INNER)
    return pl.pallas_call(
        functools.partial(inner_kernel, count),
        out_shape=(
            shaped(CELLS, 1, F32), shaped(CELLS, 1, F32),
            shaped(96, rows, F32), shaped(48, coarse_rows, F32),
            shaped(288, 2, F32), shaped(144, 1, F32),
        ),
        scratch_shapes=[
            scratch(192, rows, BF), scratch(96, coarse_rows, BF),
            scratch(288, rows, BF), scratch(256, rows, BF),
            scratch(144, coarse_rows, BF), scratch(128, coarse_rows, BF),
        ],
        compiler_params=params(),
        cost_estimate=pl.CostEstimate(flops=10**9, bytes_accessed=4 * 10**6, transcendentals=10**5),
        name="inner_rows",
    )(*own, wo, wq)


def rest_kernel(
    counts, sides,
    even_ref, odd_ref,
    pst_own, jf_own, gst_own, pre_own, prb_own, rg_own, rgb_own,
    out_inner, gf_inner, ro_inner, rq_inner, rf_inner, rc_inner,
    wo_ref, wg_ref, wc_ref, wq_ref,
    out_ref, gf_ref, gw_ref,
    halo_ref, jst_ref, gst_ref, gsb_ref, pst_ref, psb_ref, qst_ref,
    pre_ref, prb_ref, rg_ref, rgb_ref, ro_ref, rq_ref, gl_ref, jl_ref, pl_ref, ql_ref, flat_ref,
):
    w = lax.axis_index("wide")
    there = column_masks(counts[1])
    flag = lambda is_there: jnp.where(is_there, 1.0, 0.0)
    has_above, has_below = flag(w > 0), flag(w < counts[0] - 1)

    odd = w % 2
    halo_ref[1 - odd] = even_ref[...]
    inside = flag((w > 0) & (w < counts[0] - 1))
    halo_ref[odd] = (odd_ref[...].astype(F32) * inside).astype(BF)
    columns = [
        [halo_ref[i, :, row(SLOTS + side)].astype(F32) for side in range(sides)] for i in range(2)
    ]

    for i in range(2):
        lane = HALO * (ROWS - HALO) if i == 0 else 0
        for j in range(3):
            main = halo_ref[i, :, row(2 + j)].astype(F32)
            side = beside(columns[i], 64 + lane + HALO * (j + 1 - i))
            put_cotangent(main, side, gst_ref, gsb_ref, 9 * i + j, 3 * i + j)
        gst_ref[:, row(3 + 3 * i, 3)] = gst_own[:, row(13 * i, 3)]
        rg_ref[:, row(3 * i, 3)] = dot(wg_ref[...], gst_ref[:, row(9 * i, 3)])
    rgb_ref[...] = dot(wg_ref[96:192, :], gsb_ref[...])
    for i in range(2):
        lane = HALO * (ROWS - HALO) if i == 0 else 0
        sides_f = [beside(columns[i], lane + HALO * r) for r in range(HALO)]
        near = HALO - 1 if i == 0 else 0
        for j in range(2):
            main = halo_ref[i, j * 16 : j * 16 + 16, row(1)]
            side = pooled(sides_f[2 * j], sides_f[2 * j + 1])
            put_pooled(main, side, pst_ref, psb_ref, 6 * i + j, 2 * i + j)
        pst_ref[:, row(2 + 2 * i, 2)] = pst_own[:, row(6 * i, 2)]
        pre_ref[:, row(2 * i, 2)] = dot(wc_ref[...], pst_ref[:, row(6 * i, 2)])
        put_features(halo_ref[i, :, row(0)].astype(F32), sides_f[near], jst_ref, 64, 5 * i)
        for d in range(3):
            jst_ref[d * 64 : d * 64 + 32, row(1 + 2 * i, 2)] = jf_own[d * 32 : d * 32 + 32, row(14 * i, 2)]
    prb_ref[...] = dot(wc_ref[...], psb_ref[...])

    def part(own, halo, lo, size, at, edge, length):
        if at < edge:
            return halo[lo : lo + size, row(at)]
        if at < edge + length:
            return own[lo : lo + size, row(at - edge)]
        return halo[lo : lo + size, row(at - length)]

    for k, at in enumerate((0, 1, 8, 9)):
        keep = has_above if at == 0 else has_below if at == 9 else 1.0
        values = [
            sum(part(own, halo, d * 32, 32, at + d, 2, 8) for d in range(3))
            for own, halo in ((pre_own, pre_ref), (prb_own, prb_ref))
        ]
        totals = [
            sum(
                part(own, halo, lo + d * 32, 32, r + d, 3, ROWS)
                for r in (2 * at, 2 * at + 1)
                for d in range(3)
            )
            for own, halo, lo in ((rg_own, rg_ref, 96), (rgb_own, rgb_ref, 0))
        ]
        acts, grads = coarse_row(values, totals, (keep, keep * there))
        for d in range(3):
            for r in ((0,), (1, 2), (3, 4), (5,))[k]:
                jst_ref[d * 64 + 32 : d * 64 + 64, row(r)] = acts[d]
            qst_ref[d * 32 : d * 32 + 32, row(k)] = grads[d]

    put_joined(jst_ref, row(1, 4), jl_ref, row(0, 4))
    ql_ref[0:96, :] = jnp.zeros((96, 2 * COLS), BF)
    ql_ref[96:128, :] = qst_ref[32:64, row(1, 2)]
    for i in range(2):
        for ky in range(3):
            gl_ref[ky * 96 : ky * 96 + 96, row(2 * i, 2)] = gst_ref[:, row(4 + 4 * i - ky, 2)]
            pl_ref[ky * 48 : ky * 48 + 48, row(i)] = pst_ref[:, row(1 + 3 * i + ky)]
    rf = rf_inner[...] + dot_nt(gl_ref[...], jl_ref[...])
    rc = rc_inner[...] + dot_nt(pl_ref[...], ql_ref[...])
    ro_ref[...] = dot(wo_ref[...], jst_ref[...])
    rq_ref[...] = dot(wq_ref[...], qst_ref[...])
    fine, coarse = {}, {}
    for ky in range(3):
        for kx in range(3):
            lo = ky * 96 + (2 - kx) * 32
            fine[ky, 0, kx] = rf[lo + 16 : lo + 32, 0:128]
            fine[ky, 1, kx] = rf[lo : lo + 16, 0:128] + rf[lo + 16 : lo + 32, 128:256]
            fine[ky, 2, kx] = rf[lo : lo + 16, 128:256]
            coarse[ky, kx] = rc[ky * 48 + kx * 16 : ky * 48 + kx * 16 + 16] * 0.5
    lane16 = lanes_of((16, COLS))
    order = [(ky, kz, kx) for ky in range(3) for kz in range(3) for kx in range(3)]
    for i in range(16):
        value = jnp.zeros((16, COLS), F32)
        if i < 14:
            value = jnp.where(lane16 < 48, fine[order[i]], value)
        if i < 13:
            value = jnp.where((lane16 >= 48) & (lane16 < 96), fine[order[14 + i]], value)
        if i < 9:
            value = jnp.where(lane16 >= 96, coarse[i // 3, i % 3], value)
        gw_ref[i * 16 : i * 16 + 16, :] = value.astype(BF)

    flat_ref[0] = out_inner[...]
    flat_ref[1] = gf_inner[...]
    for y in (0, 1, 2, 13, 14, 15):
        value = sum(part(ro_inner, ro_ref, d * 32, 32, y + d, 3, len(FINE)) for d in range(3))
        for z in range(2):
            put_field(flat_ref.at[0], y, z, value[z * 16 : z * 16 + 16])
    out_ref[...] = flat_ref[0].astype(BF)

    for at in (0, 1, 6, 7):
        coarse = sum(part(rq_inner, rq_ref, d * 16, 16, at + d, 2, len(INNER)) for d in range(3))
        coarse = coarse.astype(BF).astype(F32) * 0.125
        for y in (2 * at, 2 * at + 1):
            for z in range(2):
                lo = z * 16
                value = sum(part(rg_own, rg_ref, lo + d * 32, 16, y + 2 + d, 3, ROWS) for d in range(3))
                put_field(flat_ref.at[1], y, z, value + coarse)
    gf_ref[...] = flat_ref[1].astype(BF)


def rest(messages, own, inner, matrices, counts, sides):
    return pl.pallas_call(
        functools.partial(rest_kernel, counts, sides),
        out_shape=(
            pltpu.VMEM((CELLS, COLS), BF),
            pltpu.VMEM((CELLS, COLS), BF),
            jax.ShapeDtypeStruct((256, COLS), BF),
        ),
        scratch_shapes=[
            pltpu.VMEM((2, 32, (SLOTS + sides) * COLS), BF),
            scratch(192, 6, BF),
            scratch(96, 12, BF), scratch(96, 6, BF),
            scratch(48, 8, BF), scratch(48, 4, BF),
            scratch(96, 4, BF),
            scratch(96, 4, F32), scratch(96, 4, F32),
            scratch(192, 6, F32), scratch(96, 6, F32),
            scratch(96, 6, F32),
            scratch(48, 4, F32),
            scratch(288, 4, BF), scratch(256, 4, BF), scratch(144, 2, BF), scratch(128, 2, BF),
            pltpu.VMEM((2, CELLS, COLS), F32),
        ],
        compiler_params=params(),
        cost_estimate=pl.CostEstimate(flops=10**9, bytes_accessed=4 * 10**6, transcendentals=10**5),
        name="rest",
    )(*messages, *own, *inner, *matrices)


def add_kernel(parts_ref, copies_ref):
    total = parts_ref[0].astype(F32)
    for i in range(1, parts_ref.shape[0]):
        total = total + parts_ref[i].astype(F32)
    total = total.astype(BF)
    for i in range(parts_ref.shape[0]):
        copies_ref[i] = total


def add_up(parts):
    return pl.pallas_call(
        add_kernel,
        out_shape=jax.ShapeDtypeStruct(parts.shape, BF),
        compiler_params=pltpu.CompilerParams(vmem_limit_bytes=VMEM_LIMIT),
        name="add_up",
    )(parts)


def spread_kernel(
    fine_scale, coarse_scale,
    sum_ref, out_ref, gf_ref,
    out_hbm, gf_hbm, fine_hbm, coarse_hbm,
    fine_ref, coarse_ref, field_sems, weight_sems,
):
    fields = chunks(((out_ref, out_hbm), (gf_ref, gf_hbm)), field_sems, 4)
    weights = chunks(((fine_ref, fine_hbm), (coarse_ref, coarse_hbm)), weight_sems, 3)
    for copies in fields:
        start(copies)
    for i in range(27):
        at = (i if i < 14 else i - 14) * 16
        value = sum_ref[at : at + 16, :].astype(F32)
        if i >= 14:
            value = pltpu.roll(value, 80, 1)
        fine_ref[i * 16 : i * 16 + 16, :] = value[:, 0:48] * fine_scale
        ky, kz, kx = i // 9, i // 3 % 3, i % 3
        if kz == 1:
            at = (ky * 3 + kx) * 16
            value = pltpu.roll(sum_ref[at : at + 16, :].astype(F32), 32, 1)[:, 0:32] * coarse_scale
        else:
            value = jnp.zeros((16, 32), F32)
        coarse_ref[i * 16 : i * 16 + 16, :] = value
        if i % 9 == 8:
            weights[0][ky].start()
            weights[1][ky].start()
    for copies in fields + weights:
        wait(copies)


def spread(total, output, grad_features, fine_scale, coarse_scale):
    return pl.pallas_call(
        functools.partial(spread_kernel, fine_scale, coarse_scale),
        in_specs=[pl.BlockSpec(memory_space=pltpu.VMEM)] * 3,
        out_specs=(pl.BlockSpec(memory_space=pl.ANY),) * 4,
        out_shape=(
            jax.ShapeDtypeStruct((CELLS, COLS), BF),
            jax.ShapeDtypeStruct((CELLS, COLS), BF),
            jax.ShapeDtypeStruct((TAPS, 48), F32),
            jax.ShapeDtypeStruct((TAPS, 32), F32),
        ),
        scratch_shapes=[
            pltpu.VMEM((TAPS, 48), F32),
            pltpu.VMEM((TAPS, 32), F32),
            pltpu.SemaphoreType.DMA((2, 4)),
            pltpu.SemaphoreType.DMA((2, 3)),
        ],
        compiler_params=params(),
        name="spread",
    )(total, output, grad_features)


def matrices_kernel(
    fine_hbm, coarse_hbm, wo_ref, wg_ref, wc_ref, wq_ref,
    fine_ref, coarse_ref, wide_ref, pieces_ref, blocks_ref, sems,
):
    fine_copies, coarse_copies = chunks(((fine_hbm, fine_ref), (coarse_hbm, coarse_ref)), sems, 3)
    start(fine_copies)
    start(coarse_copies)
    lane = lanes_of((C1, COLS))
    wait(fine_copies)
    wide_ref[:, 0:48] = fine_ref[...].astype(F32)
    for ky in range(3):
        for zo in range(2):
            tiles = [jnp.zeros((C1, COLS), F32) for _ in range(2)]
            for kx in range(3):
                at = ((ky * 3 + 1 - zo) * 3 + kx) * 16
                first, second = (wide_ref[at + i : at + i + 16, :] for i in (0, 48))
                both = (first + second).astype(BF).astype(F32)
                piece = jnp.where(lane < 32, pltpu.roll(second, 16, 1), pltpu.roll(both, 16, 1))
                piece = jnp.where(lane < 16, first, jnp.where(lane < 64, piece, 0.0))
                spot = (2 - kx) * 32 + zo * 16
                pieces_ref[2 - ky, spot : spot + 16, :] = piece
                tiles[kx // 2] = tiles[kx // 2] + (pltpu.roll(piece, 64, 1) if kx == 1 else piece)
            spot = ky * 32 + zo * 16
            wo_ref[spot : spot + 16, 0:128] = tiles[0].astype(BF)
            wo_ref[spot : spot + 16, 128:192] = tiles[1][:, 0:64].astype(BF)
    wait(coarse_copies)
    wide_ref[:, 0:32] = coarse_ref[...].astype(F32)
    for ky in range(3):
        total = jnp.zeros((C1, COLS), F32)
        for kx in range(3):
            at = ((ky * 3 + 1) * 3 + kx) * 16
            value = jnp.where(lane < 32, wide_ref[at : at + 16, :], 0.0)
            blocks_ref[ky, kx * 16 : kx * 16 + 16, :] = value
            spot = (2 - kx) * 32
            total = total + (pltpu.roll(value, spot, 1) if spot else value)
        wq_ref[(2 - ky) * 16 : (2 - ky) * 16 + 16, :] = total[:, 0:96].astype(BF)
    for d in range(3):
        turned = jnp.transpose(pieces_ref[d])[0:64, 0:96].astype(BF)
        wg_ref[d * 32 : d * 32 + 32, :] = turned[0:32]
        wg_ref[96 + d * 32 : 96 + d * 32 + 32, :] = turned[32:64]
        wc_ref[d * 32 : d * 32 + 32, :] = jnp.transpose(blocks_ref[d])[0:32, 0:48].astype(BF)


def weight_matrices(coarse_weight, fine_weight):
    fine = jnp.transpose(fine_weight, (2, 3, 4, 0, 1)).reshape(TAPS, 48)
    coarse = jnp.transpose(coarse_weight, (2, 3, 4, 1, 0)).reshape(TAPS, 32)
    shape = lambda *dims: jax.ShapeDtypeStruct(dims, BF)
    return pl.pallas_call(
        matrices_kernel,
        in_specs=[pl.BlockSpec(memory_space=pltpu.HBM)] * 2,
        out_shape=(shape(96, 192), shape(192, 96), shape(96, 48), shape(48, 96)),
        scratch_shapes=[
            pltpu.VMEM((TAPS, 48), BF),
            pltpu.VMEM((TAPS, 32), BF),
            pltpu.VMEM((TAPS, COLS), F32),
            pltpu.VMEM((3, COLS, COLS), F32),
            pltpu.VMEM((3, COLS, COLS), F32),
            pltpu.SemaphoreType.DMA((2, 3)),
        ],
        compiler_params=params(),
        cost_estimate=pl.CostEstimate(flops=10**6, bytes_accessed=10**6, transcendentals=0),
        name="matrices",
    )(kept_in_hbm(fine), kept_in_hbm(coarse))


def beside_blocks(outer, narrow):
    if outer.shape[1] == COLS:
        return lax.ppermute(outer, "narrow", [(0, 1), (1, 0)])
    right = lax.ppermute(outer[:, :COLS], "narrow", [(i + 1, i) for i in range(narrow - 1)])
    left = lax.ppermute(outer[:, COLS:], "narrow", [(i, i + 1) for i in range(narrow - 1)])
    return jnp.concatenate([right, left], 1)


def shards(features, cotangent, coarse_weight, fine_weight):
    wide, narrow = lax.axis_size("wide"), lax.axis_size("narrow")
    sides = 1 if narrow == 2 else 2
    own, strip, to_odd, to_even = pack(features, cotangent, sides)
    both = ("wide", "narrow")
    even_pairs = [pair for i in range(0, wide, 2) for pair in ((i, i + 1), (i + 1, i))]
    odd_pairs = [
        (i * narrow + n, j * narrow + n)
        for i in range(wide)
        for j in (i + 1 if i % 2 else i - 1,)
        if 0 <= j < wide
        for n in range(narrow)
    ]
    odd_pairs += [
        (i * narrow + n, i * narrow + (n ^ 1)) for i in (0, wide - 1) for n in range(narrow)
    ]
    columns = beside_blocks(strip, narrow)
    wo, wg, wc, wq = weight_matrices(coarse_weight, fine_weight)
    with_columns = lambda message: lax.dynamic_update_slice(message, columns, (0, SLOTS * COLS))
    odd = lax.ppermute(with_columns(to_odd), both, odd_pairs)
    even = lax.ppermute(with_columns(to_even), "wide", even_pairs)
    stacks = own_rows(own, columns, wc, wg, sides)
    inner = inner_rows(stacks, wo, wq, narrow)
    output, grad_features, grads = rest(
        (even, odd), stacks, inner, (wo, wg, wc, wq), (wide, narrow), sides
    )
    devices = wide * narrow
    share = -(-256 // devices)
    grads = jnp.pad(grads, ((0, share * devices - 256), (0, 0))).reshape(devices, share, COLS)
    parts = lax.all_to_all(grads, both, 0, 0, tiled=True)
    total = lax.all_to_all(add_up(parts), both, 0, 0, tiled=True)
    total = total.reshape(share * devices, COLS)[:256]
    all_cells = features.shape[1] * features.shape[2] * features.shape[3] * devices
    output, grad_features, grad_fine, grad_coarse = spread(
        total, output, grad_features, 1.0 / math.sqrt(all_cells), 1.0 / math.sqrt(all_cells // 8)
    )
    grad_fine = jnp.transpose(grad_fine.reshape(3, 3, 3, C1, C1 + C2), (3, 4, 0, 1, 2))
    grad_coarse = jnp.transpose(grad_coarse.reshape(3, 3, 3, C1, C2), (4, 3, 0, 1, 2))
    return (
        output.reshape(features.shape),
        grad_features.reshape(features.shape),
        grad_fine,
        grad_coarse,
    )


def solution(mesh):
    placed = P(None, "wide", None, "narrow")
    return jax.shard_map(
        shards,
        mesh=mesh,
        in_specs=(placed, placed, P(), P()),
        out_specs=(placed, placed, P(), P()),
        check_vma=False,
    )
```

```python
import functools
import math

import jax
import jax.numpy as jnp
from jax import lax
from jax.experimental import pallas as pl
from jax.experimental.pallas import tpu as pltpu
from jax.sharding import PartitionSpec as P

C1, C2 = 16, 32
ROWS, COLS = 16, 128
HALO = 4
BF, F32 = jnp.bfloat16, jnp.float32
VMEM_LIMIT = 20 * 1024 * 1024


def lanes_of(shape):
    return lax.broadcasted_iota(jnp.int32, shape, len(shape) - 1)


def row(index, count=1):
    return slice(index * COLS, (index + count) * COLS)


def pair_sum(value):
    lane = lanes_of(value.shape)
    other = jnp.where(lane % 2 == 0, pltpu.roll(value, COLS - 1, 1), pltpu.roll(value, 1, 1))
    return value + other


def pooled(first, second):
    total = first + second
    return (pair_sum(total[0:16] + total[16:32]) * 0.125).astype(BF)


def dot(a, b):
    return jnp.dot(a, b, preferred_element_type=F32)


def dot_nt(a, b):
    return lax.dot_general(a, b, (((1,), (1,)), ((), ())), preferred_element_type=F32)


def params():
    return pltpu.CompilerParams(vmem_limit_bytes=VMEM_LIMIT)


SLOTS = 5
CELLS = C1 * ROWS * 2
TAPS = 27 * C1


def chunks(pairs, sems, pieces):
    copies = []
    for i, (source, target) in enumerate(pairs):
        rows = source.shape[0] // pieces
        copies.append([
            pltpu.make_async_copy(
                source.at[pl.ds(j * rows, rows)], target.at[pl.ds(j * rows, rows)], sems.at[i, j]
            )
            for j in range(pieces)
        ])
    return copies


def start(copies):
    for copy in copies:
        copy.start()


def wait(copies):
    for copy in copies:
        copy.wait()


def pack_kernel(
    sides, f_hbm, g_hbm, s_ref, strip_ref, odd_ref, even_ref, f_ref, g_ref, wide_ref, base_ref, sems
):
    arrivals = chunks(((f_hbm, f_ref), (g_hbm, g_ref)), sems, 4)
    for copies in arrivals:
        start(copies)
    lane = lanes_of((C1, COLS))
    place = lax.axis_index("narrow")
    odd = lax.axis_index("wide") % 2
    strips = [[jnp.zeros((C1, COLS), F32) for _ in range(sides)] for _ in range(2)]
    for a in range(2):
        wait(arrivals[a])
        wide_ref[...] = (f_ref, g_ref)[a][...].astype(F32)
        for z in range(2):
            chans = slice(a * 32 + z * 16, a * 32 + z * 16 + 16)
            for y in range(ROWS):
                value = wide_ref[pl.ds(2 * y + z, C1, stride=2 * ROWS), :]
                s_ref[chans, row(y)] = value.astype(BF)
                first = 64 * a + HALO * y
                inside = (lane >= first) & (lane < first + HALO)
                for side in range(sides):
                    if sides == 2:
                        shift = (first + HALO * side) % COLS
                    else:
                        shift = lax.rem(first + HALO * (1 - place), COLS)
                    strips[z][side] = jnp.where(inside, pltpu.roll(value, shift, 1), strips[z][side])
    for z in range(2):
        for side in range(sides):
            strip_ref[z * 16 : z * 16 + 16, row(side)] = strips[z][side].astype(BF)
    for to, near, pairs, cot in ((0, ROWS - 1, (6, 7), ROWS - 3), (1, 0, (0, 1), 0)):
        base_ref[to, :, row(0)] = s_ref[0:32, row(near)]
        for i, pair in enumerate(pairs):
            first, second = (s_ref[0:32, row(2 * pair + j)].astype(F32) for j in range(2))
            base_ref[to, i * 16 : i * 16 + 16, row(1)] = pooled(first, second)
        base_ref[to, :, row(2, 3)] = s_ref[32:64, row(cot, 3)]
        for side in range(sides):
            for z in range(2):
                kept = lane % 64 >= 48 if to == 0 else lane % 64 < 16
                value = jnp.where(kept, strips[z][side], 0.0).astype(BF)
                base_ref[to, z * 16 : z * 16 + 16, row(SLOTS + side)] = value
    even_ref[...] = base_ref[odd]
    odd_ref[...] = base_ref[1 - odd]


def kept_in_hbm(array):
    return pltpu.with_memory_space_constraint(array, pltpu.HBM)


def pack(features, cotangent, sides):
    flat = lambda a: kept_in_hbm(a.reshape(CELLS, COLS))
    message = jax.ShapeDtypeStruct((32, (SLOTS + sides) * COLS), BF)
    return pl.pallas_call(
        functools.partial(pack_kernel, sides),
        in_specs=[pl.BlockSpec(memory_space=pltpu.HBM)] * 2,
        out_shape=(
            jax.ShapeDtypeStruct((64, ROWS * COLS), BF),
            jax.ShapeDtypeStruct((32, sides * COLS), BF),
            message,
            message,
        ),
        scratch_shapes=[
            pltpu.VMEM((CELLS, COLS), BF),
            pltpu.VMEM((CELLS, COLS), BF),
            pltpu.VMEM((CELLS, COLS), F32),
            pltpu.VMEM((2, 32, (SLOTS + sides) * COLS), BF),
            pltpu.SemaphoreType.DMA((2, 4)),
        ],
        compiler_params=params(),
        cost_estimate=pl.CostEstimate(flops=10**6, bytes_accessed=10**6, transcendentals=0),
        name="pack",
    )(flat(features), flat(cotangent))


def beside(columns, at):
    lane = lanes_of(columns[0].shape)
    if len(columns) == 1:
        place = lax.axis_index("narrow")
        first = (COLS - HALO) * place
        turned = pltpu.roll(columns[0], lax.rem(COLS - at + first, COLS), 1)
        return jnp.where((lane >= first) & (lane < first + HALO), turned, 0.0)
    right = pltpu.roll(columns[0], (-at) % COLS, 1)
    left = pltpu.roll(columns[1], (COLS - HALO - at) % COLS, 1)
    return jnp.where(lane < HALO, right, jnp.where(lane >= COLS - HALO, left, 0.0))


def turn(main, side, by):
    lane = lanes_of(main.shape)
    a, b = pltpu.roll(main, (-by) % COLS, 1), pltpu.roll(side, (-by) % COLS, 1)
    crossed = lane >= COLS - by if by > 0 else lane < -by
    return jnp.where(crossed, b, a), jnp.where(crossed, a, b)


def put_pooled(main, side, main_ref, side_ref, at, side_at):
    main, side = main.astype(F32), side.astype(F32)
    for d in range(3):
        a, b = (main, side) if d == 1 else turn(main, side, 2 * (d - 1))
        main_ref[d * 16 : d * 16 + 16, row(at)] = a.astype(BF)
        side_ref[d * 16 : d * 16 + 16, row(side_at)] = b.astype(BF)


def put_cotangent(main, side, main_ref, side_ref, at, side_at):
    for d in range(3):
        a, b = (main, side) if d == 1 else turn(main, side, d - 1)
        main_ref[d * 32 : d * 32 + 32, row(at)] = a.astype(BF)
        side_ref[d * 32 : d * 32 + 32, row(side_at)] = b.astype(BF)


def put_features(main, side, ref, step, at):
    for d in range(3):
        a = main if d == 1 else turn(main, side, d - 1)[0]
        ref[d * step : d * step + 32, row(at)] = a.astype(BF)


def coarse_row(values, totals, keeps):
    act, grad = [], []
    for value, total, kept in zip(values, totals, keeps):
        sig = 1.0 / (1.0 + jnp.exp(-value))
        act.append((value * sig * kept).astype(BF).astype(F32))
        grad_act = pair_sum(total).astype(BF).astype(F32)
        grad_pre = grad_act * (sig * (1.0 + value * (1.0 - sig)))
        grad.append((grad_pre * kept).astype(BF).astype(F32))
    acts = [act[0] if d == 1 else turn(act[0], act[1], d - 1)[0] for d in range(3)]
    grads = [grad[0] if d == 1 else turn(grad[0], grad[1], 2 * (d - 1))[0] for d in range(3)]
    return [a.astype(BF) for a in acts], [g.astype(BF) for g in grads]


def column_masks(count):
    n = lax.axis_index("narrow")
    flag = lambda is_there: jnp.where(is_there, 1.0, 0.0)
    return jnp.where(lanes_of((C2, COLS)) < 64, flag(n < count - 1), flag(n > 0))


INNER = range(1, ROWS // 2 - 1)


def own_kernel(
    sides,
    s_ref, columns_ref, wc_ref, wg_ref,
    pst_ref, jf_ref, gst_ref, pre_ref, prb_ref, rg_ref, rgb_ref,
    psb_ref, gsb_ref,
):
    columns = [columns_ref[:, row(side)].astype(F32) for side in range(sides)]
    last = None
    for y in range(ROWS):
        main, side = s_ref[0:32, row(y)].astype(F32), beside(columns, HALO * y)
        put_features(main, side, jf_ref, 32, y)
        if y % 2 == 1:
            means = [pooled(a, b) for a, b in zip(last, (main, side))]
            put_pooled(*means, pst_ref, psb_ref, y // 2, y // 2)
        last = (main, side)
        main, side = s_ref[32:64, row(y)].astype(F32), beside(columns, 64 + HALO * y)
        put_cotangent(main, side, gst_ref, gsb_ref, y, y)
    pre_ref[...] = dot(wc_ref[...], pst_ref[...])
    prb_ref[...] = dot(wc_ref[...], psb_ref[...])
    rg_ref[...] = dot(wg_ref[...], gst_ref[...])
    rgb_ref[...] = dot(wg_ref[96:192, :], gsb_ref[...])


def shaped(rows_, lanes_, kind):
    return jax.ShapeDtypeStruct((rows_, lanes_ * COLS), kind)


def scratch(rows_, lanes_, kind):
    return pltpu.VMEM((rows_, lanes_ * COLS), kind)


def own_rows(s, columns, wc, wg, sides):
    half = ROWS // 2
    return pl.pallas_call(
        functools.partial(own_kernel, sides),
        out_shape=(
            shaped(48, half, BF), shaped(96, ROWS, BF), shaped(96, ROWS, BF),
            shaped(96, half, F32), shaped(96, half, F32),
            shaped(192, ROWS, F32), shaped(96, ROWS, F32),
        ),
        scratch_shapes=[scratch(48, half, BF), scratch(96, ROWS, BF)],
        compiler_params=params(),
        cost_estimate=pl.CostEstimate(flops=10**9, bytes_accessed=4 * 10**6, transcendentals=0),
        name="own_rows",
    )(s, columns, wc, wg)


def put_joined(jst_ref, at, jl_ref, to):
    for lo in (0, 48):
        jl_ref[lo : lo + 16, to] = jst_ref[64:80, at]
        jl_ref[lo + 16 : lo + 48, to] = jst_ref[96:128, at]
        jl_ref[128 + lo : 128 + lo + 48, to] = jst_ref[80:128, at]
    for lo in (96, 224):
        jl_ref[lo : lo + 32, to] = jnp.zeros((32, to.stop - to.start), BF)


def put_field(flat_ref, y, plane, value):
    flat_ref[pl.ds(2 * y + plane, C1, stride=2 * ROWS), :] = value


FINE = range(2 * INNER.start, 2 * INNER.stop)


def inner_kernel(
    count,
    pst_ref, jf_ref, gst_ref, pre_ref, prb_ref, rg_ref, rgb_ref, wo_ref, wq_ref,
    out_ref, gf_ref, ro_ref, rq_ref, rf_ref, rc_ref,
    jst_ref, qst_ref, gl_ref, jl_ref, pl_ref, ql_ref,
):
    rows, coarse_rows = len(FINE), len(INNER)
    there = column_masks(count)
    for d in range(3):
        jst_ref[d * 64 : d * 64 + 32, :] = jf_ref[d * 32 : d * 32 + 32, row(FINE.start, rows)]
    for at in INNER:
        values = [
            sum(ref[d * 32 : d * 32 + 32, row(at + d - 1)] for d in range(3)) for ref in (pre_ref, prb_ref)
        ]
        totals = [
            sum(
                ref[lo + d * 32 : lo + d * 32 + 32, row(r + d - 1)]
                for r in (2 * at, 2 * at + 1)
                for d in range(3)
            )
            for ref, lo in ((rg_ref, 96), (rgb_ref, 0))
        ]
        acts, grads = coarse_row(values, totals, (1.0, there))
        for d in range(3):
            for r in (2 * at, 2 * at + 1):
                jst_ref[d * 64 + 32 : d * 64 + 64, row(r - FINE.start)] = acts[d]
            qst_ref[d * 32 : d * 32 + 32, row(at - INNER.start)] = grads[d]
    ro_ref[...] = dot(wo_ref[...], jst_ref[...])
    rq_ref[...] = dot(wq_ref[...], qst_ref[...])

    put_joined(jst_ref, row(0, rows), jl_ref, row(0, rows))
    ql_ref[0:96, :] = jnp.zeros((96, coarse_rows * COLS), BF)
    ql_ref[96:128, :] = qst_ref[32:64, :]
    for ky in range(3):
        gl_ref[ky * 96 : ky * 96 + 96, :] = gst_ref[:, row(FINE.start + 1 - ky, rows)]
        pl_ref[ky * 48 : ky * 48 + 48, :] = pst_ref[:, row(INNER.start + ky - 1, coarse_rows)]
    rf_ref[...] = dot_nt(gl_ref[...], jl_ref[...])
    rc_ref[...] = dot_nt(pl_ref[...], ql_ref[...])

    for y in range(FINE.start + 1, FINE.stop - 1):
        value = sum(ro_ref[d * 32 : d * 32 + 32, row(y - 1 + d - FINE.start)] for d in range(3))
        for z in range(2):
            put_field(out_ref, y, z, value[z * 16 : z * 16 + 16])
    for at in range(INNER.start + 1, INNER.stop - 1):
        coarse = sum(rq_ref[d * 16 : d * 16 + 16, row(at - 1 + d - INNER.start)] for d in range(3))
        coarse = coarse.astype(BF).astype(F32) * 0.125
        for y in (2 * at, 2 * at + 1):
            for z in range(2):
                lo = z * 16
                value = sum(rg_ref[lo + d * 32 : lo + d * 32 + 16, row(y - 1 + d)] for d in range(3))
                put_field(gf_ref, y, z, value + coarse)


def inner_rows(own, wo, wq, count):
    rows, coarse_rows = len(FINE), len(INNER)
    return pl.pallas_call(
        functools.partial(inner_kernel, count),
        out_shape=(
            shaped(CELLS, 1, F32), shaped(CELLS, 1, F32),
            shaped(96, rows, F32), shaped(48, coarse_rows, F32),
            shaped(288, 2, F32), shaped(144, 1, F32),
        ),
        scratch_shapes=[
            scratch(192, rows, BF), scratch(96, coarse_rows, BF),
            scratch(288, rows, BF), scratch(256, rows, BF),
            scratch(144, coarse_rows, BF), scratch(128, coarse_rows, BF),
        ],
        compiler_params=params(),
        cost_estimate=pl.CostEstimate(flops=10**9, bytes_accessed=4 * 10**6, transcendentals=10**5),
        name="inner_rows",
    )(*own, wo, wq)


def rest_kernel(
    counts, sides,
    odd_ref, even_ref, corners_ref,
    pst_own, jf_own, gst_own, pre_own, prb_own, rg_own, rgb_own,
    out_inner, gf_inner, ro_inner, rq_inner, rf_inner, rc_inner,
    wo_ref, wg_ref, wc_ref, wq_ref,
    out_ref, gf_ref, gw_ref,
    halo_ref, jst_ref, gst_ref, gsb_ref, pst_ref, psb_ref, qst_ref,
    pre_ref, prb_ref, rg_ref, rgb_ref, ro_ref, rq_ref, gl_ref, jl_ref, pl_ref, ql_ref, flat_ref,
):
    w = lax.axis_index("wide")
    there = column_masks(counts[1])
    flag = lambda is_there: jnp.where(is_there, 1.0, 0.0)
    has_above, has_below = flag(w > 0), flag(w < counts[0] - 1)

    odd = w % 2
    halo_ref[1 - odd] = even_ref[:, row(0, SLOTS)]
    inside = flag((w > 0) & (w < counts[0] - 1))
    halo_ref[odd] = (odd_ref[:, row(0, SLOTS)].astype(F32) * inside).astype(BF)
    columns = [corners_ref[:, row(side)].astype(F32) for side in range(sides)]

    for i in range(2):
        lane = HALO * (ROWS - HALO) if i == 0 else 0
        for j in range(3):
            main = halo_ref[i, :, row(2 + j)].astype(F32)
            side = beside(columns, 64 + lane + HALO * (j + 1 - i))
            put_cotangent(main, side, gst_ref, gsb_ref, 9 * i + j, 3 * i + j)
        gst_ref[:, row(3 + 3 * i, 3)] = gst_own[:, row(13 * i, 3)]
        rg_ref[:, row(3 * i, 3)] = dot(wg_ref[...], gst_ref[:, row(9 * i, 3)])
    rgb_ref[...] = dot(wg_ref[96:192, :], gsb_ref[...])
    for i in range(2):
        lane = HALO * (ROWS - HALO) if i == 0 else 0
        sides_f = [beside(columns, lane + HALO * r) for r in range(HALO)]
        near = HALO - 1 if i == 0 else 0
        for j in range(2):
            main = halo_ref[i, j * 16 : j * 16 + 16, row(1)]
            side = pooled(sides_f[2 * j], sides_f[2 * j + 1])
            put_pooled(main, side, pst_ref, psb_ref, 6 * i + j, 2 * i + j)
        pst_ref[:, row(2 + 2 * i, 2)] = pst_own[:, row(6 * i, 2)]
        pre_ref[:, row(2 * i, 2)] = dot(wc_ref[...], pst_ref[:, row(6 * i, 2)])
        put_features(halo_ref[i, :, row(0)].astype(F32), sides_f[near], jst_ref, 64, 5 * i)
        for d in range(3):
            jst_ref[d * 64 : d * 64 + 32, row(1 + 2 * i, 2)] = jf_own[d * 32 : d * 32 + 32, row(14 * i, 2)]
    prb_ref[...] = dot(wc_ref[...], psb_ref[...])

    def part(own, halo, lo, size, at, edge, length):
        if at < edge:
            return halo[lo : lo + size, row(at)]
        if at < edge + length:
            return own[lo : lo + size, row(at - edge)]
        return halo[lo : lo + size, row(at - length)]

    for k, at in enumerate((0, 1, 8, 9)):
        keep = has_above if at == 0 else has_below if at == 9 else 1.0
        values = [
            sum(part(own, halo, d * 32, 32, at + d, 2, 8) for d in range(3))
            for own, halo in ((pre_own, pre_ref), (prb_own, prb_ref))
        ]
        totals = [
            sum(
                part(own, halo, lo + d * 32, 32, r + d, 3, ROWS)
                for r in (2 * at, 2 * at + 1)
                for d in range(3)
            )
            for own, halo, lo in ((rg_own, rg_ref, 96), (rgb_own, rgb_ref, 0))
        ]
        acts, grads = coarse_row(values, totals, (keep, keep * there))
        for d in range(3):
            for r in ((0,), (1, 2), (3, 4), (5,))[k]:
                jst_ref[d * 64 + 32 : d * 64 + 64, row(r)] = acts[d]
            qst_ref[d * 32 : d * 32 + 32, row(k)] = grads[d]

    put_joined(jst_ref, row(1, 4), jl_ref, row(0, 4))
    ql_ref[0:96, :] = jnp.zeros((96, 2 * COLS), BF)
    ql_ref[96:128, :] = qst_ref[32:64, row(1, 2)]
    for i in range(2):
        for ky in range(3):
            gl_ref[ky * 96 : ky * 96 + 96, row(2 * i, 2)] = gst_ref[:, row(4 + 4 * i - ky, 2)]
            pl_ref[ky * 48 : ky * 48 + 48, row(i)] = pst_ref[:, row(1 + 3 * i + ky)]
    rf = rf_inner[...] + dot_nt(gl_ref[...], jl_ref[...])
    rc = rc_inner[...] + dot_nt(pl_ref[...], ql_ref[...])
    ro_ref[...] = dot(wo_ref[...], jst_ref[...])
    rq_ref[...] = dot(wq_ref[...], qst_ref[...])
    fine, coarse = {}, {}
    for ky in range(3):
        for kx in range(3):
            lo = ky * 96 + (2 - kx) * 32
            fine[ky, 0, kx] = rf[lo + 16 : lo + 32, 0:128]
            fine[ky, 1, kx] = rf[lo : lo + 16, 0:128] + rf[lo + 16 : lo + 32, 128:256]
            fine[ky, 2, kx] = rf[lo : lo + 16, 128:256]
            coarse[ky, kx] = rc[ky * 48 + kx * 16 : ky * 48 + kx * 16 + 16] * 0.5
    lane16 = lanes_of((16, COLS))
    order = [(ky, kz, kx) for ky in range(3) for kz in range(3) for kx in range(3)]
    for i in range(16):
        value = jnp.zeros((16, COLS), F32)
        if i < 14:
            value = jnp.where(lane16 < 48, fine[order[i]], value)
        if i < 13:
            value = jnp.where((lane16 >= 48) & (lane16 < 96), fine[order[14 + i]], value)
        if i < 9:
            value = jnp.where(lane16 >= 96, coarse[i // 3, i % 3], value)
        gw_ref[i * 16 : i * 16 + 16, :] = value.astype(BF)

    flat_ref[0] = out_inner[...]
    flat_ref[1] = gf_inner[...]
    for y in (0, 1, 2, 13, 14, 15):
        value = sum(part(ro_inner, ro_ref, d * 32, 32, y + d, 3, len(FINE)) for d in range(3))
        for z in range(2):
            put_field(flat_ref.at[0], y, z, value[z * 16 : z * 16 + 16])
    out_ref[...] = flat_ref[0].astype(BF)

    for at in (0, 1, 6, 7):
        coarse = sum(part(rq_inner, rq_ref, d * 16, 16, at + d, 2, len(INNER)) for d in range(3))
        coarse = coarse.astype(BF).astype(F32) * 0.125
        for y in (2 * at, 2 * at + 1):
            for z in range(2):
                lo = z * 16
                value = sum(part(rg_own, rg_ref, lo + d * 32, 16, y + 2 + d, 3, ROWS) for d in range(3))
                put_field(flat_ref.at[1], y, z, value + coarse)
    gf_ref[...] = flat_ref[1].astype(BF)


def rest(messages, own, inner, matrices, counts, sides):
    return pl.pallas_call(
        functools.partial(rest_kernel, counts, sides),
        out_shape=(
            pltpu.VMEM((CELLS, COLS), BF),
            pltpu.VMEM((CELLS, COLS), BF),
            jax.ShapeDtypeStruct((256, COLS), BF),
        ),
        scratch_shapes=[
            pltpu.VMEM((2, 32, SLOTS * COLS), BF),
            scratch(192, 6, BF),
            scratch(96, 12, BF), scratch(96, 6, BF),
            scratch(48, 8, BF), scratch(48, 4, BF),
            scratch(96, 4, BF),
            scratch(96, 4, F32), scratch(96, 4, F32),
            scratch(192, 6, F32), scratch(96, 6, F32),
            scratch(96, 6, F32),
            scratch(48, 4, F32),
            scratch(288, 4, BF), scratch(256, 4, BF), scratch(144, 2, BF), scratch(128, 2, BF),
            pltpu.VMEM((2, CELLS, COLS), F32),
        ],
        compiler_params=params(),
        cost_estimate=pl.CostEstimate(flops=10**9, bytes_accessed=4 * 10**6, transcendentals=10**5),
        name="rest",
    )(*messages, *own, *inner, *matrices)


def add_kernel(parts_ref, copies_ref):
    total = parts_ref[0].astype(F32)
    for i in range(1, parts_ref.shape[0]):
        total = total + parts_ref[i].astype(F32)
    total = total.astype(BF)
    for i in range(parts_ref.shape[0]):
        copies_ref[i] = total


def add_up(parts):
    return pl.pallas_call(
        add_kernel,
        out_shape=jax.ShapeDtypeStruct(parts.shape, BF),
        compiler_params=pltpu.CompilerParams(vmem_limit_bytes=VMEM_LIMIT),
        name="add_up",
    )(parts)


def spread_kernel(
    fine_scale, coarse_scale,
    sum_ref, out_ref, gf_ref,
    out_hbm, gf_hbm, fine_hbm, coarse_hbm,
    fine_ref, coarse_ref, field_sems, weight_sems,
):
    fields = chunks(((out_ref, out_hbm), (gf_ref, gf_hbm)), field_sems, 4)
    weights = chunks(((fine_ref, fine_hbm), (coarse_ref, coarse_hbm)), weight_sems, 3)
    for copies in fields:
        start(copies)
    for i in range(27):
        at = (i if i < 14 else i - 14) * 16
        value = sum_ref[at : at + 16, :].astype(F32)
        if i >= 14:
            value = pltpu.roll(value, 80, 1)
        fine_ref[i * 16 : i * 16 + 16, :] = value[:, 0:48] * fine_scale
        ky, kz, kx = i // 9, i // 3 % 3, i % 3
        if kz == 1:
            at = (ky * 3 + kx) * 16
            value = pltpu.roll(sum_ref[at : at + 16, :].astype(F32), 32, 1)[:, 0:32] * coarse_scale
        else:
            value = jnp.zeros((16, 32), F32)
        coarse_ref[i * 16 : i * 16 + 16, :] = value
        if i % 9 == 8:
            weights[0][ky].start()
            weights[1][ky].start()
    for copies in fields + weights:
        wait(copies)


def spread(total, output, grad_features, fine_scale, coarse_scale):
    return pl.pallas_call(
        functools.partial(spread_kernel, fine_scale, coarse_scale),
        in_specs=[pl.BlockSpec(memory_space=pltpu.VMEM)] * 3,
        out_specs=(pl.BlockSpec(memory_space=pl.ANY),) * 4,
        out_shape=(
            jax.ShapeDtypeStruct((CELLS, COLS), BF),
            jax.ShapeDtypeStruct((CELLS, COLS), BF),
            jax.ShapeDtypeStruct((TAPS, 48), F32),
            jax.ShapeDtypeStruct((TAPS, 32), F32),
        ),
        scratch_shapes=[
            pltpu.VMEM((TAPS, 48), F32),
            pltpu.VMEM((TAPS, 32), F32),
            pltpu.SemaphoreType.DMA((2, 4)),
            pltpu.SemaphoreType.DMA((2, 3)),
        ],
        compiler_params=params(),
        name="spread",
    )(total, output, grad_features)


def matrices_kernel(
    fine_hbm, coarse_hbm, wo_ref, wg_ref, wc_ref, wq_ref,
    fine_ref, coarse_ref, wide_ref, pieces_ref, blocks_ref, sems,
):
    fine_copies, coarse_copies = chunks(((fine_hbm, fine_ref), (coarse_hbm, coarse_ref)), sems, 3)
    start(fine_copies)
    start(coarse_copies)
    lane = lanes_of((C1, COLS))
    wait(fine_copies)
    wide_ref[:, 0:48] = fine_ref[...].astype(F32)
    for ky in range(3):
        for zo in range(2):
            tiles = [jnp.zeros((C1, COLS), F32) for _ in range(2)]
            for kx in range(3):
                at = ((ky * 3 + 1 - zo) * 3 + kx) * 16
                first, second = (wide_ref[at + i : at + i + 16, :] for i in (0, 48))
                both = (first + second).astype(BF).astype(F32)
                piece = jnp.where(lane < 32, pltpu.roll(second, 16, 1), pltpu.roll(both, 16, 1))
                piece = jnp.where(lane < 16, first, jnp.where(lane < 64, piece, 0.0))
                spot = (2 - kx) * 32 + zo * 16
                pieces_ref[2 - ky, spot : spot + 16, :] = piece
                tiles[kx // 2] = tiles[kx // 2] + (pltpu.roll(piece, 64, 1) if kx == 1 else piece)
            spot = ky * 32 + zo * 16
            wo_ref[spot : spot + 16, 0:128] = tiles[0].astype(BF)
            wo_ref[spot : spot + 16, 128:192] = tiles[1][:, 0:64].astype(BF)
    wait(coarse_copies)
    wide_ref[:, 0:32] = coarse_ref[...].astype(F32)
    for ky in range(3):
        total = jnp.zeros((C1, COLS), F32)
        for kx in range(3):
            at = ((ky * 3 + 1) * 3 + kx) * 16
            value = jnp.where(lane < 32, wide_ref[at : at + 16, :], 0.0)
            blocks_ref[ky, kx * 16 : kx * 16 + 16, :] = value
            spot = (2 - kx) * 32
            total = total + (pltpu.roll(value, spot, 1) if spot else value)
        wq_ref[(2 - ky) * 16 : (2 - ky) * 16 + 16, :] = total[:, 0:96].astype(BF)
    for d in range(3):
        turned = jnp.transpose(pieces_ref[d])[0:64, 0:96].astype(BF)
        wg_ref[d * 32 : d * 32 + 32, :] = turned[0:32]
        wg_ref[96 + d * 32 : 96 + d * 32 + 32, :] = turned[32:64]
        wc_ref[d * 32 : d * 32 + 32, :] = jnp.transpose(blocks_ref[d])[0:32, 0:48].astype(BF)


def weight_matrices(coarse_weight, fine_weight):
    fine = jnp.transpose(fine_weight, (2, 3, 4, 0, 1)).reshape(TAPS, 48)
    coarse = jnp.transpose(coarse_weight, (2, 3, 4, 1, 0)).reshape(TAPS, 32)
    shape = lambda *dims: jax.ShapeDtypeStruct(dims, BF)
    return pl.pallas_call(
        matrices_kernel,
        in_specs=[pl.BlockSpec(memory_space=pltpu.HBM)] * 2,
        out_shape=(shape(96, 192), shape(192, 96), shape(96, 48), shape(48, 96)),
        scratch_shapes=[
            pltpu.VMEM((TAPS, 48), BF),
            pltpu.VMEM((TAPS, 32), BF),
            pltpu.VMEM((TAPS, COLS), F32),
            pltpu.VMEM((3, COLS, COLS), F32),
            pltpu.VMEM((3, COLS, COLS), F32),
            pltpu.SemaphoreType.DMA((2, 3)),
        ],
        compiler_params=params(),
        cost_estimate=pl.CostEstimate(flops=10**6, bytes_accessed=10**6, transcendentals=0),
        name="matrices",
    )(kept_in_hbm(fine), kept_in_hbm(coarse))


def beside_blocks(outer, narrow):
    if outer.shape[1] == COLS:
        return lax.ppermute(outer, "narrow", [(0, 1), (1, 0)])
    right = lax.ppermute(outer[:, :COLS], "narrow", [(i + 1, i) for i in range(narrow - 1)])
    left = lax.ppermute(outer[:, COLS:], "narrow", [(i, i + 1) for i in range(narrow - 1)])
    return jnp.concatenate([right, left], 1)


def shards(features, cotangent, coarse_weight, fine_weight):
    wide, narrow = lax.axis_size("wide"), lax.axis_size("narrow")
    sides = 1 if narrow == 2 else 2
    own, strip, to_odd, to_even = pack(features, cotangent, sides)
    both = ("wide", "narrow")
    even_pairs = [pair for i in range(0, wide, 2) for pair in ((i, i + 1), (i + 1, i))]
    odd_pairs = [
        (i * narrow + n, j * narrow + n)
        for i in range(wide)
        for j in (i + 1 if i % 2 else i - 1,)
        if 0 <= j < wide
        for n in range(narrow)
    ]
    odd_pairs += [
        (i * narrow + n, i * narrow + (n ^ 1)) for i in (0, wide - 1) for n in range(narrow)
    ]
    odd = lax.ppermute(to_odd, both, odd_pairs)
    even = lax.ppermute(to_even, "wide", even_pairs)
    columns = beside_blocks(strip, narrow)
    wo, wg, wc, wq = weight_matrices(coarse_weight, fine_weight)
    place = lax.axis_index("wide")
    inside = jnp.where((place > 0) & (place < wide - 1), 1.0, 0.0).astype(BF)
    corners = odd[:, SLOTS * COLS :] * inside + even[:, SLOTS * COLS :]
    columns, _ = lax.optimization_barrier((columns, corners))
    stacks = own_rows(own, columns, wc, wg, sides)
    inner = inner_rows(stacks, wo, wq, narrow)
    corners = beside_blocks(corners, narrow)
    output, grad_features, grads = rest(
        (odd, even, corners), stacks, inner, (wo, wg, wc, wq), (wide, narrow), sides
    )
    devices = wide * narrow
    share = -(-256 // devices)
    grads = jnp.pad(grads, ((0, share * devices - 256), (0, 0))).reshape(devices, share, COLS)
    parts = lax.all_to_all(grads, both, 0, 0, tiled=True)
    total = lax.all_to_all(add_up(parts), both, 0, 0, tiled=True)
    total = total.reshape(share * devices, COLS)[:256]
    all_cells = features.shape[1] * features.shape[2] * features.shape[3] * devices
    output, grad_features, grad_fine, grad_coarse = spread(
        total, output, grad_features, 1.0 / math.sqrt(all_cells), 1.0 / math.sqrt(all_cells // 8)
    )
    grad_fine = jnp.transpose(grad_fine.reshape(3, 3, 3, C1, C1 + C2), (3, 4, 0, 1, 2))
    grad_coarse = jnp.transpose(grad_coarse.reshape(3, 3, 3, C1, C2), (4, 3, 0, 1, 2))
    return (
        output.reshape(features.shape),
        grad_features.reshape(features.shape),
        grad_fine,
        grad_coarse,
    )


def solution(mesh):
    placed = P(None, "wide", None, "narrow")
    return jax.shard_map(
        shards,
        mesh=mesh,
        in_specs=(placed, placed, P(), P()),
        out_specs=(placed, placed, P(), P()),
        check_vma=False,
    )
```

```python
import functools
import math

import jax
import jax.numpy as jnp
from jax import lax
from jax.experimental import pallas as pl
from jax.experimental.pallas import tpu as pltpu
from jax.sharding import PartitionSpec as P

C1, C2 = 16, 32
ROWS, COLS = 16, 128
HALO = 4
BF, F32 = jnp.bfloat16, jnp.float32
VMEM_LIMIT = 20 * 1024 * 1024


def lanes_of(shape):
    return lax.broadcasted_iota(jnp.int32, shape, len(shape) - 1)


def row(index, count=1):
    return slice(index * COLS, (index + count) * COLS)


def pair_sum(value):
    lane = lanes_of(value.shape)
    other = jnp.where(lane % 2 == 0, pltpu.roll(value, COLS - 1, 1), pltpu.roll(value, 1, 1))
    return value + other


def pooled(first, second):
    total = first + second
    return (pair_sum(total[0:16] + total[16:32]) * 0.125).astype(BF)


def dot(a, b):
    return jnp.dot(a, b, preferred_element_type=F32)


def dot_nt(a, b):
    return lax.dot_general(a, b, (((1,), (1,)), ((), ())), preferred_element_type=F32)


def params():
    return pltpu.CompilerParams(vmem_limit_bytes=VMEM_LIMIT)


SLOTS = 5
CELLS = C1 * ROWS * 2
TAPS = 27 * C1


def chunks(pairs, sems, pieces):
    copies = []
    for i, (source, target) in enumerate(pairs):
        rows = source.shape[0] // pieces
        copies.append([
            pltpu.make_async_copy(
                source.at[pl.ds(j * rows, rows)], target.at[pl.ds(j * rows, rows)], sems.at[i, j]
            )
            for j in range(pieces)
        ])
    return copies


def start(copies):
    for copy in copies:
        copy.start()


def wait(copies):
    for copy in copies:
        copy.wait()


def pack_kernel(
    sides, f_hbm, g_hbm, s_ref, strip_ref, odd_ref, even_ref, f_ref, g_ref, wide_ref, base_ref, sems
):
    arrivals = chunks(((f_hbm, f_ref), (g_hbm, g_ref)), sems, 2)
    for copies in arrivals:
        start(copies)
    lane = lanes_of((C1, COLS))
    place = lax.axis_index("narrow")
    odd = lax.axis_index("wide") % 2
    strips = [[jnp.zeros((C1, COLS), F32) for _ in range(sides)] for _ in range(2)]
    for a in range(2):
        wait(arrivals[a])
        wide_ref[...] = (f_ref, g_ref)[a][...].astype(F32)
        for z in range(2):
            chans = slice(a * 32 + z * 16, a * 32 + z * 16 + 16)
            for y in range(ROWS):
                value = wide_ref[pl.ds(2 * y + z, C1, stride=2 * ROWS), :]
                s_ref[chans, row(y)] = value.astype(BF)
                first = 64 * a + HALO * y
                inside = (lane >= first) & (lane < first + HALO)
                for side in range(sides):
                    if sides == 2:
                        shift = (first + HALO * side) % COLS
                    else:
                        shift = lax.rem(first + HALO * (1 - place), COLS)
                    strips[z][side] = jnp.where(inside, pltpu.roll(value, shift, 1), strips[z][side])
    for z in range(2):
        for side in range(sides):
            strip_ref[z * 16 : z * 16 + 16, row(side)] = strips[z][side].astype(BF)
    for to, near, pairs, cot in ((0, ROWS - 1, (6, 7), ROWS - 3), (1, 0, (0, 1), 0)):
        base_ref[to, :, row(0)] = s_ref[0:32, row(near)]
        for i, pair in enumerate(pairs):
            first, second = (s_ref[0:32, row(2 * pair + j)].astype(F32) for j in range(2))
            base_ref[to, i * 16 : i * 16 + 16, row(1)] = pooled(first, second)
        base_ref[to, :, row(2, 3)] = s_ref[32:64, row(cot, 3)]
    even_ref[:, row(0, SLOTS)] = base_ref[odd]
    odd_ref[:, row(0, SLOTS)] = base_ref[1 - odd]
    even_ref[:, row(SLOTS, sides)] = jnp.zeros((32, sides * COLS), BF)
    odd_ref[:, row(SLOTS, sides)] = jnp.zeros((32, sides * COLS), BF)


def kept_in_hbm(array):
    return pltpu.with_memory_space_constraint(array, pltpu.HBM)


def pack(features, cotangent, sides):
    flat = lambda a: kept_in_hbm(a.reshape(CELLS, COLS))
    message = jax.ShapeDtypeStruct((32, (SLOTS + sides) * COLS), BF)
    return pl.pallas_call(
        functools.partial(pack_kernel, sides),
        in_specs=[pl.BlockSpec(memory_space=pltpu.HBM)] * 2,
        out_shape=(
            jax.ShapeDtypeStruct((64, ROWS * COLS), BF),
            jax.ShapeDtypeStruct((32, sides * COLS), BF),
            message,
            message,
        ),
        scratch_shapes=[
            pltpu.VMEM((CELLS, COLS), BF),
            pltpu.VMEM((CELLS, COLS), BF),
            pltpu.VMEM((CELLS, COLS), F32),
            pltpu.VMEM((2, 32, SLOTS * COLS), BF),
            pltpu.SemaphoreType.DMA((2, 2)),
        ],
        compiler_params=params(),
        cost_estimate=pl.CostEstimate(flops=10**6, bytes_accessed=10**6, transcendentals=0),
        name="pack",
    )(flat(features), flat(cotangent))


def beside(columns, at):
    lane = lanes_of(columns[0].shape)
    if len(columns) == 1:
        place = lax.axis_index("narrow")
        first = (COLS - HALO) * place
        turned = pltpu.roll(columns[0], lax.rem(COLS - at + first, COLS), 1)
        return jnp.where((lane >= first) & (lane < first + HALO), turned, 0.0)
    right = pltpu.roll(columns[0], (-at) % COLS, 1)
    left = pltpu.roll(columns[1], (COLS - HALO - at) % COLS, 1)
    return jnp.where(lane < HALO, right, jnp.where(lane >= COLS - HALO, left, 0.0))


def turn(main, side, by):
    lane = lanes_of(main.shape)
    a, b = pltpu.roll(main, (-by) % COLS, 1), pltpu.roll(side, (-by) % COLS, 1)
    crossed = lane >= COLS - by if by > 0 else lane < -by
    return jnp.where(crossed, b, a), jnp.where(crossed, a, b)


def put_pooled(main, side, main_ref, side_ref, at, side_at):
    main, side = main.astype(F32), side.astype(F32)
    for d in range(3):
        a, b = (main, side) if d == 1 else turn(main, side, 2 * (d - 1))
        main_ref[d * 16 : d * 16 + 16, row(at)] = a.astype(BF)
        side_ref[d * 16 : d * 16 + 16, row(side_at)] = b.astype(BF)


def put_cotangent(main, side, main_ref, side_ref, at, side_at):
    for d in range(3):
        a, b = (main, side) if d == 1 else turn(main, side, d - 1)
        main_ref[d * 32 : d * 32 + 32, row(at)] = a.astype(BF)
        side_ref[d * 32 : d * 32 + 32, row(side_at)] = b.astype(BF)


def put_features(main, side, ref, step, at):
    for d in range(3):
        a = main if d == 1 else turn(main, side, d - 1)[0]
        ref[d * step : d * step + 32, row(at)] = a.astype(BF)


def coarse_row(values, totals, keeps):
    act, grad = [], []
    for value, total, kept in zip(values, totals, keeps):
        sig = 1.0 / (1.0 + jnp.exp(-value))
        act.append((value * sig * kept).astype(BF).astype(F32))
        grad_act = pair_sum(total).astype(BF).astype(F32)
        grad_pre = grad_act * (sig * (1.0 + value * (1.0 - sig)))
        grad.append((grad_pre * kept).astype(BF).astype(F32))
    acts = [act[0] if d == 1 else turn(act[0], act[1], d - 1)[0] for d in range(3)]
    grads = [grad[0] if d == 1 else turn(grad[0], grad[1], 2 * (d - 1))[0] for d in range(3)]
    return [a.astype(BF) for a in acts], [g.astype(BF) for g in grads]


def column_masks(count):
    n = lax.axis_index("narrow")
    flag = lambda is_there: jnp.where(is_there, 1.0, 0.0)
    return jnp.where(lanes_of((C2, COLS)) < 64, flag(n < count - 1), flag(n > 0))


INNER = range(1, ROWS // 2 - 1)


def own_kernel(
    sides,
    s_ref, columns_ref, wc_ref, wg_ref,
    pst_ref, jf_ref, gst_ref, pre_ref, prb_ref, rg_ref, rgb_ref,
    psb_ref, gsb_ref,
):
    columns = [columns_ref[:, row(side)].astype(F32) for side in range(sides)]
    last = None
    for y in range(ROWS):
        main, side = s_ref[0:32, row(y)].astype(F32), beside(columns, HALO * y)
        put_features(main, side, jf_ref, 32, y)
        if y % 2 == 1:
            means = [pooled(a, b) for a, b in zip(last, (main, side))]
            put_pooled(*means, pst_ref, psb_ref, y // 2, y // 2)
        last = (main, side)
        main, side = s_ref[32:64, row(y)].astype(F32), beside(columns, 64 + HALO * y)
        put_cotangent(main, side, gst_ref, gsb_ref, y, y)
    pre_ref[...] = dot(wc_ref[...], pst_ref[...])
    prb_ref[...] = dot(wc_ref[...], psb_ref[...])
    rg_ref[...] = dot(wg_ref[...], gst_ref[...])
    rgb_ref[...] = dot(wg_ref[96:192, :], gsb_ref[...])


def shaped(rows_, lanes_, kind):
    return jax.ShapeDtypeStruct((rows_, lanes_ * COLS), kind)


def scratch(rows_, lanes_, kind):
    return pltpu.VMEM((rows_, lanes_ * COLS), kind)


def own_rows(s, columns, wc, wg, sides):
    half = ROWS // 2
    return pl.pallas_call(
        functools.partial(own_kernel, sides),
        out_shape=(
            shaped(48, half, BF), shaped(96, ROWS, BF), shaped(96, ROWS, BF),
            shaped(96, half, F32), shaped(96, half, F32),
            shaped(192, ROWS, F32), shaped(96, ROWS, F32),
        ),
        scratch_shapes=[scratch(48, half, BF), scratch(96, ROWS, BF)],
        compiler_params=params(),
        cost_estimate=pl.CostEstimate(flops=10**9, bytes_accessed=4 * 10**6, transcendentals=0),
        name="own_rows",
    )(s, columns, wc, wg)


def put_joined(jst_ref, at, jl_ref, to):
    for lo in (0, 48):
        jl_ref[lo : lo + 16, to] = jst_ref[64:80, at]
        jl_ref[lo + 16 : lo + 48, to] = jst_ref[96:128, at]
        jl_ref[128 + lo : 128 + lo + 48, to] = jst_ref[80:128, at]
    for lo in (96, 224):
        jl_ref[lo : lo + 32, to] = jnp.zeros((32, to.stop - to.start), BF)


def put_field(flat_ref, y, plane, value):
    flat_ref[pl.ds(2 * y + plane, C1, stride=2 * ROWS), :] = value


FINE = range(2 * INNER.start, 2 * INNER.stop)


def inner_kernel(
    count,
    pst_ref, jf_ref, gst_ref, pre_ref, prb_ref, rg_ref, rgb_ref, wo_ref, wq_ref,
    out_ref, gf_ref, ro_ref, rq_ref, rf_ref, rc_ref,
    jst_ref, qst_ref, gl_ref, jl_ref, pl_ref, ql_ref,
):
    rows, coarse_rows = len(FINE), len(INNER)
    there = column_masks(count)
    for d in range(3):
        jst_ref[d * 64 : d * 64 + 32, :] = jf_ref[d * 32 : d * 32 + 32, row(FINE.start, rows)]
    for at in INNER:
        values = [
            sum(ref[d * 32 : d * 32 + 32, row(at + d - 1)] for d in range(3)) for ref in (pre_ref, prb_ref)
        ]
        totals = [
            sum(
                ref[lo + d * 32 : lo + d * 32 + 32, row(r + d - 1)]
                for r in (2 * at, 2 * at + 1)
                for d in range(3)
            )
            for ref, lo in ((rg_ref, 96), (rgb_ref, 0))
        ]
        acts, grads = coarse_row(values, totals, (1.0, there))
        for d in range(3):
            for r in (2 * at, 2 * at + 1):
                jst_ref[d * 64 + 32 : d * 64 + 64, row(r - FINE.start)] = acts[d]
            qst_ref[d * 32 : d * 32 + 32, row(at - INNER.start)] = grads[d]
    ro_ref[...] = dot(wo_ref[...], jst_ref[...])
    rq_ref[...] = dot(wq_ref[...], qst_ref[...])

    put_joined(jst_ref, row(0, rows), jl_ref, row(0, rows))
    ql_ref[0:96, :] = jnp.zeros((96, coarse_rows * COLS), BF)
    ql_ref[96:128, :] = qst_ref[32:64, :]
    for ky in range(3):
        gl_ref[ky * 96 : ky * 96 + 96, :] = gst_ref[:, row(FINE.start + 1 - ky, rows)]
        pl_ref[ky * 48 : ky * 48 + 48, :] = pst_ref[:, row(INNER.start + ky - 1, coarse_rows)]
    rf_ref[...] = dot_nt(gl_ref[...], jl_ref[...])
    rc_ref[...] = dot_nt(pl_ref[...], ql_ref[...])

    for y in range(FINE.start + 1, FINE.stop - 1):
        value = sum(ro_ref[d * 32 : d * 32 + 32, row(y - 1 + d - FINE.start)] for d in range(3))
        for z in range(2):
            put_field(out_ref, y, z, value[z * 16 : z * 16 + 16])
    for at in range(INNER.start + 1, INNER.stop - 1):
        coarse = sum(rq_ref[d * 16 : d * 16 + 16, row(at - 1 + d - INNER.start)] for d in range(3))
        coarse = coarse.astype(BF).astype(F32) * 0.125
        for y in (2 * at, 2 * at + 1):
            for z in range(2):
                lo = z * 16
                value = sum(rg_ref[lo + d * 32 : lo + d * 32 + 16, row(y - 1 + d)] for d in range(3))
                put_field(gf_ref, y, z, value + coarse)


def inner_rows(own, wo, wq, count):
    rows, coarse_rows = len(FINE), len(INNER)
    return pl.pallas_call(
        functools.partial(inner_kernel, count),
        out_shape=(
            shaped(CELLS, 1, F32), shaped(CELLS, 1, F32),
            shaped(96, rows, F32), shaped(48, coarse_rows, F32),
            shaped(288, 2, F32), shaped(144, 1, F32),
        ),
        scratch_shapes=[
            scratch(192, rows, BF), scratch(96, coarse_rows, BF),
            scratch(288, rows, BF), scratch(256, rows, BF),
            scratch(144, coarse_rows, BF), scratch(128, coarse_rows, BF),
        ],
        compiler_params=params(),
        cost_estimate=pl.CostEstimate(flops=10**9, bytes_accessed=4 * 10**6, transcendentals=10**5),
        name="inner_rows",
    )(*own, wo, wq)


def rest_kernel(
    counts, sides,
    even_ref, odd_ref,
    pst_own, jf_own, gst_own, pre_own, prb_own, rg_own, rgb_own,
    out_inner, gf_inner, ro_inner, rq_inner, rf_inner, rc_inner,
    wo_ref, wg_ref, wc_ref, wq_ref,
    out_ref, gf_ref, gw_ref,
    halo_ref, jst_ref, gst_ref, gsb_ref, pst_ref, psb_ref, qst_ref,
    pre_ref, prb_ref, rg_ref, rgb_ref, ro_ref, rq_ref, gl_ref, jl_ref, pl_ref, ql_ref, flat_ref,
):
    w = lax.axis_index("wide")
    there = column_masks(counts[1])
    flag = lambda is_there: jnp.where(is_there, 1.0, 0.0)
    has_above, has_below = flag(w > 0), flag(w < counts[0] - 1)

    odd = w % 2
    halo_ref[1 - odd] = even_ref[...]
    inside = flag((w > 0) & (w < counts[0] - 1))
    halo_ref[odd] = (odd_ref[...].astype(F32) * inside).astype(BF)
    columns = [
        [halo_ref[i, :, row(SLOTS + side)].astype(F32) for side in range(sides)] for i in range(2)
    ]

    for i in range(2):
        lane = HALO * (ROWS - HALO) if i == 0 else 0
        for j in range(3):
            main = halo_ref[i, :, row(2 + j)].astype(F32)
            side = beside(columns[i], 64 + lane + HALO * (j + 1 - i))
            put_cotangent(main, side, gst_ref, gsb_ref, 9 * i + j, 3 * i + j)
        gst_ref[:, row(3 + 3 * i, 3)] = gst_own[:, row(13 * i, 3)]
        rg_ref[:, row(3 * i, 3)] = dot(wg_ref[...], gst_ref[:, row(9 * i, 3)])
    rgb_ref[...] = dot(wg_ref[96:192, :], gsb_ref[...])
    for i in range(2):
        lane = HALO * (ROWS - HALO) if i == 0 else 0
        sides_f = [beside(columns[i], lane + HALO * r) for r in range(HALO)]
        near = HALO - 1 if i == 0 else 0
        for j in range(2):
            main = halo_ref[i, j * 16 : j * 16 + 16, row(1)]
            side = pooled(sides_f[2 * j], sides_f[2 * j + 1])
            put_pooled(main, side, pst_ref, psb_ref, 6 * i + j, 2 * i + j)
        pst_ref[:, row(2 + 2 * i, 2)] = pst_own[:, row(6 * i, 2)]
        pre_ref[:, row(2 * i, 2)] = dot(wc_ref[...], pst_ref[:, row(6 * i, 2)])
        put_features(halo_ref[i, :, row(0)].astype(F32), sides_f[near], jst_ref, 64, 5 * i)
        for d in range(3):
            jst_ref[d * 64 : d * 64 + 32, row(1 + 2 * i, 2)] = jf_own[d * 32 : d * 32 + 32, row(14 * i, 2)]
    prb_ref[...] = dot(wc_ref[...], psb_ref[...])

    def part(own, halo, lo, size, at, edge, length):
        if at < edge:
            return halo[lo : lo + size, row(at)]
        if at < edge + length:
            return own[lo : lo + size, row(at - edge)]
        return halo[lo : lo + size, row(at - length)]

    for k, at in enumerate((0, 1, 8, 9)):
        keep = has_above if at == 0 else has_below if at == 9 else 1.0
        values = [
            sum(part(own, halo, d * 32, 32, at + d, 2, 8) for d in range(3))
            for own, halo in ((pre_own, pre_ref), (prb_own, prb_ref))
        ]
        totals = [
            sum(
                part(own, halo, lo + d * 32, 32, r + d, 3, ROWS)
                for r in (2 * at, 2 * at + 1)
                for d in range(3)
            )
            for own, halo, lo in ((rg_own, rg_ref, 96), (rgb_own, rgb_ref, 0))
        ]
        acts, grads = coarse_row(values, totals, (keep, keep * there))
        for d in range(3):
            for r in ((0,), (1, 2), (3, 4), (5,))[k]:
                jst_ref[d * 64 + 32 : d * 64 + 64, row(r)] = acts[d]
            qst_ref[d * 32 : d * 32 + 32, row(k)] = grads[d]

    put_joined(jst_ref, row(1, 4), jl_ref, row(0, 4))
    ql_ref[0:96, :] = jnp.zeros((96, 2 * COLS), BF)
    ql_ref[96:128, :] = qst_ref[32:64, row(1, 2)]
    for i in range(2):
        for ky in range(3):
            gl_ref[ky * 96 : ky * 96 + 96, row(2 * i, 2)] = gst_ref[:, row(4 + 4 * i - ky, 2)]
            pl_ref[ky * 48 : ky * 48 + 48, row(i)] = pst_ref[:, row(1 + 3 * i + ky)]
    rf = rf_inner[...] + dot_nt(gl_ref[...], jl_ref[...])
    rc = rc_inner[...] + dot_nt(pl_ref[...], ql_ref[...])
    ro_ref[...] = dot(wo_ref[...], jst_ref[...])
    rq_ref[...] = dot(wq_ref[...], qst_ref[...])
    fine, coarse = {}, {}
    for ky in range(3):
        for kx in range(3):
            lo = ky * 96 + (2 - kx) * 32
            fine[ky, 0, kx] = rf[lo + 16 : lo + 32, 0:128]
            fine[ky, 1, kx] = rf[lo : lo + 16, 0:128] + rf[lo + 16 : lo + 32, 128:256]
            fine[ky, 2, kx] = rf[lo : lo + 16, 128:256]
            coarse[ky, kx] = rc[ky * 48 + kx * 16 : ky * 48 + kx * 16 + 16] * 0.5
    lane16 = lanes_of((16, COLS))
    order = [(ky, kz, kx) for ky in range(3) for kz in range(3) for kx in range(3)]
    for i in range(16):
        value = jnp.zeros((16, COLS), F32)
        if i < 14:
            value = jnp.where(lane16 < 48, fine[order[i]], value)
        if i < 13:
            value = jnp.where((lane16 >= 48) & (lane16 < 96), fine[order[14 + i]], value)
        if i < 9:
            value = jnp.where(lane16 >= 96, coarse[i // 3, i % 3], value)
        gw_ref[i * 16 : i * 16 + 16, :] = value.astype(BF)

    flat_ref[0] = out_inner[...]
    flat_ref[1] = gf_inner[...]
    for y in (0, 1, 2, 13, 14, 15):
        value = sum(part(ro_inner, ro_ref, d * 32, 32, y + d, 3, len(FINE)) for d in range(3))
        for z in range(2):
            put_field(flat_ref.at[0], y, z, value[z * 16 : z * 16 + 16])
    out_ref[...] = flat_ref[0].astype(BF)

    for at in (0, 1, 6, 7):
        coarse = sum(part(rq_inner, rq_ref, d * 16, 16, at + d, 2, len(INNER)) for d in range(3))
        coarse = coarse.astype(BF).astype(F32) * 0.125
        for y in (2 * at, 2 * at + 1):
            for z in range(2):
                lo = z * 16
                value = sum(part(rg_own, rg_ref, lo + d * 32, 16, y + 2 + d, 3, ROWS) for d in range(3))
                put_field(flat_ref.at[1], y, z, value + coarse)
    gf_ref[...] = flat_ref[1].astype(BF)


def rest(messages, own, inner, matrices, counts, sides):
    return pl.pallas_call(
        functools.partial(rest_kernel, counts, sides),
        out_shape=(
            pltpu.VMEM((CELLS, COLS), BF),
            pltpu.VMEM((CELLS, COLS), BF),
            jax.ShapeDtypeStruct((256, COLS), BF),
        ),
        scratch_shapes=[
            pltpu.VMEM((2, 32, (SLOTS + sides) * COLS), BF),
            scratch(192, 6, BF),
            scratch(96, 12, BF), scratch(96, 6, BF),
            scratch(48, 8, BF), scratch(48, 4, BF),
            scratch(96, 4, BF),
            scratch(96, 4, F32), scratch(96, 4, F32),
            scratch(192, 6, F32), scratch(96, 6, F32),
            scratch(96, 6, F32),
            scratch(48, 4, F32),
            scratch(288, 4, BF), scratch(256, 4, BF), scratch(144, 2, BF), scratch(128, 2, BF),
            pltpu.VMEM((2, CELLS, COLS), F32),
        ],
        compiler_params=params(),
        cost_estimate=pl.CostEstimate(flops=10**9, bytes_accessed=4 * 10**6, transcendentals=10**5),
        name="rest",
    )(*messages, *own, *inner, *matrices)


def add_kernel(parts_ref, copies_ref):
    total = parts_ref[0].astype(F32)
    for i in range(1, parts_ref.shape[0]):
        total = total + parts_ref[i].astype(F32)
    total = total.astype(BF)
    for i in range(parts_ref.shape[0]):
        copies_ref[i] = total


def add_up(parts):
    return pl.pallas_call(
        add_kernel,
        out_shape=jax.ShapeDtypeStruct(parts.shape, BF),
        compiler_params=pltpu.CompilerParams(vmem_limit_bytes=VMEM_LIMIT),
        name="add_up",
    )(parts)


def spread_kernel(
    fine_scale, coarse_scale,
    sum_ref, out_ref, gf_ref,
    out_hbm, gf_hbm, fine_hbm, coarse_hbm,
    fine_ref, coarse_ref, field_sems, weight_sems,
):
    fields = chunks(((out_ref, out_hbm), (gf_ref, gf_hbm)), field_sems, 4)
    weights = chunks(((fine_ref, fine_hbm), (coarse_ref, coarse_hbm)), weight_sems, 3)
    for copies in fields:
        start(copies)
    for i in range(27):
        at = (i if i < 14 else i - 14) * 16
        value = sum_ref[at : at + 16, :].astype(F32)
        if i >= 14:
            value = pltpu.roll(value, 80, 1)
        fine_ref[i * 16 : i * 16 + 16, :] = value[:, 0:48] * fine_scale
        ky, kz, kx = i // 9, i // 3 % 3, i % 3
        if kz == 1:
            at = (ky * 3 + kx) * 16
            value = pltpu.roll(sum_ref[at : at + 16, :].astype(F32), 32, 1)[:, 0:32] * coarse_scale
        else:
            value = jnp.zeros((16, 32), F32)
        coarse_ref[i * 16 : i * 16 + 16, :] = value
        if i % 9 == 8:
            weights[0][ky].start()
            weights[1][ky].start()
    for copies in fields + weights:
        wait(copies)


def spread(total, output, grad_features, fine_scale, coarse_scale):
    return pl.pallas_call(
        functools.partial(spread_kernel, fine_scale, coarse_scale),
        in_specs=[pl.BlockSpec(memory_space=pltpu.VMEM)] * 3,
        out_specs=(pl.BlockSpec(memory_space=pl.ANY),) * 4,
        out_shape=(
            jax.ShapeDtypeStruct((CELLS, COLS), BF),
            jax.ShapeDtypeStruct((CELLS, COLS), BF),
            jax.ShapeDtypeStruct((TAPS, 48), F32),
            jax.ShapeDtypeStruct((TAPS, 32), F32),
        ),
        scratch_shapes=[
            pltpu.VMEM((TAPS, 48), F32),
            pltpu.VMEM((TAPS, 32), F32),
            pltpu.SemaphoreType.DMA((2, 4)),
            pltpu.SemaphoreType.DMA((2, 3)),
        ],
        compiler_params=params(),
        name="spread",
    )(total, output, grad_features)


def matrices_kernel(
    fine_hbm, coarse_hbm, wo_ref, wg_ref, wc_ref, wq_ref,
    fine_ref, coarse_ref, wide_ref, pieces_ref, blocks_ref, sems,
):
    fine_copies, coarse_copies = chunks(((fine_hbm, fine_ref), (coarse_hbm, coarse_ref)), sems, 3)
    start(fine_copies)
    start(coarse_copies)
    lane = lanes_of((C1, COLS))
    wait(fine_copies)
    wide_ref[:, 0:48] = fine_ref[...].astype(F32)
    for ky in range(3):
        for zo in range(2):
            tiles = [jnp.zeros((C1, COLS), F32) for _ in range(2)]
            for kx in range(3):
                at = ((ky * 3 + 1 - zo) * 3 + kx) * 16
                first, second = (wide_ref[at + i : at + i + 16, :] for i in (0, 48))
                both = (first + second).astype(BF).astype(F32)
                piece = jnp.where(lane < 32, pltpu.roll(second, 16, 1), pltpu.roll(both, 16, 1))
                piece = jnp.where(lane < 16, first, jnp.where(lane < 64, piece, 0.0))
                spot = (2 - kx) * 32 + zo * 16
                pieces_ref[2 - ky, spot : spot + 16, :] = piece
                tiles[kx // 2] = tiles[kx // 2] + (pltpu.roll(piece, 64, 1) if kx == 1 else piece)
            spot = ky * 32 + zo * 16
            wo_ref[spot : spot + 16, 0:128] = tiles[0].astype(BF)
            wo_ref[spot : spot + 16, 128:192] = tiles[1][:, 0:64].astype(BF)
    wait(coarse_copies)
    wide_ref[:, 0:32] = coarse_ref[...].astype(F32)
    for ky in range(3):
        total = jnp.zeros((C1, COLS), F32)
        for kx in range(3):
            at = ((ky * 3 + 1) * 3 + kx) * 16
            value = jnp.where(lane < 32, wide_ref[at : at + 16, :], 0.0)
            blocks_ref[ky, kx * 16 : kx * 16 + 16, :] = value
            spot = (2 - kx) * 32
            total = total + (pltpu.roll(value, spot, 1) if spot else value)
        wq_ref[(2 - ky) * 16 : (2 - ky) * 16 + 16, :] = total[:, 0:96].astype(BF)
    for d in range(3):
        turned = jnp.transpose(pieces_ref[d])[0:64, 0:96].astype(BF)
        wg_ref[d * 32 : d * 32 + 32, :] = turned[0:32]
        wg_ref[96 + d * 32 : 96 + d * 32 + 32, :] = turned[32:64]
        wc_ref[d * 32 : d * 32 + 32, :] = jnp.transpose(blocks_ref[d])[0:32, 0:48].astype(BF)


def weight_matrices(coarse_weight, fine_weight):
    fine = jnp.transpose(fine_weight, (2, 3, 4, 0, 1)).reshape(TAPS, 48)
    coarse = jnp.transpose(coarse_weight, (2, 3, 4, 1, 0)).reshape(TAPS, 32)
    shape = lambda *dims: jax.ShapeDtypeStruct(dims, BF)
    return pl.pallas_call(
        matrices_kernel,
        in_specs=[pl.BlockSpec(memory_space=pltpu.HBM)] * 2,
        out_shape=(shape(96, 192), shape(192, 96), shape(96, 48), shape(48, 96)),
        scratch_shapes=[
            pltpu.VMEM((TAPS, 48), BF),
            pltpu.VMEM((TAPS, 32), BF),
            pltpu.VMEM((TAPS, COLS), F32),
            pltpu.VMEM((3, COLS, COLS), F32),
            pltpu.VMEM((3, COLS, COLS), F32),
            pltpu.SemaphoreType.DMA((2, 3)),
        ],
        compiler_params=params(),
        cost_estimate=pl.CostEstimate(flops=10**6, bytes_accessed=10**6, transcendentals=0),
        name="matrices",
    )(kept_in_hbm(fine), kept_in_hbm(coarse))


def beside_blocks(outer, narrow):
    if outer.shape[1] == COLS:
        return lax.ppermute(outer, "narrow", [(0, 1), (1, 0)])
    right = lax.ppermute(outer[:, :COLS], "narrow", [(i + 1, i) for i in range(narrow - 1)])
    left = lax.ppermute(outer[:, COLS:], "narrow", [(i, i + 1) for i in range(narrow - 1)])
    return jnp.concatenate([right, left], 1)


def shards(features, cotangent, coarse_weight, fine_weight):
    wide, narrow = lax.axis_size("wide"), lax.axis_size("narrow")
    sides = 1 if narrow == 2 else 2
    own, strip, to_odd, to_even = pack(features, cotangent, sides)
    both = ("wide", "narrow")
    even_pairs = [pair for i in range(0, wide, 2) for pair in ((i, i + 1), (i + 1, i))]
    odd_pairs = [
        (i * narrow + n, j * narrow + n)
        for i in range(wide)
        for j in (i + 1 if i % 2 else i - 1,)
        if 0 <= j < wide
        for n in range(narrow)
    ]
    odd_pairs += [
        (i * narrow + n, i * narrow + (n ^ 1)) for i in (0, wide - 1) for n in range(narrow)
    ]
    columns = beside_blocks(strip, narrow)
    wo, wg, wc, wq = weight_matrices(coarse_weight, fine_weight)
    with_columns = lambda message: lax.dynamic_update_slice(message, columns, (0, SLOTS * COLS))
    odd = lax.ppermute(with_columns(to_odd), both, odd_pairs)
    even = lax.ppermute(with_columns(to_even), "wide", even_pairs)
    stacks = own_rows(own, columns, wc, wg, sides)
    inner = inner_rows(stacks, wo, wq, narrow)
    output, grad_features, grads = rest(
        (even, odd), stacks, inner, (wo, wg, wc, wq), (wide, narrow), sides
    )
    devices = wide * narrow
    share = -(-256 // devices)
    grads = jnp.pad(grads, ((0, share * devices - 256), (0, 0))).reshape(devices, share, COLS)
    parts = lax.all_to_all(grads, both, 0, 0, tiled=True)
    total = lax.all_to_all(add_up(parts), both, 0, 0, tiled=True)
    total = total.reshape(share * devices, COLS)[:256]
    all_cells = features.shape[1] * features.shape[2] * features.shape[3] * devices
    output, grad_features, grad_fine, grad_coarse = spread(
        total, output, grad_features, 1.0 / math.sqrt(all_cells), 1.0 / math.sqrt(all_cells // 8)
    )
    grad_fine = jnp.transpose(grad_fine.reshape(3, 3, 3, C1, C1 + C2), (3, 4, 0, 1, 2))
    grad_coarse = jnp.transpose(grad_coarse.reshape(3, 3, 3, C1, C2), (4, 3, 0, 1, 2))
    return (
        output.reshape(features.shape),
        grad_features.reshape(features.shape),
        grad_fine,
        grad_coarse,
    )


def solution(mesh):
    placed = P(None, "wide", None, "narrow")
    return jax.shard_map(
        shards,
        mesh=mesh,
        in_specs=(placed, placed, P(), P()),
        out_specs=(placed, placed, P(), P()),
        check_vma=False,
    )
```
